32 devices in a mesh: tensor: 4 (over x, core), expert: 4 (over z), dp: 2 (over y).
Axes of the slice: x: 2, y: 2, z: 4, core: 2. Of those that a mesh axis runs over, the one named last changes fastest.
Arguments:
- tokens: bfloat16 [3152, 768], P(('expert', 'dp')), may hold values from -6 to 6
- routes: int32 [3152, 2], P(('expert', 'dp')), may hold values from 0 to 3, all different within a row; in each aligned block of 394 rows (0 to 393, 394 to 787, ...) at most 288 rows name the same one
- images_live: int32 [8], P(('expert', 'dp')), may hold values from 1 to 2, as said below
- ln1_gain: float32 [768], replicated, may hold values from 0.25 to 1.75
- ln1_bias: float32 [768], replicated, may hold values from -1 to 1
- w_qkv: bfloat16 [768, 3, 768], P(None, None, 'tensor'), may hold values from -0.21875 to 0.21875
- w_out: bfloat16 [768, 768], P('tensor'), may hold values from -1.75 to 1.75
- ln2_gain: float32 [768], replicated, may hold values from 0.25 to 1.75
- ln2_bias: float32 [768], replicated, may hold values from -0.5 to 0.5
- w_router: bfloat16 [768, 4], replicated, may hold values from -0.15625 to 0.15625
- w_up: bfloat16 [4, 768, 3072], P('expert', None, 'tensor'), may hold values from -0.21875 to 0.21875
- w_down: bfloat16 [4, 3072, 768], P('expert', 'tensor'), may hold values from -1.25 to 1.25
- cotangent: bfloat16 [3152, 768], P(('expert', 'dp')), may hold values from -6 to 6
Outputs:
- out: bfloat16 [3152, 768], P(('expert', 'dp'))
- grad_tokens: bfloat16 [3152, 768], P(('expert', 'dp'))
- grad_ln1_gain: float32 [768], replicated
- grad_ln1_bias: float32 [768], replicated
- grad_qkv: float32 [768, 3, 768], P(None, None, 'tensor')
- grad_out: float32 [768, 768], P('tensor')
- grad_ln2_gain: float32 [768], replicated
- grad_ln2_bias: float32 [768], replicated
- grad_router: float32 [768, 4], replicated
- grad_up: float32 [4, 768, 3072], P('expert', 'dp', 'tensor')
- grad_down: float32 [4, 3072, 768], P('expert', 'tensor', 'dp')
The draws below stay inside these ranges and needn't reach their ends.
Inputs may be any that keep to these rules, and one draw needn't show every extreme that they name: `routes`: in each group's 394 rows (aligned blocks) no expert is named by more than 288 rows, a bound that some block reaches. `images_live`: some group holds all 2 images.
All inputs are finite; a program needn't handle non-finite values.
Results may differ from the reference program's by a relative error of at most 0.03.
Values may be sent and summed in bfloat16 or wider, within the bound.
No kernel may reach another device: no remote copies, remote signals or barrier semaphores. Data moves between devices by JAX's collectives and lax.ppermute only.
A program may use at most 128 MiB of HBM per device.

```python
import math
import jax
import jax.numpy as jnp
import numpy as np
from jax import lax

D = 768
HEADS = 12
HEAD_DIM = 64
FF = 3072
SEQ = 197
TOP = 2
SLOTS = 2
EXPERTS = 4
GROUPS = 8
TG = 394
TOKENS = 3152
CAP = 288
N_TENSOR = 4


def draw_images_live(key, part):
    key = jax.random.fold_in(key, 7)
    first_key, second_key = jax.random.split(key)
    counts = jax.random.randint(first_key, (GROUPS,), 1, SLOTS + 1)
    fullest = jax.random.randint(second_key, (), 0, GROUPS)
    return counts.at[fullest].set(SLOTS).astype(jnp.int32)


def level_of(stream_key, dims, cuts, low, top_value):
    level, own = 1.0, jax.random.fold_in(stream_key, 6)
    for dim, shards_of in cuts:
        draws = jnp.exp(jax.random.uniform(jax.random.fold_in(own, dim), (shards_of,), jnp.float32, low / len(cuts), top_value / len(cuts)))
        level = level * jnp.repeat(draws, dims[dim] // shards_of).reshape([-1 if axis == dim else 1 for axis in range(len(dims))])
    return level


def shared_out(own_key, own, number, rows, amount, top, most, lean):
    sequence = jax.random.permutation(own_key, amount)
    heavy_load, ordinary = load_shares(amount, rows * top, most, lean, True), load_shares(amount, rows * top, most, lean, False)
    places = jnp.arange(amount)

    def named(lengths, rotation):
        used = int((lengths > 0).sum())
        fixed = max(1, used // 4)
        moved = fixed + (places - fixed + rotation * (used - fixed)) % max(1, amount - fixed)
        return jnp.zeros((amount,), jnp.int32).at[sequence[jnp.where(places < fixed, places, moved)]].set(jnp.asarray(lengths, jnp.int32))

    lengths = jnp.where(number % 4 == 0, named(heavy_load, number // 4), named(ordinary, number - number // 4 - 1))
    mixed = jax.random.permutation(jax.random.fold_in(own, 3), amount)
    giver, sink = mixed[0:amount // 2 * 2:2], mixed[1:amount // 2 * 2:2]
    room = jnp.minimum(lengths[giver] - 1, most - lengths[sink]) // 2
    room = jnp.where((giver == sequence[0]) | (sink == sequence[0]) | (lengths[sink] == 0), 0, jnp.maximum(room, 0))
    moved = jax.random.randint(jax.random.fold_in(own, 4), (amount // 2,), 0, 1 << 20) % (room + 1)
    lengths = lengths.at[giver].add(-moved).at[sink].add(moved)
    labels = jnp.searchsorted(jnp.cumsum(lengths), jnp.arange(rows * top), side="right").astype(jnp.int32)
    grid = labels.reshape(top, rows).T
    grid = grid[jax.random.permutation(jax.random.fold_in(own, 1), rows)]
    rotation = jax.random.randint(jax.random.fold_in(own, 2), (rows, 1), 0, top)
    return jnp.take_along_axis(grid, (jnp.arange(top)[None, :] + rotation) % top, axis=1)


def load_shares(amount, total, limit, slope, full):
    portions = [(1 << 20) // math.isqrt(grade ** slope) + 1 for grade in range(1, amount + 1)]
    largest = limit if full else min(limit, max(-(-total // amount), total * portions[0] // sum(portions)))
    least = 1 if total - largest >= amount - 1 else 0
    given, spare = [largest] + [least] * (amount - 1), total - largest - least * (amount - 1)
    while spare > 0:
        movable = [i for i in range(1, amount) if given[i] < largest] or [i for i in range(1, amount) if given[i] < limit]
        whole, left = sum([portions[i] for i in movable]), spare
        for i in movable:
            addition = min(limit - given[i], max(1, left * portions[i] // whole), spare)
            given[i] = given[i] + addition
            spare = spare - addition
    return np.array(given)


def bell_draw(rng, extent, width, reach, cuts=(), kind=jnp.bfloat16):
    entries = jax.random.normal(rng, extent, jnp.float32) * width
    if len(cuts) > 0:
        entries = level_of(rng, extent, cuts, -0.22, 0.18) * entries
    return jnp.clip(entries, min=-reach, max=reach).astype(kind)


def setup_inputs(seed: int = 0) -> dict:
    arg_keys = jax.random.split(jax.random.key(seed), 14)
    tokens = bell_draw(arg_keys[0], (TOKENS, D), 1.0, 6.0, ((0, 8),))
    routes_keys = jax.random.split(jax.random.fold_in(arg_keys[1], 1), TOKENS // TG)
    routes_turns = jax.random.permutation(jax.random.fold_in(arg_keys[1], 3), TOKENS // TG)
    routes = jax.vmap(lambda own, number: shared_out(jax.random.fold_in(arg_keys[1], 2), own, number, TG, EXPERTS, TOP, CAP, 2))(routes_keys, routes_turns).reshape((TOKENS, TOP))
    images_live = draw_images_live(jax.random.fold_in(arg_keys[13], 71), 0)
    ln1_gain = jnp.clip(1.0 + 0.15 * jax.random.normal(arg_keys[3], (D,), jnp.float32), 0.25, 1.75)
    ln1_bias = bell_draw(arg_keys[4], (D,), 0.2, 1.0, (), jnp.float32)
    w_qkv = bell_draw(arg_keys[5], (D, 3, D), D ** -0.5, 0.21875, ((2, 4),))
    w_out = bell_draw(arg_keys[6], (D, D), (D // 64) ** -0.5, 1.75, ((0, 4),))
    ln2_gain = jnp.clip(1.0 + 0.15 * jax.random.normal(arg_keys[7], (D,), jnp.float32), 0.25, 1.75)
    ln2_bias = bell_draw(arg_keys[8], (D,), 0.1, 0.5, (), jnp.float32)
    w_router = bell_draw(arg_keys[9], (D, EXPERTS), (2 * D) ** -0.5, 0.15625)
    w_up = bell_draw(arg_keys[10], (EXPERTS, D, FF), D ** -0.5, 0.21875, ((0, 4), (2, 4)))
    w_down = bell_draw(arg_keys[11], (EXPERTS, FF, D), (FF // 128) ** -0.5, 1.25, ((0, 4), (1, 4)))
    cotangent = bell_draw(arg_keys[12], (TOKENS, D), 1.0, 6.0, ((0, 8),))
    return {"tokens": tokens, "routes": routes, "images_live": images_live, "ln1_gain": ln1_gain, "ln1_bias": ln1_bias, "w_qkv": w_qkv, "w_out": w_out, "ln2_gain": ln2_gain, "ln2_bias": ln2_bias, "w_router": w_router, "w_up": w_up, "w_down": w_down, "cotangent": cotangent}


@jax.custom_vjp
def low(v):
    return lax.optimization_barrier(v.astype(jnp.bfloat16)).astype(jnp.float32)

@jax.custom_vjp
def low_back(v):
    return v

def low_keep(v):
    return (low(v), None)

def low_pass(kept, grad):
    return (grad,)

def back_keep(v):
    return (v, None)

def back_low(kept, grad):
    return (low(grad),)
low.defvjp(low_keep, low_pass)
low_back.defvjp(back_keep, back_low)
EPSILON = 1e-06
HIGHEST = lax.Precision.HIGHEST

def layer_norm(values_in, norm_gain, norm_bias):
    row_mean = lax.optimization_barrier(jnp.mean(values_in, axis=-1, keepdims=True))
    centred = values_in - row_mean
    variance = lax.optimization_barrier(jnp.mean(centred * centred, axis=-1, keepdims=True))
    return centred * lax.rsqrt(variance + EPSILON) * norm_gain + norm_bias

def route_slots(route_rows, live_rows, experts, capacity):
    flat_routes = route_rows.reshape(-1)
    alive_rows = jnp.repeat(live_rows, TOP)
    one_hot = (flat_routes[:, None] == jnp.arange(experts, dtype=jnp.int32)[None, :]).astype(jnp.int32) * alive_rows[:, None]
    before = jnp.cumsum(one_hot, axis=0) - one_hot
    slot_index = lax.optimization_barrier(jnp.sum(before * one_hot, axis=1))
    target = jnp.where(alive_rows > 0, flat_routes * capacity + slot_index, experts * capacity).astype(jnp.int32)
    anchor = jnp.arange(flat_routes.shape[0], dtype=jnp.int32) // TOP
    source = jnp.full((experts * capacity + 1,), route_rows.shape[0], jnp.int32).at[target].set(anchor)
    return (target, source[:experts * capacity])

def attend(block):
    query_rows = block[:, 0]
    key_rows = block[:, 1]
    value_rows = block[:, 2]
    scores = jnp.einsum('qhd,khd->hqk', query_rows, key_rows, precision=HIGHEST) * HEAD_DIM ** (-0.5)
    scores = low_back(scores)
    attn_probs = jax.nn.softmax(scores, axis=-1)
    probs_low = low(attn_probs)
    head_out = jnp.einsum('hqk,khd->qhd', probs_low, value_rows, precision=HIGHEST)
    return head_out.reshape(SEQ, HEADS * HEAD_DIM)

def expert_apply(expert_rows, up_weight, down_weight):
    piece_width = FF // N_TENSOR
    summed = jnp.zeros((expert_rows.shape[0], D), jnp.float32)
    for piece_index in range(N_TENSOR):
        taken_rows = low_back(expert_rows)
        lower = piece_index * piece_width
        pre_act = low_back(jnp.dot(taken_rows, up_weight[:, lower:lower + piece_width], precision=HIGHEST))
        hidden = low(jax.nn.gelu(pre_act, approximate=True))
        summed = summed + low(jnp.dot(hidden, down_weight[lower:lower + piece_width], precision=HIGHEST))
    return low_back(summed)

def forward(inputs, gain_one, bias_one, qkv_weight, out_weight, gain_two, bias_two, router_weight, up_weight, down_weight, routes, live_float, target, source):
    normed1 = low(layer_norm(inputs, gain_one, bias_one))
    mixed = jnp.dot(normed1, qkv_weight.reshape(D, 3 * D), precision=HIGHEST)
    mixed = low(low_back(mixed))
    images = mixed.reshape(TOKENS // SEQ, SEQ, 3, HEADS, HEAD_DIM)
    head_out = lax.map(jax.checkpoint(attend), images).reshape(TOKENS, D)
    head_out = low(low_back(head_out))
    branch = low_back(jnp.dot(head_out, out_weight, precision=HIGHEST))
    middle = inputs + branch
    normed2 = low(layer_norm(middle, gain_two, bias_two))
    logits = low_back(jnp.dot(normed2, router_weight, precision=HIGHEST))
    router_probs = jax.nn.softmax(logits, axis=-1)
    picked = (routes[:, :, None] == jnp.arange(EXPERTS, dtype=jnp.int32)[None, None, :]).astype(jnp.float32)
    gate_vals = lax.optimization_barrier(jnp.sum(router_probs[:, None, :] * picked, axis=-1)) * live_float[:, None]
    grouped = normed2.reshape(GROUPS, TG, D)
    padded = jnp.concatenate([grouped, jnp.zeros((GROUPS, 1, D), jnp.float32)], axis=1)
    outgoing = jax.vmap(lambda table_rows, picks: table_rows[picks])(padded, source)
    outgoing = outgoing.reshape(GROUPS, EXPERTS, CAP, D).transpose(1, 0, 2, 3).reshape(EXPERTS, GROUPS * CAP, D)
    expert_block = jax.checkpoint(expert_apply)
    results = lax.map(lambda packed: expert_block(packed[0], packed[1], packed[2]), (outgoing, up_weight, down_weight))
    returned = results.reshape(EXPERTS, GROUPS, CAP, D).transpose(1, 0, 2, 3).reshape(GROUPS, EXPERTS * CAP, D)
    returned = jnp.concatenate([returned, jnp.zeros((GROUPS, 1, D), jnp.float32)], axis=1)
    gathered = jax.vmap(lambda table_rows, picks: table_rows[picks])(returned, target.reshape(GROUPS, TG * TOP))
    gathered = gathered.reshape(TOKENS, TOP, D)
    mixture = lax.optimization_barrier(jnp.sum(gate_vals[:, :, None] * gathered, axis=1))
    return (middle + mixture) * live_float[:, None]

def reference(tokens, routes, images_live, ln1_gain, ln1_bias, w_qkv, w_out, ln2_gain, ln2_bias, w_router, w_up, w_down, cotangent):
    position = jnp.arange(TG, dtype=jnp.int32) // SEQ
    live_rows = (position[None, :] < images_live[:, None]).astype(jnp.int32)
    target, source = jax.vmap(lambda route_rows, alive: route_slots(route_rows, alive, EXPERTS, CAP))(routes.reshape(GROUPS, TG, TOP), live_rows)
    live_float = live_rows.reshape(TOKENS).astype(jnp.float32)

    def run(inputs, gain_one, bias_one, qkv_weight, out_weight, gain_two, bias_two, router_weight, up_weight, down_weight):
        return forward(inputs, gain_one, bias_one, qkv_weight, out_weight, gain_two, bias_two, router_weight, up_weight, down_weight, routes, live_float, target, source)
    floats = (tokens.astype(jnp.float32), ln1_gain.astype(jnp.float32), ln1_bias.astype(jnp.float32), w_qkv.astype(jnp.float32), w_out.astype(jnp.float32), ln2_gain.astype(jnp.float32), ln2_bias.astype(jnp.float32), w_router.astype(jnp.float32), w_up.astype(jnp.float32), w_down.astype(jnp.float32))
    result, pull = jax.vjp(run, *floats)
    grads = pull(cotangent.astype(jnp.float32))
    return (result.astype(jnp.bfloat16), grads[0].astype(jnp.bfloat16), grads[1], grads[2], grads[3], grads[4], grads[5], grads[6], grads[7], grads[8], grads[9])
```

```python
import jax
import jax.numpy as jnp
from jax import lax
from jax.sharding import PartitionSpec as P

HEAD_DIM = 64
SEQ = 197
EPSILON = 1e-06
F32 = jnp.float32
BF16 = jnp.bfloat16


def layer_norm(values_in, norm_gain, norm_bias):
    row_mean = jnp.mean(values_in, axis=-1, keepdims=True)
    centred = values_in - row_mean
    variance = jnp.mean(centred * centred, axis=-1, keepdims=True)
    return centred * lax.rsqrt(variance + EPSILON) * norm_gain + norm_bias


def norm_parts(values_in):
    row_mean = jnp.mean(values_in, axis=-1, keepdims=True)
    centred = values_in - row_mean
    variance = jnp.mean(centred * centred, axis=-1, keepdims=True)
    scale = lax.rsqrt(variance + EPSILON)
    return centred * scale, scale


def norm_back(normed, scale, u):
    return scale * (
        u
        - jnp.mean(u, axis=-1, keepdims=True)
        - normed * jnp.mean(u * normed, axis=-1, keepdims=True)
    )


def dot_f32(left, right):
    return jnp.dot(left, right, preferred_element_type=F32)


def contract_rows(left, right):
    return lax.dot_general(left, right, (((0,), (0,)), ((), ())), preferred_element_type=F32)


def contract_cols(left, right):
    return lax.dot_general(left, right, (((1,), (1,)), ((), ())), preferred_element_type=F32)


def gelu_tanh(values_in):
    return jax.nn.gelu(values_in, approximate=True)


def swap(value, axis, size, mask):
    return lax.ppermute(value, axis, [(i, i ^ mask) for i in range(size)])


def shift(value, axis, size, step):
    return lax.ppermute(value, axis, [(i, (i + step) % size) for i in range(size)])


def exchange(blocks, axis, size):
    if size > 8:
        return lax.all_to_all(blocks, axis, split_axis=0, concat_axis=0, tiled=True)
    me = lax.axis_index(axis)
    got = blocks
    for step in range(1, size):
        sent = lax.dynamic_index_in_dim(blocks, (me + step) % size, 0, keepdims=False)
        came = shift(sent, axis, size, step)
        got = lax.dynamic_update_index_in_dim(got, came, (me - step) % size, 0)
    return got


def sum_scatter(blocks, axis, size):
    if size > 8:
        return lax.psum_scatter(blocks, axis, scatter_dimension=0).astype(F32)
    me = lax.axis_index(axis)
    total = lax.dynamic_index_in_dim(blocks, me, 0, keepdims=False).astype(F32)
    for step in range(1, size):
        sent = lax.dynamic_index_in_dim(blocks, (me + step) % size, 0, keepdims=False)
        total = total + shift(sent, axis, size, step).astype(F32)
    return total


def gather_blocks(block, axis, size):
    if size > 8:
        return lax.all_gather(block, axis)
    me = lax.axis_index(axis)
    got = jnp.zeros((size,) + block.shape, block.dtype)
    got = lax.dynamic_update_index_in_dim(got, block, me, 0)
    for step in range(1, size):
        came = shift(block, axis, size, step)
        got = lax.dynamic_update_index_in_dim(got, came, (me - step) % size, 0)
    return got


def halves(value, which):
    half = value.shape[1] // 2
    first, second = value[:, :half], value[:, half:]
    kept = jnp.where(which == 0, first, second)
    other = jnp.where(which == 0, second, first)
    return kept, other


def join_halves(kept, other, which, axis=1):
    return jnp.where(
        which == 0,
        jnp.concatenate([kept, other], axis=axis),
        jnp.concatenate([other, kept], axis=axis),
    )


def make_body(n_tensor, n_expert, n_dp):
    def all_sum(value):
        rows, cols = value.shape
        dp = lax.axis_index("dp")
        if n_dp == 2:
            half = rows // 2
            first, second = value[:half], value[half:]
            kept = jnp.where(dp == 0, first, second)
            sent = jnp.where(dp == 0, second, first).astype(BF16)
            kept = kept + swap(sent, "dp", 2, 1).astype(F32)
        else:
            kept = value
        blocks = kept.astype(BF16).reshape(n_expert, -1, cols)
        mine = sum_scatter(blocks, "expert", n_expert).astype(BF16)
        whole = gather_blocks(mine, "expert", n_expert).reshape(-1, cols)
        if n_dp == 2:
            whole = join_halves(whole, swap(whole, "dp", 2, 1), dp, axis=0)
        return whole.astype(F32)

    def tensor_sum(value, core):
        kept, other = halves(value, core)
        chip = kept + swap(other.astype(BF16), "tensor", n_tensor, 1).astype(F32)
        low = chip.astype(BF16)
        both = (low.astype(F32) + swap(low, "tensor", n_tensor, 2).astype(F32)).astype(BF16)
        return join_halves(both, swap(both, "tensor", n_tensor, 1), core)

    def body(
        tokens,
        routes,
        images_live,
        ln1_gain,
        ln1_bias,
        w_qkv,
        w_out,
        ln2_gain,
        ln2_bias,
        w_router,
        w_up,
        w_down,
        cotangent,
    ):
        rows_here, width = tokens.shape
        heads_here = w_qkv.shape[2] // HEAD_DIM
        inner = heads_here * HEAD_DIM
        experts = w_router.shape[1]
        capacity = max(2, 3 * rows_here // experts // 8 * 8)
        images_here = rows_here // SEQ
        score_scale = HEAD_DIM ** (-0.5)
        rank = lax.axis_index("tensor")
        core = rank % 2
        owner = lax.axis_index("expert")

        position = jnp.arange(rows_here, dtype=jnp.int32) // SEQ
        live_rows = position < images_live[0]
        live_float = live_rows.astype(F32)[:, None]

        names = jnp.any(
            routes[:, :, None] == jnp.arange(experts, dtype=jnp.int32)[None, None, :], axis=1
        ) & live_rows[:, None]
        names_f = names.astype(BF16)
        earlier = (
            jnp.arange(rows_here)[:, None] > jnp.arange(rows_here)[None, :]
        ).astype(BF16)
        slot = dot_f32(earlier, names_f).astype(jnp.int32)
        slot = jnp.where(names, slot, -1)
        table = (
            slot.T[:, None, :] == jnp.arange(capacity, dtype=jnp.int32)[None, :, None]
        ).astype(BF16).reshape(experts * capacity, rows_here)

        def dispatch(values_low):
            half = width // 2
            mine = lax.dynamic_slice_in_dim(values_low, core * half, half, axis=1)
            packed = dot_f32(table, mine).astype(BF16).reshape(experts, capacity, half)
            got = exchange(packed, "expert", n_expert).reshape(-1, half)
            return join_halves(got, swap(got, "tensor", n_tensor, 1), core)

        def collect(partial):
            kept, other = halves(partial, core)
            chip = kept + swap(other.astype(BF16), "tensor", n_tensor, 1).astype(F32)
            half = width // 2
            back = exchange(
                chip.astype(BF16).reshape(experts, capacity, half), "expert", n_expert
            ).reshape(-1, half)
            low = contract_rows(table, back).astype(BF16)
            both = (low.astype(F32) + swap(low, "tensor", n_tensor, 2).astype(F32)).astype(BF16)
            return join_halves(both, swap(both, "tensor", n_tensor, 1), core).astype(F32)

        d_rows_in = dispatch(cotangent)
        out_pair = swap(w_out, "tensor", n_tensor, 1)
        out_chip = join_halves(w_out, out_pair, core, axis=0)
        out_far = swap(out_chip, "tensor", n_tensor, 2)
        far = rank // 2
        out_full = join_halves(out_chip, out_far, far, axis=0)

        inputs = tokens.astype(F32)
        unit1, scale1 = norm_parts(inputs)
        normed1_low = (unit1 * ln1_gain + ln1_bias).astype(BF16)
        w_mix = w_qkv.reshape(width, 3 * inner)
        mixed = dot_f32(normed1_low, w_mix).astype(BF16)
        images = mixed.reshape(images_here, SEQ, 3, heads_here, HEAD_DIM)
        query_rows = images[:, :, 0]
        key_rows = images[:, :, 1]
        value_rows = images[:, :, 2]
        scores = (
            jnp.einsum("bqhd,bkhd->bhqk", query_rows, key_rows, preferred_element_type=F32)
            * score_scale
        )
        row_max = jnp.max(scores, axis=-1, keepdims=True)
        log_total = row_max + jnp.log(jnp.sum(jnp.exp(scores - row_max), axis=-1, keepdims=True))
        probs = jnp.exp(scores - log_total)
        probs_low = probs.astype(BF16)
        head_out = jnp.einsum("bhqk,bkhd->bqhd", probs_low, value_rows, preferred_element_type=F32)
        head_out = head_out.reshape(rows_here, inner).astype(BF16)

        head_chip = join_halves(head_out, swap(head_out, "tensor", n_tensor, 1), core)
        head_full = join_halves(head_chip, swap(head_chip, "tensor", n_tensor, 2), far)
        middle = inputs + dot_f32(head_full, out_full)
        unit2, scale2 = norm_parts(middle)
        normed2_low = (unit2 * ln2_gain + ln2_bias).astype(BF16)

        rows_in = dispatch(normed2_low)
        logits = dot_f32(rows_in, w_router)
        probs_r = jax.nn.softmax(logits, axis=-1)
        mine = (jnp.arange(experts, dtype=jnp.int32) == owner).astype(F32)[None, :]
        gate = jnp.sum(probs_r * mine, axis=-1, keepdims=True)
        up_here = w_up[0]
        down_here = w_down[0]
        d_rows_f = d_rows_in.astype(F32)
        d_result = (gate * d_rows_f).astype(BF16)
        pre_act = dot_f32(rows_in, up_here)
        hidden, gelu_pull = jax.vjp(gelu_tanh, pre_act)
        hidden = hidden.astype(BF16)
        result = dot_f32(hidden, down_here)
        d_gate = jnp.sum(d_rows_f * result, axis=-1, keepdims=True)
        d_hidden = contract_cols(d_result, down_here)
        d_pre = gelu_pull(d_hidden)[0].astype(BF16)
        d_logits = (d_gate * gate * (mine - probs_r)).astype(BF16)
        d_back = contract_cols(d_pre, up_here) + contract_cols(d_logits, w_router)
        router_part = contract_rows(d_logits, rows_in)

        d_normed2 = collect(d_back)
        d_out = cotangent.astype(F32) * live_float
        gain2_part = jnp.sum(d_normed2 * unit2, axis=0)
        bias2_part = jnp.sum(d_normed2, axis=0)
        d_middle = d_out + norm_back(unit2, scale2, d_normed2 * ln2_gain)
        d_branch = d_middle.astype(BF16)

        d_head = (
            contract_cols(d_branch, w_out)
            .astype(BF16)
            .reshape(images_here, SEQ, heads_here, HEAD_DIM)
        )
        d_probs = jnp.einsum("bqhd,bkhd->bhqk", d_head, value_rows, preferred_element_type=F32)
        grad_value = jnp.einsum("bhqk,bqhd->bkhd", probs_low, d_head, preferred_element_type=F32)
        row_delta = jnp.sum(d_probs * probs, axis=-1, keepdims=True)
        d_scores = (probs * (d_probs - row_delta)).astype(BF16)
        grad_query = (
            jnp.einsum("bhqk,bkhd->bqhd", d_scores, key_rows, preferred_element_type=F32)
            * score_scale
        )
        grad_key = (
            jnp.einsum("bhqk,bqhd->bkhd", d_scores, query_rows, preferred_element_type=F32)
            * score_scale
        )
        d_mixed = jnp.stack([grad_query, grad_key, grad_value], axis=2).astype(BF16)
        d_mixed = d_mixed.reshape(rows_here, 3 * inner)

        grad_qkv = all_sum(contract_rows(normed1_low, d_mixed)).reshape(width, 3, inner)
        d_normed1_part = contract_cols(d_mixed, w_mix)
        gain1_part = jnp.sum(d_normed1_part * unit1, axis=0)
        bias1_part = jnp.sum(d_normed1_part, axis=0)
        d_normed1 = tensor_sum(d_normed1_part, core).astype(F32)
        grad_tokens = (
            d_middle + norm_back(unit1, scale1, d_normed1 * ln1_gain)
        ).astype(BF16)

        grad_out = all_sum(contract_rows(d_branch, head_out)).T

        small = jnp.concatenate(
            [
                jnp.stack([gain1_part, bias1_part, gain2_part * 0.25, bias2_part * 0.25]),
                router_part,
            ],
            axis=0,
        )
        small = small + swap(small, "tensor", n_tensor, 1)
        small = small + swap(small, "tensor", n_tensor, 2)
        if n_expert > 8:
            small = lax.psum(small, ("expert", "dp"))
        else:
            small = small + swap(small, "dp", n_dp, 1)
            small = small + swap(small, "expert", n_expert, 1)
            small = small + swap(small, "expert", n_expert, 2)

        dp = lax.axis_index("dp")
        up_part = contract_rows(rows_in, d_pre)
        down_part = contract_rows(hidden, d_result)
        half = up_part.shape[0] // 2
        up_kept = jnp.where(dp == 0, up_part[:half], up_part[half:])
        up_sent = jnp.where(dp == 0, up_part[half:], up_part[:half]).astype(BF16)
        grad_up = (up_kept + swap(up_sent, "dp", n_dp, 1).astype(F32))[None]
        down_kept, down_sent = halves(down_part, dp)
        grad_down = (down_kept + swap(down_sent.astype(BF16), "dp", n_dp, 1).astype(F32))[None]

        mixture = collect(gate * result)
        out = ((middle + mixture) * live_float).astype(BF16)
        return (
            out,
            grad_tokens,
            small[0],
            small[1],
            grad_qkv,
            grad_out,
            small[2],
            small[3],
            small[4:].T,
            grad_up,
            grad_down,
        )

    return body


def solution(mesh):
    in_specs = (
        P(("expert", "dp"), None),
        P(("expert", "dp"), None),
        P(("expert", "dp")),
        P(),
        P(),
        P(None, None, "tensor"),
        P("tensor", None),
        P(),
        P(),
        P(),
        P("expert", None, "tensor"),
        P("expert", "tensor", None),
        P(("expert", "dp"), None),
    )
    out_specs = (
        P(("expert", "dp"), None),
        P(("expert", "dp"), None),
        P(),
        P(),
        P(None, None, "tensor"),
        P("tensor", None),
        P(),
        P(),
        P(),
        P("expert", "dp", "tensor"),
        P("expert", "tensor", "dp"),
    )
    body = make_body(mesh.shape["tensor"], mesh.shape["expert"], mesh.shape["dp"])
    return jax.shard_map(body, mesh=mesh, in_specs=in_specs, out_specs=out_specs, check_vma=False)
```

```python
import functools

import jax
import jax.numpy as jnp
from jax import lax
from jax.experimental import pallas as pl
from jax.experimental.pallas import tpu as pltpu
from jax.sharding import PartitionSpec as P

HEAD_DIM = 64
SEQ = 197
EPSILON = 1e-06
F32 = jnp.float32
BF16 = jnp.bfloat16
LANES = 128
SMALL = 16


def dot_nn(left, right):
    return lax.dot_general(left, right, (((1,), (0,)), ((), ())), preferred_element_type=F32)


def dot_tn(left, right):
    return lax.dot_general(left, right, (((0,), (0,)), ((), ())), preferred_element_type=F32)


def dot_nt(left, right):
    return lax.dot_general(left, right, (((1,), (1,)), ((), ())), preferred_element_type=F32)


def norm_parts(values_in):
    row_mean = jnp.mean(values_in, axis=-1, keepdims=True)
    centred = values_in - row_mean
    variance = jnp.mean(centred * centred, axis=-1, keepdims=True)
    scale = lax.rsqrt(variance + EPSILON)
    return centred * scale, scale


def norm_back(normed, scale, u):
    return scale * (
        u
        - jnp.mean(u, axis=-1, keepdims=True)
        - normed * jnp.mean(u * normed, axis=-1, keepdims=True)
    )


def iota(shape, dim):
    return lax.broadcasted_iota(jnp.int32, shape, dim)


def head_mask(head, width):
    lane = iota((1, width), 1)
    return ((lane >= head * HEAD_DIM) & (lane < (head + 1) * HEAD_DIM)).astype(BF16)


def image_of(shape, dim, images):
    at = iota(shape, dim)
    image = jnp.zeros(shape, jnp.int32)
    for number in range(1, images):
        image = image + (at >= number * SEQ).astype(jnp.int32)
    return image


T_ID, C_ID, E_ID, D_ID, G_ID, L_ID = range(6)


def plan_kernel(experts, ids, routes, cot, router, table, router_pad, *blocks):
    rows = cot.shape[0]
    cap = table.shape[2]
    picks = routes[...]
    lane = iota((rows, LANES), 1)
    named = picks[:, 0:1] == lane
    for k in range(1, picks.shape[1]):
        named = named | (picks[:, k : k + 1] == lane)
    named = named & (iota((rows, LANES), 0) < ids[L_ID])
    marks = jnp.where(named, 1.0, 0.0).astype(BF16)
    earlier = jnp.where(iota((rows, rows), 0) > iota((rows, rows), 1), 1.0, 0.0).astype(BF16)
    slot = dot_nn(earlier, marks)
    first = (ids[C_ID] * cap).astype(F32)
    slot = jnp.where(named, slot - first, -1.0)
    column = iota((rows, cap), 1).astype(F32)
    for x in range(experts):
        table[x] = jnp.where(slot[:, x : x + 1] == column, 1.0, 0.0).astype(BF16)
    for k in range(experts):
        blocks[k][...] = dot_tn(table[ids[E_ID] ^ k], cot[...]).astype(BF16)
    router_pad[...] = jnp.zeros_like(router_pad)
    router_pad[:experts, :] = router[...]


def attend_kernel(images, tokens, gain, bias, weight, normed, query, key, value, probs, head_out):
    rows = tokens.shape[0]
    inner = query.shape[1]
    heads = inner // HEAD_DIM
    unit, _ = norm_parts(tokens[...].astype(F32))
    normed[...] = (unit * gain[...] + bias[...]).astype(BF16)
    query[...] = dot_nt(normed[...], weight[:inner]).astype(BF16)
    key[...] = dot_nt(normed[...], weight[inner : 2 * inner]).astype(BF16)
    value[...] = dot_nt(normed[...], weight[2 * inner :]).astype(BF16)
    same = image_of((rows, 1), 0, images) == image_of((1, rows), 1, images)
    total = jnp.zeros((rows, inner), F32)
    for head in range(heads):
        mask = head_mask(head, inner)
        scores = dot_nt(query[...] * mask, key[...]) * (HEAD_DIM**-0.5)
        scores = jnp.where(same, scores, -1e30)
        top = jnp.max(scores, axis=-1, keepdims=True)
        weights = jnp.exp(scores - top)
        weights = weights * (1.0 / jnp.sum(weights, axis=-1, keepdims=True))
        probs[head] = weights.astype(BF16)
        total = total + dot_nn(probs[head], value[...] * mask)
    head_out[...] = total.astype(BF16)


def middle_kernel(
    n_tensor, experts, ids, tokens, gain, bias, table, *rest
):
    heads = rest[:n_tensor]
    weights = rest[n_tensor : 2 * n_tensor]
    middle = rest[2 * n_tensor]
    blocks = rest[2 * n_tensor + 1 : 2 * n_tensor + 1 + experts]
    held_heads, held_weights, low = rest[2 * n_tensor + 1 + experts :]
    for j in range(n_tensor):
        held_heads[j] = heads[j][...]
        held_weights[j] = weights[j][...]
    total = tokens[...].astype(F32)
    for rank in range(n_tensor):
        place = ids[T_ID] ^ rank
        total = total + dot_nn(held_heads[place], held_weights[place])
    middle[...] = total
    unit, _ = norm_parts(total)
    low[...] = (unit * gain[...] + bias[...]).astype(BF16)
    for k in range(experts):
        blocks[k][...] = dot_tn(table[ids[E_ID] ^ k], low[...]).astype(BF16)


def expert_kernel(
    experts, ids, rows_in, d_out, up_a, up_b, down_a, down_b, router,
    d_back, gated, d_result, hidden_a, hidden_b, d_pre_a, d_pre_b, router_part,
):
    count = rows_in.shape[0]
    lane = iota((count, LANES), 1)
    logits = dot_nt(rows_in[...], router[...])
    logits = jnp.where(lane < experts, logits, -1e30)
    top = jnp.max(logits, axis=-1, keepdims=True)
    odds = jnp.exp(logits - top)
    odds = odds / jnp.sum(odds, axis=-1, keepdims=True)
    mine = (lane == ids[E_ID]).astype(F32)
    gate = jnp.sum(odds * mine, axis=-1, keepdims=True)
    d_out_f = d_out[...].astype(F32)
    d_result[...] = (gate * d_out_f).astype(BF16)
    result = jnp.zeros(d_out.shape, F32)
    back = jnp.zeros(d_out.shape, F32)
    scale = 0.7978845608028654
    for up, down, hidden, d_pre in (
        (up_a, down_a, hidden_a, d_pre_a),
        (up_b, down_b, hidden_b, d_pre_b),
    ):
        act = dot_nn(rows_in[...], up[...])
        square = act * act
        bend = jnp.tanh(scale * act * (1.0 + 0.044715 * square))
        half = 0.5 * (1.0 + bend)
        hidden[...] = (act * half).astype(BF16)
        slope = half + 0.5 * act * (1.0 - bend * bend) * (
            scale * (1.0 + 3 * 0.044715 * square)
        )
        result = result + dot_nn(hidden[...], down[...])
        d_pre[...] = (dot_nt(d_result[...], down[...]) * slope).astype(BF16)
        back = back + dot_nt(d_pre[...], up[...])
    d_gate = jnp.sum(d_out_f * result, axis=-1, keepdims=True)
    d_logits = (d_gate * gate * (mine - odds)).astype(BF16)
    d_back[...] = (back + dot_nn(d_logits, router[...])).astype(BF16)
    gated[...] = (gate * result).astype(BF16)
    router_part[...] = dot_tn(d_logits, rows_in[...])[: router_part.shape[0]]


def weight_grad_kernel(count, *refs):
    rows = refs[:count]
    d_pre_a = refs[count : 2 * count]
    d_pre_b = refs[2 * count : 3 * count]
    hidden_a = refs[3 * count : 4 * count]
    hidden_b = refs[4 * count : 5 * count]
    d_result = refs[5 * count : 6 * count]
    up_a, up_b, down_a, down_b = refs[6 * count :]
    for out, lefts, rights in (
        (up_b, rows, d_pre_b),
        (down_b, hidden_b, d_result),
        (up_a, rows, d_pre_a),
        (down_a, hidden_a, d_result),
    ):
        total = dot_tn(lefts[0][...], rights[0][...])
        for k in range(1, count):
            total = total + dot_tn(lefts[k][...], rights[k][...])
        out[...] = total.astype(BF16)


def combine_kernel(experts, ids, table, *refs):
    blocks = refs[:experts]
    kept, sent, total = refs[experts:]
    value = dot_nn(table[ids[E_ID]], blocks[0][...])
    for k in range(1, experts):
        value = value + dot_nn(table[ids[E_ID] ^ k], blocks[k][...])
    total[...] = value
    half = kept.shape[1]
    kept[...] = total[:, pl.ds(pl.multiple_of(ids[C_ID] * half, LANES), half)].astype(BF16)
    sent[...] = total[:, pl.ds(pl.multiple_of((1 - ids[C_ID]) * half, LANES), half)].astype(BF16)


def joined(ids, own, other, whole):
    half = own.shape[1]
    whole[:, pl.ds(pl.multiple_of(ids[C_ID] * half, LANES), half)] = own[...].astype(F32)
    whole[:, pl.ds(pl.multiple_of((1 - ids[C_ID]) * half, LANES), half)] = other[...].astype(F32)


def back_kernel(
    blocks_n, ids, own, other, middle, cot, gain, w_out, head_out, normed, query, key, value,
    probs, weight, *rest
):
    d_middle, kept, sent, small = rest[:4]
    blocks = rest[4 : 4 + blocks_n]
    whole, grads = rest[4 + blocks_n :]
    rows, inner = query.shape
    heads = inner // HEAD_DIM
    joined(ids, own, other, whole)
    d_normed = whole[...]
    unit, scale = norm_parts(middle[...])
    small[...] = jnp.zeros_like(small)
    small[2:3, :] = jnp.sum(d_normed * unit, axis=0, keepdims=True)
    small[3:4, :] = jnp.sum(d_normed, axis=0, keepdims=True)
    live = iota((rows, 1), 0) < ids[L_ID]
    d_out = jnp.where(live, cot[...].astype(F32), 0.0)
    d_mid = d_out + norm_back(unit, scale, d_normed * gain[...])
    d_middle[...] = d_mid
    d_branch = d_mid.astype(BF16)
    d_head = dot_nt(d_branch, w_out[...]).astype(BF16)
    grads[3 * inner :, :] = dot_tn(head_out[...], d_branch).astype(BF16)
    d_query = jnp.zeros((rows, inner), F32)
    d_key = jnp.zeros((rows, inner), F32)
    d_value = jnp.zeros((rows, inner), F32)
    for head in range(heads):
        mask = head_mask(head, inner)
        chance = probs[head].astype(F32)
        d_probs = dot_nt(d_head, value[...] * mask)
        delta = jnp.sum(d_probs * chance, axis=-1, keepdims=True)
        d_scores = (chance * (d_probs - delta)).astype(BF16)
        d_value = d_value + dot_tn(probs[head], d_head * mask)
        d_query = d_query + dot_nn(d_scores, key[...] * mask)
        d_key = d_key + dot_tn(d_scores, query[...] * mask)
    d_query = (d_query * (HEAD_DIM**-0.5)).astype(BF16)
    d_key = (d_key * (HEAD_DIM**-0.5)).astype(BF16)
    d_value = d_value.astype(BF16)
    grads[:inner, :] = dot_tn(d_query, normed[...]).astype(BF16)
    grads[inner : 2 * inner, :] = dot_tn(d_key, normed[...]).astype(BF16)
    grads[2 * inner : 3 * inner, :] = dot_tn(d_value, normed[...]).astype(BF16)
    if blocks_n == 1:
        blocks[0][...] = grads[...]
    else:
        size = blocks[0].shape[0]
        for m in range(blocks_n):
            at = pl.multiple_of((ids[G_ID] ^ m) * size, 16)
            blocks[m][...] = grads[pl.ds(at, size), :]
    d_in = dot_nn(d_query, weight[:inner])
    d_in = d_in + dot_nn(d_key, weight[inner : 2 * inner])
    whole[...] = d_in + dot_nn(d_value, weight[2 * inner :])
    half = kept.shape[1]
    kept[...] = whole[:, pl.ds(pl.multiple_of(ids[C_ID] * half, LANES), half)].astype(BF16)
    sent[...] = whole[:, pl.ds(pl.multiple_of((1 - ids[C_ID]) * half, LANES), half)].astype(BF16)


def last_norm_kernel(ids, own, other, tokens, d_middle, gain, small2, router, grad_tokens, small, whole):
    joined(ids, own, other, whole)
    d_normed = whole[...]
    unit, scale = norm_parts(tokens[...].astype(F32))
    small[...] = small2[...]
    small[0:1, :] = jnp.sum(d_normed * unit, axis=0, keepdims=True)
    small[1:2, :] = jnp.sum(d_normed, axis=0, keepdims=True)
    small[8 : 8 + router.shape[0], :] = router[...]
    grad_tokens[...] = (
        d_middle[...] + norm_back(unit, scale, d_normed * gain[...])
    ).astype(BF16)


def sum_kernel(count, small, *refs):
    blocks = refs[:count]
    out = refs[count]
    size = blocks[0].shape[0]
    total = blocks[0][...].astype(F32)
    for m in range(1, count):
        total = total + blocks[m][...].astype(F32)
    out[:size, :] = total.astype(BF16)
    out[size:, :] = small[...].astype(BF16)


def spread_kernel(count, ids, *refs):
    parts = refs[:count]
    grad_qkv, grad_out, small, grads, held = refs[count:]
    size = parts[0].shape[0] - SMALL
    for m in range(count):
        group = ids[G_ID] ^ m
        grads[pl.ds(pl.multiple_of(group * size, 16), size), :] = parts[m][:size, :].astype(F32)
        held[group] = parts[m][size:, :].astype(F32)
    total = held[0]
    for group in range(1, count):
        total = total + held[group]
    small[...] = total
    inner = grad_qkv.shape[0]
    grad_qkv[...] = grads[:inner, :]
    grad_out[...] = grads[inner:, :]


def run(kernel, outs, args, scratch=(), micros=1.0):
    smem = pl.BlockSpec(memory_space=pltpu.SMEM)
    vmem = pl.BlockSpec(memory_space=pltpu.VMEM)
    return pl.pallas_call(
        kernel,
        out_shape=[jax.ShapeDtypeStruct(shape, kind) for shape, kind in outs],
        in_specs=[smem if arg.dtype == jnp.int32 and arg.ndim == 1 else vmem for arg in args],
        out_specs=[vmem] * len(outs),
        scratch_shapes=[pltpu.VMEM(shape, kind) for shape, kind in scratch],
        compiler_params=pltpu.CompilerParams(vmem_limit_bytes=40 * 1024 * 1024),
        cost_estimate=pl.CostEstimate(
            flops=int(micros * 1.15e9), bytes_accessed=1024, transcendentals=0
        ),
    )(*args)


def make_body(n_tensor, n_expert, n_dp):
    groups = n_expert * n_dp
    small_slice = n_expert <= 8

    def tensor_swap(value, mask):
        return lax.ppermute(value, "tensor", [(i, i ^ mask) for i in range(n_tensor)])

    def expert_swap(value, mask):
        return lax.ppermute(value, "expert", [(i, i ^ mask) for i in range(n_expert)])

    def dp_swap(value):
        return lax.ppermute(value, "dp", [(i, i ^ 1) for i in range(n_dp)])

    def group_swap(value, mask):
        pairs = [(i, i ^ mask) for i in range(groups)]
        return lax.ppermute(value, ("expert", "dp"), pairs)

    def exchange(blocks):
        if small_slice:
            return [blocks[0]] + [expert_swap(blocks[k], k) for k in range(1, n_expert)]
        order = jnp.arange(n_expert) ^ lax.axis_index("expert")
        stacked = lax.all_to_all(
            jnp.stack(blocks)[order], "expert", split_axis=0, concat_axis=0, tiled=True
        )[order]
        return [stacked[k] for k in range(n_expert)]

    def tensor_sum(kept, sent):
        chip = (kept.astype(F32) + tensor_swap(sent, 1).astype(F32)).astype(BF16)
        own = (chip.astype(F32) + tensor_swap(chip, 2).astype(F32)).astype(BF16)
        return own, tensor_swap(own, 1)

    def body(
        tokens,
        routes,
        images_live,
        ln1_gain,
        ln1_bias,
        w_qkv,
        w_out,
        ln2_gain,
        ln2_bias,
        w_router,
        w_up,
        w_down,
        cotangent,
    ):
        rows, width = tokens.shape
        inner = w_qkv.shape[2]
        heads = inner // HEAD_DIM
        experts = w_router.shape[1]
        capacity = max(2, 3 * rows // experts // 8 * 8)
        cap = capacity // 2
        images = rows // SEQ
        half = width // 2
        rank = lax.axis_index("tensor")
        owner = lax.axis_index("expert")
        copy = lax.axis_index("dp")
        ids = jnp.stack(
            [
                rank,
                rank % 2,
                owner,
                copy,
                owner * n_dp + copy,
                jnp.minimum(images_live[0] * SEQ, rows),
                rank,
                rank,
            ]
        ).astype(jnp.int32)
        gain1, bias1 = ln1_gain.reshape(1, width), ln1_bias.reshape(1, width)
        gain2, bias2 = ln2_gain.reshape(1, width), ln2_bias.reshape(1, width)
        weight = w_qkv.transpose(1, 2, 0).reshape(3 * inner, width)
        up_a, down_a = w_up[0], w_down[0]

        table, router, *cot_blocks = run(
            functools.partial(plan_kernel, experts),
            [((experts, rows, cap), BF16), ((LANES, width), BF16)]
            + [((cap, width), BF16)] * experts,
            [ids, routes, cotangent, w_router.T],
            micros=3,
        )
        outs = [w_out] + [tensor_swap(w_out, mask) for mask in range(1, n_tensor)]
        d_rows_in = exchange(cot_blocks)
        up_b, down_b = tensor_swap(up_a, 1), tensor_swap(down_a, 1)

        normed, query, key, value, probs, head_out = run(
            functools.partial(attend_kernel, images),
            [((rows, width), BF16)]
            + [((rows, inner), BF16)] * 3
            + [((heads, rows, rows), BF16), ((rows, inner), BF16)],
            [tokens, gain1, bias1, weight],
            micros=8,
        )
        heads_all = [head_out] + [tensor_swap(head_out, mask) for mask in range(1, n_tensor)]
        middle, *row_blocks = run(
            functools.partial(middle_kernel, n_tensor, experts),
            [((rows, width), F32)] + [((cap, width), BF16)] * experts,
            [ids, tokens, gain2, bias2, table] + heads_all + outs,
            scratch=[
                ((n_tensor, rows, inner), BF16),
                ((n_tensor, inner, width), BF16),
                ((rows, width), BF16),
            ],
            micros=4,
        )
        rows_in = exchange(row_blocks)
        if not small_slice:
            rows_in = [jnp.concatenate(rows_in, axis=0)]
            d_rows_in = [jnp.concatenate(d_rows_in, axis=0)]
        part_rows = max(8, -(-experts // 8) * 8)

        worked = []
        for at in range(len(rows_in)):
            count = rows_in[at].shape[0]
            worked.append(
                run(
                    functools.partial(expert_kernel, experts),
                    [((count, width), BF16)] * 3
                    + [((count, up_a.shape[1]), BF16)] * 4
                    + [((part_rows, width), F32)],
                    [ids, rows_in[at], d_rows_in[at], up_a, up_b, down_a, down_b, router],
                    micros=4,
                )
            )
        d_back = [one[0] for one in worked]
        gated = [one[1] for one in worked]
        if not small_slice:
            d_back = list(d_back[0].reshape(experts, cap, width))
            gated = list(gated[0].reshape(experts, cap, width))

        def collect(blocks):
            kept, sent = run(
                functools.partial(combine_kernel, experts),
                [((rows, half), BF16)] * 2,
                [ids, table] + blocks,
                scratch=[((rows, width), F32)],
                micros=2,
            )
            return tensor_sum(kept, sent)

        d_home = exchange(d_back)
        own, other = collect(d_home)

        parts = groups if small_slice else 1
        d_middle, kept1, sent1, small2, *grad_blocks = run(
            functools.partial(back_kernel, parts),
            [((rows, width), F32)]
            + [((rows, half), BF16)] * 2
            + [((SMALL, width), F32)]
            + [((4 * inner // parts, width), BF16)] * parts,
            [
                ids, own, other, middle, cotangent, gain2, w_out, head_out, normed, query, key,
                value, probs, weight,
            ],
            scratch=[((rows, width), F32), ((4 * inner, width), BF16)],
            micros=8,
        )

        router_part = worked[0][7]
        for one in worked[1:]:
            router_part = router_part + one[7]
        router_part = router_part + tensor_swap(router_part, 1)
        router_part = router_part + tensor_swap(router_part, 2)

        count = len(worked)
        fields = [[one[at] for one in worked] for at in (5, 6, 3, 4, 2)]
        up_own, up_pair, down_own, down_pair = run(
            functools.partial(weight_grad_kernel, count),
            [((width, up_a.shape[1]), BF16)] * 2 + [((up_a.shape[1], width), BF16)] * 2,
            rows_in + [one for field in fields for one in field],
            micros=8,
        )
        up_sum = up_own.astype(F32) + tensor_swap(up_pair, 1).astype(F32)
        down_sum = down_own.astype(F32) + tensor_swap(down_pair, 1).astype(F32)
        cut = width // 2
        up_kept = jnp.where(copy == 0, up_sum[:cut], up_sum[cut:])
        up_sent = jnp.where(copy == 0, up_sum[cut:], up_sum[:cut]).astype(BF16)
        down_kept = jnp.where(copy == 0, down_sum[:, :cut], down_sum[:, cut:])
        down_sent = jnp.where(copy == 0, down_sum[:, cut:], down_sum[:, :cut]).astype(BF16)
        grad_up = (up_kept + dp_swap(up_sent).astype(F32))[None]
        grad_down = (down_kept + dp_swap(down_sent).astype(F32))[None]

        gated, d_home = lax.optimization_barrier((gated, d_home))
        mix_own, mix_other = collect(exchange(gated))
        mixture = jnp.where(
            rank % 2 == 0,
            jnp.concatenate([mix_own, mix_other], axis=1),
            jnp.concatenate([mix_other, mix_own], axis=1),
        ).astype(F32)
        alive = (jnp.arange(rows, dtype=jnp.int32) < images_live[0] * SEQ)[:, None]
        out = jnp.where(alive, middle + mixture, 0.0).astype(BF16)

        own1, other1 = tensor_sum(kept1, sent1)
        grad_tokens, small = run(
            last_norm_kernel,
            [((rows, width), BF16), ((SMALL, width), F32)]
            if small_slice
            else [((rows, width), BF16), ((8 + part_rows, width), F32)],
            [ids, own1, other1, tokens, d_middle, gain1, small2, router_part]
            if small_slice
            else [
                ids, own1, other1, tokens, d_middle, gain1,
                jnp.zeros((8 + part_rows, width), F32).at[:SMALL].set(small2), router_part,
            ],
            scratch=[((rows, width), F32)],
            micros=3,
        )
        if small_slice:
            arrived = [grad_blocks[0]] + [
                group_swap(grad_blocks[m], m) for m in range(1, groups)
            ]
            size = grad_blocks[0].shape[0]
            (ready,) = run(
                functools.partial(sum_kernel, groups),
                [((size + SMALL, width), BF16)],
                [small] + arrived,
                micros=1,
            )
            everything = [ready] + [group_swap(ready, m) for m in range(1, groups)]
            grad_qkv, grad_out, small_sum = run(
                functools.partial(spread_kernel, groups),
                [((3 * inner, width), F32), ((inner, width), F32), ((SMALL, width), F32)],
                [ids] + everything,
                scratch=[((4 * inner, width), F32), ((groups, SMALL, width), F32)],
                micros=3,
            )
        else:
            grads = lax.psum(grad_blocks[0], ("expert", "dp")).astype(F32)
            grad_qkv, grad_out = grads[: 3 * inner], grads[3 * inner :]
            small_sum = lax.psum(small, ("expert", "dp"))
        return (
            out,
            grad_tokens,
            small_sum[0],
            small_sum[1],
            grad_qkv.reshape(3, inner, width).transpose(2, 0, 1),
            grad_out,
            small_sum[2],
            small_sum[3],
            small_sum[8 : 8 + experts].T,
            grad_up,
            grad_down,
        )

    return body


def solution(mesh):
    in_specs = (
        P(("expert", "dp"), None),
        P(("expert", "dp"), None),
        P(("expert", "dp")),
        P(),
        P(),
        P(None, None, "tensor"),
        P("tensor", None),
        P(),
        P(),
        P(),
        P("expert", None, "tensor"),
        P("expert", "tensor", None),
        P(("expert", "dp"), None),
    )
    out_specs = (
        P(("expert", "dp"), None),
        P(("expert", "dp"), None),
        P(),
        P(),
        P(None, None, "tensor"),
        P("tensor", None),
        P(),
        P(),
        P(),
        P("expert", "dp", "tensor"),
        P("expert", "tensor", "dp"),
    )
    body = make_body(mesh.shape["tensor"], mesh.shape["expert"], mesh.shape["dp"])
    return jax.shard_map(body, mesh=mesh, in_specs=in_specs, out_specs=out_specs, check_vma=False)
```

```python
import functools

import jax
import jax.numpy as jnp
from jax import lax
from jax.experimental import pallas as pl
from jax.experimental.pallas import tpu as pltpu
from jax.sharding import PartitionSpec as P

HEAD_DIM = 64
SEQ = 197
EPSILON = 1e-06
F32 = jnp.float32
BF16 = jnp.bfloat16
LANES = 128
SMALL = 16


def dot_nn(left, right):
    return lax.dot_general(left, right, (((1,), (0,)), ((), ())), preferred_element_type=F32)


def dot_tn(left, right):
    return lax.dot_general(left, right, (((0,), (0,)), ((), ())), preferred_element_type=F32)


def dot_nt(left, right):
    return lax.dot_general(left, right, (((1,), (1,)), ((), ())), preferred_element_type=F32)


def norm_parts(values_in):
    row_mean = jnp.mean(values_in, axis=-1, keepdims=True)
    centred = values_in - row_mean
    variance = jnp.mean(centred * centred, axis=-1, keepdims=True)
    scale = lax.rsqrt(variance + EPSILON)
    return centred * scale, scale


def norm_back(normed, scale, u):
    return scale * (
        u
        - jnp.mean(u, axis=-1, keepdims=True)
        - normed * jnp.mean(u * normed, axis=-1, keepdims=True)
    )


def iota(shape, dim):
    return lax.broadcasted_iota(jnp.int32, shape, dim)


def row_of(vector):
    return vector[...].reshape(1, vector.shape[0])


def head_mask(head, width):
    lane = iota((1, width), 1)
    return ((lane >= head * HEAD_DIM) & (lane < (head + 1) * HEAD_DIM)).astype(BF16)


def image_of(shape, dim, images):
    at = iota(shape, dim)
    image = jnp.zeros(shape, jnp.int32)
    for number in range(1, images):
        image = image + (at >= number * SEQ).astype(jnp.int32)
    return image


T_ID, C_ID, E_ID, D_ID, Q_ID, L_ID = range(6)


def plan_kernel(experts, ids, routes, cot, router, table, router_pad, *blocks):
    rows = cot.shape[0]
    cap = table.shape[1]
    tall = max(16, -(-experts // 16) * 16)
    picks = routes[...]
    expert = iota((tall, rows), 0)
    named = picks[0:1, :] == expert
    for k in range(1, picks.shape[0]):
        named = named | (picks[k : k + 1, :] == expert)
    named = named & (iota((tall, rows), 1) < ids[L_ID])
    marks = jnp.where(named, 1.0, 0.0).astype(BF16)
    earlier = jnp.where(iota((rows, rows), 0) < iota((rows, rows), 1), 1.0, 0.0).astype(BF16)
    slot = dot_nn(marks, earlier)
    first = (ids[C_ID] * cap).astype(F32)
    slot = jnp.where(named, slot - first, -1.0)
    place = iota((cap, rows), 0).astype(F32)
    for x in range(experts):
        table[x] = jnp.where(slot[x : x + 1, :] == place, 1.0, 0.0).astype(BF16)
    for k in range(experts):
        blocks[k][...] = dot_nn(table[ids[E_ID] ^ k], cot[...]).astype(BF16)
    router_pad[...] = jnp.zeros_like(router_pad)
    router_pad[:experts, :] = router[...]


def attend_kernel(images, tokens, gain, bias, weight, normed, query, key, value, probs, head_out):
    rows = tokens.shape[0]
    inner = query.shape[1]
    heads = inner // HEAD_DIM
    unit, _ = norm_parts(tokens[...].astype(F32))
    normed[...] = (unit * row_of(gain) + row_of(bias)).astype(BF16)
    query[...] = dot_nt(normed[...], weight[:inner]).astype(BF16)
    key[...] = dot_nt(normed[...], weight[inner : 2 * inner]).astype(BF16)
    value[...] = dot_nt(normed[...], weight[2 * inner :]).astype(BF16)
    same = image_of((rows, 1), 0, images) == image_of((1, rows), 1, images)
    total = jnp.zeros((rows, inner), F32)
    for head in range(heads):
        mask = head_mask(head, inner)
        scores = dot_nt(query[...] * mask, key[...]) * (HEAD_DIM**-0.5)
        scores = jnp.where(same, scores, -1e30)
        top = jnp.max(scores, axis=-1, keepdims=True)
        weights = jnp.exp(scores - top)
        weights = weights * (1.0 / jnp.sum(weights, axis=-1, keepdims=True))
        probs[head] = weights.astype(BF16)
        total = total + dot_nn(probs[head], value[...] * mask)
    head_out[...] = total.astype(BF16)


def middle_kernel(
    n_tensor, experts, ids, tokens, gain, bias, table, *rest
):
    heads = rest[:n_tensor]
    weights = rest[n_tensor : 2 * n_tensor]
    middle = rest[2 * n_tensor]
    blocks = rest[2 * n_tensor + 1 : 2 * n_tensor + 1 + experts]
    held_heads, held_weights, low = rest[2 * n_tensor + 1 + experts :]
    for j in range(n_tensor):
        held_heads[j] = heads[j][...]
        held_weights[j] = weights[j][...]
    total = tokens[...].astype(F32)
    for rank in range(n_tensor):
        place = ids[T_ID] ^ rank
        total = total + dot_nn(held_heads[place], held_weights[place])
    middle[...] = total
    unit, _ = norm_parts(total)
    low[...] = (unit * row_of(gain) + row_of(bias)).astype(BF16)
    for k in range(experts):
        blocks[k][...] = dot_nn(table[ids[E_ID] ^ k], low[...]).astype(BF16)


def expert_kernel(experts, number, ids, up_a, up_b, down_a, down_b, router, *refs):
    row_blocks, out_blocks = refs[:number], refs[number : 2 * number]
    refs = refs[2 * number :]
    back_blocks, gated_blocks = refs[:number], refs[number : 2 * number]
    rows_in, d_result, hidden_a, hidden_b, d_pre_a, d_pre_b, router_part, d_out = refs[2 * number :]
    size = row_blocks[0].shape[0]
    count = size * number
    for k in range(number):
        rows_in[k * size : (k + 1) * size, :] = row_blocks[k][...]
        d_out[k * size : (k + 1) * size, :] = out_blocks[k][...].astype(F32)
    lane = iota((count, LANES), 1)
    logits = dot_nt(rows_in[...], router[...])
    logits = jnp.where(lane < experts, logits, -1e30)
    top = jnp.max(logits, axis=-1, keepdims=True)
    odds = jnp.exp(logits - top)
    odds = odds / jnp.sum(odds, axis=-1, keepdims=True)
    mine = (lane == ids[E_ID]).astype(F32)
    gate = jnp.sum(odds * mine, axis=-1, keepdims=True)
    d_result[...] = (gate * d_out[...]).astype(BF16)
    result = jnp.zeros(d_out.shape, F32)
    back = jnp.zeros(d_out.shape, F32)
    scale = 0.7978845608028654
    for up, down, hidden, d_pre in (
        (up_a, down_a, hidden_a, d_pre_a),
        (up_b, down_b, hidden_b, d_pre_b),
    ):
        act = dot_nn(rows_in[...], up[...])
        square = act * act
        bend = jnp.tanh(scale * act * (1.0 + 0.044715 * square))
        half = 0.5 * (1.0 + bend)
        hidden[...] = (act * half).astype(BF16)
        slope = half + 0.5 * act * (1.0 - bend * bend) * (
            scale * (1.0 + 3 * 0.044715 * square)
        )
        result = result + dot_nn(hidden[...], down[...])
        d_pre[...] = (dot_nt(d_result[...], down[...]) * slope).astype(BF16)
        back = back + dot_nt(d_pre[...], up[...])
    d_gate = jnp.sum(d_out[...] * result, axis=-1, keepdims=True)
    d_logits = (d_gate * gate * (mine - odds)).astype(BF16)
    back = (back + dot_nn(d_logits, router[...])).astype(BF16)
    gated = (gate * result).astype(BF16)
    for k in range(number):
        back_blocks[k][...] = back[k * size : (k + 1) * size, :]
        gated_blocks[k][...] = gated[k * size : (k + 1) * size, :]
    router_part[...] = dot_tn(d_logits, rows_in[...])[: router_part.shape[0]]


def weight_grad_kernel(count, *refs):
    rows = refs[:count]
    d_pre_a = refs[count : 2 * count]
    d_pre_b = refs[2 * count : 3 * count]
    hidden_a = refs[3 * count : 4 * count]
    hidden_b = refs[4 * count : 5 * count]
    d_result = refs[5 * count : 6 * count]
    own, pair = refs[6 * count :]
    width = own.shape[0] // 2
    for out, at, lefts, rights in (
        (pair, 0, rows, d_pre_b),
        (pair, width, hidden_b, d_result),
        (own, 0, rows, d_pre_a),
        (own, width, hidden_a, d_result),
    ):
        total = dot_tn(lefts[0][...], rights[0][...])
        for k in range(1, count):
            total = total + dot_tn(lefts[k][...], rights[k][...])
        out[at : at + width, :] = total.astype(BF16)


def split_grad_kernel(ids, own, came, kept, sent, total):
    total[...] = own[...].astype(F32) + came[...].astype(F32)
    width = own.shape[1]
    half = width // 2
    for out, which in ((kept, ids[D_ID]), (sent, 1 - ids[D_ID])):
        out[:half, :] = total[pl.ds(pl.multiple_of(which * half, 16), half), :].astype(out.dtype)
        column = pl.ds(pl.multiple_of(which * half, LANES), half)
        out[half:, :half] = total[width : width + half, column].astype(out.dtype)
        out[half:, half:] = total[width + half :, column].astype(out.dtype)


def join_grad_kernel(kept, came, grad_up, grad_down):
    half = kept.shape[1] // 2
    grad_up[...] = kept[:half, :] + came[:half, :].astype(F32)
    grad_down[:half, :] = kept[half:, :half] + came[half:, :half].astype(F32)
    grad_down[half:, :] = kept[half:, half:] + came[half:, half:].astype(F32)


def combine_kernel(experts, parts, base, ids, table, *refs):
    blocks = refs[:experts]
    routers = refs[experts : experts + parts]
    kept, sent, total = refs[experts + parts :]
    value = dot_tn(table[ids[E_ID]], blocks[0][...])
    for k in range(1, experts):
        value = value + dot_tn(table[ids[E_ID] ^ k], blocks[k][...])
    total[...] = jnp.zeros_like(total)
    total[: value.shape[0], :] = value
    if parts:
        added = routers[0][...]
        for k in range(1, parts):
            added = added + routers[k][...]
        total[base : base + added.shape[0], :] = added
    half = kept.shape[1]
    kept[...] = total[:, pl.ds(pl.multiple_of(ids[C_ID] * half, LANES), half)].astype(BF16)
    sent[...] = total[:, pl.ds(pl.multiple_of((1 - ids[C_ID]) * half, LANES), half)].astype(BF16)


def joined(ids, own, other, whole):
    half = own.shape[1]
    whole[:, pl.ds(pl.multiple_of(ids[C_ID] * half, LANES), half)] = own[...].astype(F32)
    whole[:, pl.ds(pl.multiple_of((1 - ids[C_ID]) * half, LANES), half)] = other[...].astype(F32)


def back_kernel(
    blocks_n, ids, own, other, middle, cot, gain, w_out, head_out, normed, query, key, value,
    probs, weight, *rest
):
    d_middle, kept, sent, small = rest[:4]
    blocks = rest[4 : 4 + blocks_n]
    whole, grads = rest[4 + blocks_n :]
    rows, inner = query.shape
    heads = inner // HEAD_DIM
    joined(ids, own, other, whole)
    d_normed = whole[:rows, :]
    unit, scale = norm_parts(middle[...])
    small[...] = jnp.zeros_like(small)
    base = -(-rows // 16) * 16
    small[8:, :] = whole[base : base + small.shape[0] - 8, :]
    small[2:3, :] = jnp.sum(d_normed * unit, axis=0, keepdims=True)
    small[3:4, :] = jnp.sum(d_normed, axis=0, keepdims=True)
    live = iota((rows, 1), 0) < ids[L_ID]
    d_out = jnp.where(live, cot[...].astype(F32), 0.0)
    d_mid = d_out + norm_back(unit, scale, d_normed * row_of(gain))
    d_middle[...] = d_mid
    d_branch = d_mid.astype(BF16)
    d_head = dot_nt(d_branch, w_out[...]).astype(BF16)
    grads[3 * inner :, :] = dot_tn(head_out[...], d_branch).astype(BF16)
    d_query = jnp.zeros((rows, inner), F32)
    d_key = jnp.zeros((rows, inner), F32)
    d_value = jnp.zeros((rows, inner), F32)
    for head in range(heads):
        mask = head_mask(head, inner)
        chance = probs[head].astype(F32)
        d_probs = dot_nt(d_head, value[...] * mask)
        delta = jnp.sum(d_probs * chance, axis=-1, keepdims=True)
        d_scores = (chance * (d_probs - delta)).astype(BF16)
        d_value = d_value + dot_tn(probs[head], d_head * mask)
        d_query = d_query + dot_nn(d_scores, key[...] * mask)
        d_key = d_key + dot_tn(d_scores, query[...] * mask)
    d_query = (d_query * (HEAD_DIM**-0.5)).astype(BF16)
    d_key = (d_key * (HEAD_DIM**-0.5)).astype(BF16)
    d_value = d_value.astype(BF16)
    grads[:inner, :] = dot_tn(d_query, normed[...]).astype(BF16)
    grads[inner : 2 * inner, :] = dot_tn(d_key, normed[...]).astype(BF16)
    grads[2 * inner : 3 * inner, :] = dot_tn(d_value, normed[...]).astype(BF16)
    if blocks_n == 1:
        blocks[0][...] = grads[...]
    else:
        size = blocks[0].shape[0]
        for m in range(blocks_n):
            at = pl.multiple_of((ids[Q_ID] ^ m) * size, 16)
            blocks[m][...] = grads[pl.ds(at, size), :]
    d_in = dot_nn(d_query, weight[:inner])
    d_in = d_in + dot_nn(d_key, weight[inner : 2 * inner])
    whole[:rows, :] = d_in + dot_nn(d_value, weight[2 * inner :])
    half = kept.shape[1]
    kept[...] = whole[:rows, pl.ds(pl.multiple_of(ids[C_ID] * half, LANES), half)].astype(BF16)
    sent[...] = whole[:rows, pl.ds(pl.multiple_of((1 - ids[C_ID]) * half, LANES), half)].astype(BF16)


def last_norm_kernel(ids, own, other, tokens, d_middle, gain, small2, grad_tokens, small, whole):
    joined(ids, own, other, whole)
    d_normed = whole[...]
    unit, scale = norm_parts(tokens[...].astype(F32))
    small[...] = small2[...]
    small[0:1, :] = jnp.sum(d_normed * unit, axis=0, keepdims=True)
    small[1:2, :] = jnp.sum(d_normed, axis=0, keepdims=True)
    grad_tokens[...] = (
        d_middle[...] + norm_back(unit, scale, d_normed * row_of(gain))
    ).astype(BF16)


def sum_kernel(count, *refs):
    total = refs[0][...].astype(F32)
    for m in range(1, count):
        total = total + refs[m][...].astype(F32)
    refs[count][...] = total.astype(BF16)


def pair_kernel(own, came, small, small_came, out):
    size = own.shape[0]
    out[:size, :] = (own[...].astype(F32) + came[...].astype(F32)).astype(BF16)
    out[size:, :] = (small[...] + small_came[...]).astype(BF16)


def spread_kernel(count, ids, *refs):
    parts = refs[:count]
    grad_qkv, grad_out, small, grads, held = refs[count:]
    size = grads.shape[0] // count
    for m in range(count):
        quarter = ids[Q_ID] ^ m
        grads[pl.ds(pl.multiple_of(quarter * size, 16), size), :] = parts[m][:size, :].astype(F32)
        held[quarter] = parts[m][size:, :].astype(F32)
    total = held[0]
    for quarter in range(1, count):
        total = total + held[quarter]
    small[...] = total
    inner = grad_qkv.shape[0]
    grad_qkv[...] = grads[:inner, :]
    grad_out[...] = grads[inner:, :]


def after(value, *others):
    return lax.optimization_barrier((value,) + others)[0]


def run(kernel, outs, args, scratch=(), micros=1.0, limit=16):
    smem = pl.BlockSpec(memory_space=pltpu.SMEM)
    vmem = pl.BlockSpec(memory_space=pltpu.VMEM)
    return pl.pallas_call(
        kernel,
        out_shape=[jax.ShapeDtypeStruct(shape, kind) for shape, kind in outs],
        in_specs=[smem if arg.dtype == jnp.int32 and arg.ndim == 1 else vmem for arg in args],
        out_specs=[vmem] * len(outs),
        scratch_shapes=[pltpu.VMEM(shape, kind) for shape, kind in scratch],
        compiler_params=pltpu.CompilerParams(vmem_limit_bytes=limit * 1024 * 1024),
        cost_estimate=pl.CostEstimate(
            flops=int(micros * 1.15e9), bytes_accessed=1024, transcendentals=0
        ),
    )(*args)


def make_body(n_tensor, n_expert, n_dp):
    small_slice = n_expert == 4 and n_dp == 2

    def tensor_swap(value, mask):
        return lax.ppermute(value, "tensor", [(i, i ^ mask) for i in range(n_tensor)])

    def expert_swap(value, mask):
        return lax.ppermute(value, "expert", [(i, i ^ mask) for i in range(n_expert)])

    def dp_swap(value):
        return lax.ppermute(value, "dp", [(i, i ^ 1) for i in range(n_dp)])

    def quarter_swap(value, mask):
        pairs = [(i, i ^ mask) for i in range(n_expert * n_dp)]
        return lax.ppermute(value, ("expert", "dp"), pairs)

    def exchange(blocks):
        if small_slice:
            came = {k: expert_swap(blocks[k], k) for k in (3, 2, 1)}
            return [blocks[0]] + [came[k] for k in range(1, n_expert)]
        order = jnp.arange(n_expert) ^ lax.axis_index("expert")
        stacked = lax.all_to_all(
            jnp.stack(blocks)[order], "expert", split_axis=0, concat_axis=0, tiled=True
        )[order]
        return [stacked[k] for k in range(n_expert)]

    def tensor_sum(kept, sent):
        chip = (kept.astype(F32) + tensor_swap(sent, 1).astype(F32)).astype(BF16)
        own = (chip.astype(F32) + tensor_swap(chip, 2).astype(F32)).astype(BF16)
        return own, tensor_swap(own, 1)

    def body(
        tokens,
        routes,
        images_live,
        ln1_gain,
        ln1_bias,
        w_qkv,
        w_out,
        ln2_gain,
        ln2_bias,
        w_router,
        w_up,
        w_down,
        cotangent,
    ):
        rows, width = tokens.shape
        inner = w_qkv.shape[2]
        heads = inner // HEAD_DIM
        experts = w_router.shape[1]
        capacity = max(2, 3 * rows // experts // 8 * 8)
        cap = capacity // 2
        images = rows // SEQ
        half = width // 2
        hidden_width = w_up.shape[2]
        rank = lax.axis_index("tensor")
        owner = lax.axis_index("expert")
        copy = lax.axis_index("dp")
        ids = jnp.stack(
            [
                rank,
                rank % 2,
                owner,
                copy,
                (owner % 2) * 2 + copy,
                jnp.minimum(images_live[0] * SEQ, rows),
                rank,
                rank,
            ]
        ).astype(jnp.int32)
        weight = w_qkv.transpose(1, 2, 0).reshape(3 * inner, width)
        up_a, down_a = w_up[0], w_down[0]
        part_rows = max(8, -(-experts // 8) * 8)
        small_rows = 8 + part_rows
        base = -(-rows // 16) * 16
        tall = base + -(-part_rows // 16) * 16

        out_x, out_c = tensor_swap(w_out, 2), tensor_swap(w_out, 1)
        up_b, down_b = tensor_swap(up_a, 1), tensor_swap(down_a, 1)
        table, router, *cot_blocks = run(
            functools.partial(plan_kernel, experts),
            [((experts, cap, rows), BF16), ((LANES, width), BF16)]
            + [((cap, width), BF16)] * experts,
            [ids, routes.T, cotangent, w_router.T],
            micros=3,
        )
        d_rows_in = exchange(cot_blocks)
        normed, query, key, value, probs, head_out = run(
            functools.partial(attend_kernel, images),
            [((rows, width), BF16)]
            + [((rows, inner), BF16)] * 3
            + [((heads, rows, rows), BF16), ((rows, inner), BF16)],
            [after(tokens, table), ln1_gain, ln1_bias, weight],
            micros=4,
        )
        head_out, out_x, up_b, down_b = lax.optimization_barrier((head_out, out_x, up_b, down_b))
        head_x, head_c = tensor_swap(head_out, 2), tensor_swap(head_out, 1)
        out_all = [w_out, out_c, out_x, tensor_swap(out_x, 1)]
        heads_all = [head_out, head_c, head_x, tensor_swap(head_x, 1)]
        middle, *row_blocks = run(
            functools.partial(middle_kernel, n_tensor, experts),
            [((rows, width), F32)] + [((cap, width), BF16)] * experts,
            [ids, tokens, ln2_gain, ln2_bias, table] + heads_all + out_all,
            scratch=[
                ((n_tensor, rows, inner), BF16),
                ((n_tensor, inner, width), BF16),
                ((rows, width), BF16),
            ],
            micros=3,
        )
        rows_in = exchange(row_blocks)

        calls = [(0, 1), (2, 3)] if small_slice else [tuple(range(experts))]
        worked = []
        d_back, gated = [], []
        for call in calls:
            count = cap * len(call)
            results = run(
                functools.partial(expert_kernel, experts, len(call)),
                [((cap, width), BF16)] * (2 * len(call))
                + [((count, width), BF16)] * 2
                + [((count, hidden_width), BF16)] * 4
                + [((part_rows, width), F32)],
                [ids, up_a, up_b, down_a, down_b, router]
                + [rows_in[k] for k in call]
                + [d_rows_in[k] for k in call],
                scratch=[((count, width), F32)],
                micros=7,
            )
            d_back += results[: len(call)]
            gated += results[len(call) : 2 * len(call)]
            worked.append(results[2 * len(call) :])

        def collect(blocks, routers):
            kept, sent = run(
                functools.partial(combine_kernel, experts, len(routers), base),
                [((tall if routers else base, half), BF16)] * 2,
                [ids, table] + blocks + routers,
                scratch=[((tall if routers else base, width), F32)],
                micros=2,
            )
            return tensor_sum(kept, sent)

        d_home = exchange(d_back)

        fields = [[one[at] for one in worked] for at in (0, 4, 5, 2, 3, 1)]
        grad_own, grad_pair = run(
            functools.partial(weight_grad_kernel, len(worked)),
            [((2 * width, hidden_width), BF16)] * 2,
            [one for field in fields for one in field],
            micros=6,
            limit=24,
        )
        grad_kept, grad_sent = run(
            split_grad_kernel,
            [((width, width), F32), ((width, width), BF16)],
            [ids, grad_own, tensor_swap(grad_pair, 1)],
            scratch=[((2 * width, width), F32)],
            micros=2,
            limit=24,
        )
        grad_came = dp_swap(grad_sent)

        d_home = list(lax.optimization_barrier(tuple(d_home) + (grad_sent,))[:-1])
        own, other = collect(d_home, [one[6] for one in worked])

        parts = 4 if small_slice else 1
        d_middle, kept1, sent1, small2, *grad_blocks = run(
            functools.partial(back_kernel, parts),
            [((rows, width), F32)]
            + [((rows, half), BF16)] * 2
            + [((small_rows, width), F32)]
            + [((4 * inner // parts, width), BF16)] * parts,
            [
                ids, own, other, middle, cotangent, ln2_gain, w_out, head_out, normed, query,
                key, value, probs, weight,
            ],
            scratch=[((tall, width), F32), ((4 * inner, width), BF16)],
            micros=6,
        )

        own1, other1 = tensor_sum(kept1, sent1)
        grad_tokens, small = run(
            last_norm_kernel,
            [((rows, width), BF16), ((small_rows, width), F32)],
            [ids, own1, other1, tokens, d_middle, ln1_gain, small2],
            scratch=[((rows, width), F32)],
            micros=2,
        )
        if small_slice:
            arrived = [grad_blocks[0]] + [quarter_swap(grad_blocks[m], m) for m in (1, 2, 3)]
            size = grad_blocks[0].shape[0]
            (summed,) = run(
                functools.partial(sum_kernel, 4), [((size, width), BF16)], arrived, micros=1
            )
            (ready,) = run(
                pair_kernel,
                [((size + small_rows, width), BF16)],
                [summed, expert_swap(summed, 2), small, expert_swap(small, 2)],
                micros=1,
            )
            everything = [ready] + [quarter_swap(ready, m) for m in (1, 2, 3)]
            grad_qkv, grad_out, small_sum = run(
                functools.partial(spread_kernel, 4),
                [((3 * inner, width), F32), ((inner, width), F32), ((small_rows, width), F32)],
                [ids] + everything,
                scratch=[((4 * inner, width), F32), ((4, small_rows, width), F32)],
                micros=3,
            )
        else:
            grads = lax.psum(grad_blocks[0], ("expert", "dp")).astype(F32)
            grad_qkv, grad_out = grads[: 3 * inner], grads[3 * inner :]
            small_sum = lax.psum(small, ("expert", "dp"))

        grad_up, grad_down = run(
            join_grad_kernel,
            [((half, hidden_width), F32), ((hidden_width, half), F32)],
            [after(grad_kept, grad_blocks[0]), grad_came],
            micros=2,
        )

        gated = list(lax.optimization_barrier(tuple(gated) + tuple(d_home))[:experts])
        gated_home = exchange(gated)
        gated_home = list(lax.optimization_barrier(tuple(gated_home) + (d_middle,))[:-1])
        mix_own, mix_other = collect(gated_home, [])
        mixture = jnp.where(
            rank % 2 == 0,
            jnp.concatenate([mix_own, mix_other], axis=1),
            jnp.concatenate([mix_other, mix_own], axis=1),
        )[:rows].astype(F32)
        alive = (jnp.arange(rows, dtype=jnp.int32) < images_live[0] * SEQ)[:, None]
        out = jnp.where(alive, middle + mixture, 0.0).astype(BF16)
        return (
            out,
            grad_tokens,
            small_sum[0],
            small_sum[1],
            grad_qkv.reshape(3, inner, width).transpose(2, 0, 1),
            grad_out,
            small_sum[2],
            small_sum[3],
            small_sum[8 : 8 + experts].T,
            grad_up[None],
            grad_down[None],
        )

    return body


def solution(mesh):
    in_specs = (
        P(("expert", "dp"), None),
        P(("expert", "dp"), None),
        P(("expert", "dp")),
        P(),
        P(),
        P(None, None, "tensor"),
        P("tensor", None),
        P(),
        P(),
        P(),
        P("expert", None, "tensor"),
        P("expert", "tensor", None),
        P(("expert", "dp"), None),
    )
    out_specs = (
        P(("expert", "dp"), None),
        P(("expert", "dp"), None),
        P(),
        P(),
        P(None, None, "tensor"),
        P("tensor", None),
        P(),
        P(),
        P(),
        P("expert", "dp", "tensor"),
        P("expert", "tensor", "dp"),
    )
    body = make_body(mesh.shape["tensor"], mesh.shape["expert"], mesh.shape["dp"])
    return jax.shard_map(body, mesh=mesh, in_specs=in_specs, out_specs=out_specs, check_vma=False)
```

```python
import functools

import jax
import jax.numpy as jnp
from jax import lax
from jax.experimental import pallas as pl
from jax.experimental.pallas import tpu as pltpu
from jax.sharding import PartitionSpec as P

HEAD_DIM = 64
SEQ = 197
EPSILON = 1e-06
F32 = jnp.float32
BF16 = jnp.bfloat16
LANES = 128
SMALL = 16


def dot_nn(left, right):
    return lax.dot_general(left, right, (((1,), (0,)), ((), ())), preferred_element_type=F32)


def dot_tn(left, right):
    return lax.dot_general(left, right, (((0,), (0,)), ((), ())), preferred_element_type=F32)


def dot_nt(left, right):
    return lax.dot_general(left, right, (((1,), (1,)), ((), ())), preferred_element_type=F32)


def norm_parts(values_in):
    row_mean = jnp.mean(values_in, axis=-1, keepdims=True)
    centred = values_in - row_mean
    variance = jnp.mean(centred * centred, axis=-1, keepdims=True)
    scale = lax.rsqrt(variance + EPSILON)
    return centred * scale, scale


def norm_back(normed, scale, u):
    return scale * (
        u
        - jnp.mean(u, axis=-1, keepdims=True)
        - normed * jnp.mean(u * normed, axis=-1, keepdims=True)
    )


def iota(shape, dim):
    return lax.broadcasted_iota(jnp.int32, shape, dim)


def row_of(vector):
    return vector[...].reshape(1, vector.shape[0])


def head_mask(head, width):
    lane = iota((1, width), 1)
    return ((lane >= head * HEAD_DIM) & (lane < (head + 1) * HEAD_DIM)).astype(BF16)


def image_of(shape, dim, images):
    at = iota(shape, dim)
    image = jnp.zeros(shape, jnp.int32)
    for number in range(1, images):
        image = image + (at >= number * SEQ).astype(jnp.int32)
    return image


T_ID, C_ID, E_ID, D_ID, Q_ID, L_ID = range(6)


def plan_kernel(experts, ids, routes, cot, router, table, part, router_pad, *blocks):
    rows = cot.shape[0]
    cap = table.shape[1]
    tall = max(16, -(-experts // 16) * 16)
    picks = routes[...]
    expert = iota((tall, rows), 0)
    named = picks[0:1, :] == expert
    for k in range(1, picks.shape[0]):
        named = named | (picks[k : k + 1, :] == expert)
    named = named & (iota((tall, rows), 1) < ids[L_ID])
    marks = jnp.where(named, 1.0, 0.0).astype(BF16)
    earlier = jnp.where(iota((rows, rows), 0) < iota((rows, rows), 1), 1.0, 0.0).astype(BF16)
    slot = dot_nn(marks, earlier)
    first = (ids[C_ID] * cap).astype(F32)
    slot = jnp.where(named, slot - first, -1.0)
    place = iota((cap, rows), 0).astype(F32)
    for x in range(experts):
        table[x] = jnp.where(slot[x : x + 1, :] == place, 1.0, 0.0).astype(BF16)
    quarter = part.shape[1]
    first = ((ids[T_ID] // 2) * quarter).astype(F32)
    place = iota((quarter, rows), 0).astype(F32) + first
    for x in range(experts):
        part[x] = jnp.where(slot[x : x + 1, :] == place, 1.0, 0.0).astype(BF16)
    for k in range(experts):
        source = table if blocks[k].shape[0] == cap else part
        blocks[k][...] = dot_nn(source[ids[E_ID] ^ k], cot[...]).astype(BF16)
    router_pad[...] = jnp.zeros_like(router_pad)
    router_pad[:experts, :] = router[...]


def attend_kernel(images, tokens, gain, bias, weight, normed, query, key, value, probs, head_out):
    rows = tokens.shape[0]
    inner = query.shape[1]
    heads = inner // HEAD_DIM
    unit, _ = norm_parts(tokens[...].astype(F32))
    normed[...] = (unit * row_of(gain) + row_of(bias)).astype(BF16)
    query[...] = dot_nt(normed[...], weight[:inner]).astype(BF16)
    key[...] = dot_nt(normed[...], weight[inner : 2 * inner]).astype(BF16)
    value[...] = dot_nt(normed[...], weight[2 * inner :]).astype(BF16)
    same = image_of((rows, 1), 0, images) == image_of((1, rows), 1, images)
    total = jnp.zeros((rows, inner), F32)
    for head in range(heads):
        mask = head_mask(head, inner)
        scores = dot_nt(query[...] * mask, key[...]) * (HEAD_DIM**-0.5)
        scores = jnp.where(same, scores, -1e30)
        top = jnp.max(scores, axis=-1, keepdims=True)
        weights = jnp.exp(scores - top)
        weights = weights * (1.0 / jnp.sum(weights, axis=-1, keepdims=True))
        probs[head] = weights.astype(BF16)
        total = total + dot_nn(probs[head], value[...] * mask)
    head_out[...] = total.astype(BF16)


def middle_kernel(
    n_tensor, experts, ids, tokens, gain, bias, table, *rest
):
    heads = rest[:n_tensor]
    weights = rest[n_tensor : 2 * n_tensor]
    middle = rest[2 * n_tensor]
    blocks = rest[2 * n_tensor + 1 : 2 * n_tensor + 1 + experts]
    held_heads, held_weights, low = rest[2 * n_tensor + 1 + experts :]
    for j in range(n_tensor):
        held_heads[j] = heads[j][...]
        held_weights[j] = weights[j][...]
    total = tokens[...].astype(F32)
    for rank in range(n_tensor):
        place = ids[T_ID] ^ rank
        total = total + dot_nn(held_heads[place], held_weights[place])
    middle[...] = total
    unit, _ = norm_parts(total)
    low[...] = (unit * row_of(gain) + row_of(bias)).astype(BF16)
    for k in range(experts):
        blocks[k][...] = dot_nn(table[ids[E_ID] ^ k], low[...]).astype(BF16)


def expert_kernel(
    experts, places, with_grads, ids, up_a, up_b, down_a, down_b, router, pair_out, *refs
):
    number = len(places)
    row_blocks, out_blocks = refs[:number], refs[number : 2 * number]
    refs = refs[2 * number :]
    back_blocks, gated_kept, gated_sent = refs[:number], refs[number], refs[number + 1]
    refs = refs[number + 2 :]
    rows_in, d_result, hidden_a, hidden_b, d_pre_a, d_pre_b, router_part = refs[:7]
    d_out = refs[-1]
    size = row_blocks[0].shape[0]
    count = size * number
    far = ids[T_ID] // 2
    for k in range(number):
        rows_in[k * size : (k + 1) * size, :] = row_blocks[k][...]
        quarter = out_blocks[k].shape[0]
        if quarter == size:
            d_out[k * size : (k + 1) * size, :] = out_blocks[k][...].astype(F32)
        else:
            here = pl.multiple_of(k * size + far * quarter, 8)
            there = pl.multiple_of(k * size + (1 - far) * quarter, 8)
            d_out[pl.ds(here, quarter), :] = out_blocks[k][...].astype(F32)
            d_out[pl.ds(there, quarter), :] = pair_out[places[k] - 1].astype(F32)
    lane = iota((count, LANES), 1)
    logits = dot_nt(rows_in[...], router[...])
    logits = jnp.where(lane < experts, logits, -1e30)
    top = jnp.max(logits, axis=-1, keepdims=True)
    odds = jnp.exp(logits - top)
    odds = odds / jnp.sum(odds, axis=-1, keepdims=True)
    mine = (lane == ids[E_ID]).astype(F32)
    gate = jnp.sum(odds * mine, axis=-1, keepdims=True)
    d_result[...] = (gate * d_out[...]).astype(BF16)
    result = jnp.zeros(d_out.shape, F32)
    back = jnp.zeros(d_out.shape, F32)
    scale = 0.7978845608028654
    for up, down, hidden, d_pre in (
        (up_a, down_a, hidden_a, d_pre_a),
        (up_b, down_b, hidden_b, d_pre_b),
    ):
        act = dot_nn(rows_in[...], up[...])
        square = act * act
        bend = jnp.tanh(scale * act * (1.0 + 0.044715 * square))
        half = 0.5 * (1.0 + bend)
        hidden[...] = (act * half).astype(BF16)
        slope = half + 0.5 * act * (1.0 - bend * bend) * (
            scale * (1.0 + 3 * 0.044715 * square)
        )
        result = result + dot_nn(hidden[...], down[...])
        d_pre[...] = (dot_nt(d_result[...], down[...]) * slope).astype(BF16)
        back = back + dot_nt(d_pre[...], up[...])
    d_gate = jnp.sum(d_out[...] * result, axis=-1, keepdims=True)
    d_logits = (d_gate * gate * (mine - odds)).astype(BF16)
    back = (back + dot_nn(d_logits, router[...])).astype(BF16)
    for k in range(number):
        back_blocks[k][...] = back[k * size : (k + 1) * size, :]
    d_out[...] = gate * result
    quarter = gated_kept.shape[1]
    for k in range(number):
        if quarter == size:
            gated_kept[k] = d_out[k * size : (k + 1) * size, :].astype(BF16)
        else:
            here = pl.multiple_of(k * size + far * quarter, 8)
            there = pl.multiple_of(k * size + (1 - far) * quarter, 8)
            gated_kept[k] = d_out[pl.ds(here, quarter), :].astype(BF16)
            gated_sent[k] = d_out[pl.ds(there, quarter), :].astype(BF16)
    if quarter == size:
        gated_sent[...] = jnp.zeros_like(gated_sent)
    router_part[...] = dot_tn(d_logits, rows_in[...])[: router_part.shape[0]]
    if with_grads:
        own, pair = refs[7:9]
        weight_grads(rows_in, d_pre_a, d_pre_b, hidden_a, hidden_b, d_result, None, None, own, pair)


def weight_grads(
    rows, d_pre_a, d_pre_b, hidden_a, hidden_b, d_result, own_before, pair_before, own, pair
):
    width = own.shape[0] // 2
    for out, before, at, left, right in (
        (pair, pair_before, 0, rows, d_pre_b),
        (pair, pair_before, width, hidden_b, d_result),
        (own, own_before, 0, rows, d_pre_a),
        (own, own_before, width, hidden_a, d_result),
    ):
        total = dot_tn(left[...], right[...])
        if before is not None:
            total = total + before[at : at + width, :].astype(F32)
        out[at : at + width, :] = total.astype(BF16)


def gated_sum_kernel(kept_a, came_a, kept_b, came_b, *blocks):
    for k in range(4):
        kept, came = (kept_a, came_a) if k < 2 else (kept_b, came_b)
        blocks[k][...] = (kept[k % 2].astype(F32) + came[k % 2].astype(F32)).astype(BF16)


def weight_grad_kernel(*refs):
    rows, d_pre_a, d_pre_b, hidden_a, hidden_b, d_result = refs[:6]
    own_before, pair_before = refs[6:8] if len(refs) == 10 else (None, None)
    weight_grads(
        rows, d_pre_a, d_pre_b, hidden_a, hidden_b, d_result, own_before, pair_before, *refs[-2:]
    )


def split_grad_kernel(ids, own, came, kept, sent_first, sent_rest, total, sent):
    total[...] = own[...].astype(F32) + came[...].astype(F32)
    width = own.shape[1]
    half = width // 2
    mine, other = ids[D_ID], 1 - ids[D_ID]
    kept[:half, :] = total[pl.ds(pl.multiple_of(mine * half, 16), half), :]
    sent[:half, :] = total[pl.ds(pl.multiple_of(other * half, 16), half), :].astype(BF16)
    column = pl.ds(pl.multiple_of(mine * half, LANES), half)
    kept[half:, :half] = total[width : width + half, column]
    kept[half:, half:] = total[width + half :, column]
    column = pl.ds(pl.multiple_of(other * half, LANES), half)
    sent[half:, :half] = total[width : width + half, column].astype(BF16)
    sent[half:, half:] = total[width + half :, column].astype(BF16)
    first = sent_first.shape[0]
    sent_first[...] = sent[:first, :]
    sent_rest[...] = sent[first:, :]


def join_grad_kernel(kept, came_first, came_rest, grad_up, grad_down, came):
    first = came_first.shape[0]
    came[:first, :] = came_first[...]
    came[first:, :] = came_rest[...]
    half = kept.shape[1] // 2
    grad_up[...] = kept[:half, :] + came[:half, :].astype(F32)
    grad_down[:half, :] = kept[half:, :half] + came[half:, :half].astype(F32)
    grad_down[half:, :] = kept[half:, half:] + came[half:, half:].astype(F32)


def combine_kernel(experts, parts, base, ids, table, *refs):
    blocks = refs[:experts]
    routers = refs[experts : experts + parts]
    kept, sent, total = refs[experts + parts :]
    value = dot_tn(table[ids[E_ID]], blocks[0][...])
    for k in range(1, experts):
        value = value + dot_tn(table[ids[E_ID] ^ k], blocks[k][...])
    total[...] = jnp.zeros_like(total)
    total[: value.shape[0], :] = value
    if parts:
        added = routers[0][...]
        for k in range(1, parts):
            added = added + routers[k][...]
        total[base : base + added.shape[0], :] = added
    half = kept.shape[1]
    kept[...] = total[:, pl.ds(pl.multiple_of(ids[C_ID] * half, LANES), half)].astype(BF16)
    sent[...] = total[:, pl.ds(pl.multiple_of((1 - ids[C_ID]) * half, LANES), half)].astype(BF16)


def joined(ids, own, other, whole):
    half = own.shape[1]
    whole[:, pl.ds(pl.multiple_of(ids[C_ID] * half, LANES), half)] = own[...].astype(F32)
    whole[:, pl.ds(pl.multiple_of((1 - ids[C_ID]) * half, LANES), half)] = other[...].astype(F32)


def back_kernel(
    blocks_n, ids, own, other, middle, cot, gain, w_out, head_out, normed, query, key, value,
    probs, weight, *rest
):
    d_middle, kept, sent, small = rest[:4]
    blocks = rest[4 : 4 + blocks_n]
    whole, grads = rest[4 + blocks_n :]
    rows, inner = query.shape
    heads = inner // HEAD_DIM
    joined(ids, own, other, whole)
    d_normed = whole[:rows, :]
    unit, scale = norm_parts(middle[...])
    small[...] = jnp.zeros_like(small)
    base = -(-rows // 16) * 16
    small[8:, :] = whole[base : base + small.shape[0] - 8, :]
    small[2:3, :] = jnp.sum(d_normed * unit, axis=0, keepdims=True)
    small[3:4, :] = jnp.sum(d_normed, axis=0, keepdims=True)
    live = iota((rows, 1), 0) < ids[L_ID]
    d_out = jnp.where(live, cot[...].astype(F32), 0.0)
    d_mid = d_out + norm_back(unit, scale, d_normed * row_of(gain))
    d_middle[...] = d_mid
    d_branch = d_mid.astype(BF16)
    d_head = dot_nt(d_branch, w_out[...]).astype(BF16)
    grads[3 * inner :, :] = dot_tn(head_out[...], d_branch).astype(BF16)
    d_query = jnp.zeros((rows, inner), F32)
    d_key = jnp.zeros((rows, inner), F32)
    d_value = jnp.zeros((rows, inner), F32)
    for head in range(heads):
        mask = head_mask(head, inner)
        chance = probs[head].astype(F32)
        d_probs = dot_nt(d_head, value[...] * mask)
        delta = jnp.sum(d_probs * chance, axis=-1, keepdims=True)
        d_scores = (chance * (d_probs - delta)).astype(BF16)
        d_value = d_value + dot_tn(probs[head], d_head * mask)
        d_query = d_query + dot_nn(d_scores, key[...] * mask)
        d_key = d_key + dot_tn(d_scores, query[...] * mask)
    d_query = (d_query * (HEAD_DIM**-0.5)).astype(BF16)
    d_key = (d_key * (HEAD_DIM**-0.5)).astype(BF16)
    d_value = d_value.astype(BF16)
    grads[:inner, :] = dot_tn(d_query, normed[...]).astype(BF16)
    grads[inner : 2 * inner, :] = dot_tn(d_key, normed[...]).astype(BF16)
    grads[2 * inner : 3 * inner, :] = dot_tn(d_value, normed[...]).astype(BF16)
    if blocks_n == 1:
        blocks[0][...] = grads[...]
    else:
        size = blocks[0].shape[0]
        for m in range(blocks_n):
            at = pl.multiple_of((ids[Q_ID] ^ m) * size, 16)
            blocks[m][...] = grads[pl.ds(at, size), :]
    d_in = dot_nn(d_query, weight[:inner])
    d_in = d_in + dot_nn(d_key, weight[inner : 2 * inner])
    whole[:rows, :] = d_in + dot_nn(d_value, weight[2 * inner :])
    half = kept.shape[1]
    kept[...] = whole[:rows, pl.ds(pl.multiple_of(ids[C_ID] * half, LANES), half)].astype(BF16)
    sent[...] = whole[:rows, pl.ds(pl.multiple_of((1 - ids[C_ID]) * half, LANES), half)].astype(BF16)


def last_norm_kernel(ids, own, other, tokens, d_middle, gain, small2, grad_tokens, small, whole):
    joined(ids, own, other, whole)
    d_normed = whole[...]
    unit, scale = norm_parts(tokens[...].astype(F32))
    small[...] = small2[...]
    small[0:1, :] = jnp.sum(d_normed * unit, axis=0, keepdims=True)
    small[1:2, :] = jnp.sum(d_normed, axis=0, keepdims=True)
    grad_tokens[...] = (
        d_middle[...] + norm_back(unit, scale, d_normed * row_of(gain))
    ).astype(BF16)


def sum_kernel(count, *refs):
    size = refs[0].shape[0] // 2
    for half in range(2):
        part = pl.ds(half * size, size)
        total = refs[0][part, :].astype(F32)
        for m in range(1, count):
            total = total + refs[m][part, :].astype(F32)
        refs[count + half][...] = total.astype(BF16)


def pair_kernel(own_a, own_b, came_a, came_b, small, small_came, out):
    size = own_a.shape[0]
    out[:size, :] = (own_a[...].astype(F32) + came_a[...].astype(F32)).astype(BF16)
    out[size : 2 * size, :] = (own_b[...].astype(F32) + came_b[...].astype(F32)).astype(BF16)
    out[2 * size :, :] = (small[...] + small_came[...]).astype(BF16)


def spread_kernel(count, ids, *refs):
    parts = refs[:count]
    grad_qkv, grad_out, gain1, bias1, gain2, bias2, router, grads, held = refs[count:]
    size = grads.shape[0] // count
    for m in range(count):
        quarter = ids[Q_ID] ^ m
        grads[pl.ds(pl.multiple_of(quarter * size, 16), size), :] = parts[m][:size, :].astype(F32)
        held[quarter] = parts[m][size:, :].astype(F32)
    total = held[0]
    for quarter in range(1, count):
        total = total + held[quarter]
    for row, out in enumerate((gain1, bias1, gain2, bias2)):
        out[...] = total[row : row + 1, :].reshape(out.shape)
    router[...] = total[8 : 8 + router.shape[0], :]
    inner = grad_qkv.shape[0]
    grad_qkv[...] = grads[:inner, :]
    grad_out[...] = grads[inner:, :]


def after(value, *others):
    return lax.optimization_barrier((value,) + others)[0]


def run(kernel, outs, args, scratch=(), micros=1.0, limit=16):
    smem = pl.BlockSpec(memory_space=pltpu.SMEM)
    vmem = pl.BlockSpec(memory_space=pltpu.VMEM)
    return pl.pallas_call(
        kernel,
        out_shape=[jax.ShapeDtypeStruct(shape, kind) for shape, kind in outs],
        in_specs=[smem if arg.dtype == jnp.int32 and arg.ndim == 1 else vmem for arg in args],
        out_specs=[vmem] * len(outs),
        scratch_shapes=[pltpu.VMEM(shape, kind) for shape, kind in scratch],
        compiler_params=pltpu.CompilerParams(vmem_limit_bytes=limit * 1024 * 1024),
        cost_estimate=pl.CostEstimate(
            flops=int(micros * 1.15e9), bytes_accessed=1024, transcendentals=0
        ),
    )(*args)


def make_body(n_tensor, n_expert, n_dp):
    small_slice = n_expert == 4 and n_dp == 2

    def tensor_swap(value, mask):
        return lax.ppermute(value, "tensor", [(i, i ^ mask) for i in range(n_tensor)])

    def expert_swap(value, mask):
        return lax.ppermute(value, "expert", [(i, i ^ mask) for i in range(n_expert)])

    def dp_swap(value):
        return lax.ppermute(value, "dp", [(i, i ^ 1) for i in range(n_dp)])

    def quarter_swap(value, mask):
        pairs = [(i, i ^ mask) for i in range(n_expert * n_dp)]
        return lax.ppermute(value, ("expert", "dp"), pairs)

    def exchange(blocks):
        if small_slice:
            came = {k: expert_swap(blocks[k], k) for k in (3, 2, 1)}
            return [blocks[0]] + [came[k] for k in range(1, n_expert)]
        order = jnp.arange(n_expert) ^ lax.axis_index("expert")
        stacked = lax.all_to_all(
            jnp.stack(blocks)[order], "expert", split_axis=0, concat_axis=0, tiled=True
        )[order]
        return [stacked[k] for k in range(n_expert)]

    def body(
        tokens,
        routes,
        images_live,
        ln1_gain,
        ln1_bias,
        w_qkv,
        w_out,
        ln2_gain,
        ln2_bias,
        w_router,
        w_up,
        w_down,
        cotangent,
    ):
        rows, width = tokens.shape
        inner = w_qkv.shape[2]
        heads = inner // HEAD_DIM
        experts = w_router.shape[1]
        capacity = max(2, 3 * rows // experts // 8 * 8)
        cap = capacity // 2
        images = rows // SEQ
        half = width // 2
        hidden_width = w_up.shape[2]
        rank = lax.axis_index("tensor")
        owner = lax.axis_index("expert")
        copy = lax.axis_index("dp")
        ids = jnp.stack(
            [
                rank,
                rank % 2,
                owner,
                copy,
                (owner % 2) * 2 + copy,
                jnp.minimum(images_live[0] * SEQ, rows),
                rank,
                rank,
            ]
        ).astype(jnp.int32)
        weight = w_qkv.transpose(1, 2, 0).reshape(3 * inner, width)
        up_a, down_a = w_up[0], w_down[0]
        part_rows = max(8, -(-experts // 8) * 8)
        small_rows = 8 + part_rows
        base = -(-rows // 16) * 16
        tall = base + -(-part_rows // 16) * 16

        out_x, out_c = tensor_swap(w_out, 2), tensor_swap(w_out, 1)
        up_b, down_b = tensor_swap(up_a, 1), tensor_swap(down_a, 1)
        normed, query, key, value, probs, head_out = run(
            functools.partial(attend_kernel, images),
            [((rows, width), BF16)]
            + [((rows, inner), BF16)] * 3
            + [((heads, rows, rows), BF16), ((rows, inner), BF16)],
            [tokens, ln1_gain, ln1_bias, weight],
            micros=4,
        )
        head_out, out_x, out_c, up_b, down_b = lax.optimization_barrier(
            (head_out, out_x, out_c, up_b, down_b)
        )
        head_x, head_c = tensor_swap(head_out, 2), tensor_swap(head_out, 1)
        quarter = cap // 2
        cot_shapes = [(cap, width)] + [(quarter if small_slice else cap, width)] * (experts - 1)
        table, part, router, *cot_blocks = run(
            functools.partial(plan_kernel, experts),
            [((experts, cap, rows), BF16), ((experts, quarter, rows), BF16)]
            + [((LANES, width), BF16)]
            + [(shape, BF16) for shape in cot_shapes],
            [ids, after(routes.T, head_out), cotangent, w_router.T],
            micros=2,
        )
        head_x = after(head_x, table)
        d_rows_in = exchange(cot_blocks)
        out_all = [w_out, out_c, out_x, tensor_swap(out_x, 1)]
        heads_all = [head_out, head_c, head_x, tensor_swap(head_x, 1)]
        middle, *row_blocks = run(
            functools.partial(middle_kernel, n_tensor, experts),
            [((rows, width), F32)] + [((cap, width), BF16)] * experts,
            [ids, tokens, ln2_gain, ln2_bias, table] + heads_all + out_all,
            scratch=[
                ((n_tensor, rows, inner), BF16),
                ((n_tensor, inner, width), BF16),
                ((rows, width), BF16),
            ],
            micros=3,
        )
        rows_in = exchange(row_blocks)
        middle, *d_rows_in = lax.optimization_barrier((middle, *d_rows_in))
        if small_slice:
            pair_out = tensor_swap(jnp.stack(d_rows_in[1:]), 2)
        else:
            pair_out = router

        calls = [(0, 1), (2, 3)] if small_slice else [tuple(range(experts))]
        worked = []
        d_back, gated = [], []
        for number, call in enumerate(calls):
            count = cap * len(call)
            last = number == len(calls) - 1
            grads = [] if last else [((2 * width, hidden_width), BF16)] * 2
            results = run(
                functools.partial(expert_kernel, experts, call, not last),
                [((cap, width), BF16)] * len(call)
                + [((len(call), quarter if small_slice else cap, width), BF16)] * 2
                + [((count, width), BF16)] * 2
                + [((count, hidden_width), BF16)] * 4
                + [((part_rows, width), F32)]
                + grads,
                [ids, up_a, up_b, down_a, down_b]
                + [after(router, worked[-1][6]) if worked else router, pair_out]
                + [rows_in[k] for k in call]
                + [d_rows_in[k] for k in call],
                scratch=[((count, width), F32)],
                micros=7,
                limit=24,
            )
            d_back += results[: len(call)]
            gated.append(results[len(call) : len(call) + 2])
            worked.append(results[len(call) + 2 :])

        def combine(blocks, spots, routers):
            return run(
                functools.partial(combine_kernel, experts, len(routers), base),
                [((tall if routers else base, half), BF16)] * 2,
                [ids, spots] + blocks + routers,
                scratch=[((tall if routers else base, width), F32)],
                micros=2,
            )

        d_home = exchange(d_back)

        grad_own, grad_pair = run(
            weight_grad_kernel,
            [((2 * width, hidden_width), BF16)] * 2,
            [worked[-1][at] for at in (0, 4, 5, 2, 3, 1)] + list(worked[0][7:]),
            micros=4,
            limit=24,
        )
        third = width // 48 * 16
        grad_kept, sent_first, sent_rest = run(
            split_grad_kernel,
            [((width, width), F32), ((third, width), BF16), ((width - third, width), BF16)],
            [ids, grad_own, tensor_swap(grad_pair, 1)],
            scratch=[((2 * width, width), F32), ((width, width), BF16)],
            micros=2,
            limit=24,
        )

        if small_slice:
            (kept_a, sent_a), (kept_b, sent_b) = gated
            gated_blocks = run(
                gated_sum_kernel,
                [((quarter, width), BF16)] * 4,
                [kept_a, tensor_swap(sent_a, 2), kept_b, tensor_swap(sent_b, 2)],
            )
            spots = part
        else:
            gated_blocks = [gated[0][0][k] for k in range(experts)]
            spots = table

        *d_home, sent_first = lax.optimization_barrier((*d_home, *gated_blocks, sent_first))
        d_home, gated_blocks = d_home[:experts], d_home[experts:]
        kept, sent = combine(list(d_home), table, [one[6] for one in worked])
        chip = (kept.astype(F32) + tensor_swap(sent, 1).astype(F32)).astype(BF16)
        own = (chip.astype(F32) + tensor_swap(chip, 2).astype(F32)).astype(BF16)
        gated_home = exchange(list(gated_blocks))
        came_first = dp_swap(sent_first)
        own, came_first, *gated_home = lax.optimization_barrier((own, came_first, *gated_home))
        other = tensor_swap(own, 1)

        parts = 4 if small_slice else 1
        d_middle, kept1, sent1, small2, *grad_blocks = run(
            functools.partial(back_kernel, parts),
            [((rows, width), F32)]
            + [((rows, half), BF16)] * 2
            + [((small_rows, width), F32)]
            + [((4 * inner // parts, width), BF16)] * parts,
            [
                ids, own, other, middle, cotangent, ln2_gain, w_out, head_out, normed, query,
                key, value, probs, weight,
            ],
            scratch=[((tall, width), F32), ((4 * inner, width), BF16)],
            micros=6,
        )

        *gated_home, _ = lax.optimization_barrier((*gated_home, d_middle))
        kept_y, sent_y = combine(list(gated_home), spots, [])

        if small_slice:
            arrived = [grad_blocks[0]] + [quarter_swap(grad_blocks[m], m) for m in (3, 1, 2)]
            arrived[0], kept_y, sent_y = lax.optimization_barrier((arrived[0], kept_y, sent_y))
            size = grad_blocks[0].shape[0]
            summed_a, summed_b = run(
                functools.partial(sum_kernel, 4), [((size // 2, width), BF16)] * 2, arrived
            )
            sent_rest = after(sent_rest, summed_a)
            came_a = expert_swap(summed_a, 2)
            came_b = expert_swap(after(summed_b, came_a), 2)
        chip_y = (kept_y.astype(F32) + tensor_swap(sent_y, 1).astype(F32)).astype(BF16)
        own_y = (chip_y.astype(F32) + tensor_swap(chip_y, 2).astype(F32)).astype(BF16)

        chip1 = (kept1.astype(F32) + tensor_swap(sent1, 1).astype(F32)).astype(BF16)
        own1 = (chip1.astype(F32) + tensor_swap(chip1, 2).astype(F32)).astype(BF16)
        if small_slice:
            own1 = after(own1, summed_a)
        other1 = tensor_swap(own1, 1)
        grad_tokens, small = run(
            last_norm_kernel,
            [((rows, width), BF16), ((small_rows, width), F32)],
            [ids, own1, other1, tokens, d_middle, ln1_gain, small2],
            scratch=[((rows, width), F32)],
            micros=2,
        )
        if small_slice:
            (ready,) = run(
                pair_kernel,
                [((size + small_rows, width), BF16)],
                [summed_a, summed_b, came_a, came_b, small, expert_swap(small, 2)],
                micros=1,
            )
            own_y, ready = lax.optimization_barrier((own_y, ready))
            everything = [ready] + [quarter_swap(ready, m) for m in (1, 2, 3)]
            grad_qkv, grad_out, *sums, grad_router = run(
                functools.partial(spread_kernel, 4),
                [((3 * inner, width), F32), ((inner, width), F32)]
                + [((width,), F32)] * 4
                + [((experts, width), F32)],
                [ids] + everything,
                scratch=[((4 * inner, width), F32), ((4, small_rows, width), F32)],
                micros=3,
            )
        else:
            grads = lax.psum(grad_blocks[0], ("expert", "dp")).astype(F32)
            grad_qkv, grad_out = grads[: 3 * inner], grads[3 * inner :]
            small_sum = lax.psum(small, ("expert", "dp"))
            sums, grad_router = list(small_sum[:4]), small_sum[8 : 8 + experts]

        grad_up, grad_down = run(
            join_grad_kernel,
            [((half, hidden_width), F32), ((hidden_width, half), F32)],
            [grad_kept, came_first, dp_swap(sent_rest)],
            scratch=[((width, width), BF16)],
            micros=2,
        )

        mix_own, mix_other = own_y, tensor_swap(own_y, 1)
        mixture = jnp.where(
            rank % 2 == 0,
            jnp.concatenate([mix_own, mix_other], axis=1),
            jnp.concatenate([mix_other, mix_own], axis=1),
        )[:rows].astype(F32)
        alive = (jnp.arange(rows, dtype=jnp.int32) < images_live[0] * SEQ)[:, None]
        out = jnp.where(alive, middle + mixture, 0.0).astype(BF16)
        return (
            out,
            grad_tokens,
            sums[0],
            sums[1],
            grad_qkv.reshape(3, inner, width).transpose(2, 0, 1),
            grad_out,
            sums[2],
            sums[3],
            grad_router.T,
            grad_up[None],
            grad_down[None],
        )

    return body


def solution(mesh):
    in_specs = (
        P(("expert", "dp"), None),
        P(("expert", "dp"), None),
        P(("expert", "dp")),
        P(),
        P(),
        P(None, None, "tensor"),
        P("tensor", None),
        P(),
        P(),
        P(),
        P("expert", None, "tensor"),
        P("expert", "tensor", None),
        P(("expert", "dp"), None),
    )
    out_specs = (
        P(("expert", "dp"), None),
        P(("expert", "dp"), None),
        P(),
        P(),
        P(None, None, "tensor"),
        P("tensor", None),
        P(),
        P(),
        P(),
        P("expert", "dp", "tensor"),
        P("expert", "tensor", "dp"),
    )
    body = make_body(mesh.shape["tensor"], mesh.shape["expert"], mesh.shape["dp"])
    return jax.shard_map(body, mesh=mesh, in_specs=in_specs, out_specs=out_specs, check_vma=False)
```

```python
import functools

import jax
import jax.numpy as jnp
from jax import lax
from jax.experimental import pallas as pl
from jax.experimental.pallas import tpu as pltpu
from jax.sharding import PartitionSpec as P

HEAD_DIM = 64
SEQ = 197
EPSILON = 1e-06
F32 = jnp.float32
BF16 = jnp.bfloat16
LANES = 128
SMALL = 16


def dot_nn(left, right):
    return lax.dot_general(left, right, (((1,), (0,)), ((), ())), preferred_element_type=F32)


def dot_tn(left, right):
    return lax.dot_general(left, right, (((0,), (0,)), ((), ())), preferred_element_type=F32)


def dot_nt(left, right):
    return lax.dot_general(left, right, (((1,), (1,)), ((), ())), preferred_element_type=F32)


def norm_parts(values_in):
    row_mean = jnp.mean(values_in, axis=-1, keepdims=True)
    centred = values_in - row_mean
    variance = jnp.mean(centred * centred, axis=-1, keepdims=True)
    scale = lax.rsqrt(variance + EPSILON)
    return centred * scale, scale


def norm_back(normed, scale, u):
    return scale * (
        u
        - jnp.mean(u, axis=-1, keepdims=True)
        - normed * jnp.mean(u * normed, axis=-1, keepdims=True)
    )


def iota(shape, dim):
    return lax.broadcasted_iota(jnp.int32, shape, dim)


def row_of(vector):
    return vector[...].reshape(1, vector.shape[0])


def head_mask(head, width):
    lane = iota((1, width), 1)
    return ((lane >= head * HEAD_DIM) & (lane < (head + 1) * HEAD_DIM)).astype(BF16)


def image_of(shape, dim, images):
    at = iota(shape, dim)
    image = jnp.zeros(shape, jnp.int32)
    for number in range(1, images):
        image = image + (at >= number * SEQ).astype(jnp.int32)
    return image


T_ID, C_ID, E_ID, D_ID, Q_ID, L_ID = range(6)


def plan_kernel(experts, ids, routes, cot, router, table, part, router_pad, *blocks):
    rows = cot.shape[0]
    cap = table.shape[1]
    tall = max(16, -(-experts // 16) * 16)
    picks = routes[...]
    expert = iota((tall, rows), 0)
    named = picks[0:1, :] == expert
    for k in range(1, picks.shape[0]):
        named = named | (picks[k : k + 1, :] == expert)
    named = named & (iota((tall, rows), 1) < ids[L_ID])
    marks = jnp.where(named, 1.0, 0.0).astype(BF16)
    earlier = jnp.where(iota((rows, rows), 0) < iota((rows, rows), 1), 1.0, 0.0).astype(BF16)
    slot = dot_nn(marks, earlier)
    first = (ids[C_ID] * cap).astype(F32)
    slot = jnp.where(named, slot - first, -1.0)
    place = iota((cap, rows), 0).astype(F32)
    for x in range(experts):
        table[x] = jnp.where(slot[x : x + 1, :] == place, 1.0, 0.0).astype(BF16)
    quarter = part.shape[1]
    first = ((ids[T_ID] // 2) * quarter).astype(F32)
    place = iota((quarter, rows), 0).astype(F32) + first
    for x in range(experts):
        part[x] = jnp.where(slot[x : x + 1, :] == place, 1.0, 0.0).astype(BF16)
    for k in range(experts):
        source = table if blocks[k].shape[0] == cap else part
        blocks[k][...] = dot_nn(source[ids[E_ID] ^ k], cot[...]).astype(BF16)
    router_pad[...] = jnp.zeros_like(router_pad)
    router_pad[:experts, :] = router[...]


def attend_kernel(
    images, tokens_far, gain_far, bias_far, weight_far,
    normed, query, key, value, probs, head_out,
    tokens, gain, bias, weight, arrivals,
):
    copies = [
        pltpu.make_async_copy(source, target, arrivals.at[at])
        for at, (source, target) in enumerate(
            ((tokens_far, tokens), (gain_far, gain), (bias_far, bias), (weight_far, weight))
        )
    ]
    for copy in copies:
        copy.start()
    for copy in copies:
        copy.wait()
    rows = tokens.shape[0]
    inner = query.shape[1]
    heads = inner // HEAD_DIM
    unit, _ = norm_parts(tokens[...].astype(F32))
    normed[...] = (unit * row_of(gain) + row_of(bias)).astype(BF16)
    query[...] = dot_nt(normed[...], weight[:inner]).astype(BF16)
    key[...] = dot_nt(normed[...], weight[inner : 2 * inner]).astype(BF16)
    value[...] = dot_nt(normed[...], weight[2 * inner :]).astype(BF16)
    same = image_of((rows, 1), 0, images) == image_of((1, rows), 1, images)
    total = jnp.zeros((rows, inner), F32)
    for head in range(heads):
        mask = head_mask(head, inner)
        scores = dot_nt(query[...] * mask, key[...]) * (HEAD_DIM**-0.5)
        scores = jnp.where(same, scores, -1e30)
        top = jnp.max(scores, axis=-1, keepdims=True)
        weights = jnp.exp(scores - top)
        weights = weights * (1.0 / jnp.sum(weights, axis=-1, keepdims=True))
        probs[head] = weights.astype(BF16)
        total = total + dot_nn(probs[head], value[...] * mask)
    head_out[...] = total.astype(BF16)


def middle_kernel(
    n_tensor, experts, ids, tokens, gain, bias, table, *rest
):
    heads = rest[:n_tensor]
    weights = rest[n_tensor : 2 * n_tensor]
    middle = rest[2 * n_tensor]
    blocks = rest[2 * n_tensor + 1 : 2 * n_tensor + 1 + experts]
    held_heads, held_weights, low = rest[2 * n_tensor + 1 + experts :]
    for j in range(n_tensor):
        held_heads[j] = heads[j][...]
        held_weights[j] = weights[j][...]
    total = tokens[...].astype(F32)
    for rank in range(n_tensor):
        place = ids[T_ID] ^ rank
        total = total + dot_nn(held_heads[place], held_weights[place])
    middle[...] = total
    unit, _ = norm_parts(total)
    low[...] = (unit * row_of(gain) + row_of(bias)).astype(BF16)
    for k in range(experts):
        blocks[k][...] = dot_nn(table[ids[E_ID] ^ k], low[...]).astype(BF16)


def expert_kernel(
    experts, places, with_grads, ids, up_a, up_b, down_a, down_b, router, pair_out, *refs
):
    number = len(places)
    row_blocks, out_blocks = refs[:number], refs[number : 2 * number]
    refs = refs[2 * number :]
    back_blocks, gated_kept, gated_sent = refs[:number], refs[number], refs[number + 1]
    refs = refs[number + 2 :]
    rows_in, d_result, hidden_a, hidden_b, d_pre_a, d_pre_b, router_part = refs[:7]
    d_out = refs[-1]
    size = row_blocks[0].shape[0]
    count = size * number
    far = ids[T_ID] // 2
    for k in range(number):
        rows_in[k * size : (k + 1) * size, :] = row_blocks[k][...]
        quarter = out_blocks[k].shape[0]
        if quarter == size:
            d_out[k * size : (k + 1) * size, :] = out_blocks[k][...].astype(F32)
        else:
            here = pl.multiple_of(k * size + far * quarter, 8)
            there = pl.multiple_of(k * size + (1 - far) * quarter, 8)
            d_out[pl.ds(here, quarter), :] = out_blocks[k][...].astype(F32)
            d_out[pl.ds(there, quarter), :] = pair_out[places[k] - 2].astype(F32)
    lane = iota((count, LANES), 1)
    logits = dot_nt(rows_in[...], router[...])
    logits = jnp.where(lane < experts, logits, -1e30)
    top = jnp.max(logits, axis=-1, keepdims=True)
    odds = jnp.exp(logits - top)
    odds = odds / jnp.sum(odds, axis=-1, keepdims=True)
    mine = (lane == ids[E_ID]).astype(F32)
    gate = jnp.sum(odds * mine, axis=-1, keepdims=True)
    d_result[...] = (gate * d_out[...]).astype(BF16)
    result = jnp.zeros(d_out.shape, F32)
    back = jnp.zeros(d_out.shape, F32)
    scale = 0.7978845608028654
    for up, down, hidden, d_pre in (
        (up_a, down_a, hidden_a, d_pre_a),
        (up_b, down_b, hidden_b, d_pre_b),
    ):
        act = dot_nn(rows_in[...], up[...])
        square = act * act
        bend = jnp.tanh(scale * act * (1.0 + 0.044715 * square))
        half = 0.5 * (1.0 + bend)
        hidden[...] = (act * half).astype(BF16)
        slope = half + 0.5 * act * (1.0 - bend * bend) * (
            scale * (1.0 + 3 * 0.044715 * square)
        )
        result = result + dot_nn(hidden[...], down[...])
        d_pre[...] = (dot_nt(d_result[...], down[...]) * slope).astype(BF16)
        back = back + dot_nt(d_pre[...], up[...])
    d_gate = jnp.sum(d_out[...] * result, axis=-1, keepdims=True)
    d_logits = (d_gate * gate * (mine - odds)).astype(BF16)
    back = (back + dot_nn(d_logits, router[...])).astype(BF16)
    for k in range(number):
        back_blocks[k][...] = back[k * size : (k + 1) * size, :]
    d_out[...] = gate * result
    quarter = gated_kept.shape[1]
    for k in range(number):
        if quarter == size:
            gated_kept[k] = d_out[k * size : (k + 1) * size, :].astype(BF16)
        else:
            here = pl.multiple_of(k * size + far * quarter, 8)
            there = pl.multiple_of(k * size + (1 - far) * quarter, 8)
            gated_kept[k] = d_out[pl.ds(here, quarter), :].astype(BF16)
            gated_sent[k] = d_out[pl.ds(there, quarter), :].astype(BF16)
    if quarter == size:
        gated_sent[...] = jnp.zeros_like(gated_sent)
    router_part[...] = dot_tn(d_logits, rows_in[...])[: router_part.shape[0]]
    if with_grads:
        own, pair = refs[7:9]
        weight_grads(rows_in, d_pre_a, d_pre_b, hidden_a, hidden_b, d_result, None, None, own, pair)


def weight_grads(
    rows, d_pre_a, d_pre_b, hidden_a, hidden_b, d_result, own_before, pair_before, own, pair
):
    width = own.shape[0] // 2
    for out, before, at, left, right in (
        (pair, pair_before, 0, rows, d_pre_b),
        (pair, pair_before, width, hidden_b, d_result),
        (own, own_before, 0, rows, d_pre_a),
        (own, own_before, width, hidden_a, d_result),
    ):
        total = dot_tn(left[...], right[...])
        if before is not None:
            total = total + before[at : at + width, :].astype(F32)
        out[at : at + width, :] = total.astype(BF16)


def gated_sum_kernel(kept, came, out):
    out[...] = (kept[...].astype(F32) + came[...].astype(F32)).astype(BF16)


def weight_grad_kernel(*refs):
    rows, d_pre_a, d_pre_b, hidden_a, hidden_b, d_result = refs[:6]
    own_before, pair_before = refs[6:8] if len(refs) == 10 else (None, None)
    weight_grads(
        rows, d_pre_a, d_pre_b, hidden_a, hidden_b, d_result, own_before, pair_before, *refs[-2:]
    )


def split_grad_kernel(ids, own, came, kept, sent_first, sent_rest, total, sent):
    total[...] = own[...].astype(F32) + came[...].astype(F32)
    width = own.shape[1]
    half = width // 2
    mine, other = ids[D_ID], 1 - ids[D_ID]
    kept[:half, :] = total[pl.ds(pl.multiple_of(mine * half, 16), half), :]
    sent[:half, :] = total[pl.ds(pl.multiple_of(other * half, 16), half), :].astype(BF16)
    column = pl.ds(pl.multiple_of(mine * half, LANES), half)
    kept[half:, :half] = total[width : width + half, column]
    kept[half:, half:] = total[width + half :, column]
    column = pl.ds(pl.multiple_of(other * half, LANES), half)
    sent[half:, :half] = total[width : width + half, column].astype(BF16)
    sent[half:, half:] = total[width + half :, column].astype(BF16)
    first = sent_first.shape[0]
    sent_first[...] = sent[:first, :]
    sent_rest[...] = sent[first:, :]


def join_grad_kernel(kept, came_first, came_rest, grad_up, grad_down, came):
    first = came_first.shape[0]
    came[:first, :] = came_first[...]
    came[first:, :] = came_rest[...]
    half = kept.shape[1] // 2
    grad_up[...] = kept[:half, :] + came[:half, :].astype(F32)
    grad_down[:half, :] = kept[half:, :half] + came[half:, :half].astype(F32)
    grad_down[half:, :] = kept[half:, half:] + came[half:, half:].astype(F32)


def combine_kernel(experts, parts, base, ids, table, part, *refs):
    blocks = refs[:experts]
    routers = refs[experts : experts + parts]
    kept, sent, total = refs[experts + parts :]
    value = dot_tn(table[ids[E_ID]], blocks[0][...])
    for k in range(1, experts):
        spots = table if blocks[k].shape[0] == table.shape[1] else part
        value = value + dot_tn(spots[ids[E_ID] ^ k], blocks[k][...])
    total[...] = jnp.zeros_like(total)
    total[: value.shape[0], :] = value
    if parts:
        added = routers[0][...]
        for k in range(1, parts):
            added = added + routers[k][...]
        total[base : base + added.shape[0], :] = added
    half = kept.shape[1]
    kept[...] = total[:, pl.ds(pl.multiple_of(ids[C_ID] * half, LANES), half)].astype(BF16)
    sent[...] = total[:, pl.ds(pl.multiple_of((1 - ids[C_ID]) * half, LANES), half)].astype(BF16)


def joined(ids, own, other, whole):
    half = own.shape[1]
    whole[:, pl.ds(pl.multiple_of(ids[C_ID] * half, LANES), half)] = own[...].astype(F32)
    whole[:, pl.ds(pl.multiple_of((1 - ids[C_ID]) * half, LANES), half)] = other[...].astype(F32)


def back_kernel(
    split, ids, own, other, middle, cot, gain, w_out, head_out, normed, query, key, value,
    probs, weight, *rest
):
    d_middle, kept, sent, small = rest[:4]
    blocks = rest[4:-2]
    whole, grads = rest[-2:]
    rows, inner = query.shape
    heads = inner // HEAD_DIM
    joined(ids, own, other, whole)
    d_normed = whole[:rows, :]
    unit, scale = norm_parts(middle[...])
    small[...] = jnp.zeros_like(small)
    base = -(-rows // 16) * 16
    small[8:, :] = whole[base : base + small.shape[0] - 8, :]
    small[2:3, :] = jnp.sum(d_normed * unit, axis=0, keepdims=True)
    small[3:4, :] = jnp.sum(d_normed, axis=0, keepdims=True)
    live = iota((rows, 1), 0) < ids[L_ID]
    d_out = jnp.where(live, cot[...].astype(F32), 0.0)
    d_mid = d_out + norm_back(unit, scale, d_normed * row_of(gain))
    d_middle[...] = d_mid
    d_branch = d_mid.astype(BF16)
    d_head = dot_nt(d_branch, w_out[...]).astype(BF16)
    grads[3 * inner :, :] = dot_tn(head_out[...], d_branch).astype(BF16)
    d_query = jnp.zeros((rows, inner), F32)
    d_key = jnp.zeros((rows, inner), F32)
    d_value = jnp.zeros((rows, inner), F32)
    for head in range(heads):
        mask = head_mask(head, inner)
        chance = probs[head].astype(F32)
        d_probs = dot_nt(d_head, value[...] * mask)
        delta = jnp.sum(d_probs * chance, axis=-1, keepdims=True)
        d_scores = (chance * (d_probs - delta)).astype(BF16)
        d_value = d_value + dot_tn(probs[head], d_head * mask)
        d_query = d_query + dot_nn(d_scores, key[...] * mask)
        d_key = d_key + dot_tn(d_scores, query[...] * mask)
    d_query = (d_query * (HEAD_DIM**-0.5)).astype(BF16)
    d_key = (d_key * (HEAD_DIM**-0.5)).astype(BF16)
    d_value = d_value.astype(BF16)
    grads[:inner, :] = dot_tn(d_query, normed[...]).astype(BF16)
    grads[inner : 2 * inner, :] = dot_tn(d_key, normed[...]).astype(BF16)
    grads[2 * inner : 3 * inner, :] = dot_tn(d_value, normed[...]).astype(BF16)
    if not split:
        blocks[0][...] = grads[...]
    else:
        mine, over_y, over_z, kept_left, kept_right = blocks
        size, half = kept_left.shape

        def piece(mask):
            return pl.ds(pl.multiple_of((ids[Q_ID] ^ mask) * size, 16), size)

        mine[...] = grads[piece(0), :]
        over_y[0] = grads[piece(1), :half]
        over_y[1] = grads[piece(3), :half]
        over_z[0] = grads[piece(2), half:]
        over_z[1] = grads[piece(3), half:]
        kept_left[...] = grads[piece(2), :half]
        kept_right[...] = grads[piece(1), half:]
    d_in = dot_nn(d_query, weight[:inner])
    d_in = d_in + dot_nn(d_key, weight[inner : 2 * inner])
    whole[:rows, :] = d_in + dot_nn(d_value, weight[2 * inner :])
    half = kept.shape[1]
    kept[...] = whole[:rows, pl.ds(pl.multiple_of(ids[C_ID] * half, LANES), half)].astype(BF16)
    sent[...] = whole[:rows, pl.ds(pl.multiple_of((1 - ids[C_ID]) * half, LANES), half)].astype(BF16)


def last_norm_kernel(ids, own, other, tokens, d_middle, gain, small2, grad_tokens, small, whole):
    joined(ids, own, other, whole)
    d_normed = whole[...]
    unit, scale = norm_parts(tokens[...].astype(F32))
    small[...] = small2[...]
    small[0:1, :] = jnp.sum(d_normed * unit, axis=0, keepdims=True)
    small[1:2, :] = jnp.sum(d_normed, axis=0, keepdims=True)
    grad_tokens[...] = (
        d_middle[...] + norm_back(unit, scale, d_normed * row_of(gain))
    ).astype(BF16)


def scatter_kernel(mine, kept_left, kept_right, came_y, came_z, total, next_z, next_y):
    half = kept_left.shape[1]
    total[:, :half] = mine[:, :half].astype(F32) + came_y[0].astype(F32)
    total[:, half:] = mine[:, half:].astype(F32) + came_z[0].astype(F32)
    next_z[...] = (kept_left[...].astype(F32) + came_y[1].astype(F32)).astype(BF16)
    next_y[...] = (kept_right[...].astype(F32) + came_z[1].astype(F32)).astype(BF16)


def sum_kernel(total, came_z, came_y, out_a, out_b):
    size, half = came_z.shape
    size = size // 2
    for out, at in ((out_a, 0), (out_b, size)):
        part = pl.ds(at, size)
        out[:, :half] = (total[part, :half] + came_z[part, :].astype(F32)).astype(BF16)
        out[:, half:] = (total[part, half:] + came_y[part, :].astype(F32)).astype(BF16)


def pair_kernel(own_a, own_b, came_a, came_b, small, small_came, out):
    size = own_a.shape[0]
    out[:size, :] = (own_a[...].astype(F32) + came_a[...].astype(F32)).astype(BF16)
    out[size : 2 * size, :] = (own_b[...].astype(F32) + came_b[...].astype(F32)).astype(BF16)
    out[2 * size :, :] = (small[...] + small_came[...]).astype(BF16)


def spread_kernel(count, ids, *refs):
    parts = refs[:count]
    grad_qkv, grad_out, gain1, bias1, gain2, bias2, router, grads, held = refs[count:]
    size = grads.shape[0] // count
    for m in range(count):
        quarter = ids[Q_ID] ^ m
        grads[pl.ds(pl.multiple_of(quarter * size, 16), size), :] = parts[m][:size, :].astype(F32)
        held[quarter] = parts[m][size:, :].astype(F32)
    total = held[0]
    for quarter in range(1, count):
        total = total + held[quarter]
    for row, out in enumerate((gain1, bias1, gain2, bias2)):
        out[...] = total[row : row + 1, :].reshape(out.shape)
    router[...] = total[8 : 8 + router.shape[0], :]
    inner = grad_qkv.shape[0]
    grad_qkv[...] = grads[:inner, :]
    grad_out[...] = grads[inner:, :]


def after(value, *others):
    return lax.optimization_barrier((value,) + others)[0]


def run(kernel, outs, args, scratch=(), micros=1.0, limit=16, far=False):
    smem = pl.BlockSpec(memory_space=pltpu.SMEM)
    vmem = pl.BlockSpec(memory_space=pltpu.VMEM)
    held = pl.BlockSpec(memory_space=pltpu.HBM) if far else vmem
    kinds = [pltpu.VMEM(shape, kind) for shape, kind in scratch]
    if far:
        kinds.append(pltpu.SemaphoreType.DMA((len(args),)))
    return pl.pallas_call(
        kernel,
        out_shape=[jax.ShapeDtypeStruct(shape, kind) for shape, kind in outs],
        in_specs=[smem if arg.dtype == jnp.int32 and arg.ndim == 1 else held for arg in args],
        out_specs=[vmem] * len(outs),
        scratch_shapes=kinds,
        compiler_params=pltpu.CompilerParams(vmem_limit_bytes=limit * 1024 * 1024),
        cost_estimate=pl.CostEstimate(
            flops=int(micros * 2e7), bytes_accessed=1024, transcendentals=0
        ),
    )(*args)


def make_body(n_tensor, n_expert, n_dp):
    small_slice = n_expert == 4 and n_dp == 2

    def tensor_swap(value, mask):
        return lax.ppermute(value, "tensor", [(i, i ^ mask) for i in range(n_tensor)])

    def expert_swap(value, mask):
        return lax.ppermute(value, "expert", [(i, i ^ mask) for i in range(n_expert)])

    def dp_swap(value):
        return lax.ppermute(value, "dp", [(i, i ^ 1) for i in range(n_dp)])

    def quarter_swap(value, mask):
        pairs = [(i, i ^ mask) for i in range(n_expert * n_dp)]
        return lax.ppermute(value, ("expert", "dp"), pairs)

    def exchange(blocks):
        if small_slice:
            came = {k: expert_swap(blocks[k], k) for k in (3, 2, 1)}
            return [blocks[0]] + [came[k] for k in range(1, n_expert)]
        order = jnp.arange(n_expert) ^ lax.axis_index("expert")
        stacked = lax.all_to_all(
            jnp.stack(blocks)[order], "expert", split_axis=0, concat_axis=0, tiled=True
        )[order]
        return [stacked[k] for k in range(n_expert)]

    def body(
        tokens,
        routes,
        images_live,
        ln1_gain,
        ln1_bias,
        w_qkv,
        w_out,
        ln2_gain,
        ln2_bias,
        w_router,
        w_up,
        w_down,
        cotangent,
    ):
        rows, width = tokens.shape
        inner = w_qkv.shape[2]
        heads = inner // HEAD_DIM
        experts = w_router.shape[1]
        capacity = max(2, 3 * rows // experts // 8 * 8)
        cap = capacity // 2
        images = rows // SEQ
        half = width // 2
        hidden_width = w_up.shape[2]
        rank = lax.axis_index("tensor")
        owner = lax.axis_index("expert")
        copy = lax.axis_index("dp")
        ids = jnp.stack(
            [
                rank,
                rank % 2,
                owner,
                copy,
                (owner % 2) * 2 + copy,
                jnp.minimum(images_live[0] * SEQ, rows),
                rank,
                rank,
            ]
        ).astype(jnp.int32)
        weight = w_qkv.transpose(1, 2, 0).reshape(3 * inner, width)
        up_a, down_a = w_up[0], w_down[0]
        part_rows = max(8, -(-experts // 8) * 8)
        small_rows = 8 + part_rows
        base = -(-rows // 16) * 16
        tall = base + -(-part_rows // 16) * 16

        out_c = tensor_swap(w_out, 1)
        up_b, down_b = tensor_swap(up_a, 1), tensor_swap(down_a, 1)
        normed, query, key, value, probs, head_out = run(
            functools.partial(attend_kernel, images),
            [((rows, width), BF16)]
            + [((rows, inner), BF16)] * 3
            + [((heads, rows, rows), BF16), ((rows, inner), BF16)],
            [tokens, ln1_gain, ln1_bias, weight],
            scratch=[
                ((rows, width), BF16), ((width,), F32), ((width,), F32), ((3 * inner, width), BF16)
            ],
            micros=4,
            far=True,
        )
        head_out, out_c, up_b, down_b = lax.optimization_barrier((head_out, out_c, up_b, down_b))
        out_x = tensor_swap(after(w_out, head_out), 2)
        head_x, head_c = tensor_swap(head_out, 2), tensor_swap(head_out, 1)
        quarter = cap // 2
        cot_shapes = [(quarter if small_slice and k > 1 else cap, width) for k in range(experts)]
        table, part, router, *cot_blocks = run(
            functools.partial(plan_kernel, experts),
            [((experts, cap, rows), BF16), ((experts, quarter, rows), BF16)]
            + [((LANES, width), BF16)]
            + [(shape, BF16) for shape in cot_shapes],
            [ids, after(routes.T, head_out), cotangent, w_router.T],
            micros=2,
        )
        head_x = after(head_x, table)
        d_rows_in = exchange(cot_blocks)
        out_all = [w_out, out_c, out_x, tensor_swap(out_x, 1)]
        heads_all = [head_out, head_c, head_x, tensor_swap(head_x, 1)]
        middle, *row_blocks = run(
            functools.partial(middle_kernel, n_tensor, experts),
            [((rows, width), F32)] + [((cap, width), BF16)] * experts,
            [ids, tokens, ln2_gain, ln2_bias, table] + heads_all + out_all,
            scratch=[
                ((n_tensor, rows, inner), BF16),
                ((n_tensor, inner, width), BF16),
                ((rows, width), BF16),
            ],
            micros=3,
        )
        rows_in = exchange(row_blocks)
        if small_slice:
            rows_in[1], *far_out = lax.optimization_barrier((rows_in[1], *d_rows_in[2:]))
            d_rows_in[2:] = far_out
            pair_out = tensor_swap(jnp.stack(far_out), 2)
        else:
            pair_out = router

        calls = [(0, 1), (2, 3)] if small_slice else [tuple(range(experts))]
        worked = []
        d_back, gated = [], []
        for number, call in enumerate(calls):
            count = cap * len(call)
            last = number == len(calls) - 1
            grads = [] if last else [((2 * width, hidden_width), BF16)] * 2
            results = run(
                functools.partial(expert_kernel, experts, call, not last),
                [((cap, width), BF16)] * len(call)
                + [((len(call), quarter if worked else cap, width), BF16)] * 2
                + [((count, width), BF16)] * 2
                + [((count, hidden_width), BF16)] * 4
                + [((part_rows, width), F32)]
                + grads,
                [ids, up_a, up_b, down_a, down_b]
                + [after(router, worked[-1][6]) if worked else router]
                + [pair_out if worked or not small_slice else router]
                + [rows_in[k] for k in call]
                + [d_rows_in[k] for k in call],
                scratch=[((count, width), F32)],
                micros=7,
                limit=24,
            )
            d_back += results[: len(call)]
            gated.append(results[len(call) : len(call) + 2])
            worked.append(results[len(call) + 2 :])

        def combine(blocks, routers):
            return run(
                functools.partial(combine_kernel, experts, len(routers), base),
                [((tall if routers else base, half), BF16)] * 2,
                [ids, table, part] + blocks + routers,
                scratch=[((tall if routers else base, width), F32)],
                micros=2,
            )

        if small_slice:
            home = {k: expert_swap(d_back[k], k) for k in (3, 1)}
            home[2] = expert_swap(after(d_back[2], home[3]), 2)
            d_home = [d_back[0]] + [home[k] for k in (1, 2, 3)]
        else:
            d_home = exchange(d_back)

        grad_own, grad_pair = run(
            weight_grad_kernel,
            [((2 * width, hidden_width), BF16)] * 2,
            [worked[-1][at] for at in (0, 4, 5, 2, 3, 1)] + list(worked[0][7:]),
            micros=4,
            limit=24,
        )
        third = width // 48 * 16
        grad_kept, sent_first, sent_rest = run(
            split_grad_kernel,
            [((width, width), F32), ((third, width), BF16), ((width - third, width), BF16)],
            [ids, grad_own, tensor_swap(grad_pair, 1)],
            scratch=[((2 * width, width), F32), ((width, width), BF16)],
            micros=2,
            limit=24,
        )

        if small_slice:
            (gated_far,) = run(
                gated_sum_kernel,
                [((2, quarter, width), BF16)],
                [gated[1][0], tensor_swap(gated[1][1], 2)],
            )
            gated_near = [gated[0][0][0], gated[0][0][1]]
            *d_home, gated_far, sent_first = lax.optimization_barrier(
                (*d_home, gated_far, sent_first)
            )
        else:
            gated_home = exchange([gated[0][0][k] for k in range(experts)])
            *d_home, sent_first = lax.optimization_barrier((*d_home, sent_first))
        kept, sent = combine(list(d_home), [one[6] for one in worked])
        chip = (kept.astype(F32) + tensor_swap(sent, 1).astype(F32)).astype(BF16)
        own = (chip.astype(F32) + tensor_swap(chip, 2).astype(F32)).astype(BF16)
        came_first = dp_swap(sent_first)
        if small_slice:
            far_home = expert_swap(gated_far, 2)
            near_home = expert_swap(gated_near[1], 1)
            own, came_first, far_home, near_home = lax.optimization_barrier(
                (own, came_first, far_home, near_home)
            )
            gated_home = [gated_near[0], near_home, far_home[0], expert_swap(far_home[1], 1)]
        other = tensor_swap(own, 1)

        size = inner
        if small_slice:
            grad_shapes = [(size, width), (2, size, half), (2, size, half), (size, half), (size, half)]
        else:
            grad_shapes = [(4 * size, width)]
        d_middle, kept1, sent1, small2, *grad_blocks = run(
            functools.partial(back_kernel, small_slice),
            [((rows, width), F32)]
            + [((rows, half), BF16)] * 2
            + [((small_rows, width), F32)]
            + [(shape, BF16) for shape in grad_shapes],
            [
                ids, own, other, middle, cotangent, ln2_gain, w_out, head_out, normed, query,
                key, value, probs, weight,
            ],
            scratch=[((tall, width), F32), ((4 * inner, width), BF16)],
            micros=6,
        )

        *gated_home, _ = lax.optimization_barrier((*gated_home, d_middle))
        kept_y, sent_y = combine(list(gated_home), [])

        if small_slice:
            mine, over_y, over_z, kept_left, kept_right = grad_blocks
            total, next_z, next_y = run(
                scatter_kernel,
                [((size, width), F32)] + [((size, half), BF16)] * 2,
                [mine, kept_left, kept_right, dp_swap(over_y), expert_swap(over_z, 1)],
            )
        chip1 = (kept1.astype(F32) + tensor_swap(sent1, 1).astype(F32)).astype(BF16)
        own1 = (chip1.astype(F32) + tensor_swap(chip1, 2).astype(F32)).astype(BF16)
        if small_slice:
            total, kept_y, sent_y, own1 = lax.optimization_barrier((total, kept_y, sent_y, own1))
            summed_a, summed_b = run(
                sum_kernel,
                [((size // 2, width), BF16)] * 2,
                [total, expert_swap(next_z, 1), dp_swap(next_y)],
            )
            sent_rest = after(sent_rest, summed_a)
            came_a = expert_swap(summed_a, 2)
        other1 = tensor_swap(own1, 1)
        grad_tokens, small = run(
            last_norm_kernel,
            [((rows, width), BF16), ((small_rows, width), F32)],
            [ids, own1, other1, tokens, d_middle, ln1_gain, small2],
            scratch=[((rows, width), F32)],
            micros=2,
        )
        chip_y = (kept_y.astype(F32) + tensor_swap(sent_y, 1).astype(F32)).astype(BF16)
        own_y = (chip_y.astype(F32) + tensor_swap(chip_y, 2).astype(F32)).astype(BF16)
        if small_slice:
            came_b = expert_swap(after(summed_b, came_a, small), 2)
            (ready,) = run(
                pair_kernel,
                [((size + small_rows, width), BF16)],
                [summed_a, summed_b, came_a, came_b, small, expert_swap(small, 2)],
                micros=1,
            )
            own_y, ready = lax.optimization_barrier((own_y, ready))
            everything = [ready] + [quarter_swap(ready, m) for m in (1, 2, 3)]
            grad_qkv, grad_out, *sums, grad_router = run(
                functools.partial(spread_kernel, 4),
                [((3 * inner, width), F32), ((inner, width), F32)]
                + [((width,), F32)] * 4
                + [((experts, width), F32)],
                [ids] + everything,
                scratch=[((4 * inner, width), F32), ((4, small_rows, width), F32)],
                micros=3,
            )
        else:
            grads = lax.psum(grad_blocks[0], ("expert", "dp")).astype(F32)
            grad_qkv, grad_out = grads[: 3 * inner], grads[3 * inner :]
            small_sum = lax.psum(small, ("expert", "dp"))
            sums, grad_router = list(small_sum[:4]), small_sum[8 : 8 + experts]

        grad_up, grad_down = run(
            join_grad_kernel,
            [((half, hidden_width), F32), ((hidden_width, half), F32)],
            [grad_kept, came_first, dp_swap(sent_rest)],
            scratch=[((width, width), BF16)],
            micros=2,
        )

        mix_own, mix_other = own_y, tensor_swap(own_y, 1)
        mixture = jnp.where(
            rank % 2 == 0,
            jnp.concatenate([mix_own, mix_other], axis=1),
            jnp.concatenate([mix_other, mix_own], axis=1),
        )[:rows].astype(F32)
        alive = (jnp.arange(rows, dtype=jnp.int32) < images_live[0] * SEQ)[:, None]
        out = jnp.where(alive, middle + mixture, 0.0).astype(BF16)
        return (
            out,
            grad_tokens,
            sums[0],
            sums[1],
            grad_qkv.reshape(3, inner, width).transpose(2, 0, 1),
            grad_out,
            sums[2],
            sums[3],
            grad_router.T,
            grad_up[None],
            grad_down[None],
        )

    return body


def solution(mesh):
    in_specs = (
        P(("expert", "dp"), None),
        P(("expert", "dp"), None),
        P(("expert", "dp")),
        P(),
        P(),
        P(None, None, "tensor"),
        P("tensor", None),
        P(),
        P(),
        P(),
        P("expert", None, "tensor"),
        P("expert", "tensor", None),
        P(("expert", "dp"), None),
    )
    out_specs = (
        P(("expert", "dp"), None),
        P(("expert", "dp"), None),
        P(),
        P(),
        P(None, None, "tensor"),
        P("tensor", None),
        P(),
        P(),
        P(),
        P("expert", "dp", "tensor"),
        P("expert", "tensor", "dp"),
    )
    body = make_body(mesh.shape["tensor"], mesh.shape["expert"], mesh.shape["dp"])
    return jax.shard_map(body, mesh=mesh, in_specs=in_specs, out_specs=out_specs, check_vma=False)
```

```python
import functools

import jax
import jax.numpy as jnp
from jax import lax
from jax.experimental import pallas as pl
from jax.experimental.pallas import tpu as pltpu
from jax.sharding import PartitionSpec as P

HEAD_DIM = 64
SEQ = 197
EPSILON = 1e-06
F32 = jnp.float32
BF16 = jnp.bfloat16
LANES = 128
SMALL = 16


def dot_nn(left, right):
    return lax.dot_general(left, right, (((1,), (0,)), ((), ())), preferred_element_type=F32)


def dot_tn(left, right):
    return lax.dot_general(left, right, (((0,), (0,)), ((), ())), preferred_element_type=F32)


def dot_nt(left, right):
    return lax.dot_general(left, right, (((1,), (1,)), ((), ())), preferred_element_type=F32)


def norm_parts(values_in):
    row_mean = jnp.mean(values_in, axis=-1, keepdims=True)
    centred = values_in - row_mean
    variance = jnp.mean(centred * centred, axis=-1, keepdims=True)
    scale = lax.rsqrt(variance + EPSILON)
    return centred * scale, scale


def norm_back(normed, scale, u):
    return scale * (
        u
        - jnp.mean(u, axis=-1, keepdims=True)
        - normed * jnp.mean(u * normed, axis=-1, keepdims=True)
    )


def iota(shape, dim):
    return lax.broadcasted_iota(jnp.int32, shape, dim)


def row_of(vector):
    return vector[...].reshape(1, vector.shape[0])


def head_mask(head, width):
    lane = iota((1, width), 1)
    return ((lane >= head * HEAD_DIM) & (lane < (head + 1) * HEAD_DIM)).astype(BF16)


def image_of(shape, dim, images):
    at = iota(shape, dim)
    image = jnp.zeros(shape, jnp.int32)
    for number in range(1, images):
        image = image + (at >= number * SEQ).astype(jnp.int32)
    return image


T_ID, C_ID, E_ID, D_ID, Q_ID, L_ID = range(6)


def plan_kernel(experts, ids, routes, cot, router, table, part, router_pad, *blocks):
    rows = cot.shape[0]
    cap = table.shape[1]
    tall = max(16, -(-experts // 16) * 16)
    picks = routes[...]
    expert = iota((tall, rows), 0)
    named = picks[0:1, :] == expert
    for k in range(1, picks.shape[0]):
        named = named | (picks[k : k + 1, :] == expert)
    named = named & (iota((tall, rows), 1) < ids[L_ID])
    marks = jnp.where(named, 1.0, 0.0).astype(BF16)
    earlier = jnp.where(iota((rows, rows), 0) < iota((rows, rows), 1), 1.0, 0.0).astype(BF16)
    slot = dot_nn(marks, earlier)
    first = (ids[C_ID] * cap).astype(F32)
    slot = jnp.where(named, slot - first, -1.0)
    place = iota((cap, rows), 0).astype(F32)
    for x in range(experts):
        table[x] = jnp.where(slot[x : x + 1, :] == place, 1.0, 0.0).astype(BF16)
    quarter = part.shape[1]
    first = ((ids[T_ID] // 2) * quarter).astype(F32)
    place = iota((quarter, rows), 0).astype(F32) + first
    for x in range(experts):
        part[x] = jnp.where(slot[x : x + 1, :] == place, 1.0, 0.0).astype(BF16)
    for k in range(experts):
        source = table if blocks[k].shape[0] == cap else part
        blocks[k][...] = dot_nn(source[ids[E_ID] ^ k], cot[...]).astype(BF16)
    router_pad[...] = jnp.zeros_like(router_pad)
    router_pad[:experts, :] = router[...]


def attend_kernel(images, tokens, gain, bias, weight, normed, query, key, value, probs, head_out):
    rows = tokens.shape[0]
    inner = query.shape[1]
    heads = inner // HEAD_DIM
    unit, _ = norm_parts(tokens[...].astype(F32))
    normed[...] = (unit * row_of(gain) + row_of(bias)).astype(BF16)
    query[...] = dot_nt(normed[...], weight[:inner]).astype(BF16)
    key[...] = dot_nt(normed[...], weight[inner : 2 * inner]).astype(BF16)
    value[...] = dot_nt(normed[...], weight[2 * inner :]).astype(BF16)
    same = image_of((rows, 1), 0, images) == image_of((1, rows), 1, images)
    total = jnp.zeros((rows, inner), F32)
    for head in range(heads):
        mask = head_mask(head, inner)
        scores = dot_nt(query[...] * mask, key[...]) * (HEAD_DIM**-0.5)
        scores = jnp.where(same, scores, -1e30)
        top = jnp.max(scores, axis=-1, keepdims=True)
        weights = jnp.exp(scores - top)
        weights = weights * (1.0 / jnp.sum(weights, axis=-1, keepdims=True))
        probs[head] = weights.astype(BF16)
        total = total + dot_nn(probs[head], value[...] * mask)
    head_out[...] = total.astype(BF16)


def middle_kernel(
    n_tensor, experts, ids, tokens, gain, bias, table, *rest
):
    heads = rest[:n_tensor]
    weights = rest[n_tensor : 2 * n_tensor]
    middle = rest[2 * n_tensor]
    blocks = rest[2 * n_tensor + 1 : 2 * n_tensor + 1 + experts]
    held_heads, held_weights, low = rest[2 * n_tensor + 1 + experts :]
    for j in range(n_tensor):
        held_heads[j] = heads[j][...]
        held_weights[j] = weights[j][...]
    total = tokens[...].astype(F32)
    for rank in range(n_tensor):
        place = ids[T_ID] ^ rank
        total = total + dot_nn(held_heads[place], held_weights[place])
    middle[...] = total
    unit, _ = norm_parts(total)
    low[...] = (unit * row_of(gain) + row_of(bias)).astype(BF16)
    for k in range(experts):
        blocks[k][...] = dot_nn(table[ids[E_ID] ^ k], low[...]).astype(BF16)


def expert_kernel(
    experts, places, with_grads, ids, up_a, up_b, down_a, down_b, router, pair_out, *refs
):
    number = len(places)
    row_blocks, out_blocks = refs[:number], refs[number : 2 * number]
    refs = refs[2 * number :]
    back_blocks, gated_kept, gated_sent = refs[:number], refs[number], refs[number + 1]
    refs = refs[number + 2 :]
    rows_in, d_result, hidden_a, hidden_b, d_pre_a, d_pre_b, router_part = refs[:7]
    d_out = refs[-1]
    size = row_blocks[0].shape[0]
    count = size * number
    far = ids[T_ID] // 2
    for k in range(number):
        rows_in[k * size : (k + 1) * size, :] = row_blocks[k][...]
        quarter = out_blocks[k].shape[0]
        if quarter == size:
            d_out[k * size : (k + 1) * size, :] = out_blocks[k][...].astype(F32)
        else:
            here = pl.multiple_of(k * size + far * quarter, 8)
            there = pl.multiple_of(k * size + (1 - far) * quarter, 8)
            d_out[pl.ds(here, quarter), :] = out_blocks[k][...].astype(F32)
            d_out[pl.ds(there, quarter), :] = pair_out[places[k] - 2].astype(F32)
    lane = iota((count, LANES), 1)
    logits = dot_nt(rows_in[...], router[...])
    logits = jnp.where(lane < experts, logits, -1e30)
    top = jnp.max(logits, axis=-1, keepdims=True)
    odds = jnp.exp(logits - top)
    odds = odds / jnp.sum(odds, axis=-1, keepdims=True)
    mine = (lane == ids[E_ID]).astype(F32)
    gate = jnp.sum(odds * mine, axis=-1, keepdims=True)
    d_result[...] = (gate * d_out[...]).astype(BF16)
    result = jnp.zeros(d_out.shape, F32)
    back = jnp.zeros(d_out.shape, F32)
    scale = 0.7978845608028654
    for up, down, hidden, d_pre in (
        (up_a, down_a, hidden_a, d_pre_a),
        (up_b, down_b, hidden_b, d_pre_b),
    ):
        act = dot_nn(rows_in[...], up[...])
        square = act * act
        bend = jnp.tanh(scale * act * (1.0 + 0.044715 * square))
        half = 0.5 * (1.0 + bend)
        hidden[...] = (act * half).astype(BF16)
        slope = half + 0.5 * act * (1.0 - bend * bend) * (
            scale * (1.0 + 3 * 0.044715 * square)
        )
        result = result + dot_nn(hidden[...], down[...])
        d_pre[...] = (dot_nt(d_result[...], down[...]) * slope).astype(BF16)
        back = back + dot_nt(d_pre[...], up[...])
    d_gate = jnp.sum(d_out[...] * result, axis=-1, keepdims=True)
    d_logits = (d_gate * gate * (mine - odds)).astype(BF16)
    back = (back + dot_nn(d_logits, router[...])).astype(BF16)
    for k in range(number):
        back_blocks[k][...] = back[k * size : (k + 1) * size, :]
    d_out[...] = gate * result
    quarter = gated_kept.shape[1]
    for k in range(number):
        if quarter == size:
            gated_kept[k] = d_out[k * size : (k + 1) * size, :].astype(BF16)
        else:
            here = pl.multiple_of(k * size + far * quarter, 8)
            there = pl.multiple_of(k * size + (1 - far) * quarter, 8)
            gated_kept[k] = d_out[pl.ds(here, quarter), :].astype(BF16)
            gated_sent[k] = d_out[pl.ds(there, quarter), :].astype(BF16)
    if quarter == size:
        gated_sent[...] = jnp.zeros_like(gated_sent)
    router_part[...] = dot_tn(d_logits, rows_in[...])[: router_part.shape[0]]
    if with_grads:
        own, pair = refs[7:9]
        weight_grads(rows_in, d_pre_a, d_pre_b, hidden_a, hidden_b, d_result, None, None, own, pair)


def weight_grads(
    rows, d_pre_a, d_pre_b, hidden_a, hidden_b, d_result, own_before, pair_before, own, pair
):
    width = own.shape[0] // 2
    for out, before, at, left, right in (
        (pair, pair_before, 0, rows, d_pre_b),
        (pair, pair_before, width, hidden_b, d_result),
        (own, own_before, 0, rows, d_pre_a),
        (own, own_before, width, hidden_a, d_result),
    ):
        total = dot_tn(left[...], right[...])
        if before is not None:
            total = total + before[at : at + width, :].astype(F32)
        out[at : at + width, :] = total.astype(BF16)


def gated_sum_kernel(kept, came, *blocks):
    for k, out in enumerate(blocks):
        out[...] = (kept[k].astype(F32) + came[k].astype(F32)).astype(BF16)


def weight_grad_kernel(*refs):
    rows, d_pre_a, d_pre_b, hidden_a, hidden_b, d_result = refs[:6]
    own_before, pair_before = refs[6:8] if len(refs) == 10 else (None, None)
    weight_grads(
        rows, d_pre_a, d_pre_b, hidden_a, hidden_b, d_result, own_before, pair_before, *refs[-2:]
    )


def split_grad_kernel(ids, own, came, kept, sent_first, sent_rest, total, sent):
    total[...] = own[...].astype(F32) + came[...].astype(F32)
    width = own.shape[1]
    half = width // 2
    mine, other = ids[D_ID], 1 - ids[D_ID]
    kept[:half, :] = total[pl.ds(pl.multiple_of(mine * half, 16), half), :]
    sent[:half, :] = total[pl.ds(pl.multiple_of(other * half, 16), half), :].astype(BF16)
    column = pl.ds(pl.multiple_of(mine * half, LANES), half)
    kept[half:, :half] = total[width : width + half, column]
    kept[half:, half:] = total[width + half :, column]
    column = pl.ds(pl.multiple_of(other * half, LANES), half)
    sent[half:, :half] = total[width : width + half, column].astype(BF16)
    sent[half:, half:] = total[width + half :, column].astype(BF16)
    first = sent_first.shape[0]
    sent_first[...] = sent[:first, :]
    sent_rest[...] = sent[first:, :]


def join_grad_kernel(kept, came_first, came_rest, grad_up, grad_down, came):
    first = came_first.shape[0]
    came[:first, :] = came_first[...]
    came[first:, :] = came_rest[...]
    half = kept.shape[1] // 2
    grad_up[...] = kept[:half, :] + came[:half, :].astype(F32)
    grad_down[:half, :] = kept[half:, :half] + came[half:, :half].astype(F32)
    grad_down[half:, :] = kept[half:, half:] + came[half:, half:].astype(F32)


def combine_kernel(experts, parts, base, ids, table, part, *refs):
    blocks = refs[:experts]
    routers = refs[experts : experts + parts]
    kept, sent, total = refs[experts + parts :]
    value = dot_tn(table[ids[E_ID]], blocks[0][...])
    for k in range(1, experts):
        spots = table if blocks[k].shape[0] == table.shape[1] else part
        value = value + dot_tn(spots[ids[E_ID] ^ k], blocks[k][...])
    total[...] = jnp.zeros_like(total)
    total[: value.shape[0], :] = value
    if parts:
        added = routers[0][...]
        for k in range(1, parts):
            added = added + routers[k][...]
        total[base : base + added.shape[0], :] = added
    half = kept.shape[1]
    kept[...] = total[:, pl.ds(pl.multiple_of(ids[C_ID] * half, LANES), half)].astype(BF16)
    sent[...] = total[:, pl.ds(pl.multiple_of((1 - ids[C_ID]) * half, LANES), half)].astype(BF16)


def joined(ids, own, other, whole):
    half = own.shape[1]
    whole[:, pl.ds(pl.multiple_of(ids[C_ID] * half, LANES), half)] = own[...].astype(F32)
    whole[:, pl.ds(pl.multiple_of((1 - ids[C_ID]) * half, LANES), half)] = other[...].astype(F32)


def back_kernel(
    blocks_n, ids, own, other, middle, cot, gain, w_out, head_out, normed, query, key, value,
    probs, weight, *rest
):
    d_middle, kept, sent, small = rest[:4]
    blocks = rest[4 : 4 + blocks_n]
    whole, grads = rest[4 + blocks_n :]
    rows, inner = query.shape
    heads = inner // HEAD_DIM
    joined(ids, own, other, whole)
    d_normed = whole[:rows, :]
    unit, scale = norm_parts(middle[...])
    small[...] = jnp.zeros_like(small)
    base = -(-rows // 16) * 16
    small[8:, :] = whole[base : base + small.shape[0] - 8, :]
    small[2:3, :] = jnp.sum(d_normed * unit, axis=0, keepdims=True)
    small[3:4, :] = jnp.sum(d_normed, axis=0, keepdims=True)
    live = iota((rows, 1), 0) < ids[L_ID]
    d_out = jnp.where(live, cot[...].astype(F32), 0.0)
    d_mid = d_out + norm_back(unit, scale, d_normed * row_of(gain))
    d_middle[...] = d_mid
    d_branch = d_mid.astype(BF16)
    d_head = dot_nt(d_branch, w_out[...]).astype(BF16)
    grads[3 * inner :, :] = dot_tn(head_out[...], d_branch).astype(BF16)
    d_query = jnp.zeros((rows, inner), F32)
    d_key = jnp.zeros((rows, inner), F32)
    d_value = jnp.zeros((rows, inner), F32)
    for head in range(heads):
        mask = head_mask(head, inner)
        chance = probs[head].astype(F32)
        d_probs = dot_nt(d_head, value[...] * mask)
        delta = jnp.sum(d_probs * chance, axis=-1, keepdims=True)
        d_scores = (chance * (d_probs - delta)).astype(BF16)
        d_value = d_value + dot_tn(probs[head], d_head * mask)
        d_query = d_query + dot_nn(d_scores, key[...] * mask)
        d_key = d_key + dot_tn(d_scores, query[...] * mask)
    d_query = (d_query * (HEAD_DIM**-0.5)).astype(BF16)
    d_key = (d_key * (HEAD_DIM**-0.5)).astype(BF16)
    d_value = d_value.astype(BF16)
    grads[:inner, :] = dot_tn(d_query, normed[...]).astype(BF16)
    grads[inner : 2 * inner, :] = dot_tn(d_key, normed[...]).astype(BF16)
    grads[2 * inner : 3 * inner, :] = dot_tn(d_value, normed[...]).astype(BF16)
    if blocks_n == 1:
        blocks[0][...] = grads[...]
    else:
        size = blocks[0].shape[0]
        for m in range(blocks_n):
            at = pl.multiple_of((ids[Q_ID] ^ m) * size, 16)
            blocks[m][...] = grads[pl.ds(at, size), :]
    d_in = dot_nn(d_query, weight[:inner])
    d_in = d_in + dot_nn(d_key, weight[inner : 2 * inner])
    whole[:rows, :] = d_in + dot_nn(d_value, weight[2 * inner :])
    half = kept.shape[1]
    kept[...] = whole[:rows, pl.ds(pl.multiple_of(ids[C_ID] * half, LANES), half)].astype(BF16)
    sent[...] = whole[:rows, pl.ds(pl.multiple_of((1 - ids[C_ID]) * half, LANES), half)].astype(BF16)


def last_norm_kernel(ids, own, other, tokens, d_middle, gain, small2, grad_tokens, small, whole):
    joined(ids, own, other, whole)
    d_normed = whole[...]
    unit, scale = norm_parts(tokens[...].astype(F32))
    small[...] = small2[...]
    small[0:1, :] = jnp.sum(d_normed * unit, axis=0, keepdims=True)
    small[1:2, :] = jnp.sum(d_normed, axis=0, keepdims=True)
    grad_tokens[...] = (
        d_middle[...] + norm_back(unit, scale, d_normed * row_of(gain))
    ).astype(BF16)


def sum_kernel(count, *refs):
    total = refs[0][...].astype(F32)
    for m in range(1, count):
        total = total + refs[m][...].astype(F32)
    refs[count][...] = total.astype(BF16)


def pair_kernel(own, came, small, small_came, out):
    size = own.shape[0]
    out[:size, :] = (own[...].astype(F32) + came[...].astype(F32)).astype(BF16)
    out[size:, :] = (small[...] + small_came[...]).astype(BF16)


def spread_kernel(count, ids, *refs):
    parts = refs[:count]
    grad_qkv, grad_out, gain1, bias1, gain2, bias2, router, grads, held = refs[count:]
    size = grads.shape[0] // count
    for m in range(count):
        quarter = ids[Q_ID] ^ m
        grads[pl.ds(pl.multiple_of(quarter * size, 16), size), :] = parts[m][:size, :].astype(F32)
        held[quarter] = parts[m][size:, :].astype(F32)
    total = held[0]
    for quarter in range(1, count):
        total = total + held[quarter]
    for row, out in enumerate((gain1, bias1, gain2, bias2)):
        out[...] = total[row : row + 1, :].reshape(out.shape)
    router[...] = total[8 : 8 + router.shape[0], :]
    inner = grad_qkv.shape[0]
    grad_qkv[...] = grads[:inner, :]
    grad_out[...] = grads[inner:, :]


def after(value, *others):
    return lax.optimization_barrier((value,) + others)[0]


def run(kernel, outs, args, scratch=(), micros=1.0, limit=16):
    smem = pl.BlockSpec(memory_space=pltpu.SMEM)
    vmem = pl.BlockSpec(memory_space=pltpu.VMEM)
    return pl.pallas_call(
        kernel,
        out_shape=[jax.ShapeDtypeStruct(shape, kind) for shape, kind in outs],
        in_specs=[smem if arg.dtype == jnp.int32 and arg.ndim == 1 else vmem for arg in args],
        out_specs=[vmem] * len(outs),
        scratch_shapes=[pltpu.VMEM(shape, kind) for shape, kind in scratch],
        compiler_params=pltpu.CompilerParams(vmem_limit_bytes=limit * 1024 * 1024),
        cost_estimate=pl.CostEstimate(
            flops=int(micros * 1.15e9), bytes_accessed=1024, transcendentals=0
        ),
    )(*args)


def make_body(n_tensor, n_expert, n_dp):
    small_slice = n_expert == 4 and n_dp == 2

    def tensor_swap(value, mask):
        return lax.ppermute(value, "tensor", [(i, i ^ mask) for i in range(n_tensor)])

    def expert_swap(value, mask):
        return lax.ppermute(value, "expert", [(i, i ^ mask) for i in range(n_expert)])

    def dp_swap(value):
        return lax.ppermute(value, "dp", [(i, i ^ 1) for i in range(n_dp)])

    def quarter_swap(value, mask):
        pairs = [(i, i ^ mask) for i in range(n_expert * n_dp)]
        return lax.ppermute(value, ("expert", "dp"), pairs)

    def exchange(blocks):
        if small_slice:
            came = {k: expert_swap(blocks[k], k) for k in (3, 2, 1)}
            return [blocks[0]] + [came[k] for k in range(1, n_expert)]
        order = jnp.arange(n_expert) ^ lax.axis_index("expert")
        stacked = lax.all_to_all(
            jnp.stack(blocks)[order], "expert", split_axis=0, concat_axis=0, tiled=True
        )[order]
        return [stacked[k] for k in range(n_expert)]

    def body(
        tokens,
        routes,
        images_live,
        ln1_gain,
        ln1_bias,
        w_qkv,
        w_out,
        ln2_gain,
        ln2_bias,
        w_router,
        w_up,
        w_down,
        cotangent,
    ):
        rows, width = tokens.shape
        inner = w_qkv.shape[2]
        heads = inner // HEAD_DIM
        experts = w_router.shape[1]
        capacity = max(2, 3 * rows // experts // 8 * 8)
        cap = capacity // 2
        images = rows // SEQ
        half = width // 2
        hidden_width = w_up.shape[2]
        rank = lax.axis_index("tensor")
        owner = lax.axis_index("expert")
        copy = lax.axis_index("dp")
        ids = jnp.stack(
            [
                rank,
                rank % 2,
                owner,
                copy,
                (owner % 2) * 2 + copy,
                jnp.minimum(images_live[0] * SEQ, rows),
                rank,
                rank,
            ]
        ).astype(jnp.int32)
        weight = w_qkv.transpose(1, 2, 0).reshape(3 * inner, width)
        up_a, down_a = w_up[0], w_down[0]
        part_rows = max(8, -(-experts // 8) * 8)
        small_rows = 8 + part_rows
        base = -(-rows // 16) * 16
        tall = base + -(-part_rows // 16) * 16

        out_x, out_c = tensor_swap(w_out, 2), tensor_swap(w_out, 1)
        up_b, down_b = tensor_swap(up_a, 1), tensor_swap(down_a, 1)
        normed, query, key, value, probs, head_out = run(
            functools.partial(attend_kernel, images),
            [((rows, width), BF16)]
            + [((rows, inner), BF16)] * 3
            + [((heads, rows, rows), BF16), ((rows, inner), BF16)],
            [tokens, ln1_gain, ln1_bias, weight],
            micros=4,
        )
        head_out, out_x, out_c, up_b, down_b = lax.optimization_barrier(
            (head_out, out_x, out_c, up_b, down_b)
        )
        head_x, head_c = tensor_swap(head_out, 2), tensor_swap(head_out, 1)
        quarter = cap // 2
        cot_shapes = [(quarter if small_slice and k > 1 else cap, width) for k in range(experts)]
        table, part, router, *cot_blocks = run(
            functools.partial(plan_kernel, experts),
            [((experts, cap, rows), BF16), ((experts, quarter, rows), BF16)]
            + [((LANES, width), BF16)]
            + [(shape, BF16) for shape in cot_shapes],
            [ids, after(routes.T, head_out), cotangent, w_router.T],
            micros=2,
        )
        head_x = after(head_x, table)
        if small_slice:
            d_rows_in = cot_blocks[:2] + [expert_swap(cot_blocks[k], k) for k in (2, 3)]
        else:
            d_rows_in = exchange(cot_blocks)
        out_all = [w_out, out_c, out_x, tensor_swap(out_x, 1)]
        heads_all = [head_out, head_c, head_x, tensor_swap(head_x, 1)]
        middle, *row_blocks = run(
            functools.partial(middle_kernel, n_tensor, experts),
            [((rows, width), F32)] + [((cap, width), BF16)] * experts,
            [ids, tokens, ln2_gain, ln2_bias, table] + heads_all + out_all,
            scratch=[
                ((n_tensor, rows, inner), BF16),
                ((n_tensor, inner, width), BF16),
                ((rows, width), BF16),
            ],
            micros=3,
        )
        if small_slice:
            *row_blocks, far_2, far_3 = lax.optimization_barrier((*row_blocks, *d_rows_in[2:]))
            d_rows_in[2:] = [far_2, far_3]
            d_rows_in[1] = expert_swap(after(d_rows_in[1], middle), 1)
            pair_out = tensor_swap(jnp.stack([far_2, far_3]), 2)
        else:
            pair_out = router
        rows_in = exchange(list(row_blocks))

        calls = [(0, 1), (2, 3)] if small_slice else [tuple(range(experts))]
        worked = []
        d_back, gated = [], []
        for number, call in enumerate(calls):
            count = cap * len(call)
            last = number == len(calls) - 1
            grads = [] if last else [((2 * width, hidden_width), BF16)] * 2
            results = run(
                functools.partial(expert_kernel, experts, call, not last),
                [((cap, width), BF16)] * len(call)
                + [((len(call), quarter if worked else cap, width), BF16)] * 2
                + [((count, width), BF16)] * 2
                + [((count, hidden_width), BF16)] * 4
                + [((part_rows, width), F32)]
                + grads,
                [ids, up_a, up_b, down_a, down_b]
                + [after(router, worked[-1][6]) if worked else router]
                + [pair_out if worked or not small_slice else router]
                + [rows_in[k] for k in call]
                + [d_rows_in[k] for k in call],
                scratch=[((count, width), F32)],
                micros=7,
                limit=24,
            )
            d_back += results[: len(call)]
            gated.append(results[len(call) : len(call) + 2])
            worked.append(results[len(call) + 2 :])

        def combine(blocks, routers):
            return run(
                functools.partial(combine_kernel, experts, len(routers), base),
                [((tall if routers else base, half), BF16)] * 2,
                [ids, table, part] + blocks + routers,
                scratch=[((tall if routers else base, width), F32)],
                micros=2,
            )

        d_home = exchange(d_back)

        grad_own, grad_pair = run(
            weight_grad_kernel,
            [((2 * width, hidden_width), BF16)] * 2,
            [worked[-1][at] for at in (0, 4, 5, 2, 3, 1)] + list(worked[0][7:]),
            micros=4,
            limit=24,
        )
        third = width // 48 * 16
        grad_kept, sent_first, sent_rest = run(
            split_grad_kernel,
            [((width, width), F32), ((third, width), BF16), ((width - third, width), BF16)],
            [ids, grad_own, tensor_swap(grad_pair, 1)],
            scratch=[((2 * width, width), F32), ((width, width), BF16)],
            micros=2,
            limit=24,
        )

        if small_slice:
            far_blocks = run(
                gated_sum_kernel,
                [((quarter, width), BF16)] * 2,
                [gated[1][0], tensor_swap(gated[1][1], 2)],
            )
            gated_blocks = [gated[0][0][0], gated[0][0][1], *far_blocks]
        else:
            gated_blocks = [gated[0][0][k] for k in range(experts)]

        *d_home, sent_first = lax.optimization_barrier((*d_home, *gated_blocks, sent_first))
        d_home, gated_blocks = d_home[:experts], d_home[experts:]
        kept, sent = combine(list(d_home), [one[6] for one in worked])
        chip = (kept.astype(F32) + tensor_swap(sent, 1).astype(F32)).astype(BF16)
        own = (chip.astype(F32) + tensor_swap(chip, 2).astype(F32)).astype(BF16)
        gated_home = exchange(list(gated_blocks))
        came_first = dp_swap(sent_first)
        own, came_first, *gated_home = lax.optimization_barrier((own, came_first, *gated_home))
        other = tensor_swap(own, 1)

        parts = 4 if small_slice else 1
        d_middle, kept1, sent1, small2, *grad_blocks = run(
            functools.partial(back_kernel, parts),
            [((rows, width), F32)]
            + [((rows, half), BF16)] * 2
            + [((small_rows, width), F32)]
            + [((4 * inner // parts, width), BF16)] * parts,
            [
                ids, own, other, middle, cotangent, ln2_gain, w_out, head_out, normed, query,
                key, value, probs, weight,
            ],
            scratch=[((tall, width), F32), ((4 * inner, width), BF16)],
            micros=6,
        )

        *gated_home, _ = lax.optimization_barrier((*gated_home, d_middle))
        kept_y, sent_y = combine(list(gated_home), [])

        chip1 = (kept1.astype(F32) + tensor_swap(sent1, 1).astype(F32)).astype(BF16)
        own1 = (chip1.astype(F32) + tensor_swap(chip1, 2).astype(F32)).astype(BF16)
        if small_slice:
            arrived = [grad_blocks[0]] + [quarter_swap(grad_blocks[m], m) for m in (3, 1, 2)]
            arrived[0], kept_y, sent_y = lax.optimization_barrier((arrived[0], kept_y, sent_y))
            size = grad_blocks[0].shape[0]
            (summed,) = run(
                functools.partial(sum_kernel, 4), [((size, width), BF16)], arrived, micros=0.5
            )
            sent_rest, own1 = lax.optimization_barrier((sent_rest, own1, summed))[:2]
        other1 = tensor_swap(own1, 1)
        grad_tokens, small = run(
            last_norm_kernel,
            [((rows, width), BF16), ((small_rows, width), F32)],
            [ids, own1, other1, tokens, d_middle, ln1_gain, small2],
            scratch=[((rows, width), F32)],
            micros=0.01,
        )
        chip_y = (kept_y.astype(F32) + tensor_swap(sent_y, 1).astype(F32)).astype(BF16)
        own_y = (chip_y.astype(F32) + tensor_swap(chip_y, 2).astype(F32)).astype(BF16)
        if small_slice:
            (ready,) = run(
                pair_kernel,
                [((size + small_rows, width), BF16)],
                [summed, expert_swap(summed, 2), small, expert_swap(small, 2)],
                micros=1,
            )
            own_y, ready = lax.optimization_barrier((own_y, ready))
            everything = [ready] + [quarter_swap(ready, m) for m in (1, 2, 3)]
            grad_qkv, grad_out, *sums, grad_router = run(
                functools.partial(spread_kernel, 4),
                [((3 * inner, width), F32), ((inner, width), F32)]
                + [((width,), F32)] * 4
                + [((experts, width), F32)],
                [ids] + everything,
                scratch=[((4 * inner, width), F32), ((4, small_rows, width), F32)],
                micros=3,
            )
        else:
            grads = lax.psum(grad_blocks[0], ("expert", "dp")).astype(F32)
            grad_qkv, grad_out = grads[: 3 * inner], grads[3 * inner :]
            small_sum = lax.psum(small, ("expert", "dp"))
            sums, grad_router = list(small_sum[:4]), small_sum[8 : 8 + experts]

        grad_up, grad_down = run(
            join_grad_kernel,
            [((half, hidden_width), F32), ((hidden_width, half), F32)],
            [grad_kept, came_first, dp_swap(sent_rest)],
            scratch=[((width, width), BF16)],
            micros=2,
        )

        mix_own, mix_other = own_y, tensor_swap(own_y, 1)
        mixture = jnp.where(
            rank % 2 == 0,
            jnp.concatenate([mix_own, mix_other], axis=1),
            jnp.concatenate([mix_other, mix_own], axis=1),
        )[:rows].astype(F32)
        alive = (jnp.arange(rows, dtype=jnp.int32) < images_live[0] * SEQ)[:, None]
        out = jnp.where(alive, middle + mixture, 0.0).astype(BF16)
        return (
            out,
            grad_tokens,
            sums[0],
            sums[1],
            grad_qkv.reshape(3, inner, width).transpose(2, 0, 1),
            grad_out,
            sums[2],
            sums[3],
            grad_router.T,
            grad_up[None],
            grad_down[None],
        )

    return body


def solution(mesh):
    in_specs = (
        P(("expert", "dp"), None),
        P(("expert", "dp"), None),
        P(("expert", "dp")),
        P(),
        P(),
        P(None, None, "tensor"),
        P("tensor", None),
        P(),
        P(),
        P(),
        P("expert", None, "tensor"),
        P("expert", "tensor", None),
        P(("expert", "dp"), None),
    )
    out_specs = (
        P(("expert", "dp"), None),
        P(("expert", "dp"), None),
        P(),
        P(),
        P(None, None, "tensor"),
        P("tensor", None),
        P(),
        P(),
        P(),
        P("expert", "dp", "tensor"),
        P("expert", "tensor", "dp"),
    )
    body = make_body(mesh.shape["tensor"], mesh.shape["expert"], mesh.shape["dp"])
    return jax.shard_map(body, mesh=mesh, in_specs=in_specs, out_specs=out_specs, check_vma=False)
```

```python
import functools

import jax
import jax.numpy as jnp
from jax import lax
from jax.experimental import pallas as pl
from jax.experimental.pallas import tpu as pltpu
from jax.sharding import PartitionSpec as P

HEAD_DIM = 64
SEQ = 197
EPSILON = 1e-06
F32 = jnp.float32
BF16 = jnp.bfloat16
LANES = 128
SMALL = 16


def dot_nn(left, right):
    return lax.dot_general(left, right, (((1,), (0,)), ((), ())), preferred_element_type=F32)


def dot_tn(left, right):
    return lax.dot_general(left, right, (((0,), (0,)), ((), ())), preferred_element_type=F32)


def dot_nt(left, right):
    return lax.dot_general(left, right, (((1,), (1,)), ((), ())), preferred_element_type=F32)


def norm_parts(values_in):
    row_mean = jnp.mean(values_in, axis=-1, keepdims=True)
    centred = values_in - row_mean
    variance = jnp.mean(centred * centred, axis=-1, keepdims=True)
    scale = lax.rsqrt(variance + EPSILON)
    return centred * scale, scale


def norm_back(normed, scale, u):
    return scale * (
        u
        - jnp.mean(u, axis=-1, keepdims=True)
        - normed * jnp.mean(u * normed, axis=-1, keepdims=True)
    )


def iota(shape, dim):
    return lax.broadcasted_iota(jnp.int32, shape, dim)


def row_of(vector):
    return vector[...].reshape(1, vector.shape[0])


def head_mask(head, width):
    lane = iota((1, width), 1)
    return ((lane >= head * HEAD_DIM) & (lane < (head + 1) * HEAD_DIM)).astype(BF16)


def image_of(shape, dim, images):
    at = iota(shape, dim)
    image = jnp.zeros(shape, jnp.int32)
    for number in range(1, images):
        image = image + (at >= number * SEQ).astype(jnp.int32)
    return image


T_ID, C_ID, E_ID, D_ID, Q_ID, L_ID = range(6)


def plan_kernel(experts, ids, routes, cot, router, table, part, router_pad, *blocks):
    rows = cot.shape[0]
    cap = table.shape[1]
    tall = max(16, -(-experts // 16) * 16)
    picks = routes[...]
    expert = iota((tall, rows), 0)
    named = picks[0:1, :] == expert
    for k in range(1, picks.shape[0]):
        named = named | (picks[k : k + 1, :] == expert)
    named = named & (iota((tall, rows), 1) < ids[L_ID])
    marks = jnp.where(named, 1.0, 0.0).astype(BF16)
    earlier = jnp.where(iota((rows, rows), 0) < iota((rows, rows), 1), 1.0, 0.0).astype(BF16)
    slot = dot_nn(marks, earlier)
    first = (ids[C_ID] * cap).astype(F32)
    slot = jnp.where(named, slot - first, -1.0)
    place = iota((cap, rows), 0).astype(F32)
    for x in range(experts):
        table[x] = jnp.where(slot[x : x + 1, :] == place, 1.0, 0.0).astype(BF16)
    quarter = part.shape[1]
    first = ((ids[T_ID] // 2) * quarter).astype(F32)
    place = iota((quarter, rows), 0).astype(F32) + first
    for x in range(experts):
        part[x] = jnp.where(slot[x : x + 1, :] == place, 1.0, 0.0).astype(BF16)
    for k in range(experts):
        source = table if blocks[k].shape[0] == cap else part
        blocks[k][...] = dot_nn(source[ids[E_ID] ^ k], cot[...]).astype(BF16)
    router_pad[...] = jnp.zeros_like(router_pad)
    router_pad[:experts, :] = router[...]


def attend_kernel(images, tokens, gain, bias, weight, normed, query, key, value, probs, head_out):
    rows = tokens.shape[0]
    inner = query.shape[1]
    heads = inner // HEAD_DIM
    unit, _ = norm_parts(tokens[...].astype(F32))
    normed[...] = (unit * row_of(gain) + row_of(bias)).astype(BF16)
    query[...] = dot_nt(normed[...], weight[:inner]).astype(BF16)
    key[...] = dot_nt(normed[...], weight[inner : 2 * inner]).astype(BF16)
    value[...] = dot_nt(normed[...], weight[2 * inner :]).astype(BF16)
    same = image_of((rows, 1), 0, images) == image_of((1, rows), 1, images)
    total = jnp.zeros((rows, inner), F32)
    for head in range(heads):
        mask = head_mask(head, inner)
        scores = dot_nt(query[...] * mask, key[...]) * (HEAD_DIM**-0.5)
        scores = jnp.where(same, scores, -1e30)
        top = jnp.max(scores, axis=-1, keepdims=True)
        weights = jnp.exp(scores - top)
        weights = weights * (1.0 / jnp.sum(weights, axis=-1, keepdims=True))
        probs[head] = weights.astype(BF16)
        total = total + dot_nn(probs[head], value[...] * mask)
    head_out[...] = total.astype(BF16)


def middle_kernel(
    n_tensor, experts, ids, tokens, gain, bias, table, *rest
):
    heads = rest[:n_tensor]
    weights = rest[n_tensor : 2 * n_tensor]
    middle = rest[2 * n_tensor]
    blocks = rest[2 * n_tensor + 1 : 2 * n_tensor + 1 + experts]
    held_heads, held_weights, low = rest[2 * n_tensor + 1 + experts :]
    for j in range(n_tensor):
        held_heads[j] = heads[j][...]
        held_weights[j] = weights[j][...]
    total = tokens[...].astype(F32)
    for rank in range(n_tensor):
        place = ids[T_ID] ^ rank
        total = total + dot_nn(held_heads[place], held_weights[place])
    middle[...] = total
    unit, _ = norm_parts(total)
    low[...] = (unit * row_of(gain) + row_of(bias)).astype(BF16)
    for k in range(experts):
        blocks[k][...] = dot_nn(table[ids[E_ID] ^ k], low[...]).astype(BF16)


def expert_kernel(
    experts, places, with_grads, ids, up_a, up_b, down_a, down_b, router, pair_out, *refs
):
    number = len(places)
    row_blocks, out_blocks = refs[:number], refs[number : 2 * number]
    refs = refs[2 * number :]
    back_blocks, gated_kept, gated_sent = refs[:number], refs[number], refs[number + 1]
    refs = refs[number + 2 :]
    rows_in, d_result, hidden_a, hidden_b, d_pre_a, d_pre_b, router_part = refs[:7]
    d_out = refs[-1]
    size = row_blocks[0].shape[0]
    count = size * number
    far = ids[T_ID] // 2
    for k in range(number):
        rows_in[k * size : (k + 1) * size, :] = row_blocks[k][...]
        quarter = out_blocks[k].shape[0]
        if quarter == size:
            d_out[k * size : (k + 1) * size, :] = out_blocks[k][...].astype(F32)
        else:
            here = pl.multiple_of(k * size + far * quarter, 8)
            there = pl.multiple_of(k * size + (1 - far) * quarter, 8)
            d_out[pl.ds(here, quarter), :] = out_blocks[k][...].astype(F32)
            d_out[pl.ds(there, quarter), :] = pair_out[places[k] - 2].astype(F32)
    lane = iota((count, LANES), 1)
    logits = dot_nt(rows_in[...], router[...])
    logits = jnp.where(lane < experts, logits, -1e30)
    top = jnp.max(logits, axis=-1, keepdims=True)
    odds = jnp.exp(logits - top)
    odds = odds / jnp.sum(odds, axis=-1, keepdims=True)
    mine = (lane == ids[E_ID]).astype(F32)
    gate = jnp.sum(odds * mine, axis=-1, keepdims=True)
    d_result[...] = (gate * d_out[...]).astype(BF16)
    result = jnp.zeros(d_out.shape, F32)
    back = jnp.zeros(d_out.shape, F32)
    scale = 0.7978845608028654
    for up, down, hidden, d_pre in (
        (up_a, down_a, hidden_a, d_pre_a),
        (up_b, down_b, hidden_b, d_pre_b),
    ):
        act = dot_nn(rows_in[...], up[...])
        square = act * act
        bend = jnp.tanh(scale * act * (1.0 + 0.044715 * square))
        half = 0.5 * (1.0 + bend)
        hidden[...] = (act * half).astype(BF16)
        slope = half + 0.5 * act * (1.0 - bend * bend) * (
            scale * (1.0 + 3 * 0.044715 * square)
        )
        result = result + dot_nn(hidden[...], down[...])
        d_pre[...] = (dot_nt(d_result[...], down[...]) * slope).astype(BF16)
        back = back + dot_nt(d_pre[...], up[...])
    d_gate = jnp.sum(d_out[...] * result, axis=-1, keepdims=True)
    d_logits = (d_gate * gate * (mine - odds)).astype(BF16)
    back = (back + dot_nn(d_logits, router[...])).astype(BF16)
    for k in range(number):
        back_blocks[k][...] = back[k * size : (k + 1) * size, :]
    d_out[...] = gate * result
    quarter = gated_kept.shape[1]
    for k in range(number):
        if quarter == size:
            gated_kept[k] = d_out[k * size : (k + 1) * size, :].astype(BF16)
        else:
            here = pl.multiple_of(k * size + far * quarter, 8)
            there = pl.multiple_of(k * size + (1 - far) * quarter, 8)
            gated_kept[k] = d_out[pl.ds(here, quarter), :].astype(BF16)
            gated_sent[k] = d_out[pl.ds(there, quarter), :].astype(BF16)
    if quarter == size:
        gated_sent[...] = jnp.zeros_like(gated_sent)
    router_part[...] = dot_tn(d_logits, rows_in[...])[: router_part.shape[0]]
    if with_grads:
        own, pair = refs[7:9]
        weight_grads(rows_in, d_pre_a, d_pre_b, hidden_a, hidden_b, d_result, None, None, own, pair)


def weight_grads(
    rows, d_pre_a, d_pre_b, hidden_a, hidden_b, d_result, own_before, pair_before, own, pair
):
    width = own.shape[0] // 2
    for out, before, at, left, right in (
        (pair, pair_before, 0, rows, d_pre_b),
        (pair, pair_before, width, hidden_b, d_result),
        (own, own_before, 0, rows, d_pre_a),
        (own, own_before, width, hidden_a, d_result),
    ):
        total = dot_tn(left[...], right[...])
        if before is not None:
            total = total + before[at : at + width, :].astype(F32)
        out[at : at + width, :] = total.astype(BF16)


def gated_sum_kernel(kept, came, *blocks):
    for k, out in enumerate(blocks):
        out[...] = (kept[k].astype(F32) + came[k].astype(F32)).astype(BF16)


def weight_grad_kernel(*refs):
    rows, d_pre_a, d_pre_b, hidden_a, hidden_b, d_result = refs[:6]
    own_before, pair_before = refs[6:8] if len(refs) == 10 else (None, None)
    weight_grads(
        rows, d_pre_a, d_pre_b, hidden_a, hidden_b, d_result, own_before, pair_before, *refs[-2:]
    )


def split_grad_kernel(ids, own, came, kept, sent_first, sent_rest, total, sent):
    total[...] = own[...].astype(F32) + came[...].astype(F32)
    width = own.shape[1]
    half = width // 2
    mine, other = ids[D_ID], 1 - ids[D_ID]
    kept[:half, :] = total[pl.ds(pl.multiple_of(mine * half, 16), half), :]
    sent[:half, :] = total[pl.ds(pl.multiple_of(other * half, 16), half), :].astype(BF16)
    column = pl.ds(pl.multiple_of(mine * half, LANES), half)
    kept[half:, :half] = total[width : width + half, column]
    kept[half:, half:] = total[width + half :, column]
    column = pl.ds(pl.multiple_of(other * half, LANES), half)
    sent[half:, :half] = total[width : width + half, column].astype(BF16)
    sent[half:, half:] = total[width + half :, column].astype(BF16)
    first = sent_first.shape[0]
    sent_first[...] = sent[:first, :]
    sent_rest[...] = sent[first:, :]


def join_grad_kernel(kept, came_first, came_rest, grad_up, grad_down, came):
    first = came_first.shape[0]
    came[:first, :] = came_first[...]
    came[first:, :] = came_rest[...]
    half = kept.shape[1] // 2
    grad_up[...] = kept[:half, :] + came[:half, :].astype(F32)
    grad_down[:half, :] = kept[half:, :half] + came[half:, :half].astype(F32)
    grad_down[half:, :] = kept[half:, half:] + came[half:, half:].astype(F32)


def combine_kernel(experts, parts, base, ids, table, part, *refs):
    blocks = refs[:experts]
    routers = refs[experts : experts + parts]
    kept, sent, total = refs[experts + parts :]
    value = dot_tn(table[ids[E_ID]], blocks[0][...])
    for k in range(1, experts):
        spots = table if blocks[k].shape[0] == table.shape[1] else part
        value = value + dot_tn(spots[ids[E_ID] ^ k], blocks[k][...])
    total[...] = jnp.zeros_like(total)
    total[: value.shape[0], :] = value
    if parts:
        added = routers[0][...]
        for k in range(1, parts):
            added = added + routers[k][...]
        total[base : base + added.shape[0], :] = added
    half = kept.shape[1]
    kept[...] = total[:, pl.ds(pl.multiple_of(ids[C_ID] * half, LANES), half)].astype(BF16)
    sent[...] = total[:, pl.ds(pl.multiple_of((1 - ids[C_ID]) * half, LANES), half)].astype(BF16)


def joined(ids, own, other, whole):
    half = own.shape[1]
    whole[:, pl.ds(pl.multiple_of(ids[C_ID] * half, LANES), half)] = own[...].astype(F32)
    whole[:, pl.ds(pl.multiple_of((1 - ids[C_ID]) * half, LANES), half)] = other[...].astype(F32)


def back_kernel(
    blocks_n, ids, own, other, middle, cot, gain, w_out, head_out, normed, query, key, value,
    probs, weight, *rest
):
    d_middle, kept, sent, small = rest[:4]
    blocks = rest[4 : 4 + blocks_n]
    whole, grads = rest[4 + blocks_n :]
    rows, inner = query.shape
    heads = inner // HEAD_DIM
    joined(ids, own, other, whole)
    d_normed = whole[:rows, :]
    unit, scale = norm_parts(middle[...])
    small[...] = jnp.zeros_like(small)
    base = -(-rows // 16) * 16
    small[8:, :] = whole[base : base + small.shape[0] - 8, :]
    small[2:3, :] = jnp.sum(d_normed * unit, axis=0, keepdims=True)
    small[3:4, :] = jnp.sum(d_normed, axis=0, keepdims=True)
    live = iota((rows, 1), 0) < ids[L_ID]
    d_out = jnp.where(live, cot[...].astype(F32), 0.0)
    d_mid = d_out + norm_back(unit, scale, d_normed * row_of(gain))
    d_middle[...] = d_mid
    d_branch = d_mid.astype(BF16)
    d_head = dot_nt(d_branch, w_out[...]).astype(BF16)
    grads[3 * inner :, :] = dot_tn(head_out[...], d_branch).astype(BF16)
    d_query = jnp.zeros((rows, inner), F32)
    d_key = jnp.zeros((rows, inner), F32)
    d_value = jnp.zeros((rows, inner), F32)
    for head in range(heads):
        mask = head_mask(head, inner)
        chance = probs[head].astype(F32)
        d_probs = dot_nt(d_head, value[...] * mask)
        delta = jnp.sum(d_probs * chance, axis=-1, keepdims=True)
        d_scores = (chance * (d_probs - delta)).astype(BF16)
        d_value = d_value + dot_tn(probs[head], d_head * mask)
        d_query = d_query + dot_nn(d_scores, key[...] * mask)
        d_key = d_key + dot_tn(d_scores, query[...] * mask)
    d_query = (d_query * (HEAD_DIM**-0.5)).astype(BF16)
    d_key = (d_key * (HEAD_DIM**-0.5)).astype(BF16)
    d_value = d_value.astype(BF16)
    grads[:inner, :] = dot_tn(d_query, normed[...]).astype(BF16)
    grads[inner : 2 * inner, :] = dot_tn(d_key, normed[...]).astype(BF16)
    grads[2 * inner : 3 * inner, :] = dot_tn(d_value, normed[...]).astype(BF16)
    if blocks_n == 1:
        blocks[0][...] = grads[...]
    else:
        size = blocks[0].shape[0]
        for m in range(blocks_n):
            at = pl.multiple_of((ids[Q_ID] ^ m) * size, 16)
            blocks[m][...] = grads[pl.ds(at, size), :]
    d_in = dot_nn(d_query, weight[:inner])
    d_in = d_in + dot_nn(d_key, weight[inner : 2 * inner])
    whole[:rows, :] = d_in + dot_nn(d_value, weight[2 * inner :])
    half = kept.shape[1]
    kept[...] = whole[:rows, pl.ds(pl.multiple_of(ids[C_ID] * half, LANES), half)].astype(BF16)
    sent[...] = whole[:rows, pl.ds(pl.multiple_of((1 - ids[C_ID]) * half, LANES), half)].astype(BF16)


def last_norm_kernel(ids, own, other, tokens, d_middle, gain, small2, grad_tokens, small, whole):
    joined(ids, own, other, whole)
    d_normed = whole[...]
    unit, scale = norm_parts(tokens[...].astype(F32))
    small[...] = small2[...]
    small[0:1, :] = jnp.sum(d_normed * unit, axis=0, keepdims=True)
    small[1:2, :] = jnp.sum(d_normed, axis=0, keepdims=True)
    grad_tokens[...] = (
        d_middle[...] + norm_back(unit, scale, d_normed * row_of(gain))
    ).astype(BF16)


def sum_kernel(count, *refs):
    total = refs[0][...].astype(F32)
    for m in range(1, count):
        total = total + refs[m][...].astype(F32)
    refs[count][...] = total.astype(BF16)


def pair_kernel(own, came, small, small_came, out):
    size = own.shape[0]
    out[:size, :] = (own[...].astype(F32) + came[...].astype(F32)).astype(BF16)
    out[size:, :] = (small[...] + small_came[...]).astype(BF16)


def spread_kernel(count, ids, *refs):
    parts = refs[:count]
    grad_qkv, grad_out, gain1, bias1, gain2, bias2, router, grads, held = refs[count:]
    size = grads.shape[0] // count
    for m in range(count):
        quarter = ids[Q_ID] ^ m
        grads[pl.ds(pl.multiple_of(quarter * size, 16), size), :] = parts[m][:size, :].astype(F32)
        held[quarter] = parts[m][size:, :].astype(F32)
    total = held[0]
    for quarter in range(1, count):
        total = total + held[quarter]
    for row, out in enumerate((gain1, bias1, gain2, bias2)):
        out[...] = total[row : row + 1, :].reshape(out.shape)
    router[...] = total[8 : 8 + router.shape[0], :]
    inner = grad_qkv.shape[0]
    grad_qkv[...] = grads[:inner, :]
    grad_out[...] = grads[inner:, :]


def run(kernel, outs, args, scratch=(), micros=1.0, limit=16):
    smem = pl.BlockSpec(memory_space=pltpu.SMEM)
    vmem = pl.BlockSpec(memory_space=pltpu.VMEM)
    return pl.pallas_call(
        kernel,
        out_shape=[jax.ShapeDtypeStruct(shape, kind) for shape, kind in outs],
        in_specs=[smem if arg.dtype == jnp.int32 and arg.ndim == 1 else vmem for arg in args],
        out_specs=[vmem] * len(outs),
        scratch_shapes=[pltpu.VMEM(shape, kind) for shape, kind in scratch],
        compiler_params=pltpu.CompilerParams(vmem_limit_bytes=limit * 1024 * 1024),
        cost_estimate=pl.CostEstimate(
            flops=int(micros * 1.15e9), bytes_accessed=1024, transcendentals=0
        ),
    )(*args)


def make_body(n_tensor, n_expert, n_dp):
    small_slice = n_expert == 4 and n_dp == 2

    def tensor_swap(value, mask):
        return lax.ppermute(value, "tensor", [(i, i ^ mask) for i in range(n_tensor)])

    def expert_swap(value, mask):
        return lax.ppermute(value, "expert", [(i, i ^ mask) for i in range(n_expert)])

    def dp_swap(value):
        return lax.ppermute(value, "dp", [(i, i ^ 1) for i in range(n_dp)])

    def quarter_swap(value, mask):
        pairs = [(i, i ^ mask) for i in range(n_expert * n_dp)]
        return lax.ppermute(value, ("expert", "dp"), pairs)

    def exchange(blocks):
        if small_slice:
            came = {k: expert_swap(blocks[k], k) for k in (3, 2, 1)}
            return [blocks[0]] + [came[k] for k in range(1, n_expert)]
        order = jnp.arange(n_expert) ^ lax.axis_index("expert")
        stacked = lax.all_to_all(
            jnp.stack(blocks)[order], "expert", split_axis=0, concat_axis=0, tiled=True
        )[order]
        return [stacked[k] for k in range(n_expert)]

    def body(
        tokens,
        routes,
        images_live,
        ln1_gain,
        ln1_bias,
        w_qkv,
        w_out,
        ln2_gain,
        ln2_bias,
        w_router,
        w_up,
        w_down,
        cotangent,
    ):
        rows, width = tokens.shape
        inner = w_qkv.shape[2]
        heads = inner // HEAD_DIM
        experts = w_router.shape[1]
        capacity = max(2, 3 * rows // experts // 8 * 8)
        cap = capacity // 2
        images = rows // SEQ
        half = width // 2
        hidden_width = w_up.shape[2]
        rank = lax.axis_index("tensor")
        owner = lax.axis_index("expert")
        copy = lax.axis_index("dp")
        ids = jnp.stack(
            [
                rank,
                rank % 2,
                owner,
                copy,
                (owner % 2) * 2 + copy,
                jnp.minimum(images_live[0] * SEQ, rows),
                rank,
                rank,
            ]
        ).astype(jnp.int32)
        weight = w_qkv.transpose(1, 2, 0).reshape(3 * inner, width)
        up_a, down_a = w_up[0], w_down[0]
        part_rows = max(8, -(-experts // 8) * 8)
        small_rows = 8 + part_rows
        base = -(-rows // 16) * 16
        tall = base + -(-part_rows // 16) * 16

        out_x, out_c = tensor_swap(w_out, 2), tensor_swap(w_out, 1)
        up_b, down_b = tensor_swap(up_a, 1), tensor_swap(down_a, 1)
        quarter = cap // 2
        cot_shapes = [(quarter if small_slice and k > 1 else cap, width) for k in range(experts)]
        table, part, router, *cot_blocks = run(
            functools.partial(plan_kernel, experts),
            [((experts, cap, rows), BF16), ((experts, quarter, rows), BF16)]
            + [((LANES, width), BF16)]
            + [(shape, BF16) for shape in cot_shapes],
            [ids, routes.T, cotangent, w_router.T],
            micros=2,
        )
        tokens_first, table, part = lax.optimization_barrier((tokens, table, part))
        normed, query, key, value, probs, head_out = run(
            functools.partial(attend_kernel, images),
            [((rows, width), BF16)]
            + [((rows, inner), BF16)] * 3
            + [((heads, rows, rows), BF16), ((rows, inner), BF16)],
            [tokens_first, ln1_gain, ln1_bias, weight],
            micros=4,
        )
        if small_slice:
            cot_blocks[3] = expert_swap(cot_blocks[3], 3)
        head_out, out_x, out_c, up_b, down_b, cot_blocks[-1] = lax.optimization_barrier(
            (head_out, out_x, out_c, up_b, down_b, cot_blocks[-1])
        )
        head_x, head_c = tensor_swap(head_out, 2), tensor_swap(head_out, 1)
        if small_slice:
            cot_blocks[2] = expert_swap(cot_blocks[2], 2)
            d_rows_in = cot_blocks
        else:
            d_rows_in = exchange(cot_blocks)
        out_all = [w_out, out_c, out_x, tensor_swap(out_x, 1)]
        heads_all = [head_out, head_c, head_x, tensor_swap(head_x, 1)]
        spots = table
        if small_slice:
            spots, d_rows_in[2], d_rows_in[3] = lax.optimization_barrier(
                (table, d_rows_in[2], d_rows_in[3])
            )
        middle, *row_blocks = run(
            functools.partial(middle_kernel, n_tensor, experts),
            [((rows, width), F32)] + [((cap, width), BF16)] * experts,
            [ids, tokens, ln2_gain, ln2_bias, spots] + heads_all + out_all,
            scratch=[
                ((n_tensor, rows, inner), BF16),
                ((n_tensor, inner, width), BF16),
                ((rows, width), BF16),
            ],
            micros=3,
        )
        if small_slice:
            pair_out = jnp.stack(d_rows_in[2:])
            d_rows_in[1], middle = lax.optimization_barrier((d_rows_in[1], middle))
            d_rows_in[1] = expert_swap(d_rows_in[1], 1)
        else:
            pair_out = router
        rows_in = exchange(list(row_blocks))

        calls = [(0, 1), (2, 3)] if small_slice else [tuple(range(experts))]
        worked = []
        d_back, gated = [], []
        for number, call in enumerate(calls):
            if number == 1:
                router, pair_out, d_back[1] = lax.optimization_barrier((router, pair_out, d_back[1]))
                pair_out = tensor_swap(pair_out, 2)
            count = cap * len(call)
            last = number == len(calls) - 1
            grads = [] if last else [((2 * width, hidden_width), BF16)] * 2
            results = run(
                functools.partial(expert_kernel, experts, call, not last),
                [((cap, width), BF16)] * len(call)
                + [((len(call), quarter if worked else cap, width), BF16)] * 2
                + [((count, width), BF16)] * 2
                + [((count, hidden_width), BF16)] * 4
                + [((part_rows, width), F32)]
                + grads,
                [ids, up_a, up_b, down_a, down_b]
                + [router]
                + [pair_out if worked or not small_slice else router]
                + [rows_in[k] for k in call]
                + [d_rows_in[k] for k in call],
                scratch=[((count, width), F32)],
                micros=7,
                limit=24,
            )
            d_back += results[: len(call)]
            gated.append(results[len(call) : len(call) + 2])
            worked.append(results[len(call) + 2 :])

        def combine(blocks, routers):
            return run(
                functools.partial(combine_kernel, experts, len(routers), base),
                [((tall if routers else base, half), BF16)] * 2,
                [ids, table, part] + blocks + routers,
                scratch=[((tall if routers else base, width), F32)],
                micros=2,
            )

        if small_slice:
            home = {k: expert_swap(d_back[k], k) for k in (3, 2, 1)}
            d_home = [d_back[0]] + [home[k] for k in (1, 2, 3)]
        else:
            d_home = exchange(d_back)

        grad_own, grad_pair = run(
            weight_grad_kernel,
            [((2 * width, hidden_width), BF16)] * 2,
            [worked[-1][at] for at in (0, 4, 5, 2, 3, 1)] + list(worked[0][7:]),
            micros=4,
            limit=24,
        )
        third = width // 48 * 16
        grad_kept, sent_first, sent_rest = run(
            split_grad_kernel,
            [((width, width), F32), ((third, width), BF16), ((width - third, width), BF16)],
            [ids, grad_own, tensor_swap(grad_pair, 1)],
            scratch=[((2 * width, width), F32), ((width, width), BF16)],
            micros=2,
            limit=24,
        )

        if small_slice:
            far_blocks = run(
                gated_sum_kernel,
                [((quarter, width), BF16)] * 2,
                [gated[1][0], tensor_swap(gated[1][1], 2)],
            )
            gated_blocks = [gated[0][0][0], gated[0][0][1], *far_blocks]
        else:
            gated_blocks = [gated[0][0][k] for k in range(experts)]

        *d_home, sent_first = lax.optimization_barrier((*d_home, *gated_blocks, sent_first))
        d_home, gated_blocks = d_home[:experts], d_home[experts:]
        kept, sent = combine(list(d_home), [one[6] for one in worked])
        chip = (kept.astype(F32) + tensor_swap(sent, 1).astype(F32)).astype(BF16)
        own = (chip.astype(F32) + tensor_swap(chip, 2).astype(F32)).astype(BF16)
        came_first = dp_swap(sent_first)
        if small_slice:
            gated_home = [gated_blocks[0]] + [expert_swap(gated_blocks[k], k) for k in (1, 2)]
        else:
            gated_home = exchange(list(gated_blocks))
        own, came_first, *gated_home = lax.optimization_barrier((own, came_first, *gated_home))
        other = tensor_swap(own, 1)

        parts = 4 if small_slice else 1
        d_middle, kept1, sent1, small2, *grad_blocks = run(
            functools.partial(back_kernel, parts),
            [((rows, width), F32)]
            + [((rows, half), BF16)] * 2
            + [((small_rows, width), F32)]
            + [((4 * inner // parts, width), BF16)] * parts,
            [
                ids, own, other, middle, cotangent, ln2_gain, w_out, head_out, normed, query,
                key, value, probs, weight,
            ],
            scratch=[((tall, width), F32), ((4 * inner, width), BF16)],
            micros=6,
        )

        if small_slice:
            last_block, d_middle = lax.optimization_barrier((gated_blocks[3], d_middle))
            gated_home = list(gated_home) + [expert_swap(last_block, 3)]
        *gated_home, d_middle = lax.optimization_barrier((*gated_home, d_middle))
        kept_y, sent_y = combine(list(gated_home), [])

        chip1 = (kept1.astype(F32) + tensor_swap(sent1, 1).astype(F32)).astype(BF16)
        own1 = (chip1.astype(F32) + tensor_swap(chip1, 2).astype(F32)).astype(BF16)
        if small_slice:
            arrived = [grad_blocks[0]] + [quarter_swap(grad_blocks[m], m) for m in (3, 1, 2)]
            arrived[0], kept_y, sent_y = lax.optimization_barrier((arrived[0], kept_y, sent_y))
            size = grad_blocks[0].shape[0]
            (summed,) = run(
                functools.partial(sum_kernel, 4), [((size, width), BF16)], arrived, micros=0.5
            )
            sent_rest, own1, summed = lax.optimization_barrier((sent_rest, own1, summed))
            came_rest = dp_swap(sent_rest)
            summed_came = expert_swap(summed, 2)
        other1 = tensor_swap(own1, 1)
        grad_tokens, small = run(
            last_norm_kernel,
            [((rows, width), BF16), ((small_rows, width), F32)],
            [ids, own1, other1, tokens, d_middle, ln1_gain, small2],
            scratch=[((rows, width), F32)],
            micros=0.01,
        )
        chip_y = (kept_y.astype(F32) + tensor_swap(sent_y, 1).astype(F32)).astype(BF16)
        own_y = (chip_y.astype(F32) + tensor_swap(chip_y, 2).astype(F32)).astype(BF16)
        if small_slice:
            summed, came_rest = lax.optimization_barrier((summed, came_rest))
            (ready,) = run(
                pair_kernel,
                [((size + small_rows, width), BF16)],
                [summed, summed_came, small, expert_swap(small, 2)],
                micros=1,
            )
            own_y, ready = lax.optimization_barrier((own_y, ready))
            everything = [ready] + [quarter_swap(ready, m) for m in (1, 2, 3)]
            grad_qkv, grad_out, *sums, grad_router = run(
                functools.partial(spread_kernel, 4),
                [((3 * inner, width), F32), ((inner, width), F32)]
                + [((width,), F32)] * 4
                + [((experts, width), F32)],
                [ids] + everything,
                scratch=[((4 * inner, width), F32), ((4, small_rows, width), F32)],
                micros=3,
            )
        else:
            grads = lax.psum(grad_blocks[0], ("expert", "dp")).astype(F32)
            grad_qkv, grad_out = grads[: 3 * inner], grads[3 * inner :]
            small_sum = lax.psum(small, ("expert", "dp"))
            came_rest = dp_swap(sent_rest)
            sums, grad_router = list(small_sum[:4]), small_sum[8 : 8 + experts]

        grad_up, grad_down = run(
            join_grad_kernel,
            [((half, hidden_width), F32), ((hidden_width, half), F32)],
            [grad_kept, came_first, came_rest],
            scratch=[((width, width), BF16)],
            micros=2,
        )

        mix_own, mix_other = own_y, tensor_swap(own_y, 1)
        mixture = jnp.where(
            rank % 2 == 0,
            jnp.concatenate([mix_own, mix_other], axis=1),
            jnp.concatenate([mix_other, mix_own], axis=1),
        )[:rows].astype(F32)
        alive = (jnp.arange(rows, dtype=jnp.int32) < images_live[0] * SEQ)[:, None]
        out = jnp.where(alive, middle + mixture, 0.0).astype(BF16)
        return (
            out,
            grad_tokens,
            sums[0],
            sums[1],
            grad_qkv.reshape(3, inner, width).transpose(2, 0, 1),
            grad_out,
            sums[2],
            sums[3],
            grad_router.T,
            grad_up[None],
            grad_down[None],
        )

    return body


def solution(mesh):
    in_specs = (
        P(("expert", "dp"), None),
        P(("expert", "dp"), None),
        P(("expert", "dp")),
        P(),
        P(),
        P(None, None, "tensor"),
        P("tensor", None),
        P(),
        P(),
        P(),
        P("expert", None, "tensor"),
        P("expert", "tensor", None),
        P(("expert", "dp"), None),
    )
    out_specs = (
        P(("expert", "dp"), None),
        P(("expert", "dp"), None),
        P(),
        P(),
        P(None, None, "tensor"),
        P("tensor", None),
        P(),
        P(),
        P(),
        P("expert", "dp", "tensor"),
        P("expert", "tensor", "dp"),
    )
    body = make_body(mesh.shape["tensor"], mesh.shape["expert"], mesh.shape["dp"])
    return jax.shard_map(body, mesh=mesh, in_specs=in_specs, out_specs=out_specs, check_vma=False)
```

```python
import functools

import jax
import jax.numpy as jnp
from jax import lax
from jax.experimental import pallas as pl
from jax.experimental.pallas import tpu as pltpu
from jax.sharding import PartitionSpec as P

HEAD_DIM = 64
SEQ = 197
EPSILON = 1e-06
F32 = jnp.float32
BF16 = jnp.bfloat16
LANES = 128
SMALL = 16


def dot_nn(left, right):
    return lax.dot_general(left, right, (((1,), (0,)), ((), ())), preferred_element_type=F32)


def dot_tn(left, right):
    return lax.dot_general(left, right, (((0,), (0,)), ((), ())), preferred_element_type=F32)


def dot_nt(left, right):
    return lax.dot_general(left, right, (((1,), (1,)), ((), ())), preferred_element_type=F32)


def norm_parts(values_in):
    row_mean = jnp.mean(values_in, axis=-1, keepdims=True)
    centred = values_in - row_mean
    variance = jnp.mean(centred * centred, axis=-1, keepdims=True)
    scale = lax.rsqrt(variance + EPSILON)
    return centred * scale, scale


def norm_back(normed, scale, u):
    return scale * (
        u
        - jnp.mean(u, axis=-1, keepdims=True)
        - normed * jnp.mean(u * normed, axis=-1, keepdims=True)
    )


def iota(shape, dim):
    return lax.broadcasted_iota(jnp.int32, shape, dim)


def row_of(vector):
    return vector[...].reshape(1, vector.shape[0])


def head_mask(head, width):
    lane = iota((1, width), 1)
    return ((lane >= head * HEAD_DIM) & (lane < (head + 1) * HEAD_DIM)).astype(BF16)


def image_of(shape, dim, images):
    at = iota(shape, dim)
    image = jnp.zeros(shape, jnp.int32)
    for number in range(1, images):
        image = image + (at >= number * SEQ).astype(jnp.int32)
    return image


T_ID, C_ID, E_ID, D_ID, Q_ID, L_ID = range(6)


def plan_kernel(experts, ids, routes, cot, router, table, part, router_pad, *blocks):
    rows = cot.shape[0]
    cap = table.shape[1]
    tall = max(16, -(-experts // 16) * 16)
    picks = routes[...]
    expert = iota((tall, rows), 0)
    named = picks[0:1, :] == expert
    for k in range(1, picks.shape[0]):
        named = named | (picks[k : k + 1, :] == expert)
    named = named & (iota((tall, rows), 1) < ids[L_ID])
    marks = jnp.where(named, 1.0, 0.0).astype(BF16)
    earlier = jnp.where(iota((rows, rows), 0) < iota((rows, rows), 1), 1.0, 0.0).astype(BF16)
    slot = dot_nn(marks, earlier)
    first = (ids[C_ID] * cap).astype(F32)
    slot = jnp.where(named, slot - first, -1.0)
    place = iota((cap, rows), 0).astype(F32)
    for x in range(experts):
        table[x] = jnp.where(slot[x : x + 1, :] == place, 1.0, 0.0).astype(BF16)
    quarter = part.shape[1]
    first = ((ids[T_ID] // 2) * quarter).astype(F32)
    place = iota((quarter, rows), 0).astype(F32) + first
    for x in range(experts):
        part[x] = jnp.where(slot[x : x + 1, :] == place, 1.0, 0.0).astype(BF16)
    for k in range(experts):
        source = table if blocks[k].shape[0] == cap else part
        blocks[k][...] = dot_nn(source[ids[E_ID] ^ k], cot[...]).astype(BF16)
    router_pad[...] = jnp.zeros_like(router_pad)
    router_pad[:experts, :] = router[...]


def attend_kernel(images, tokens, gain, bias, weight, normed, query, key, value, probs, head_out):
    rows = tokens.shape[0]
    inner = query.shape[1]
    heads = inner // HEAD_DIM
    unit, _ = norm_parts(tokens[...].astype(F32))
    normed[...] = (unit * row_of(gain) + row_of(bias)).astype(BF16)
    query[...] = dot_nt(normed[...], weight[:inner]).astype(BF16)
    key[...] = dot_nt(normed[...], weight[inner : 2 * inner]).astype(BF16)
    value[...] = dot_nt(normed[...], weight[2 * inner :]).astype(BF16)
    same = image_of((rows, 1), 0, images) == image_of((1, rows), 1, images)
    total = jnp.zeros((rows, inner), F32)
    for head in range(heads):
        mask = head_mask(head, inner)
        scores = dot_nt(query[...] * mask, key[...]) * (HEAD_DIM**-0.5)
        scores = jnp.where(same, scores, -1e30)
        top = jnp.max(scores, axis=-1, keepdims=True)
        weights = jnp.exp(scores - top)
        weights = weights * (1.0 / jnp.sum(weights, axis=-1, keepdims=True))
        probs[head] = weights.astype(BF16)
        total = total + dot_nn(probs[head], value[...] * mask)
    head_out[...] = total.astype(BF16)


def middle_kernel(
    n_tensor, experts, ids, tokens, gain, bias, table, *rest
):
    heads = rest[:n_tensor]
    weights = rest[n_tensor : 2 * n_tensor]
    middle = rest[2 * n_tensor]
    blocks = rest[2 * n_tensor + 1 : 2 * n_tensor + 1 + experts]
    held_heads, held_weights, low = rest[2 * n_tensor + 1 + experts :]
    for j in range(n_tensor):
        held_heads[j] = heads[j][...]
        held_weights[j] = weights[j][...]
    total = tokens[...].astype(F32)
    for rank in range(n_tensor):
        place = ids[T_ID] ^ rank
        total = total + dot_nn(held_heads[place], held_weights[place])
    middle[...] = total
    unit, _ = norm_parts(total)
    low[...] = (unit * row_of(gain) + row_of(bias)).astype(BF16)
    for k in range(experts):
        blocks[k][...] = dot_nn(table[ids[E_ID] ^ k], low[...]).astype(BF16)


def expert_kernel(
    experts, places, with_grads, ids, up_a, up_b, down_a, down_b, router, pair_out, *refs
):
    number = len(places)
    row_blocks, out_blocks = refs[:number], refs[number : 2 * number]
    refs = refs[2 * number :]
    back_blocks, gated_kept, gated_sent = refs[:number], refs[number], refs[number + 1]
    refs = refs[number + 2 :]
    rows_in, d_result, hidden_a, hidden_b, d_pre_a, d_pre_b, router_part = refs[:7]
    d_out = refs[-1]
    size = row_blocks[0].shape[0]
    count = size * number
    far = ids[T_ID] // 2
    for k in range(number):
        rows_in[k * size : (k + 1) * size, :] = row_blocks[k][...]
        quarter = out_blocks[k].shape[0]
        if quarter == size:
            d_out[k * size : (k + 1) * size, :] = out_blocks[k][...].astype(F32)
        else:
            here = pl.multiple_of(k * size + far * quarter, 8)
            there = pl.multiple_of(k * size + (1 - far) * quarter, 8)
            d_out[pl.ds(here, quarter), :] = out_blocks[k][...].astype(F32)
            d_out[pl.ds(there, quarter), :] = pair_out[places[k] - 2].astype(F32)
    lane = iota((count, LANES), 1)
    logits = dot_nt(rows_in[...], router[...])
    logits = jnp.where(lane < experts, logits, -1e30)
    top = jnp.max(logits, axis=-1, keepdims=True)
    odds = jnp.exp(logits - top)
    odds = odds / jnp.sum(odds, axis=-1, keepdims=True)
    mine = (lane == ids[E_ID]).astype(F32)
    gate = jnp.sum(odds * mine, axis=-1, keepdims=True)
    d_result[...] = (gate * d_out[...]).astype(BF16)
    result = jnp.zeros(d_out.shape, F32)
    back = jnp.zeros(d_out.shape, F32)
    scale = 0.7978845608028654
    for up, down, hidden, d_pre in (
        (up_a, down_a, hidden_a, d_pre_a),
        (up_b, down_b, hidden_b, d_pre_b),
    ):
        act = dot_nn(rows_in[...], up[...])
        square = act * act
        bend = jnp.tanh(scale * act * (1.0 + 0.044715 * square))
        half = 0.5 * (1.0 + bend)
        hidden[...] = (act * half).astype(BF16)
        slope = half + 0.5 * act * (1.0 - bend * bend) * (
            scale * (1.0 + 3 * 0.044715 * square)
        )
        result = result + dot_nn(hidden[...], down[...])
        d_pre[...] = (dot_nt(d_result[...], down[...]) * slope).astype(BF16)
        back = back + dot_nt(d_pre[...], up[...])
    d_gate = jnp.sum(d_out[...] * result, axis=-1, keepdims=True)
    d_logits = (d_gate * gate * (mine - odds)).astype(BF16)
    back = (back + dot_nn(d_logits, router[...])).astype(BF16)
    for k in range(number):
        back_blocks[k][...] = back[k * size : (k + 1) * size, :]
    d_out[...] = gate * result
    quarter = gated_kept.shape[1]
    for k in range(number):
        if quarter == size:
            gated_kept[k] = d_out[k * size : (k + 1) * size, :].astype(BF16)
        else:
            here = pl.multiple_of(k * size + far * quarter, 8)
            there = pl.multiple_of(k * size + (1 - far) * quarter, 8)
            gated_kept[k] = d_out[pl.ds(here, quarter), :].astype(BF16)
            gated_sent[k] = d_out[pl.ds(there, quarter), :].astype(BF16)
    if quarter == size:
        gated_sent[...] = jnp.zeros_like(gated_sent)
    router_part[...] = dot_tn(d_logits, rows_in[...])[: router_part.shape[0]]
    if with_grads:
        own, pair = refs[7:9]
        weight_grads(rows_in, d_pre_a, d_pre_b, hidden_a, hidden_b, d_result, None, None, own, pair)


def weight_grads(
    rows, d_pre_a, d_pre_b, hidden_a, hidden_b, d_result, own_before, pair_before, own, pair
):
    width = own.shape[0] // 2
    for out, before, at, left, right in (
        (pair, pair_before, 0, rows, d_pre_b),
        (pair, pair_before, width, hidden_b, d_result),
        (own, own_before, 0, rows, d_pre_a),
        (own, own_before, width, hidden_a, d_result),
    ):
        total = dot_tn(left[...], right[...])
        if before is not None:
            total = total + before[at : at + width, :].astype(F32)
        out[at : at + width, :] = total.astype(BF16)


def gated_sum_kernel(kept, came, *blocks):
    for k, out in enumerate(blocks):
        out[...] = (kept[k].astype(F32) + came[k].astype(F32)).astype(BF16)


def weight_grad_kernel(*refs):
    rows, d_pre_a, d_pre_b, hidden_a, hidden_b, d_result = refs[:6]
    own_before, pair_before = refs[6:8] if len(refs) == 10 else (None, None)
    weight_grads(
        rows, d_pre_a, d_pre_b, hidden_a, hidden_b, d_result, own_before, pair_before, *refs[-2:]
    )


def split_grad_kernel(ids, own, came, kept, sent_first, sent_rest, total, sent):
    total[...] = own[...].astype(F32) + came[...].astype(F32)
    width = own.shape[1]
    half = width // 2
    mine, other = ids[D_ID], 1 - ids[D_ID]
    kept[:half, :] = total[pl.ds(pl.multiple_of(mine * half, 16), half), :]
    sent[:half, :] = total[pl.ds(pl.multiple_of(other * half, 16), half), :].astype(BF16)
    column = pl.ds(pl.multiple_of(mine * half, LANES), half)
    kept[half:, :half] = total[width : width + half, column]
    kept[half:, half:] = total[width + half :, column]
    column = pl.ds(pl.multiple_of(other * half, LANES), half)
    sent[half:, :half] = total[width : width + half, column].astype(BF16)
    sent[half:, half:] = total[width + half :, column].astype(BF16)
    first = sent_first.shape[0]
    sent_first[...] = sent[:first, :]
    sent_rest[...] = sent[first:, :]


def join_grad_kernel(kept, came_first, came_rest, grad_up, grad_down, came):
    first = came_first.shape[0]
    came[:first, :] = came_first[...]
    came[first:, :] = came_rest[...]
    half = kept.shape[1] // 2
    grad_up[...] = kept[:half, :] + came[:half, :].astype(F32)
    grad_down[:half, :] = kept[half:, :half] + came[half:, :half].astype(F32)
    grad_down[half:, :] = kept[half:, half:] + came[half:, half:].astype(F32)


def combine_kernel(experts, parts, base, ids, table, part, *refs):
    blocks = refs[:experts]
    routers = refs[experts : experts + parts]
    kept, sent, total = refs[experts + parts :]
    value = dot_tn(table[ids[E_ID]], blocks[0][...])
    for k in range(1, experts):
        spots = table if blocks[k].shape[0] == table.shape[1] else part
        value = value + dot_tn(spots[ids[E_ID] ^ k], blocks[k][...])
    total[...] = jnp.zeros_like(total)
    total[: value.shape[0], :] = value
    if parts:
        added = routers[0][...]
        for k in range(1, parts):
            added = added + routers[k][...]
        total[base : base + added.shape[0], :] = added
    half = kept.shape[1]
    kept[...] = total[:, pl.ds(pl.multiple_of(ids[C_ID] * half, LANES), half)].astype(BF16)
    sent[...] = total[:, pl.ds(pl.multiple_of((1 - ids[C_ID]) * half, LANES), half)].astype(BF16)


def joined(ids, own, other, whole):
    half = own.shape[1]
    whole[:, pl.ds(pl.multiple_of(ids[C_ID] * half, LANES), half)] = own[...].astype(F32)
    whole[:, pl.ds(pl.multiple_of((1 - ids[C_ID]) * half, LANES), half)] = other[...].astype(F32)


def back_kernel(
    blocks_n, ids, own, other, middle, cot, gain, w_out, head_out, normed, query, key, value,
    probs, weight, *rest
):
    d_middle, kept, sent, small = rest[:4]
    blocks = rest[4 : 4 + blocks_n]
    whole, grads = rest[4 + blocks_n :]
    rows, inner = query.shape
    heads = inner // HEAD_DIM
    joined(ids, own, other, whole)
    d_normed = whole[:rows, :]
    unit, scale = norm_parts(middle[...])
    small[...] = jnp.zeros_like(small)
    base = -(-rows // 16) * 16
    small[8:, :] = whole[base : base + small.shape[0] - 8, :]
    small[2:3, :] = jnp.sum(d_normed * unit, axis=0, keepdims=True)
    small[3:4, :] = jnp.sum(d_normed, axis=0, keepdims=True)
    live = iota((rows, 1), 0) < ids[L_ID]
    d_out = jnp.where(live, cot[...].astype(F32), 0.0)
    d_mid = d_out + norm_back(unit, scale, d_normed * row_of(gain))
    d_middle[...] = d_mid
    d_branch = d_mid.astype(BF16)
    d_head = dot_nt(d_branch, w_out[...]).astype(BF16)
    grads[3 * inner :, :] = dot_tn(head_out[...], d_branch).astype(BF16)
    d_query = jnp.zeros((rows, inner), F32)
    d_key = jnp.zeros((rows, inner), F32)
    d_value = jnp.zeros((rows, inner), F32)
    for head in range(heads):
        mask = head_mask(head, inner)
        chance = probs[head].astype(F32)
        d_probs = dot_nt(d_head, value[...] * mask)
        delta = jnp.sum(d_probs * chance, axis=-1, keepdims=True)
        d_scores = (chance * (d_probs - delta)).astype(BF16)
        d_value = d_value + dot_tn(probs[head], d_head * mask)
        d_query = d_query + dot_nn(d_scores, key[...] * mask)
        d_key = d_key + dot_tn(d_scores, query[...] * mask)
    d_query = (d_query * (HEAD_DIM**-0.5)).astype(BF16)
    d_key = (d_key * (HEAD_DIM**-0.5)).astype(BF16)
    d_value = d_value.astype(BF16)
    grads[:inner, :] = dot_tn(d_query, normed[...]).astype(BF16)
    grads[inner : 2 * inner, :] = dot_tn(d_key, normed[...]).astype(BF16)
    grads[2 * inner : 3 * inner, :] = dot_tn(d_value, normed[...]).astype(BF16)
    if blocks_n == 1:
        blocks[0][...] = grads[...]
    else:
        size = blocks[0].shape[0]
        for m in range(blocks_n):
            at = pl.multiple_of((ids[Q_ID] ^ m) * size, 16)
            blocks[m][...] = grads[pl.ds(at, size), :]
    d_in = dot_nn(d_query, weight[:inner])
    d_in = d_in + dot_nn(d_key, weight[inner : 2 * inner])
    whole[:rows, :] = d_in + dot_nn(d_value, weight[2 * inner :])
    half = kept.shape[1]
    kept[...] = whole[:rows, pl.ds(pl.multiple_of(ids[C_ID] * half, LANES), half)].astype(BF16)
    sent[...] = whole[:rows, pl.ds(pl.multiple_of((1 - ids[C_ID]) * half, LANES), half)].astype(BF16)


def last_norm_kernel(ids, own, other, tokens, d_middle, gain, small2, grad_tokens, small, whole):
    joined(ids, own, other, whole)
    d_normed = whole[...]
    unit, scale = norm_parts(tokens[...].astype(F32))
    small[...] = small2[...]
    small[0:1, :] = jnp.sum(d_normed * unit, axis=0, keepdims=True)
    small[1:2, :] = jnp.sum(d_normed, axis=0, keepdims=True)
    grad_tokens[...] = (
        d_middle[...] + norm_back(unit, scale, d_normed * row_of(gain))
    ).astype(BF16)


def sum_kernel(count, *refs):
    total = refs[0][...].astype(F32)
    for m in range(1, count):
        total = total + refs[m][...].astype(F32)
    refs[count][...] = total.astype(BF16)


def pair_kernel(own, came, small, small_came, out):
    size = own.shape[0]
    out[:size, :] = (own[...].astype(F32) + came[...].astype(F32)).astype(BF16)
    out[size:, :] = (small[...] + small_came[...]).astype(BF16)


def spread_kernel(count, ids, *refs):
    parts = refs[:count]
    grad_qkv, grad_out, gain1, bias1, gain2, bias2, router, grads, held = refs[count:]
    size = grads.shape[0] // count
    for m in range(count):
        quarter = ids[Q_ID] ^ m
        grads[pl.ds(pl.multiple_of(quarter * size, 16), size), :] = parts[m][:size, :].astype(F32)
        held[quarter] = parts[m][size:, :].astype(F32)
    total = held[0]
    for quarter in range(1, count):
        total = total + held[quarter]
    for row, out in enumerate((gain1, bias1, gain2, bias2)):
        out[...] = total[row : row + 1, :].reshape(out.shape)
    router[...] = total[8 : 8 + router.shape[0], :]
    inner = grad_qkv.shape[0]
    grad_qkv[...] = grads[:inner, :]
    grad_out[...] = grads[inner:, :]


def after(value, *others):
    return lax.optimization_barrier((value,) + others)[0]


def run(kernel, outs, args, scratch=(), micros=1.0, limit=16):
    smem = pl.BlockSpec(memory_space=pltpu.SMEM)
    vmem = pl.BlockSpec(memory_space=pltpu.VMEM)
    return pl.pallas_call(
        kernel,
        out_shape=[jax.ShapeDtypeStruct(shape, kind) for shape, kind in outs],
        in_specs=[smem if arg.dtype == jnp.int32 and arg.ndim == 1 else vmem for arg in args],
        out_specs=[vmem] * len(outs),
        scratch_shapes=[pltpu.VMEM(shape, kind) for shape, kind in scratch],
        compiler_params=pltpu.CompilerParams(vmem_limit_bytes=limit * 1024 * 1024),
        cost_estimate=pl.CostEstimate(
            flops=int(micros * 1.15e9), bytes_accessed=1024, transcendentals=0
        ),
    )(*args)


def make_body(n_tensor, n_expert, n_dp):
    small_slice = n_expert == 4 and n_dp == 2

    def tensor_swap(value, mask):
        return lax.ppermute(value, "tensor", [(i, i ^ mask) for i in range(n_tensor)])

    def expert_swap(value, mask):
        return lax.ppermute(value, "expert", [(i, i ^ mask) for i in range(n_expert)])

    def dp_swap(value):
        return lax.ppermute(value, "dp", [(i, i ^ 1) for i in range(n_dp)])

    def quarter_swap(value, mask):
        pairs = [(i, i ^ mask) for i in range(n_expert * n_dp)]
        return lax.ppermute(value, ("expert", "dp"), pairs)

    def exchange(blocks):
        if small_slice:
            came = {k: expert_swap(blocks[k], k) for k in (3, 2, 1)}
            return [blocks[0]] + [came[k] for k in range(1, n_expert)]
        order = jnp.arange(n_expert) ^ lax.axis_index("expert")
        stacked = lax.all_to_all(
            jnp.stack(blocks)[order], "expert", split_axis=0, concat_axis=0, tiled=True
        )[order]
        return [stacked[k] for k in range(n_expert)]

    def body(
        tokens,
        routes,
        images_live,
        ln1_gain,
        ln1_bias,
        w_qkv,
        w_out,
        ln2_gain,
        ln2_bias,
        w_router,
        w_up,
        w_down,
        cotangent,
    ):
        rows, width = tokens.shape
        inner = w_qkv.shape[2]
        heads = inner // HEAD_DIM
        experts = w_router.shape[1]
        capacity = max(2, 3 * rows // experts // 8 * 8)
        cap = capacity // 2
        images = rows // SEQ
        half = width // 2
        hidden_width = w_up.shape[2]
        rank = lax.axis_index("tensor")
        owner = lax.axis_index("expert")
        copy = lax.axis_index("dp")
        ids = jnp.stack(
            [
                rank,
                rank % 2,
                owner,
                copy,
                (owner % 2) * 2 + copy,
                jnp.minimum(images_live[0] * SEQ, rows),
                rank,
                rank,
            ]
        ).astype(jnp.int32)
        weight = w_qkv.transpose(1, 2, 0).reshape(3 * inner, width)
        up_a, down_a = w_up[0], w_down[0]
        part_rows = max(8, -(-experts // 8) * 8)
        small_rows = 8 + part_rows
        base = -(-rows // 16) * 16
        tall = base + -(-part_rows // 16) * 16

        out_x, out_c = tensor_swap(w_out, 2), tensor_swap(w_out, 1)
        up_b, down_b = tensor_swap(up_a, 1), tensor_swap(down_a, 1)
        normed, query, key, value, probs, head_out = run(
            functools.partial(attend_kernel, images),
            [((rows, width), BF16)]
            + [((rows, inner), BF16)] * 3
            + [((heads, rows, rows), BF16), ((rows, inner), BF16)],
            [tokens, ln1_gain, ln1_bias, weight],
            micros=4,
        )
        head_out, out_x, out_c, up_b, down_b = lax.optimization_barrier(
            (head_out, out_x, out_c, up_b, down_b)
        )
        head_x, head_c = tensor_swap(head_out, 2), tensor_swap(head_out, 1)
        quarter = cap // 2
        cot_shapes = [(quarter if small_slice and k > 1 else cap, width) for k in range(experts)]
        table, part, router, *cot_blocks = run(
            functools.partial(plan_kernel, experts),
            [((experts, cap, rows), BF16), ((experts, quarter, rows), BF16)]
            + [((LANES, width), BF16)]
            + [(shape, BF16) for shape in cot_shapes],
            [ids, after(routes.T, head_out), cotangent, w_router.T],
            micros=2,
        )
        head_x = after(head_x, table)
        if small_slice:
            d_rows_in = cot_blocks[:2] + [expert_swap(cot_blocks[k], k) for k in (2, 3)]
        else:
            d_rows_in = exchange(cot_blocks)
        out_all = [w_out, out_c, out_x, tensor_swap(out_x, 1)]
        heads_all = [head_out, head_c, head_x, tensor_swap(head_x, 1)]
        middle, *row_blocks = run(
            functools.partial(middle_kernel, n_tensor, experts),
            [((rows, width), F32)] + [((cap, width), BF16)] * experts,
            [ids, tokens, ln2_gain, ln2_bias, table] + heads_all + out_all,
            scratch=[
                ((n_tensor, rows, inner), BF16),
                ((n_tensor, inner, width), BF16),
                ((rows, width), BF16),
            ],
            micros=3,
        )
        if small_slice:
            *row_blocks, far_2, far_3 = lax.optimization_barrier((*row_blocks, *d_rows_in[2:]))
            d_rows_in[2:] = [far_2, far_3]
            d_rows_in[1] = expert_swap(after(d_rows_in[1], middle), 1)
            pair_out = tensor_swap(jnp.stack([far_2, far_3]), 2)
        else:
            pair_out = router
        rows_in = exchange(list(row_blocks))

        calls = [(0, 1), (2, 3)] if small_slice else [tuple(range(experts))]
        worked = []
        d_back, gated = [], []
        for number, call in enumerate(calls):
            if number == 1:
                router, d_back[1] = lax.optimization_barrier((router, d_back[1]))
            count = cap * len(call)
            last = number == len(calls) - 1
            grads = [] if last else [((2 * width, hidden_width), BF16)] * 2
            results = run(
                functools.partial(expert_kernel, experts, call, not last),
                [((cap, width), BF16)] * len(call)
                + [((len(call), quarter if worked else cap, width), BF16)] * 2
                + [((count, width), BF16)] * 2
                + [((count, hidden_width), BF16)] * 4
                + [((part_rows, width), F32)]
                + grads,
                [ids, up_a, up_b, down_a, down_b]
                + [router]
                + [pair_out if worked or not small_slice else router]
                + [rows_in[k] for k in call]
                + [d_rows_in[k] for k in call],
                scratch=[((count, width), F32)],
                micros=0.05,
                limit=24,
            )
            d_back += results[: len(call)]
            gated.append(results[len(call) : len(call) + 2])
            worked.append(results[len(call) + 2 :])

        def combine(blocks, routers):
            return run(
                functools.partial(combine_kernel, experts, len(routers), base),
                [((tall if routers else base, half), BF16)] * 2,
                [ids, table, part] + blocks + routers,
                scratch=[((tall if routers else base, width), F32)],
                micros=2,
            )

        d_home = exchange(d_back)

        grad_own, grad_pair = run(
            weight_grad_kernel,
            [((2 * width, hidden_width), BF16)] * 2,
            [worked[-1][at] for at in (0, 4, 5, 2, 3, 1)] + list(worked[0][7:]),
            micros=4,
            limit=24,
        )
        third = width // 48 * 16
        grad_kept, sent_first, sent_rest = run(
            split_grad_kernel,
            [((width, width), F32), ((third, width), BF16), ((width - third, width), BF16)],
            [ids, grad_own, tensor_swap(grad_pair, 1)],
            scratch=[((2 * width, width), F32), ((width, width), BF16)],
            micros=2,
            limit=24,
        )

        if small_slice:
            far_blocks = run(
                gated_sum_kernel,
                [((quarter, width), BF16)] * 2,
                [gated[1][0], tensor_swap(gated[1][1], 2)],
            )
            gated_blocks = [gated[0][0][0], gated[0][0][1], *far_blocks]
        else:
            gated_blocks = [gated[0][0][k] for k in range(experts)]

        *d_home, sent_first = lax.optimization_barrier((*d_home, *gated_blocks, sent_first))
        d_home, gated_blocks = d_home[:experts], d_home[experts:]
        kept, sent = combine(list(d_home), [one[6] for one in worked])
        chip = (kept.astype(F32) + tensor_swap(sent, 1).astype(F32)).astype(BF16)
        own = (chip.astype(F32) + tensor_swap(chip, 2).astype(F32)).astype(BF16)
        gated_home = exchange(list(gated_blocks))
        came_first = dp_swap(sent_first)
        own, came_first, *gated_home = lax.optimization_barrier((own, came_first, *gated_home))
        other = tensor_swap(own, 1)

        parts = 4 if small_slice else 1
        d_middle, kept1, sent1, small2, *grad_blocks = run(
            functools.partial(back_kernel, parts),
            [((rows, width), F32)]
            + [((rows, half), BF16)] * 2
            + [((small_rows, width), F32)]
            + [((4 * inner // parts, width), BF16)] * parts,
            [
                ids, own, other, middle, cotangent, ln2_gain, w_out, head_out, normed, query,
                key, value, probs, weight,
            ],
            scratch=[((tall, width), F32), ((4 * inner, width), BF16)],
            micros=6,
        )

        *gated_home, _ = lax.optimization_barrier((*gated_home, d_middle))
        kept_y, sent_y = combine(list(gated_home), [])

        chip1 = (kept1.astype(F32) + tensor_swap(sent1, 1).astype(F32)).astype(BF16)
        own1 = (chip1.astype(F32) + tensor_swap(chip1, 2).astype(F32)).astype(BF16)
        if small_slice:
            arrived = [grad_blocks[0]] + [quarter_swap(grad_blocks[m], m) for m in (3, 1, 2)]
            arrived[0], kept_y, sent_y = lax.optimization_barrier((arrived[0], kept_y, sent_y))
            size = grad_blocks[0].shape[0]
            (summed,) = run(
                functools.partial(sum_kernel, 4), [((size, width), BF16)], arrived, micros=0.5
            )
            sent_rest, own1 = lax.optimization_barrier((sent_rest, own1, summed))[:2]
        other1 = tensor_swap(own1, 1)
        grad_tokens, small = run(
            last_norm_kernel,
            [((rows, width), BF16), ((small_rows, width), F32)],
            [ids, own1, other1, tokens, d_middle, ln1_gain, small2],
            scratch=[((rows, width), F32)],
            micros=0.01,
        )
        chip_y = (kept_y.astype(F32) + tensor_swap(sent_y, 1).astype(F32)).astype(BF16)
        own_y = (chip_y.astype(F32) + tensor_swap(chip_y, 2).astype(F32)).astype(BF16)
        grad_up, grad_down = run(
            join_grad_kernel,
            [((half, hidden_width), F32), ((hidden_width, half), F32)],
            [grad_kept, came_first, dp_swap(sent_rest)],
            scratch=[((width, width), BF16)],
            micros=2,
        )
        if small_slice:
            (ready,) = run(
                pair_kernel,
                [((size + small_rows, width), BF16)],
                [summed, expert_swap(summed, 2), small, expert_swap(small, 2)],
                micros=1,
            )
            own_y, ready = lax.optimization_barrier((own_y, ready))
            everything = [quarter_swap(ready, m) for m in (1, 2, 3)]
            ready, grad_up, grad_down = lax.optimization_barrier((ready, grad_up, grad_down))
            everything = [ready] + everything
            grad_qkv, grad_out, *sums, grad_router = run(
                functools.partial(spread_kernel, 4),
                [((3 * inner, width), F32), ((inner, width), F32)]
                + [((width,), F32)] * 4
                + [((experts, width), F32)],
                [ids] + everything,
                scratch=[((4 * inner, width), F32), ((4, small_rows, width), F32)],
                micros=3,
            )
        else:
            grads = lax.psum(grad_blocks[0], ("expert", "dp")).astype(F32)
            grad_qkv, grad_out = grads[: 3 * inner], grads[3 * inner :]
            small_sum = lax.psum(small, ("expert", "dp"))
            sums, grad_router = list(small_sum[:4]), small_sum[8 : 8 + experts]

        mix_own, mix_other = own_y, tensor_swap(own_y, 1)
        mixture = jnp.where(
            rank % 2 == 0,
            jnp.concatenate([mix_own, mix_other], axis=1),
            jnp.concatenate([mix_other, mix_own], axis=1),
        )[:rows].astype(F32)
        alive = (jnp.arange(rows, dtype=jnp.int32) < images_live[0] * SEQ)[:, None]
        out = jnp.where(alive, middle + mixture, 0.0).astype(BF16)
        return (
            out,
            grad_tokens,
            sums[0],
            sums[1],
            grad_qkv.reshape(3, inner, width).transpose(2, 0, 1),
            grad_out,
            sums[2],
            sums[3],
            grad_router.T,
            grad_up[None],
            grad_down[None],
        )

    return body


def solution(mesh):
    in_specs = (
        P(("expert", "dp"), None),
        P(("expert", "dp"), None),
        P(("expert", "dp")),
        P(),
        P(),
        P(None, None, "tensor"),
        P("tensor", None),
        P(),
        P(),
        P(),
        P("expert", None, "tensor"),
        P("expert", "tensor", None),
        P(("expert", "dp"), None),
    )
    out_specs = (
        P(("expert", "dp"), None),
        P(("expert", "dp"), None),
        P(),
        P(),
        P(None, None, "tensor"),
        P("tensor", None),
        P(),
        P(),
        P(),
        P("expert", "dp", "tensor"),
        P("expert", "tensor", "dp"),
    )
    body = make_body(mesh.shape["tensor"], mesh.shape["expert"], mesh.shape["dp"])
    return jax.shard_map(body, mesh=mesh, in_specs=in_specs, out_specs=out_specs, check_vma=False)
```

```python
import functools

import jax
import jax.numpy as jnp
from jax import lax
from jax.experimental import pallas as pl
from jax.experimental.pallas import tpu as pltpu
from jax.sharding import PartitionSpec as P

HEAD_DIM = 64
SEQ = 197
EPSILON = 1e-06
F32 = jnp.float32
BF16 = jnp.bfloat16
LANES = 128
SMALL = 16


def dot_nn(left, right):
    return lax.dot_general(left, right, (((1,), (0,)), ((), ())), preferred_element_type=F32)


def dot_tn(left, right):
    return lax.dot_general(left, right, (((0,), (0,)), ((), ())), preferred_element_type=F32)


def dot_nt(left, right):
    return lax.dot_general(left, right, (((1,), (1,)), ((), ())), preferred_element_type=F32)


def norm_parts(values_in):
    row_mean = jnp.mean(values_in, axis=-1, keepdims=True)
    centred = values_in - row_mean
    variance = jnp.mean(centred * centred, axis=-1, keepdims=True)
    scale = lax.rsqrt(variance + EPSILON)
    return centred * scale, scale


def norm_back(normed, scale, u):
    return scale * (
        u
        - jnp.mean(u, axis=-1, keepdims=True)
        - normed * jnp.mean(u * normed, axis=-1, keepdims=True)
    )


def iota(shape, dim):
    return lax.broadcasted_iota(jnp.int32, shape, dim)


def row_of(vector):
    return vector[...].reshape(1, vector.shape[0])


def head_mask(head, width):
    lane = iota((1, width), 1)
    return ((lane >= head * HEAD_DIM) & (lane < (head + 1) * HEAD_DIM)).astype(BF16)


def image_of(shape, dim, images):
    at = iota(shape, dim)
    image = jnp.zeros(shape, jnp.int32)
    for number in range(1, images):
        image = image + (at >= number * SEQ).astype(jnp.int32)
    return image


T_ID, C_ID, E_ID, D_ID, Q_ID, L_ID = range(6)


def plan_kernel(experts, ids, routes, cot, router, table, part, router_pad, *blocks):
    rows = cot.shape[0]
    cap = table.shape[1]
    tall = max(16, -(-experts // 16) * 16)
    picks = routes[...]
    expert = iota((tall, rows), 0)
    named = picks[0:1, :] == expert
    for k in range(1, picks.shape[0]):
        named = named | (picks[k : k + 1, :] == expert)
    named = named & (iota((tall, rows), 1) < ids[L_ID])
    marks = jnp.where(named, 1.0, 0.0).astype(BF16)
    earlier = jnp.where(iota((rows, rows), 0) < iota((rows, rows), 1), 1.0, 0.0).astype(BF16)
    slot = dot_nn(marks, earlier)
    first = (ids[C_ID] * cap).astype(F32)
    slot = jnp.where(named, slot - first, -1.0)
    place = iota((cap, rows), 0).astype(F32)
    for x in range(experts):
        table[x] = jnp.where(slot[x : x + 1, :] == place, 1.0, 0.0).astype(BF16)
    quarter = part.shape[1]
    first = ((ids[T_ID] // 2) * quarter).astype(F32)
    place = iota((quarter, rows), 0).astype(F32) + first
    for x in range(experts):
        part[x] = jnp.where(slot[x : x + 1, :] == place, 1.0, 0.0).astype(BF16)
    for k in range(experts):
        source = table if blocks[k].shape[0] == cap else part
        blocks[k][...] = dot_nn(source[ids[E_ID] ^ k], cot[...]).astype(BF16)
    router_pad[...] = jnp.zeros_like(router_pad)
    router_pad[:experts, :] = router[...]


def attend_kernel(images, tokens, gain, bias, weight, normed, query, key, value, probs, head_out):
    rows = tokens.shape[0]
    inner = query.shape[1]
    heads = inner // HEAD_DIM
    unit, _ = norm_parts(tokens[...].astype(F32))
    normed[...] = (unit * row_of(gain) + row_of(bias)).astype(BF16)
    query[...] = dot_nt(normed[...], weight[:inner]).astype(BF16)
    key[...] = dot_nt(normed[...], weight[inner : 2 * inner]).astype(BF16)
    value[...] = dot_nt(normed[...], weight[2 * inner :]).astype(BF16)
    same = image_of((rows, 1), 0, images) == image_of((1, rows), 1, images)
    total = jnp.zeros((rows, inner), F32)
    for head in range(heads):
        mask = head_mask(head, inner)
        scores = dot_nt(query[...] * mask, key[...]) * (HEAD_DIM**-0.5)
        scores = jnp.where(same, scores, -1e30)
        top = jnp.max(scores, axis=-1, keepdims=True)
        weights = jnp.exp(scores - top)
        weights = weights * (1.0 / jnp.sum(weights, axis=-1, keepdims=True))
        probs[head] = weights.astype(BF16)
        total = total + dot_nn(probs[head], value[...] * mask)
    head_out[...] = total.astype(BF16)


def middle_kernel(
    n_tensor, experts, ids, tokens, gain, bias, table, *rest
):
    heads = rest[:n_tensor]
    weights = rest[n_tensor : 2 * n_tensor]
    middle = rest[2 * n_tensor]
    blocks = rest[2 * n_tensor + 1 : 2 * n_tensor + 1 + experts]
    held_heads, held_weights, low = rest[2 * n_tensor + 1 + experts :]
    for j in range(n_tensor):
        held_heads[j] = heads[j][...]
        held_weights[j] = weights[j][...]
    total = tokens[...].astype(F32)
    for rank in range(n_tensor):
        place = ids[T_ID] ^ rank
        total = total + dot_nn(held_heads[place], held_weights[place])
    middle[...] = total
    unit, _ = norm_parts(total)
    low[...] = (unit * row_of(gain) + row_of(bias)).astype(BF16)
    for k in range(experts):
        blocks[k][...] = dot_nn(table[ids[E_ID] ^ k], low[...]).astype(BF16)


def expert_kernel(
    experts, places, with_grads, ids, up_a, up_b, down_a, down_b, router, *refs
):
    number = len(places)
    row_blocks, out_blocks = refs[:number], refs[number : 2 * number]
    pair_out = refs[2 * number]
    refs = refs[2 * number + 1 :]
    back_blocks, gated_kept, gated_sent = refs[:number], refs[number], refs[number + 1]
    refs = refs[number + 2 :]
    rows_in, d_result, hidden_a, hidden_b, d_pre_a, d_pre_b, router_part = refs[:7]
    d_out = refs[-1]
    size = row_blocks[0].shape[0]
    count = size * number
    far = ids[T_ID] // 2
    for k in range(number):
        rows_in[k * size : (k + 1) * size, :] = row_blocks[k][...]
        quarter = out_blocks[k].shape[0]
        if quarter == size:
            d_out[k * size : (k + 1) * size, :] = out_blocks[k][...].astype(F32)
        else:
            here = pl.multiple_of(k * size + far * quarter, 8)
            there = pl.multiple_of(k * size + (1 - far) * quarter, 8)
            d_out[pl.ds(here, quarter), :] = out_blocks[k][...].astype(F32)
            d_out[pl.ds(there, quarter), :] = pair_out[places[k] - 2].astype(F32)
    lane = iota((count, LANES), 1)
    logits = dot_nt(rows_in[...], router[...])
    logits = jnp.where(lane < experts, logits, -1e30)
    top = jnp.max(logits, axis=-1, keepdims=True)
    odds = jnp.exp(logits - top)
    odds = odds / jnp.sum(odds, axis=-1, keepdims=True)
    mine = (lane == ids[E_ID]).astype(F32)
    gate = jnp.sum(odds * mine, axis=-1, keepdims=True)
    d_result[...] = (gate * d_out[...]).astype(BF16)
    result = jnp.zeros(d_out.shape, F32)
    back = jnp.zeros(d_out.shape, F32)
    scale = 0.7978845608028654
    for up, down, hidden, d_pre in (
        (up_a, down_a, hidden_a, d_pre_a),
        (up_b, down_b, hidden_b, d_pre_b),
    ):
        act = dot_nn(rows_in[...], up[...])
        square = act * act
        bend = jnp.tanh(scale * act * (1.0 + 0.044715 * square))
        half = 0.5 * (1.0 + bend)
        hidden[...] = (act * half).astype(BF16)
        slope = half + 0.5 * act * (1.0 - bend * bend) * (
            scale * (1.0 + 3 * 0.044715 * square)
        )
        result = result + dot_nn(hidden[...], down[...])
        d_pre[...] = (dot_nt(d_result[...], down[...]) * slope).astype(BF16)
        back = back + dot_nt(d_pre[...], up[...])
    d_gate = jnp.sum(d_out[...] * result, axis=-1, keepdims=True)
    d_logits = (d_gate * gate * (mine - odds)).astype(BF16)
    back = (back + dot_nn(d_logits, router[...])).astype(BF16)
    for k in range(number):
        back_blocks[k][...] = back[k * size : (k + 1) * size, :]
    d_out[...] = gate * result
    quarter = gated_kept.shape[1]
    for k in range(number):
        if quarter == size:
            gated_kept[k] = d_out[k * size : (k + 1) * size, :].astype(BF16)
        else:
            here = pl.multiple_of(k * size + far * quarter, 8)
            there = pl.multiple_of(k * size + (1 - far) * quarter, 8)
            gated_kept[k] = d_out[pl.ds(here, quarter), :].astype(BF16)
            gated_sent[k] = d_out[pl.ds(there, quarter), :].astype(BF16)
    if quarter == size:
        gated_sent[...] = jnp.zeros_like(gated_sent)
    router_part[...] = dot_tn(d_logits, rows_in[...])[: router_part.shape[0]]
    if with_grads:
        own, pair = refs[7:9]
        weight_grads(rows_in, d_pre_a, d_pre_b, hidden_a, hidden_b, d_result, None, None, own, pair)


def weight_grads(
    rows, d_pre_a, d_pre_b, hidden_a, hidden_b, d_result, own_before, pair_before, own, pair
):
    width = own.shape[0] // 2
    for out, before, at, left, right in (
        (pair, pair_before, 0, rows, d_pre_b),
        (pair, pair_before, width, hidden_b, d_result),
        (own, own_before, 0, rows, d_pre_a),
        (own, own_before, width, hidden_a, d_result),
    ):
        total = dot_tn(left[...], right[...])
        if before is not None:
            total = total + before[at : at + width, :].astype(F32)
        out[at : at + width, :] = total.astype(BF16)


def gated_sum_kernel(kept, came, *blocks):
    for k, out in enumerate(blocks):
        out[...] = (kept[k].astype(F32) + came[k].astype(F32)).astype(BF16)


def weight_grad_kernel(*refs):
    rows, d_pre_a, d_pre_b, hidden_a, hidden_b, d_result = refs[:6]
    own_before, pair_before = refs[6:8] if len(refs) == 10 else (None, None)
    weight_grads(
        rows, d_pre_a, d_pre_b, hidden_a, hidden_b, d_result, own_before, pair_before, *refs[-2:]
    )


def split_grad_kernel(ids, own, came, kept, sent_first, sent_rest, total, sent):
    total[...] = own[...].astype(F32) + came[...].astype(F32)
    width = own.shape[1]
    half = width // 2
    mine, other = ids[D_ID], 1 - ids[D_ID]
    kept[:half, :] = total[pl.ds(pl.multiple_of(mine * half, 16), half), :]
    sent[:half, :] = total[pl.ds(pl.multiple_of(other * half, 16), half), :].astype(BF16)
    column = pl.ds(pl.multiple_of(mine * half, LANES), half)
    kept[half:, :half] = total[width : width + half, column]
    kept[half:, half:] = total[width + half :, column]
    column = pl.ds(pl.multiple_of(other * half, LANES), half)
    sent[half:, :half] = total[width : width + half, column].astype(BF16)
    sent[half:, half:] = total[width + half :, column].astype(BF16)
    first = sent_first.shape[0]
    sent_first[...] = sent[:first, :]
    sent_rest[...] = sent[first:, :]


def join_grad_kernel(kept, came_first, came_rest, grad_up, grad_down, came):
    first = came_first.shape[0]
    came[:first, :] = came_first[...]
    came[first:, :] = came_rest[...]
    half = kept.shape[1] // 2
    grad_up[...] = kept[:half, :] + came[:half, :].astype(F32)
    grad_down[:half, :] = kept[half:, :half] + came[half:, :half].astype(F32)
    grad_down[half:, :] = kept[half:, half:] + came[half:, half:].astype(F32)


def combine_kernel(order, parts, base, ids, table, part, *refs):
    experts = len(order)
    blocks = refs[:experts]
    routers = refs[experts : experts + parts]
    kept, sent, total = refs[experts + parts :]
    value = dot_tn(table[ids[E_ID]], blocks[0][...])
    for block, k in zip(blocks[1:], order[1:]):
        spots = table if block.shape[0] == table.shape[1] else part
        value = value + dot_tn(spots[ids[E_ID] ^ k], block[...])
    total[...] = jnp.zeros_like(total)
    total[: value.shape[0], :] = value
    if parts:
        added = routers[0][...]
        for k in range(1, parts):
            added = added + routers[k][...]
        total[base : base + added.shape[0], :] = added
    half = kept.shape[1]
    kept[...] = total[:, pl.ds(pl.multiple_of(ids[C_ID] * half, LANES), half)].astype(BF16)
    sent[...] = total[:, pl.ds(pl.multiple_of((1 - ids[C_ID]) * half, LANES), half)].astype(BF16)


def joined(ids, own, other, whole):
    half = own.shape[1]
    whole[:, pl.ds(pl.multiple_of(ids[C_ID] * half, LANES), half)] = own[...].astype(F32)
    whole[:, pl.ds(pl.multiple_of((1 - ids[C_ID]) * half, LANES), half)] = other[...].astype(F32)


def back_kernel(
    blocks_n, ids, own, other, middle, cot, gain, w_out, head_out, normed, query, key, value,
    probs, weight, *rest
):
    d_middle, kept, sent, small = rest[:4]
    blocks = rest[4 : 4 + blocks_n]
    whole, grads = rest[4 + blocks_n :]
    rows, inner = query.shape
    heads = inner // HEAD_DIM
    joined(ids, own, other, whole)
    d_normed = whole[:rows, :]
    unit, scale = norm_parts(middle[...])
    small[...] = jnp.zeros_like(small)
    base = -(-rows // 16) * 16
    small[8:, :] = whole[base : base + small.shape[0] - 8, :]
    small[2:3, :] = jnp.sum(d_normed * unit, axis=0, keepdims=True)
    small[3:4, :] = jnp.sum(d_normed, axis=0, keepdims=True)
    live = iota((rows, 1), 0) < ids[L_ID]
    d_out = jnp.where(live, cot[...].astype(F32), 0.0)
    d_mid = d_out + norm_back(unit, scale, d_normed * row_of(gain))
    d_middle[...] = d_mid
    d_branch = d_mid.astype(BF16)
    d_head = dot_nt(d_branch, w_out[...]).astype(BF16)
    grads[3 * inner :, :] = dot_tn(head_out[...], d_branch).astype(BF16)
    d_query = jnp.zeros((rows, inner), F32)
    d_key = jnp.zeros((rows, inner), F32)
    d_value = jnp.zeros((rows, inner), F32)
    for head in range(heads):
        mask = head_mask(head, inner)
        chance = probs[head].astype(F32)
        d_probs = dot_nt(d_head, value[...] * mask)
        delta = jnp.sum(d_probs * chance, axis=-1, keepdims=True)
        d_scores = (chance * (d_probs - delta)).astype(BF16)
        d_value = d_value + dot_tn(probs[head], d_head * mask)
        d_query = d_query + dot_nn(d_scores, key[...] * mask)
        d_key = d_key + dot_tn(d_scores, query[...] * mask)
    d_query = (d_query * (HEAD_DIM**-0.5)).astype(BF16)
    d_key = (d_key * (HEAD_DIM**-0.5)).astype(BF16)
    d_value = d_value.astype(BF16)
    grads[:inner, :] = dot_tn(d_query, normed[...]).astype(BF16)
    grads[inner : 2 * inner, :] = dot_tn(d_key, normed[...]).astype(BF16)
    grads[2 * inner : 3 * inner, :] = dot_tn(d_value, normed[...]).astype(BF16)
    if blocks_n == 1:
        blocks[0][...] = grads[...]
    else:
        size = blocks[0].shape[0]
        for m in range(blocks_n):
            at = pl.multiple_of((ids[Q_ID] ^ m) * size, 16)
            blocks[m][...] = grads[pl.ds(at, size), :]
    d_in = dot_nn(d_query, weight[:inner])
    d_in = d_in + dot_nn(d_key, weight[inner : 2 * inner])
    whole[:rows, :] = d_in + dot_nn(d_value, weight[2 * inner :])
    half = kept.shape[1]
    kept[...] = whole[:rows, pl.ds(pl.multiple_of(ids[C_ID] * half, LANES), half)].astype(BF16)
    sent[...] = whole[:rows, pl.ds(pl.multiple_of((1 - ids[C_ID]) * half, LANES), half)].astype(BF16)


def last_norm_kernel(ids, own, other, tokens, d_middle, gain, small2, grad_tokens, small, whole):
    joined(ids, own, other, whole)
    d_normed = whole[...]
    unit, scale = norm_parts(tokens[...].astype(F32))
    small[...] = small2[...]
    small[0:1, :] = jnp.sum(d_normed * unit, axis=0, keepdims=True)
    small[1:2, :] = jnp.sum(d_normed, axis=0, keepdims=True)
    grad_tokens[...] = (
        d_middle[...] + norm_back(unit, scale, d_normed * row_of(gain))
    ).astype(BF16)


def sum_kernel(count, *refs):
    total = refs[0][...].astype(F32)
    for m in range(1, count):
        total = total + refs[m][...].astype(F32)
    refs[count][...] = total.astype(BF16)


def pair_kernel(own, came, small, small_came, out):
    size = own.shape[0]
    out[:size, :] = (own[...].astype(F32) + came[...].astype(F32)).astype(BF16)
    out[size:, :] = (small[...] + small_came[...]).astype(BF16)


def spread_kernel(masks, ids, *refs):
    count = len(masks)
    parts = refs[:count]
    grad_qkv, grad_out, gain1, bias1, gain2, bias2, router, grads, held = refs[count:]
    size = grads.shape[0] // count
    for mask, block in zip(masks, parts):
        quarter = ids[Q_ID] ^ mask
        grads[pl.ds(pl.multiple_of(quarter * size, 16), size), :] = block[:size, :].astype(F32)
        held[quarter] = block[size:, :].astype(F32)
    total = held[0]
    for quarter in range(1, count):
        total = total + held[quarter]
    for row, out in enumerate((gain1, bias1, gain2, bias2)):
        out[...] = total[row : row + 1, :].reshape(out.shape)
    router[...] = total[8 : 8 + router.shape[0], :]
    inner = grad_qkv.shape[0]
    grad_qkv[...] = grads[:inner, :]
    grad_out[...] = grads[inner:, :]


def after(value, *others):
    return lax.optimization_barrier((value,) + others)[0]


def run(kernel, outs, args, scratch=(), micros=1.0, limit=16):
    smem = pl.BlockSpec(memory_space=pltpu.SMEM)
    vmem = pl.BlockSpec(memory_space=pltpu.VMEM)
    return pl.pallas_call(
        kernel,
        out_shape=[jax.ShapeDtypeStruct(shape, kind) for shape, kind in outs],
        in_specs=[smem if arg.dtype == jnp.int32 and arg.ndim == 1 else vmem for arg in args],
        out_specs=[vmem] * len(outs),
        scratch_shapes=[pltpu.VMEM(shape, kind) for shape, kind in scratch],
        compiler_params=pltpu.CompilerParams(vmem_limit_bytes=limit * 1024 * 1024),
        cost_estimate=pl.CostEstimate(
            flops=int(micros * 1.15e9), bytes_accessed=1024, transcendentals=0
        ),
    )(*args)


def make_body(n_tensor, n_expert, n_dp):
    small_slice = n_expert == 4 and n_dp == 2

    def tensor_swap(value, mask):
        return lax.ppermute(value, "tensor", [(i, i ^ mask) for i in range(n_tensor)])

    def expert_swap(value, mask):
        return lax.ppermute(value, "expert", [(i, i ^ mask) for i in range(n_expert)])

    def dp_swap(value):
        return lax.ppermute(value, "dp", [(i, i ^ 1) for i in range(n_dp)])

    def quarter_swap(value, mask):
        pairs = [(i, i ^ mask) for i in range(n_expert * n_dp)]
        return lax.ppermute(value, ("expert", "dp"), pairs)

    def exchange(blocks):
        if small_slice:
            came = {k: expert_swap(blocks[k], k) for k in (3, 2, 1)}
            return [blocks[0]] + [came[k] for k in range(1, n_expert)]
        order = jnp.arange(n_expert) ^ lax.axis_index("expert")
        stacked = lax.all_to_all(
            jnp.stack(blocks)[order], "expert", split_axis=0, concat_axis=0, tiled=True
        )[order]
        return [stacked[k] for k in range(n_expert)]

    def body(
        tokens,
        routes,
        images_live,
        ln1_gain,
        ln1_bias,
        w_qkv,
        w_out,
        ln2_gain,
        ln2_bias,
        w_router,
        w_up,
        w_down,
        cotangent,
    ):
        rows, width = tokens.shape
        inner = w_qkv.shape[2]
        heads = inner // HEAD_DIM
        experts = w_router.shape[1]
        capacity = max(2, 3 * rows // experts // 8 * 8)
        cap = capacity // 2
        images = rows // SEQ
        half = width // 2
        hidden_width = w_up.shape[2]
        rank = lax.axis_index("tensor")
        owner = lax.axis_index("expert")
        copy = lax.axis_index("dp")
        ids = jnp.stack(
            [
                rank,
                rank % 2,
                owner,
                copy,
                (owner % 2) * 2 + copy,
                jnp.minimum(images_live[0] * SEQ, rows),
                rank,
                rank,
            ]
        ).astype(jnp.int32)
        weight = w_qkv.transpose(1, 2, 0).reshape(3 * inner, width)
        up_a, down_a = w_up[0], w_down[0]
        part_rows = max(8, -(-experts // 8) * 8)
        small_rows = 8 + part_rows
        base = -(-rows // 16) * 16
        tall = base + -(-part_rows // 16) * 16

        out_x, out_c = tensor_swap(w_out, 2), tensor_swap(w_out, 1)
        up_b, down_b = tensor_swap(up_a, 1), tensor_swap(down_a, 1)
        normed, query, key, value, probs, head_out = run(
            functools.partial(attend_kernel, images),
            [((rows, width), BF16)]
            + [((rows, inner), BF16)] * 3
            + [((heads, rows, rows), BF16), ((rows, inner), BF16)],
            [tokens, ln1_gain, ln1_bias, weight],
            micros=4,
        )
        head_out, out_x, out_c, up_b, down_b = lax.optimization_barrier(
            (head_out, out_x, out_c, up_b, down_b)
        )
        head_x, head_c = tensor_swap(head_out, 2), tensor_swap(head_out, 1)
        quarter = cap // 2
        cot_shapes = [(quarter if small_slice and k > 1 else cap, width) for k in range(experts)]
        table, part, router, *cot_blocks = run(
            functools.partial(plan_kernel, experts),
            [((experts, cap, rows), BF16), ((experts, quarter, rows), BF16)]
            + [((LANES, width), BF16)]
            + [(shape, BF16) for shape in cot_shapes],
            [ids, after(routes.T, head_out), cotangent, w_router.T],
            micros=2,
        )
        head_x = after(head_x, table)
        if small_slice:
            d_rows_in = cot_blocks[:2] + [expert_swap(cot_blocks[k], k) for k in (2, 3)]
        else:
            d_rows_in = exchange(cot_blocks)
        out_all = [w_out, out_c, out_x, tensor_swap(out_x, 1)]
        heads_all = [head_out, head_c, head_x, tensor_swap(head_x, 1)]
        middle, *row_blocks = run(
            functools.partial(middle_kernel, n_tensor, experts),
            [((rows, width), F32)] + [((cap, width), BF16)] * experts,
            [ids, tokens, ln2_gain, ln2_bias, table] + heads_all + out_all,
            scratch=[
                ((n_tensor, rows, inner), BF16),
                ((n_tensor, inner, width), BF16),
                ((rows, width), BF16),
            ],
            micros=3,
        )
        if small_slice:
            *row_blocks, far_2, far_3 = lax.optimization_barrier((*row_blocks, *d_rows_in[2:]))
            d_rows_in[2:] = [far_2, far_3]
            d_rows_in[1], middle = lax.optimization_barrier((d_rows_in[1], middle))
            d_rows_in[1] = expert_swap(d_rows_in[1], 1)
            pair_out = tensor_swap(jnp.stack([far_2, far_3]), 2)
        else:
            pair_out = router
        rows_in = exchange(list(row_blocks))

        calls = [(0, 1), (2, 3)] if small_slice else [tuple(range(experts))]
        worked = []
        d_back, gated = [], []
        for number, call in enumerate(calls):
            if number == 1:
                router, d_back[1] = lax.optimization_barrier((router, d_back[1]))
            count = cap * len(call)
            last = number == len(calls) - 1
            grads = [] if last else [((2 * width, hidden_width), BF16)] * 2
            results = run(
                functools.partial(expert_kernel, experts, call, not last),
                [((cap, width), BF16)] * len(call)
                + [((len(call), quarter if worked else cap, width), BF16)] * 2
                + [((count, width), BF16)] * 2
                + [((count, hidden_width), BF16)] * 4
                + [((part_rows, width), F32)]
                + grads,
                [ids, up_a, up_b, down_a, down_b]
                + [router]
                + [rows_in[k] for k in call]
                + [d_rows_in[k] for k in call]
                + [pair_out if worked or not small_slice else router],
                scratch=[((count, width), F32)],
                micros=0.05,
                limit=24,
            )
            d_back += results[: len(call)]
            gated.append(results[len(call) : len(call) + 2])
            worked.append(results[len(call) + 2 :])

        order = [0] + list(range(experts - 1, 0, -1))

        def combine(blocks, routers):
            blocks = [blocks[k] for k in order]
            return run(
                functools.partial(combine_kernel, order, len(routers), base),
                [((tall if routers else base, half), BF16)] * 2,
                [ids, table, part] + blocks + routers,
                scratch=[((tall if routers else base, width), F32)],
                micros=2,
            )

        if small_slice:
            d_back[1], d_back[2] = lax.optimization_barrier((d_back[1], d_back[2]))
        d_home = exchange(d_back)

        grad_own, grad_pair = run(
            weight_grad_kernel,
            [((2 * width, hidden_width), BF16)] * 2,
            [worked[-1][at] for at in (0, 4, 5, 2, 3, 1)] + list(worked[0][7:]),
            micros=4,
            limit=24,
        )
        third = width // 48 * 16
        grad_kept, sent_first, sent_rest = run(
            split_grad_kernel,
            [((width, width), F32), ((third, width), BF16), ((width - third, width), BF16)],
            [ids, grad_own, tensor_swap(grad_pair, 1)],
            scratch=[((2 * width, width), F32), ((width, width), BF16)],
            micros=2,
            limit=24,
        )

        if small_slice:
            far_blocks = run(
                gated_sum_kernel,
                [((quarter, width), BF16)] * 2,
                [gated[1][0], tensor_swap(gated[1][1], 2)],
            )
            gated_blocks = [gated[0][0][0], expert_swap(gated[0][0][1], 1), *far_blocks]
        else:
            gated_blocks = [gated[0][0][k] for k in range(experts)]

        *gated_blocks, sent_first = lax.optimization_barrier(
            (*d_home[::-1], *gated_blocks, sent_first)
        )
        d_home, gated_blocks = gated_blocks[:experts][::-1], gated_blocks[experts:]
        kept, sent = combine(list(d_home), [one[6] for one in worked])
        chip = (kept.astype(F32) + tensor_swap(sent, 1).astype(F32)).astype(BF16)
        own = (chip.astype(F32) + tensor_swap(chip, 2).astype(F32)).astype(BF16)
        if small_slice:
            gated_home = gated_blocks[:2] + [expert_swap(gated_blocks[k], k) for k in (3, 2)][::-1]
        else:
            gated_home = exchange(list(gated_blocks))
        came_first = dp_swap(sent_first)
        own, *gated_home, came_first = lax.optimization_barrier((own, *gated_home, came_first))
        other = tensor_swap(own, 1)

        parts = 4 if small_slice else 1
        d_middle, kept1, sent1, small2, *grad_blocks = run(
            functools.partial(back_kernel, parts),
            [((rows, width), F32)]
            + [((rows, half), BF16)] * 2
            + [((small_rows, width), F32)]
            + [((4 * inner // parts, width), BF16)] * parts,
            [
                ids, own, other, middle, cotangent, ln2_gain, w_out, head_out, normed, query,
                key, value, probs, weight,
            ],
            scratch=[((tall, width), F32), ((4 * inner, width), BF16)],
            micros=6,
        )

        *gated_home, _ = lax.optimization_barrier((*gated_home, d_middle))
        kept_y, sent_y = combine(list(gated_home), [])

        chip1 = (kept1.astype(F32) + tensor_swap(sent1, 1).astype(F32)).astype(BF16)
        own1 = (chip1.astype(F32) + tensor_swap(chip1, 2).astype(F32)).astype(BF16)
        if small_slice:
            arrived = [grad_blocks[0]] + [quarter_swap(grad_blocks[m], m) for m in (3, 1, 2)]
            arrived[0], kept_y, sent_y = lax.optimization_barrier((arrived[0], kept_y, sent_y))
            size = grad_blocks[0].shape[0]
            (summed,) = run(
                functools.partial(sum_kernel, 4), [((size, width), BF16)], arrived, micros=0.5
            )
            sent_rest, own1 = lax.optimization_barrier((sent_rest, own1, summed))[:2]
        other1 = tensor_swap(own1, 1)
        grad_tokens, small = run(
            last_norm_kernel,
            [((rows, width), BF16), ((small_rows, width), F32)],
            [ids, own1, other1, tokens, d_middle, ln1_gain, small2],
            scratch=[((rows, width), F32)],
            micros=0.01,
        )
        chip_y = (kept_y.astype(F32) + tensor_swap(sent_y, 1).astype(F32)).astype(BF16)
        own_y = (chip_y.astype(F32) + tensor_swap(chip_y, 2).astype(F32)).astype(BF16)
        grad_up, grad_down = run(
            join_grad_kernel,
            [((half, hidden_width), F32), ((hidden_width, half), F32)],
            [grad_kept, came_first, dp_swap(sent_rest)],
            scratch=[((width, width), BF16)],
            micros=2,
        )
        if small_slice:
            (ready,) = run(
                pair_kernel,
                [((size + small_rows, width), BF16)],
                [summed, expert_swap(summed, 2), small, expert_swap(small, 2)],
                micros=1,
            )
            own_y, ready = lax.optimization_barrier((own_y, ready))
            everything = [quarter_swap(ready, m) for m in (3, 1, 2)]
            ready, grad_up, grad_down = lax.optimization_barrier((ready, grad_up, grad_down))
            everything = [ready] + everything
            grad_qkv, grad_out, *sums, grad_router = run(
                functools.partial(spread_kernel, (0, 3, 1, 2)),
                [((3 * inner, width), F32), ((inner, width), F32)]
                + [((width,), F32)] * 4
                + [((experts, width), F32)],
                [ids] + everything,
                scratch=[((4 * inner, width), F32), ((4, small_rows, width), F32)],
                micros=3,
            )
        else:
            grads = lax.psum(grad_blocks[0], ("expert", "dp")).astype(F32)
            grad_qkv, grad_out = grads[: 3 * inner], grads[3 * inner :]
            small_sum = lax.psum(small, ("expert", "dp"))
            sums, grad_router = list(small_sum[:4]), small_sum[8 : 8 + experts]

        mix_own, mix_other = own_y, tensor_swap(own_y, 1)
        mixture = jnp.where(
            rank % 2 == 0,
            jnp.concatenate([mix_own, mix_other], axis=1),
            jnp.concatenate([mix_other, mix_own], axis=1),
        )[:rows].astype(F32)
        alive = (jnp.arange(rows, dtype=jnp.int32) < images_live[0] * SEQ)[:, None]
        out = jnp.where(alive, middle + mixture, 0.0).astype(BF16)
        return (
            out,
            grad_tokens,
            sums[0],
            sums[1],
            grad_qkv.reshape(3, inner, width).transpose(2, 0, 1),
            grad_out,
            sums[2],
            sums[3],
            grad_router.T,
            grad_up[None],
            grad_down[None],
        )

    return body


def solution(mesh):
    in_specs = (
        P(("expert", "dp"), None),
        P(("expert", "dp"), None),
        P(("expert", "dp")),
        P(),
        P(),
        P(None, None, "tensor"),
        P("tensor", None),
        P(),
        P(),
        P(),
        P("expert", None, "tensor"),
        P("expert", "tensor", None),
        P(("expert", "dp"), None),
    )
    out_specs = (
        P(("expert", "dp"), None),
        P(("expert", "dp"), None),
        P(),
        P(),
        P(None, None, "tensor"),
        P("tensor", None),
        P(),
        P(),
        P(),
        P("expert", "dp", "tensor"),
        P("expert", "tensor", "dp"),
    )
    body = make_body(mesh.shape["tensor"], mesh.shape["expert"], mesh.shape["dp"])
    return jax.shard_map(body, mesh=mesh, in_specs=in_specs, out_specs=out_specs, check_vma=False)
```

```python
import functools

import jax
import jax.numpy as jnp
from jax import lax
from jax.experimental import pallas as pl
from jax.experimental.pallas import tpu as pltpu
from jax.sharding import PartitionSpec as P

HEAD_DIM = 64
SEQ = 197
EPSILON = 1e-06
F32 = jnp.float32
BF16 = jnp.bfloat16
LANES = 128
SMALL = 16


def dot_nn(left, right):
    return lax.dot_general(left, right, (((1,), (0,)), ((), ())), preferred_element_type=F32)


def dot_tn(left, right):
    return lax.dot_general(left, right, (((0,), (0,)), ((), ())), preferred_element_type=F32)


def dot_nt(left, right):
    return lax.dot_general(left, right, (((1,), (1,)), ((), ())), preferred_element_type=F32)


def norm_parts(values_in):
    row_mean = jnp.mean(values_in, axis=-1, keepdims=True)
    centred = values_in - row_mean
    variance = jnp.mean(centred * centred, axis=-1, keepdims=True)
    scale = lax.rsqrt(variance + EPSILON)
    return centred * scale, scale


def norm_back(normed, scale, u):
    return scale * (
        u
        - jnp.mean(u, axis=-1, keepdims=True)
        - normed * jnp.mean(u * normed, axis=-1, keepdims=True)
    )


def iota(shape, dim):
    return lax.broadcasted_iota(jnp.int32, shape, dim)


def row_of(vector):
    return vector[...].reshape(1, vector.shape[0])


def head_mask(head, width):
    lane = iota((1, width), 1)
    return ((lane >= head * HEAD_DIM) & (lane < (head + 1) * HEAD_DIM)).astype(BF16)


def image_of(shape, dim, images):
    at = iota(shape, dim)
    image = jnp.zeros(shape, jnp.int32)
    for number in range(1, images):
        image = image + (at >= number * SEQ).astype(jnp.int32)
    return image


T_ID, C_ID, E_ID, D_ID, Q_ID, L_ID = range(6)


def plan_kernel(experts, ids, routes, cot, router, table, part, router_pad, *blocks):
    rows = cot.shape[0]
    cap = table.shape[1]
    tall = max(16, -(-experts // 16) * 16)
    picks = routes[...]
    expert = iota((tall, rows), 0)
    named = picks[0:1, :] == expert
    for k in range(1, picks.shape[0]):
        named = named | (picks[k : k + 1, :] == expert)
    named = named & (iota((tall, rows), 1) < ids[L_ID])
    marks = jnp.where(named, 1.0, 0.0).astype(BF16)
    earlier = jnp.where(iota((rows, rows), 0) < iota((rows, rows), 1), 1.0, 0.0).astype(BF16)
    slot = dot_nn(marks, earlier)
    first = (ids[C_ID] * cap).astype(F32)
    slot = jnp.where(named, slot - first, -1.0)
    place = iota((cap, rows), 0).astype(F32)
    for x in range(experts):
        table[x] = jnp.where(slot[x : x + 1, :] == place, 1.0, 0.0).astype(BF16)
    quarter = part.shape[1]
    first = ((ids[T_ID] // 2) * quarter).astype(F32)
    place = iota((quarter, rows), 0).astype(F32) + first
    for x in range(experts):
        part[x] = jnp.where(slot[x : x + 1, :] == place, 1.0, 0.0).astype(BF16)
    for k in range(experts):
        source = table if blocks[k].shape[0] == cap else part
        blocks[k][...] = dot_nn(source[ids[E_ID] ^ k], cot[...]).astype(BF16)
    router_pad[...] = jnp.zeros_like(router_pad)
    router_pad[:experts, :] = router[...]


def attend_kernel(images, tokens, gain, bias, weight, normed, query, key, value, probs, head_out):
    rows = tokens.shape[0]
    inner = query.shape[1]
    heads = inner // HEAD_DIM
    unit, _ = norm_parts(tokens[...].astype(F32))
    normed[...] = (unit * row_of(gain) + row_of(bias)).astype(BF16)
    query[...] = dot_nt(normed[...], weight[:inner]).astype(BF16)
    key[...] = dot_nt(normed[...], weight[inner : 2 * inner]).astype(BF16)
    value[...] = dot_nt(normed[...], weight[2 * inner :]).astype(BF16)
    same = image_of((rows, 1), 0, images) == image_of((1, rows), 1, images)
    total = jnp.zeros((rows, inner), F32)
    for head in range(heads):
        mask = head_mask(head, inner)
        scores = dot_nt(query[...] * mask, key[...]) * (HEAD_DIM**-0.5)
        scores = jnp.where(same, scores, -1e30)
        top = jnp.max(scores, axis=-1, keepdims=True)
        weights = jnp.exp(scores - top)
        weights = weights * (1.0 / jnp.sum(weights, axis=-1, keepdims=True))
        probs[head] = weights.astype(BF16)
        total = total + dot_nn(probs[head], value[...] * mask)
    head_out[...] = total.astype(BF16)


def middle_kernel(
    n_tensor, experts, ids, tokens, gain, bias, table, *rest
):
    heads = rest[:n_tensor]
    weights = rest[n_tensor : 2 * n_tensor]
    middle = rest[2 * n_tensor]
    blocks = rest[2 * n_tensor + 1 : 2 * n_tensor + 1 + experts]
    held_heads, held_weights, low = rest[2 * n_tensor + 1 + experts :]
    for j in range(n_tensor):
        held_heads[j] = heads[j][...]
        held_weights[j] = weights[j][...]
    total = tokens[...].astype(F32)
    for rank in range(n_tensor):
        place = ids[T_ID] ^ rank
        total = total + dot_nn(held_heads[place], held_weights[place])
    middle[...] = total
    unit, _ = norm_parts(total)
    low[...] = (unit * row_of(gain) + row_of(bias)).astype(BF16)
    for k in range(experts):
        blocks[k][...] = dot_nn(table[ids[E_ID] ^ k], low[...]).astype(BF16)


def expert_kernel(
    experts, places, with_grads, ids, up_a, up_b, down_a, down_b, router, *refs
):
    number = len(places)
    row_blocks, out_blocks = refs[:number], refs[number : 2 * number]
    pair_out = refs[2 * number]
    refs = refs[2 * number + 1 :]
    back_blocks, gated_kept, gated_sent = refs[:number], refs[number], refs[number + 1]
    refs = refs[number + 2 :]
    rows_in, d_result, hidden_a, hidden_b, d_pre_a, d_pre_b, router_part = refs[:7]
    d_out = refs[-1]
    size = row_blocks[0].shape[0]
    count = size * number
    far = ids[T_ID] // 2
    for k in range(number):
        rows_in[k * size : (k + 1) * size, :] = row_blocks[k][...]
        quarter = out_blocks[k].shape[0]
        if quarter == size:
            d_out[k * size : (k + 1) * size, :] = out_blocks[k][...].astype(F32)
        else:
            here = pl.multiple_of(k * size + far * quarter, 8)
            there = pl.multiple_of(k * size + (1 - far) * quarter, 8)
            d_out[pl.ds(here, quarter), :] = out_blocks[k][...].astype(F32)
            d_out[pl.ds(there, quarter), :] = pair_out[places[k] - 2].astype(F32)
    lane = iota((count, LANES), 1)
    logits = dot_nt(rows_in[...], router[...])
    logits = jnp.where(lane < experts, logits, -1e30)
    top = jnp.max(logits, axis=-1, keepdims=True)
    odds = jnp.exp(logits - top)
    odds = odds / jnp.sum(odds, axis=-1, keepdims=True)
    mine = (lane == ids[E_ID]).astype(F32)
    gate = jnp.sum(odds * mine, axis=-1, keepdims=True)
    d_result[...] = (gate * d_out[...]).astype(BF16)
    result = jnp.zeros(d_out.shape, F32)
    back = jnp.zeros(d_out.shape, F32)
    scale = 0.7978845608028654
    for up, down, hidden, d_pre in (
        (up_a, down_a, hidden_a, d_pre_a),
        (up_b, down_b, hidden_b, d_pre_b),
    ):
        act = dot_nn(rows_in[...], up[...])
        square = act * act
        bend = jnp.tanh(scale * act * (1.0 + 0.044715 * square))
        half = 0.5 * (1.0 + bend)
        hidden[...] = (act * half).astype(BF16)
        slope = half + 0.5 * act * (1.0 - bend * bend) * (
            scale * (1.0 + 3 * 0.044715 * square)
        )
        result = result + dot_nn(hidden[...], down[...])
        d_pre[...] = (dot_nt(d_result[...], down[...]) * slope).astype(BF16)
        back = back + dot_nt(d_pre[...], up[...])
    d_gate = jnp.sum(d_out[...] * result, axis=-1, keepdims=True)
    d_logits = (d_gate * gate * (mine - odds)).astype(BF16)
    back = (back + dot_nn(d_logits, router[...])).astype(BF16)
    for k in range(number):
        back_blocks[k][...] = back[k * size : (k + 1) * size, :]
    d_out[...] = gate * result
    quarter = gated_kept.shape[1]
    for k in range(number):
        if quarter == size:
            gated_kept[k] = d_out[k * size : (k + 1) * size, :].astype(BF16)
        else:
            here = pl.multiple_of(k * size + far * quarter, 8)
            there = pl.multiple_of(k * size + (1 - far) * quarter, 8)
            gated_kept[k] = d_out[pl.ds(here, quarter), :].astype(BF16)
            gated_sent[k] = d_out[pl.ds(there, quarter), :].astype(BF16)
    if quarter == size:
        gated_sent[...] = jnp.zeros_like(gated_sent)
    router_part[...] = dot_tn(d_logits, rows_in[...])[: router_part.shape[0]]
    if with_grads:
        own, pair = refs[7:9]
        weight_grads(rows_in, d_pre_a, d_pre_b, hidden_a, hidden_b, d_result, None, None, own, pair)


def weight_grads(
    rows, d_pre_a, d_pre_b, hidden_a, hidden_b, d_result, own_before, pair_before, own, pair
):
    width = own.shape[0] // 2
    for out, before, at, left, right in (
        (pair, pair_before, 0, rows, d_pre_b),
        (pair, pair_before, width, hidden_b, d_result),
        (own, own_before, 0, rows, d_pre_a),
        (own, own_before, width, hidden_a, d_result),
    ):
        total = dot_tn(left[...], right[...])
        if before is not None:
            total = total + before[at : at + width, :].astype(F32)
        out[at : at + width, :] = total.astype(BF16)


def gated_sum_kernel(kept, came, *blocks):
    for k, out in enumerate(blocks):
        out[...] = (kept[k].astype(F32) + came[k].astype(F32)).astype(BF16)


def weight_grad_kernel(*refs):
    rows, d_pre_a, d_pre_b, hidden_a, hidden_b, d_result = refs[:6]
    own_before, pair_before = refs[6:8] if len(refs) == 10 else (None, None)
    weight_grads(
        rows, d_pre_a, d_pre_b, hidden_a, hidden_b, d_result, own_before, pair_before, *refs[-2:]
    )


def split_grad_kernel(ids, own, came, kept, sent_first, sent_rest, total, sent):
    total[...] = own[...].astype(F32) + came[...].astype(F32)
    width = own.shape[1]
    half = width // 2
    mine, other = ids[D_ID], 1 - ids[D_ID]
    kept[:half, :] = total[pl.ds(pl.multiple_of(mine * half, 16), half), :]
    sent[:half, :] = total[pl.ds(pl.multiple_of(other * half, 16), half), :].astype(BF16)
    column = pl.ds(pl.multiple_of(mine * half, LANES), half)
    kept[half:, :half] = total[width : width + half, column]
    kept[half:, half:] = total[width + half :, column]
    column = pl.ds(pl.multiple_of(other * half, LANES), half)
    sent[half:, :half] = total[width : width + half, column].astype(BF16)
    sent[half:, half:] = total[width + half :, column].astype(BF16)
    first = sent_first.shape[0]
    sent_first[...] = sent[:first, :]
    sent_rest[...] = sent[first:, :]


def join_grad_kernel(kept, came_first, came_rest, grad_up, grad_down, came):
    first = came_first.shape[0]
    came[:first, :] = came_first[...]
    came[first:, :] = came_rest[...]
    half = kept.shape[1] // 2
    grad_up[...] = kept[:half, :] + came[:half, :].astype(F32)
    grad_down[:half, :] = kept[half:, :half] + came[half:, :half].astype(F32)
    grad_down[half:, :] = kept[half:, half:] + came[half:, half:].astype(F32)


def combine_kernel(order, parts, base, ids, table, part, *refs):
    experts = len(order)
    blocks = refs[:experts]
    routers = refs[experts : experts + parts]
    kept, sent, total = refs[experts + parts :]
    value = dot_tn(table[ids[E_ID]], blocks[0][...])
    for block, k in zip(blocks[1:], order[1:]):
        spots = table if block.shape[0] == table.shape[1] else part
        value = value + dot_tn(spots[ids[E_ID] ^ k], block[...])
    total[...] = jnp.zeros_like(total)
    total[: value.shape[0], :] = value
    if parts:
        added = routers[0][...]
        for k in range(1, parts):
            added = added + routers[k][...]
        total[base : base + added.shape[0], :] = added
    half = kept.shape[1]
    kept[...] = total[:, pl.ds(pl.multiple_of(ids[C_ID] * half, LANES), half)].astype(BF16)
    sent[...] = total[:, pl.ds(pl.multiple_of((1 - ids[C_ID]) * half, LANES), half)].astype(BF16)


def joined(ids, own, other, whole):
    half = own.shape[1]
    whole[:, pl.ds(pl.multiple_of(ids[C_ID] * half, LANES), half)] = own[...].astype(F32)
    whole[:, pl.ds(pl.multiple_of((1 - ids[C_ID]) * half, LANES), half)] = other[...].astype(F32)


def back_kernel(
    blocks_n, ids, own, other, middle, cot, gain, w_out, head_out, normed, query, key, value,
    probs, weight, *rest
):
    d_middle, kept, sent, small = rest[:4]
    blocks = rest[4 : 4 + blocks_n]
    whole, grads = rest[4 + blocks_n :]
    rows, inner = query.shape
    heads = inner // HEAD_DIM
    joined(ids, own, other, whole)
    d_normed = whole[:rows, :]
    unit, scale = norm_parts(middle[...])
    small[...] = jnp.zeros_like(small)
    base = -(-rows // 16) * 16
    small[8:, :] = whole[base : base + small.shape[0] - 8, :]
    small[2:3, :] = jnp.sum(d_normed * unit, axis=0, keepdims=True)
    small[3:4, :] = jnp.sum(d_normed, axis=0, keepdims=True)
    live = iota((rows, 1), 0) < ids[L_ID]
    d_out = jnp.where(live, cot[...].astype(F32), 0.0)
    d_mid = d_out + norm_back(unit, scale, d_normed * row_of(gain))
    d_middle[...] = d_mid
    d_branch = d_mid.astype(BF16)
    d_head = dot_nt(d_branch, w_out[...]).astype(BF16)
    grads[3 * inner :, :] = dot_tn(head_out[...], d_branch).astype(BF16)
    d_query = jnp.zeros((rows, inner), F32)
    d_key = jnp.zeros((rows, inner), F32)
    d_value = jnp.zeros((rows, inner), F32)
    for head in range(heads):
        mask = head_mask(head, inner)
        chance = probs[head].astype(F32)
        d_probs = dot_nt(d_head, value[...] * mask)
        delta = jnp.sum(d_probs * chance, axis=-1, keepdims=True)
        d_scores = (chance * (d_probs - delta)).astype(BF16)
        d_value = d_value + dot_tn(probs[head], d_head * mask)
        d_query = d_query + dot_nn(d_scores, key[...] * mask)
        d_key = d_key + dot_tn(d_scores, query[...] * mask)
    d_query = (d_query * (HEAD_DIM**-0.5)).astype(BF16)
    d_key = (d_key * (HEAD_DIM**-0.5)).astype(BF16)
    d_value = d_value.astype(BF16)
    grads[:inner, :] = dot_tn(d_query, normed[...]).astype(BF16)
    grads[inner : 2 * inner, :] = dot_tn(d_key, normed[...]).astype(BF16)
    grads[2 * inner : 3 * inner, :] = dot_tn(d_value, normed[...]).astype(BF16)
    if blocks_n == 1:
        blocks[0][...] = grads[...]
    else:
        size = blocks[0].shape[0]
        for m in range(blocks_n):
            at = pl.multiple_of((ids[Q_ID] ^ m) * size, 16)
            blocks[m][...] = grads[pl.ds(at, size), :]
    d_in = dot_nn(d_query, weight[:inner])
    d_in = d_in + dot_nn(d_key, weight[inner : 2 * inner])
    whole[:rows, :] = d_in + dot_nn(d_value, weight[2 * inner :])
    half = kept.shape[1]
    kept[...] = whole[:rows, pl.ds(pl.multiple_of(ids[C_ID] * half, LANES), half)].astype(BF16)
    sent[...] = whole[:rows, pl.ds(pl.multiple_of((1 - ids[C_ID]) * half, LANES), half)].astype(BF16)


def last_norm_kernel(ids, own, other, tokens, d_middle, gain, small2, grad_tokens, small, whole):
    joined(ids, own, other, whole)
    d_normed = whole[...]
    unit, scale = norm_parts(tokens[...].astype(F32))
    small[...] = small2[...]
    small[0:1, :] = jnp.sum(d_normed * unit, axis=0, keepdims=True)
    small[1:2, :] = jnp.sum(d_normed, axis=0, keepdims=True)
    grad_tokens[...] = (
        d_middle[...] + norm_back(unit, scale, d_normed * row_of(gain))
    ).astype(BF16)


def sum_kernel(count, *refs):
    total = refs[0][...].astype(F32)
    for m in range(1, count):
        total = total + refs[m][...].astype(F32)
    refs[count][...] = total.astype(BF16)


def pair_kernel(own, came, small, small_came, out):
    size = own.shape[0]
    out[:size, :] = (own[...].astype(F32) + came[...].astype(F32)).astype(BF16)
    out[size:, :] = (small[...] + small_came[...]).astype(BF16)


def spread_kernel(masks, ids, *refs):
    count = len(masks)
    parts = refs[:count]
    grad_qkv, grad_out, gain1, bias1, gain2, bias2, router, grads, held = refs[count:]
    size = grads.shape[0] // count
    for mask, block in zip(masks, parts):
        quarter = ids[Q_ID] ^ mask
        grads[pl.ds(pl.multiple_of(quarter * size, 16), size), :] = block[:size, :].astype(F32)
        held[quarter] = block[size:, :].astype(F32)
    total = held[0]
    for quarter in range(1, count):
        total = total + held[quarter]
    for row, out in enumerate((gain1, bias1, gain2, bias2)):
        out[...] = total[row : row + 1, :].reshape(out.shape)
    router[...] = total[8 : 8 + router.shape[0], :]
    inner = grad_qkv.shape[0]
    grad_qkv[...] = grads[:inner, :]
    grad_out[...] = grads[inner:, :]


def after(value, *others):
    return lax.optimization_barrier((value,) + others)[0]


def run(kernel, outs, args, scratch=(), micros=1.0, limit=16):
    smem = pl.BlockSpec(memory_space=pltpu.SMEM)
    vmem = pl.BlockSpec(memory_space=pltpu.VMEM)
    return pl.pallas_call(
        kernel,
        out_shape=[jax.ShapeDtypeStruct(shape, kind) for shape, kind in outs],
        in_specs=[smem if arg.dtype == jnp.int32 and arg.ndim == 1 else vmem for arg in args],
        out_specs=[vmem] * len(outs),
        scratch_shapes=[pltpu.VMEM(shape, kind) for shape, kind in scratch],
        compiler_params=pltpu.CompilerParams(vmem_limit_bytes=limit * 1024 * 1024),
        cost_estimate=pl.CostEstimate(
            flops=int(micros * 1.15e9), bytes_accessed=1024, transcendentals=0
        ),
    )(*args)


def make_body(n_tensor, n_expert, n_dp):
    small_slice = n_expert == 4 and n_dp == 2

    def tensor_swap(value, mask):
        return lax.ppermute(value, "tensor", [(i, i ^ mask) for i in range(n_tensor)])

    def expert_swap(value, mask):
        return lax.ppermute(value, "expert", [(i, i ^ mask) for i in range(n_expert)])

    def dp_swap(value):
        return lax.ppermute(value, "dp", [(i, i ^ 1) for i in range(n_dp)])

    def quarter_swap(value, mask):
        pairs = [(i, i ^ mask) for i in range(n_expert * n_dp)]
        return lax.ppermute(value, ("expert", "dp"), pairs)

    def exchange(blocks):
        if small_slice:
            came = {k: expert_swap(blocks[k], k) for k in (3, 2, 1)}
            return [blocks[0]] + [came[k] for k in range(1, n_expert)]
        order = jnp.arange(n_expert) ^ lax.axis_index("expert")
        stacked = lax.all_to_all(
            jnp.stack(blocks)[order], "expert", split_axis=0, concat_axis=0, tiled=True
        )[order]
        return [stacked[k] for k in range(n_expert)]

    def body(
        tokens,
        routes,
        images_live,
        ln1_gain,
        ln1_bias,
        w_qkv,
        w_out,
        ln2_gain,
        ln2_bias,
        w_router,
        w_up,
        w_down,
        cotangent,
    ):
        rows, width = tokens.shape
        inner = w_qkv.shape[2]
        heads = inner // HEAD_DIM
        experts = w_router.shape[1]
        capacity = max(2, 3 * rows // experts // 8 * 8)
        cap = capacity // 2
        images = rows // SEQ
        half = width // 2
        hidden_width = w_up.shape[2]
        rank = lax.axis_index("tensor")
        owner = lax.axis_index("expert")
        copy = lax.axis_index("dp")
        ids = jnp.stack(
            [
                rank,
                rank % 2,
                owner,
                copy,
                (owner % 2) * 2 + copy,
                jnp.minimum(images_live[0] * SEQ, rows),
                rank,
                rank,
            ]
        ).astype(jnp.int32)
        weight = w_qkv.transpose(1, 2, 0).reshape(3 * inner, width)
        up_a, down_a = w_up[0], w_down[0]
        part_rows = max(8, -(-experts // 8) * 8)
        small_rows = 8 + part_rows
        base = -(-rows // 16) * 16
        tall = base + -(-part_rows // 16) * 16

        out_x, out_c = tensor_swap(w_out, 2), tensor_swap(w_out, 1)
        up_b, down_b = tensor_swap(up_a, 1), tensor_swap(down_a, 1)
        normed, query, key, value, probs, head_out = run(
            functools.partial(attend_kernel, images),
            [((rows, width), BF16)]
            + [((rows, inner), BF16)] * 3
            + [((heads, rows, rows), BF16), ((rows, inner), BF16)],
            [tokens, ln1_gain, ln1_bias, weight],
            micros=4,
        )
        head_out, out_x, out_c, up_b, down_b = lax.optimization_barrier(
            (head_out, out_x, out_c, up_b, down_b)
        )
        head_x, head_c = tensor_swap(head_out, 2), tensor_swap(head_out, 1)
        quarter = cap // 2
        cot_shapes = [(quarter if small_slice and k > 1 else cap, width) for k in range(experts)]
        table, part, router, *cot_blocks = run(
            functools.partial(plan_kernel, experts),
            [((experts, cap, rows), BF16), ((experts, quarter, rows), BF16)]
            + [((LANES, width), BF16)]
            + [(shape, BF16) for shape in cot_shapes],
            [ids, after(routes.T, head_out), cotangent, w_router.T],
            micros=0.01,
        )
        head_x = after(head_x, table)
        if small_slice:
            d_rows_in = cot_blocks[:2] + [expert_swap(cot_blocks[k], k) for k in (2, 3)]
        else:
            d_rows_in = exchange(cot_blocks)
        out_all = [w_out, out_c, out_x, tensor_swap(out_x, 1)]
        heads_all = [head_out, head_c, head_x, tensor_swap(head_x, 1)]
        middle, *row_blocks = run(
            functools.partial(middle_kernel, n_tensor, experts),
            [((rows, width), F32)] + [((cap, width), BF16)] * experts,
            [ids, tokens, ln2_gain, ln2_bias, table] + heads_all + out_all,
            scratch=[
                ((n_tensor, rows, inner), BF16),
                ((n_tensor, inner, width), BF16),
                ((rows, width), BF16),
            ],
            micros=0.01,
        )
        if small_slice:
            *row_blocks, far_2, far_3 = lax.optimization_barrier((*row_blocks, *d_rows_in[2:]))
            d_rows_in[2:] = [far_2, far_3]
            d_rows_in[1], middle = lax.optimization_barrier((d_rows_in[1], middle))
            d_rows_in[1] = expert_swap(d_rows_in[1], 1)
            pair_out = tensor_swap(jnp.stack([far_2, far_3]), 2)
        else:
            pair_out = router
        rows_in = exchange(list(row_blocks))

        calls = [(0, 1), (2, 3)] if small_slice else [tuple(range(experts))]
        worked = []
        d_back, gated = [], []
        for number, call in enumerate(calls):
            if number == 1:
                router, d_back[1] = lax.optimization_barrier((router, d_back[1]))
            count = cap * len(call)
            last = number == len(calls) - 1
            grads = [] if last else [((2 * width, hidden_width), BF16)] * 2
            results = run(
                functools.partial(expert_kernel, experts, call, not last),
                [((cap, width), BF16)] * len(call)
                + [((len(call), quarter if worked else cap, width), BF16)] * 2
                + [((count, width), BF16)] * 2
                + [((count, hidden_width), BF16)] * 4
                + [((part_rows, width), F32)]
                + grads,
                [ids, up_a, up_b, down_a, down_b]
                + [router]
                + [rows_in[k] for k in call]
                + [d_rows_in[k] for k in call]
                + [pair_out if worked or not small_slice else router],
                scratch=[((count, width), F32)],
                micros=0.05,
                limit=24,
            )
            d_back += results[: len(call)]
            gated.append(results[len(call) : len(call) + 2])
            worked.append(results[len(call) + 2 :])

        order = [0] + list(range(experts - 1, 0, -1))

        def combine(blocks, routers):
            blocks = [blocks[k] for k in order]
            return run(
                functools.partial(combine_kernel, order, len(routers), base),
                [((tall if routers else base, half), BF16)] * 2,
                [ids, table, part] + blocks + routers,
                scratch=[((tall if routers else base, width), F32)],
                micros=2,
            )

        if small_slice:
            d_back[1], d_back[2] = lax.optimization_barrier((d_back[1], d_back[2]))
        d_home = exchange(d_back)

        grad_own, grad_pair = run(
            weight_grad_kernel,
            [((2 * width, hidden_width), BF16)] * 2,
            [worked[-1][at] for at in (0, 4, 5, 2, 3, 1)] + list(worked[0][7:]),
            micros=4,
            limit=24,
        )
        third = width // 48 * 16
        grad_kept, sent_first, sent_rest = run(
            split_grad_kernel,
            [((width, width), F32), ((third, width), BF16), ((width - third, width), BF16)],
            [ids, grad_own, tensor_swap(grad_pair, 1)],
            scratch=[((2 * width, width), F32), ((width, width), BF16)],
            micros=2,
            limit=24,
        )

        if small_slice:
            far_blocks = run(
                gated_sum_kernel,
                [((quarter, width), BF16)] * 2,
                [gated[1][0], tensor_swap(gated[1][1], 2)],
            )
            gated_blocks = [gated[0][0][0], gated[0][0][1], *far_blocks]
        else:
            gated_blocks = [gated[0][0][k] for k in range(experts)]

        *gated_blocks, sent_first = lax.optimization_barrier(
            (*d_home[::-1], *gated_blocks, sent_first)
        )
        d_home, gated_blocks = gated_blocks[:experts][::-1], gated_blocks[experts:]
        kept, sent = combine(list(d_home), [one[6] for one in worked])
        chip = (kept.astype(F32) + tensor_swap(sent, 1).astype(F32)).astype(BF16)
        own = (chip.astype(F32) + tensor_swap(chip, 2).astype(F32)).astype(BF16)
        if small_slice:
            home = {k: expert_swap(gated_blocks[k], k) for k in (2, 3, 1)}
            gated_home = [gated_blocks[0], home[1], home[2], home[3]]
        else:
            gated_home = exchange(list(gated_blocks))
        came_first = dp_swap(sent_first)
        own, *gated_home, came_first = lax.optimization_barrier((own, *gated_home[::-1], came_first))
        gated_home = gated_home[::-1]
        other = tensor_swap(own, 1)

        parts = 4 if small_slice else 1
        d_middle, kept1, sent1, small2, *grad_blocks = run(
            functools.partial(back_kernel, parts),
            [((rows, width), F32)]
            + [((rows, half), BF16)] * 2
            + [((small_rows, width), F32)]
            + [((4 * inner // parts, width), BF16)] * parts,
            [
                ids, own, other, middle, cotangent, ln2_gain, w_out, head_out, normed, query,
                key, value, probs, weight,
            ],
            scratch=[((tall, width), F32), ((4 * inner, width), BF16)],
            micros=6,
        )

        *gated_home, _ = lax.optimization_barrier((*gated_home, d_middle))
        kept_y, sent_y = combine(list(gated_home), [])

        chip1 = (kept1.astype(F32) + tensor_swap(sent1, 1).astype(F32)).astype(BF16)
        own1 = (chip1.astype(F32) + tensor_swap(chip1, 2).astype(F32)).astype(BF16)
        if small_slice:
            arrived = [grad_blocks[0]] + [quarter_swap(grad_blocks[m], m) for m in (3, 1, 2)]
            arrived[0], kept_y, sent_y = lax.optimization_barrier((arrived[0], kept_y, sent_y))
            size = grad_blocks[0].shape[0]
            (summed,) = run(
                functools.partial(sum_kernel, 4), [((size, width), BF16)], arrived, micros=0.5
            )
            sent_rest, own1 = lax.optimization_barrier((sent_rest, own1, summed))[:2]
        other1 = tensor_swap(own1, 1)
        grad_tokens, small = run(
            last_norm_kernel,
            [((rows, width), BF16), ((small_rows, width), F32)],
            [ids, own1, other1, tokens, d_middle, ln1_gain, small2],
            scratch=[((rows, width), F32)],
            micros=0.01,
        )
        chip_y = (kept_y.astype(F32) + tensor_swap(sent_y, 1).astype(F32)).astype(BF16)
        own_y = (chip_y.astype(F32) + tensor_swap(chip_y, 2).astype(F32)).astype(BF16)
        grad_up, grad_down = run(
            join_grad_kernel,
            [((half, hidden_width), F32), ((hidden_width, half), F32)],
            [grad_kept, came_first, dp_swap(sent_rest)],
            scratch=[((width, width), BF16)],
            micros=2,
        )
        if small_slice:
            (ready,) = run(
                pair_kernel,
                [((size + small_rows, width), BF16)],
                [summed, expert_swap(summed, 2), small, expert_swap(small, 2)],
                micros=1,
            )
            own_y, ready = lax.optimization_barrier((own_y, ready))
            everything = [quarter_swap(ready, m) for m in (3, 1, 2)]
            ready, grad_up, grad_down = lax.optimization_barrier((ready, grad_up, grad_down))
            everything = [ready] + everything
            grad_qkv, grad_out, *sums, grad_router = run(
                functools.partial(spread_kernel, (0, 3, 1, 2)),
                [((3 * inner, width), F32), ((inner, width), F32)]
                + [((width,), F32)] * 4
                + [((experts, width), F32)],
                [ids] + everything,
                scratch=[((4 * inner, width), F32), ((4, small_rows, width), F32)],
                micros=3,
            )
        else:
            grads = lax.psum(grad_blocks[0], ("expert", "dp")).astype(F32)
            grad_qkv, grad_out = grads[: 3 * inner], grads[3 * inner :]
            small_sum = lax.psum(small, ("expert", "dp"))
            sums, grad_router = list(small_sum[:4]), small_sum[8 : 8 + experts]

        mix_own, mix_other = own_y, tensor_swap(own_y, 1)
        mixture = jnp.where(
            rank % 2 == 0,
            jnp.concatenate([mix_own, mix_other], axis=1),
            jnp.concatenate([mix_other, mix_own], axis=1),
        )[:rows].astype(F32)
        alive = (jnp.arange(rows, dtype=jnp.int32) < images_live[0] * SEQ)[:, None]
        out = jnp.where(alive, middle + mixture, 0.0).astype(BF16)
        return (
            out,
            grad_tokens,
            sums[0],
            sums[1],
            grad_qkv.reshape(3, inner, width).transpose(2, 0, 1),
            grad_out,
            sums[2],
            sums[3],
            grad_router.T,
            grad_up[None],
            grad_down[None],
        )

    return body


def solution(mesh):
    in_specs = (
        P(("expert", "dp"), None),
        P(("expert", "dp"), None),
        P(("expert", "dp")),
        P(),
        P(),
        P(None, None, "tensor"),
        P("tensor", None),
        P(),
        P(),
        P(),
        P("expert", None, "tensor"),
        P("expert", "tensor", None),
        P(("expert", "dp"), None),
    )
    out_specs = (
        P(("expert", "dp"), None),
        P(("expert", "dp"), None),
        P(),
        P(),
        P(None, None, "tensor"),
        P("tensor", None),
        P(),
        P(),
        P(),
        P("expert", "dp", "tensor"),
        P("expert", "tensor", "dp"),
    )
    body = make_body(mesh.shape["tensor"], mesh.shape["expert"], mesh.shape["dp"])
    return jax.shard_map(body, mesh=mesh, in_specs=in_specs, out_specs=out_specs, check_vma=False)
```

```python
import functools

import jax
import jax.numpy as jnp
from jax import lax
from jax.experimental import pallas as pl
from jax.experimental.pallas import tpu as pltpu
from jax.sharding import PartitionSpec as P

HEAD_DIM = 64
SEQ = 197
EPSILON = 1e-06
F32 = jnp.float32
BF16 = jnp.bfloat16
LANES = 128
SMALL = 16


def dot_nn(left, right):
    return lax.dot_general(left, right, (((1,), (0,)), ((), ())), preferred_element_type=F32)


def dot_tn(left, right):
    return lax.dot_general(left, right, (((0,), (0,)), ((), ())), preferred_element_type=F32)


def dot_nt(left, right):
    return lax.dot_general(left, right, (((1,), (1,)), ((), ())), preferred_element_type=F32)


def norm_parts(values_in):
    row_mean = jnp.mean(values_in, axis=-1, keepdims=True)
    centred = values_in - row_mean
    variance = jnp.mean(centred * centred, axis=-1, keepdims=True)
    scale = lax.rsqrt(variance + EPSILON)
    return centred * scale, scale


def norm_back(normed, scale, u):
    return scale * (
        u
        - jnp.mean(u, axis=-1, keepdims=True)
        - normed * jnp.mean(u * normed, axis=-1, keepdims=True)
    )


def iota(shape, dim):
    return lax.broadcasted_iota(jnp.int32, shape, dim)


def row_of(vector):
    return vector[...].reshape(1, vector.shape[0])


def head_mask(head, width):
    lane = iota((1, width), 1)
    return ((lane >= head * HEAD_DIM) & (lane < (head + 1) * HEAD_DIM)).astype(BF16)


def image_of(shape, dim, images):
    at = iota(shape, dim)
    image = jnp.zeros(shape, jnp.int32)
    for number in range(1, images):
        image = image + (at >= number * SEQ).astype(jnp.int32)
    return image


T_ID, C_ID, E_ID, D_ID, Q_ID, L_ID = range(6)


def plan_kernel(experts, ids, routes, cot, router, table, part, router_pad, *blocks):
    rows = cot.shape[0]
    cap = table.shape[1]
    tall = max(16, -(-experts // 16) * 16)
    picks = routes[...]
    expert = iota((tall, rows), 0)
    named = picks[0:1, :] == expert
    for k in range(1, picks.shape[0]):
        named = named | (picks[k : k + 1, :] == expert)
    named = named & (iota((tall, rows), 1) < ids[L_ID])
    marks = jnp.where(named, 1.0, 0.0).astype(BF16)
    earlier = jnp.where(iota((rows, rows), 0) < iota((rows, rows), 1), 1.0, 0.0).astype(BF16)
    slot = dot_nn(marks, earlier)
    first = (ids[C_ID] * cap).astype(F32)
    slot = jnp.where(named, slot - first, -1.0)
    place = iota((cap, rows), 0).astype(F32)
    for x in range(experts):
        table[x] = jnp.where(slot[x : x + 1, :] == place, 1.0, 0.0).astype(BF16)
    quarter = part.shape[1]
    first = ((ids[T_ID] // 2) * quarter).astype(F32)
    place = iota((quarter, rows), 0).astype(F32) + first
    for x in range(experts):
        part[x] = jnp.where(slot[x : x + 1, :] == place, 1.0, 0.0).astype(BF16)
    for k in range(experts):
        source = table if blocks[k].shape[0] == cap else part
        blocks[k][...] = dot_nn(source[ids[E_ID] ^ k], cot[...]).astype(BF16)
    router_pad[...] = jnp.zeros_like(router_pad)
    router_pad[:experts, :] = router[...]


def attend_kernel(images, tokens, gain, bias, weight, normed, query, key, value, probs, head_out):
    rows = tokens.shape[0]
    inner = query.shape[1]
    heads = inner // HEAD_DIM
    unit, _ = norm_parts(tokens[...].astype(F32))
    normed[...] = (unit * row_of(gain) + row_of(bias)).astype(BF16)
    query[...] = dot_nt(normed[...], weight[:inner]).astype(BF16)
    key[...] = dot_nt(normed[...], weight[inner : 2 * inner]).astype(BF16)
    value[...] = dot_nt(normed[...], weight[2 * inner :]).astype(BF16)
    same = image_of((rows, 1), 0, images) == image_of((1, rows), 1, images)
    total = jnp.zeros((rows, inner), F32)
    for head in range(heads):
        mask = head_mask(head, inner)
        scores = dot_nt(query[...] * mask, key[...]) * (HEAD_DIM**-0.5)
        scores = jnp.where(same, scores, -1e30)
        top = jnp.max(scores, axis=-1, keepdims=True)
        weights = jnp.exp(scores - top)
        weights = weights * (1.0 / jnp.sum(weights, axis=-1, keepdims=True))
        probs[head] = weights.astype(BF16)
        total = total + dot_nn(probs[head], value[...] * mask)
    head_out[...] = total.astype(BF16)


def middle_kernel(
    n_tensor, experts, ids, tokens, gain, bias, table, *rest
):
    heads = rest[:n_tensor]
    weights = rest[n_tensor : 2 * n_tensor]
    middle = rest[2 * n_tensor]
    blocks = rest[2 * n_tensor + 1 : 2 * n_tensor + 1 + experts]
    held_heads, held_weights, low = rest[2 * n_tensor + 1 + experts :]
    for j in range(n_tensor):
        held_heads[j] = heads[j][...]
        held_weights[j] = weights[j][...]
    total = tokens[...].astype(F32)
    for rank in range(n_tensor):
        place = ids[T_ID] ^ rank
        total = total + dot_nn(held_heads[place], held_weights[place])
    middle[...] = total
    unit, _ = norm_parts(total)
    low[...] = (unit * row_of(gain) + row_of(bias)).astype(BF16)
    for k in range(experts):
        blocks[k][...] = dot_nn(table[ids[E_ID] ^ k], low[...]).astype(BF16)


def expert_kernel(
    experts, places, with_grads, ids, up_a, up_b, down_a, down_b, router, *refs
):
    number = len(places)
    row_blocks, out_blocks = refs[:number], refs[number : 2 * number]
    pair_out = refs[2 * number]
    refs = refs[2 * number + 1 :]
    back_blocks, gated_kept, gated_sent = refs[:number], refs[number], refs[number + 1]
    refs = refs[number + 2 :]
    rows_in, d_result, hidden_a, hidden_b, d_pre_a, d_pre_b, router_part = refs[:7]
    d_out = refs[-1]
    size = row_blocks[0].shape[0]
    count = size * number
    far = ids[T_ID] // 2
    for k in range(number):
        rows_in[k * size : (k + 1) * size, :] = row_blocks[k][...]
        quarter = out_blocks[k].shape[0]
        if quarter == size:
            d_out[k * size : (k + 1) * size, :] = out_blocks[k][...].astype(F32)
        else:
            here = pl.multiple_of(k * size + far * quarter, 8)
            there = pl.multiple_of(k * size + (1 - far) * quarter, 8)
            d_out[pl.ds(here, quarter), :] = out_blocks[k][...].astype(F32)
            d_out[pl.ds(there, quarter), :] = pair_out[places[k] - 2].astype(F32)
    lane = iota((count, LANES), 1)
    logits = dot_nt(rows_in[...], router[...])
    logits = jnp.where(lane < experts, logits, -1e30)
    top = jnp.max(logits, axis=-1, keepdims=True)
    odds = jnp.exp(logits - top)
    odds = odds / jnp.sum(odds, axis=-1, keepdims=True)
    mine = (lane == ids[E_ID]).astype(F32)
    gate = jnp.sum(odds * mine, axis=-1, keepdims=True)
    d_result[...] = (gate * d_out[...]).astype(BF16)
    result = jnp.zeros(d_out.shape, F32)
    back = jnp.zeros(d_out.shape, F32)
    scale = 0.7978845608028654
    for up, down, hidden, d_pre in (
        (up_a, down_a, hidden_a, d_pre_a),
        (up_b, down_b, hidden_b, d_pre_b),
    ):
        act = dot_nn(rows_in[...], up[...])
        square = act * act
        bend = jnp.tanh(scale * act * (1.0 + 0.044715 * square))
        half = 0.5 * (1.0 + bend)
        hidden[...] = (act * half).astype(BF16)
        slope = half + 0.5 * act * (1.0 - bend * bend) * (
            scale * (1.0 + 3 * 0.044715 * square)
        )
        result = result + dot_nn(hidden[...], down[...])
        d_pre[...] = (dot_nt(d_result[...], down[...]) * slope).astype(BF16)
        back = back + dot_nt(d_pre[...], up[...])
    d_gate = jnp.sum(d_out[...] * result, axis=-1, keepdims=True)
    d_logits = (d_gate * gate * (mine - odds)).astype(BF16)
    back = (back + dot_nn(d_logits, router[...])).astype(BF16)
    for k in range(number):
        back_blocks[k][...] = back[k * size : (k + 1) * size, :]
    d_out[...] = gate * result
    quarter = gated_kept.shape[1]
    for k in range(number):
        if quarter == size:
            gated_kept[k] = d_out[k * size : (k + 1) * size, :].astype(BF16)
        else:
            here = pl.multiple_of(k * size + far * quarter, 8)
            there = pl.multiple_of(k * size + (1 - far) * quarter, 8)
            gated_kept[k] = d_out[pl.ds(here, quarter), :].astype(BF16)
            gated_sent[k] = d_out[pl.ds(there, quarter), :].astype(BF16)
    if quarter == size:
        gated_sent[...] = jnp.zeros_like(gated_sent)
    router_part[...] = dot_tn(d_logits, rows_in[...])[: router_part.shape[0]]
    if with_grads:
        own, pair = refs[7:9]
        weight_grads(rows_in, d_pre_a, d_pre_b, hidden_a, hidden_b, d_result, None, None, own, pair)


def weight_grads(
    rows, d_pre_a, d_pre_b, hidden_a, hidden_b, d_result, own_before, pair_before, own, pair
):
    width = own.shape[0] // 2
    for out, before, at, left, right in (
        (pair, pair_before, 0, rows, d_pre_b),
        (pair, pair_before, width, hidden_b, d_result),
        (own, own_before, 0, rows, d_pre_a),
        (own, own_before, width, hidden_a, d_result),
    ):
        total = dot_tn(left[...], right[...])
        if before is not None:
            total = total + before[at : at + width, :].astype(F32)
        out[at : at + width, :] = total.astype(BF16)


def gated_sum_kernel(kept, came, *blocks):
    for k, out in enumerate(blocks):
        out[...] = (kept[k].astype(F32) + came[k].astype(F32)).astype(BF16)


def weight_grad_kernel(*refs):
    rows, d_pre_a, d_pre_b, hidden_a, hidden_b, d_result = refs[:6]
    own_before, pair_before = refs[6:8] if len(refs) == 10 else (None, None)
    weight_grads(
        rows, d_pre_a, d_pre_b, hidden_a, hidden_b, d_result, own_before, pair_before, *refs[-2:]
    )


def split_grad_kernel(ids, own, came, kept, sent_first, sent_rest, total, sent):
    total[...] = own[...].astype(F32) + came[...].astype(F32)
    width = own.shape[1]
    half = width // 2
    mine, other = ids[D_ID], 1 - ids[D_ID]
    kept[:half, :] = total[pl.ds(pl.multiple_of(mine * half, 16), half), :]
    sent[:half, :] = total[pl.ds(pl.multiple_of(other * half, 16), half), :].astype(BF16)
    column = pl.ds(pl.multiple_of(mine * half, LANES), half)
    kept[half:, :half] = total[width : width + half, column]
    kept[half:, half:] = total[width + half :, column]
    column = pl.ds(pl.multiple_of(other * half, LANES), half)
    sent[half:, :half] = total[width : width + half, column].astype(BF16)
    sent[half:, half:] = total[width + half :, column].astype(BF16)
    first = sent_first.shape[0]
    sent_first[...] = sent[:first, :]
    sent_rest[...] = sent[first:, :]


def join_grad_kernel(kept, came_first, came_rest, grad_up, grad_down, came):
    first = came_first.shape[0]
    came[:first, :] = came_first[...]
    came[first:, :] = came_rest[...]
    half = kept.shape[1] // 2
    grad_up[...] = kept[:half, :] + came[:half, :].astype(F32)
    grad_down[:half, :] = kept[half:, :half] + came[half:, :half].astype(F32)
    grad_down[half:, :] = kept[half:, half:] + came[half:, half:].astype(F32)


def combine_kernel(order, parts, base, ids, table, part, *refs):
    experts = len(order)
    blocks = refs[:experts]
    routers = refs[experts : experts + parts]
    kept, sent, total = refs[experts + parts :]
    value = dot_tn(table[ids[E_ID]], blocks[0][...])
    for block, k in zip(blocks[1:], order[1:]):
        spots = table if block.shape[0] == table.shape[1] else part
        value = value + dot_tn(spots[ids[E_ID] ^ k], block[...])
    total[...] = jnp.zeros_like(total)
    total[: value.shape[0], :] = value
    if parts:
        added = routers[0][...]
        for k in range(1, parts):
            added = added + routers[k][...]
        total[base : base + added.shape[0], :] = added
    half = kept.shape[1]
    kept[...] = total[:, pl.ds(pl.multiple_of(ids[C_ID] * half, LANES), half)].astype(BF16)
    sent[...] = total[:, pl.ds(pl.multiple_of((1 - ids[C_ID]) * half, LANES), half)].astype(BF16)


def joined(ids, own, other, whole):
    half = own.shape[1]
    whole[:, pl.ds(pl.multiple_of(ids[C_ID] * half, LANES), half)] = own[...].astype(F32)
    whole[:, pl.ds(pl.multiple_of((1 - ids[C_ID]) * half, LANES), half)] = other[...].astype(F32)


def back_kernel(
    blocks_n, ids, own, other, middle, cot, gain, w_out, head_out, normed, query, key, value,
    probs, weight, *rest
):
    d_middle, kept, sent, small = rest[:4]
    blocks = rest[4 : 4 + blocks_n]
    whole, grads = rest[4 + blocks_n :]
    rows, inner = query.shape
    heads = inner // HEAD_DIM
    joined(ids, own, other, whole)
    d_normed = whole[:rows, :]
    unit, scale = norm_parts(middle[...])
    small[...] = jnp.zeros_like(small)
    base = -(-rows // 16) * 16
    small[8:, :] = whole[base : base + small.shape[0] - 8, :]
    small[2:3, :] = jnp.sum(d_normed * unit, axis=0, keepdims=True)
    small[3:4, :] = jnp.sum(d_normed, axis=0, keepdims=True)
    live = iota((rows, 1), 0) < ids[L_ID]
    d_out = jnp.where(live, cot[...].astype(F32), 0.0)
    d_mid = d_out + norm_back(unit, scale, d_normed * row_of(gain))
    d_middle[...] = d_mid
    d_branch = d_mid.astype(BF16)
    d_head = dot_nt(d_branch, w_out[...]).astype(BF16)
    grads[3 * inner :, :] = dot_tn(head_out[...], d_branch).astype(BF16)
    d_query = jnp.zeros((rows, inner), F32)
    d_key = jnp.zeros((rows, inner), F32)
    d_value = jnp.zeros((rows, inner), F32)
    for head in range(heads):
        mask = head_mask(head, inner)
        chance = probs[head].astype(F32)
        d_probs = dot_nt(d_head, value[...] * mask)
        delta = jnp.sum(d_probs * chance, axis=-1, keepdims=True)
        d_scores = (chance * (d_probs - delta)).astype(BF16)
        d_value = d_value + dot_tn(probs[head], d_head * mask)
        d_query = d_query + dot_nn(d_scores, key[...] * mask)
        d_key = d_key + dot_tn(d_scores, query[...] * mask)
    d_query = (d_query * (HEAD_DIM**-0.5)).astype(BF16)
    d_key = (d_key * (HEAD_DIM**-0.5)).astype(BF16)
    d_value = d_value.astype(BF16)
    grads[:inner, :] = dot_tn(d_query, normed[...]).astype(BF16)
    grads[inner : 2 * inner, :] = dot_tn(d_key, normed[...]).astype(BF16)
    grads[2 * inner : 3 * inner, :] = dot_tn(d_value, normed[...]).astype(BF16)
    if blocks_n == 1:
        blocks[0][...] = grads[...]
    else:
        size = blocks[0].shape[0]
        for m in range(blocks_n):
            at = pl.multiple_of((ids[Q_ID] ^ m) * size, 16)
            blocks[m][...] = grads[pl.ds(at, size), :]
    d_in = dot_nn(d_query, weight[:inner])
    d_in = d_in + dot_nn(d_key, weight[inner : 2 * inner])
    whole[:rows, :] = d_in + dot_nn(d_value, weight[2 * inner :])
    half = kept.shape[1]
    kept[...] = whole[:rows, pl.ds(pl.multiple_of(ids[C_ID] * half, LANES), half)].astype(BF16)
    sent[...] = whole[:rows, pl.ds(pl.multiple_of((1 - ids[C_ID]) * half, LANES), half)].astype(BF16)


def last_norm_kernel(ids, own, other, tokens, d_middle, gain, small2, grad_tokens, small, whole):
    joined(ids, own, other, whole)
    d_normed = whole[...]
    unit, scale = norm_parts(tokens[...].astype(F32))
    small[...] = small2[...]
    small[0:1, :] = jnp.sum(d_normed * unit, axis=0, keepdims=True)
    small[1:2, :] = jnp.sum(d_normed, axis=0, keepdims=True)
    grad_tokens[...] = (
        d_middle[...] + norm_back(unit, scale, d_normed * row_of(gain))
    ).astype(BF16)


def sum_kernel(count, *refs):
    total = refs[0][...].astype(F32)
    for m in range(1, count):
        total = total + refs[m][...].astype(F32)
    refs[count][...] = total.astype(BF16)


def pair_kernel(own, came, small, small_came, out):
    size = own.shape[0]
    out[:size, :] = (own[...].astype(F32) + came[...].astype(F32)).astype(BF16)
    out[size:, :] = (small[...] + small_came[...]).astype(BF16)


def spread_kernel(masks, ids, *refs):
    count = len(masks)
    parts = refs[:count]
    grad_qkv, grad_out, gain1, bias1, gain2, bias2, router, grads, held = refs[count:]
    size = grads.shape[0] // count
    for mask, block in zip(masks, parts):
        quarter = ids[Q_ID] ^ mask
        grads[pl.ds(pl.multiple_of(quarter * size, 16), size), :] = block[:size, :].astype(F32)
        held[quarter] = block[size:, :].astype(F32)
    total = held[0]
    for quarter in range(1, count):
        total = total + held[quarter]
    for row, out in enumerate((gain1, bias1, gain2, bias2)):
        out[...] = total[row : row + 1, :].reshape(out.shape)
    router[...] = total[8 : 8 + router.shape[0], :]
    inner = grad_qkv.shape[0]
    grad_qkv[...] = grads[:inner, :]
    grad_out[...] = grads[inner:, :]


def after(value, *others):
    return lax.optimization_barrier((value,) + others)[0]


def run(kernel, outs, args, scratch=(), micros=1.0, limit=16):
    smem = pl.BlockSpec(memory_space=pltpu.SMEM)
    vmem = pl.BlockSpec(memory_space=pltpu.VMEM)
    return pl.pallas_call(
        kernel,
        out_shape=[jax.ShapeDtypeStruct(shape, kind) for shape, kind in outs],
        in_specs=[smem if arg.dtype == jnp.int32 and arg.ndim == 1 else vmem for arg in args],
        out_specs=[vmem] * len(outs),
        scratch_shapes=[pltpu.VMEM(shape, kind) for shape, kind in scratch],
        compiler_params=pltpu.CompilerParams(vmem_limit_bytes=limit * 1024 * 1024),
        cost_estimate=pl.CostEstimate(
            flops=int(micros * 1.15e9), bytes_accessed=1024, transcendentals=0
        ),
    )(*args)


def make_body(n_tensor, n_expert, n_dp):
    small_slice = n_expert == 4 and n_dp == 2

    def tensor_swap(value, mask):
        return lax.ppermute(value, "tensor", [(i, i ^ mask) for i in range(n_tensor)])

    def expert_swap(value, mask):
        return lax.ppermute(value, "expert", [(i, i ^ mask) for i in range(n_expert)])

    def dp_swap(value):
        return lax.ppermute(value, "dp", [(i, i ^ 1) for i in range(n_dp)])

    def quarter_swap(value, mask):
        pairs = [(i, i ^ mask) for i in range(n_expert * n_dp)]
        return lax.ppermute(value, ("expert", "dp"), pairs)

    def exchange(blocks):
        if small_slice:
            came = {k: expert_swap(blocks[k], k) for k in (3, 2, 1)}
            return [blocks[0]] + [came[k] for k in range(1, n_expert)]
        order = jnp.arange(n_expert) ^ lax.axis_index("expert")
        stacked = lax.all_to_all(
            jnp.stack(blocks)[order], "expert", split_axis=0, concat_axis=0, tiled=True
        )[order]
        return [stacked[k] for k in range(n_expert)]

    def body(
        tokens,
        routes,
        images_live,
        ln1_gain,
        ln1_bias,
        w_qkv,
        w_out,
        ln2_gain,
        ln2_bias,
        w_router,
        w_up,
        w_down,
        cotangent,
    ):
        rows, width = tokens.shape
        inner = w_qkv.shape[2]
        heads = inner // HEAD_DIM
        experts = w_router.shape[1]
        capacity = max(2, 3 * rows // experts // 8 * 8)
        cap = capacity // 2
        images = rows // SEQ
        half = width // 2
        hidden_width = w_up.shape[2]
        rank = lax.axis_index("tensor")
        owner = lax.axis_index("expert")
        copy = lax.axis_index("dp")
        ids = jnp.stack(
            [
                rank,
                rank % 2,
                owner,
                copy,
                (owner % 2) * 2 + copy,
                jnp.minimum(images_live[0] * SEQ, rows),
                rank,
                rank,
            ]
        ).astype(jnp.int32)
        weight = w_qkv.transpose(1, 2, 0).reshape(3 * inner, width)
        up_a, down_a = w_up[0], w_down[0]
        part_rows = max(8, -(-experts // 8) * 8)
        small_rows = 8 + part_rows
        base = -(-rows // 16) * 16
        tall = base + -(-part_rows // 16) * 16

        out_x, out_c = tensor_swap(w_out, 2), tensor_swap(w_out, 1)
        up_b, down_b = tensor_swap(up_a, 1), tensor_swap(down_a, 1)
        normed, query, key, value, probs, head_out = run(
            functools.partial(attend_kernel, images),
            [((rows, width), BF16)]
            + [((rows, inner), BF16)] * 3
            + [((heads, rows, rows), BF16), ((rows, inner), BF16)],
            [tokens, ln1_gain, ln1_bias, weight],
            micros=4,
        )
        head_out, out_x, out_c, up_b, down_b = lax.optimization_barrier(
            (head_out, out_x, out_c, up_b, down_b)
        )
        head_x, head_c = tensor_swap(head_out, 2), tensor_swap(head_out, 1)
        quarter = cap // 2
        cot_shapes = [(quarter if small_slice and k > 1 else cap, width) for k in range(experts)]
        table, part, router, *cot_blocks = run(
            functools.partial(plan_kernel, experts),
            [((experts, cap, rows), BF16), ((experts, quarter, rows), BF16)]
            + [((LANES, width), BF16)]
            + [(shape, BF16) for shape in cot_shapes],
            [ids, after(routes.T, head_out), cotangent, w_router.T],
            micros=2,
        )
        head_x = after(head_x, table)
        if small_slice:
            d_rows_in = cot_blocks[:2] + [expert_swap(cot_blocks[k], k) for k in (2, 3)]
        else:
            d_rows_in = exchange(cot_blocks)
        out_all = [w_out, out_c, out_x, tensor_swap(out_x, 1)]
        heads_all = [head_out, head_c, head_x, tensor_swap(head_x, 1)]
        middle, *row_blocks = run(
            functools.partial(middle_kernel, n_tensor, experts),
            [((rows, width), F32)] + [((cap, width), BF16)] * experts,
            [ids, tokens, ln2_gain, ln2_bias, table] + heads_all + out_all,
            scratch=[
                ((n_tensor, rows, inner), BF16),
                ((n_tensor, inner, width), BF16),
                ((rows, width), BF16),
            ],
            micros=3,
        )
        if small_slice:
            *row_blocks, far_2, far_3 = lax.optimization_barrier((*row_blocks, *d_rows_in[2:]))
            d_rows_in[2:] = [far_2, far_3]
            d_rows_in[1], middle = lax.optimization_barrier((d_rows_in[1], middle))
            d_rows_in[1] = expert_swap(d_rows_in[1], 1)
            pair_out = tensor_swap(jnp.stack([far_2, far_3]), 2)
        else:
            pair_out = router
        rows_in = exchange(list(row_blocks))

        calls = [(0, 1), (2, 3)] if small_slice else [tuple(range(experts))]
        worked = []
        d_back, gated = [], []
        for number, call in enumerate(calls):
            if number == 1:
                router, d_back[1] = lax.optimization_barrier((router, d_back[1]))
            count = cap * len(call)
            last = number == len(calls) - 1
            grads = [] if last else [((2 * width, hidden_width), BF16)] * 2
            results = run(
                functools.partial(expert_kernel, experts, call, not last),
                [((cap, width), BF16)] * len(call)
                + [((len(call), quarter if worked else cap, width), BF16)] * 2
                + [((count, width), BF16)] * 2
                + [((count, hidden_width), BF16)] * 4
                + [((part_rows, width), F32)]
                + grads,
                [ids, up_a, up_b, down_a, down_b]
                + [router]
                + [rows_in[k] for k in call]
                + [d_rows_in[k] for k in call]
                + [pair_out if worked or not small_slice else router],
                scratch=[((count, width), F32)],
                micros=0.05,
                limit=24,
            )
            d_back += results[: len(call)]
            gated.append(results[len(call) : len(call) + 2])
            worked.append(results[len(call) + 2 :])

        order = [0] + list(range(experts - 1, 0, -1))

        def combine(blocks, routers):
            blocks = [blocks[k] for k in order]
            return run(
                functools.partial(combine_kernel, order, len(routers), base),
                [((tall if routers else base, half), BF16)] * 2,
                [ids, table, part] + blocks + routers,
                scratch=[((tall if routers else base, width), F32)],
                micros=2,
            )

        if small_slice:
            d_back[1], d_back[2] = lax.optimization_barrier((d_back[1], d_back[2]))
        d_home = exchange(d_back)

        grad_own, grad_pair = run(
            weight_grad_kernel,
            [((2 * width, hidden_width), BF16)] * 2,
            [worked[-1][at] for at in (0, 4, 5, 2, 3, 1)] + list(worked[0][7:]),
            micros=4,
            limit=24,
        )
        third = width // 48 * 16
        grad_kept, sent_first, sent_rest = run(
            split_grad_kernel,
            [((width, width), F32), ((third, width), BF16), ((width - third, width), BF16)],
            [ids, grad_own, tensor_swap(grad_pair, 1)],
            scratch=[((2 * width, width), F32), ((width, width), BF16)],
            micros=2,
            limit=24,
        )

        if small_slice:
            far_blocks = run(
                gated_sum_kernel,
                [((quarter, width), BF16)] * 2,
                [gated[1][0], tensor_swap(gated[1][1], 2)],
            )
            gated_blocks = [gated[0][0][0], gated[0][0][1], *far_blocks]
        else:
            gated_blocks = [gated[0][0][k] for k in range(experts)]

        *gated_blocks, sent_first = lax.optimization_barrier(
            (*d_home[::-1], *gated_blocks, sent_first)
        )
        d_home, gated_blocks = gated_blocks[:experts][::-1], gated_blocks[experts:]
        kept, sent = combine(list(d_home), [one[6] for one in worked])
        chip = (kept.astype(F32) + tensor_swap(sent, 1).astype(F32)).astype(BF16)
        own = (chip.astype(F32) + tensor_swap(chip, 2).astype(F32)).astype(BF16)
        if small_slice:
            home = {k: expert_swap(gated_blocks[k], k) for k in (2, 3, 1)}
            gated_home = [gated_blocks[0], home[1], home[2], home[3]]
        else:
            gated_home = exchange(list(gated_blocks))
        came_first = dp_swap(sent_first)
        own, came_first, *gated_home = lax.optimization_barrier((own, came_first, *gated_home))
        other = tensor_swap(own, 1)

        parts = 4 if small_slice else 1
        d_middle, kept1, sent1, small2, *grad_blocks = run(
            functools.partial(back_kernel, parts),
            [((rows, width), F32)]
            + [((rows, half), BF16)] * 2
            + [((small_rows, width), F32)]
            + [((4 * inner // parts, width), BF16)] * parts,
            [
                ids, own, other, middle, cotangent, ln2_gain, w_out, head_out, normed, query,
                key, value, probs, weight,
            ],
            scratch=[((tall, width), F32), ((4 * inner, width), BF16)],
            micros=6,
        )

        *gated_home, _ = lax.optimization_barrier((*gated_home, d_middle))
        kept_y, sent_y = combine(list(gated_home), [])

        chip1 = (kept1.astype(F32) + tensor_swap(sent1, 1).astype(F32)).astype(BF16)
        own1 = (chip1.astype(F32) + tensor_swap(chip1, 2).astype(F32)).astype(BF16)
        if small_slice:
            arrived = [grad_blocks[0]] + [quarter_swap(grad_blocks[m], m) for m in (3, 1, 2)]
            arrived[0], kept_y, sent_y = lax.optimization_barrier((arrived[0], kept_y, sent_y))
            size = grad_blocks[0].shape[0]
            (summed,) = run(
                functools.partial(sum_kernel, 4), [((size, width), BF16)], arrived, micros=0.5
            )
            sent_rest, own1 = lax.optimization_barrier((sent_rest, own1, summed))[:2]
        other1 = tensor_swap(own1, 1)
        grad_tokens, small = run(
            last_norm_kernel,
            [((rows, width), BF16), ((small_rows, width), F32)],
            [ids, own1, other1, tokens, d_middle, ln1_gain, small2],
            scratch=[((rows, width), F32)],
            micros=0.01,
        )
        chip_y = (kept_y.astype(F32) + tensor_swap(sent_y, 1).astype(F32)).astype(BF16)
        own_y = (chip_y.astype(F32) + tensor_swap(chip_y, 2).astype(F32)).astype(BF16)
        grad_up, grad_down = run(
            join_grad_kernel,
            [((half, hidden_width), F32), ((hidden_width, half), F32)],
            [grad_kept, came_first, dp_swap(sent_rest)],
            scratch=[((width, width), BF16)],
            micros=2,
        )
        if small_slice:
            (ready,) = run(
                pair_kernel,
                [((size + small_rows, width), BF16)],
                [summed, expert_swap(summed, 2), small, expert_swap(small, 2)],
                micros=1,
            )
            own_y, ready = lax.optimization_barrier((own_y, ready))
            everything = [quarter_swap(ready, m) for m in (3, 1, 2)]
            ready, grad_up, grad_down = lax.optimization_barrier((ready, grad_up, grad_down))
            everything = [ready] + everything
            grad_qkv, grad_out, *sums, grad_router = run(
                functools.partial(spread_kernel, (0, 3, 1, 2)),
                [((3 * inner, width), F32), ((inner, width), F32)]
                + [((width,), F32)] * 4
                + [((experts, width), F32)],
                [ids] + everything,
                scratch=[((4 * inner, width), F32), ((4, small_rows, width), F32)],
                micros=3,
            )
        else:
            grads = lax.psum(grad_blocks[0], ("expert", "dp")).astype(F32)
            grad_qkv, grad_out = grads[: 3 * inner], grads[3 * inner :]
            small_sum = lax.psum(small, ("expert", "dp"))
            sums, grad_router = list(small_sum[:4]), small_sum[8 : 8 + experts]

        mix_own, mix_other = own_y, tensor_swap(own_y, 1)
        mixture = jnp.where(
            rank % 2 == 0,
            jnp.concatenate([mix_own, mix_other], axis=1),
            jnp.concatenate([mix_other, mix_own], axis=1),
        )[:rows].astype(F32)
        alive = (jnp.arange(rows, dtype=jnp.int32) < images_live[0] * SEQ)[:, None]
        out = jnp.where(alive, middle + mixture, 0.0).astype(BF16)
        return (
            out,
            grad_tokens,
            sums[0],
            sums[1],
            grad_qkv.reshape(3, inner, width).transpose(2, 0, 1),
            grad_out,
            sums[2],
            sums[3],
            grad_router.T,
            grad_up[None],
            grad_down[None],
        )

    return body


def solution(mesh):
    in_specs = (
        P(("expert", "dp"), None),
        P(("expert", "dp"), None),
        P(("expert", "dp")),
        P(),
        P(),
        P(None, None, "tensor"),
        P("tensor", None),
        P(),
        P(),
        P(),
        P("expert", None, "tensor"),
        P("expert", "tensor", None),
        P(("expert", "dp"), None),
    )
    out_specs = (
        P(("expert", "dp"), None),
        P(("expert", "dp"), None),
        P(),
        P(),
        P(None, None, "tensor"),
        P("tensor", None),
        P(),
        P(),
        P(),
        P("expert", "dp", "tensor"),
        P("expert", "tensor", "dp"),
    )
    body = make_body(mesh.shape["tensor"], mesh.shape["expert"], mesh.shape["dp"])
    return jax.shard_map(body, mesh=mesh, in_specs=in_specs, out_specs=out_specs, check_vma=False)
```

```python
import functools

import jax
import jax.numpy as jnp
from jax import lax
from jax.experimental import pallas as pl
from jax.experimental.pallas import tpu as pltpu
from jax.sharding import PartitionSpec as P

HEAD_DIM = 64
SEQ = 197
EPSILON = 1e-06
F32 = jnp.float32
BF16 = jnp.bfloat16
LANES = 128
SMALL = 16


def dot_nn(left, right):
    return lax.dot_general(left, right, (((1,), (0,)), ((), ())), preferred_element_type=F32)


def dot_tn(left, right):
    return lax.dot_general(left, right, (((0,), (0,)), ((), ())), preferred_element_type=F32)


def dot_nt(left, right):
    return lax.dot_general(left, right, (((1,), (1,)), ((), ())), preferred_element_type=F32)


def norm_parts(values_in):
    row_mean = jnp.mean(values_in, axis=-1, keepdims=True)
    centred = values_in - row_mean
    variance = jnp.mean(centred * centred, axis=-1, keepdims=True)
    scale = lax.rsqrt(variance + EPSILON)
    return centred * scale, scale


def norm_back(normed, scale, u):
    return scale * (
        u
        - jnp.mean(u, axis=-1, keepdims=True)
        - normed * jnp.mean(u * normed, axis=-1, keepdims=True)
    )


def iota(shape, dim):
    return lax.broadcasted_iota(jnp.int32, shape, dim)


def row_of(vector):
    return vector[...].reshape(1, vector.shape[0])


def head_mask(head, width):
    lane = iota((1, width), 1)
    return ((lane >= head * HEAD_DIM) & (lane < (head + 1) * HEAD_DIM)).astype(BF16)


def image_of(shape, dim, images):
    at = iota(shape, dim)
    image = jnp.zeros(shape, jnp.int32)
    for number in range(1, images):
        image = image + (at >= number * SEQ).astype(jnp.int32)
    return image


T_ID, C_ID, E_ID, D_ID, Q_ID, L_ID = range(6)


def plan_kernel(experts, ids, routes, cot, router, table, part, router_pad, *blocks):
    rows = cot.shape[0]
    cap = table.shape[1]
    tall = max(16, -(-experts // 16) * 16)
    picks = routes[...]
    expert = iota((tall, rows), 0)
    named = picks[0:1, :] == expert
    for k in range(1, picks.shape[0]):
        named = named | (picks[k : k + 1, :] == expert)
    named = named & (iota((tall, rows), 1) < ids[L_ID])
    marks = jnp.where(named, 1.0, 0.0).astype(BF16)
    earlier = jnp.where(iota((rows, rows), 0) < iota((rows, rows), 1), 1.0, 0.0).astype(BF16)
    slot = dot_nn(marks, earlier)
    first = (ids[C_ID] * cap).astype(F32)
    slot = jnp.where(named, slot - first, -1.0)
    place = iota((cap, rows), 0).astype(F32)
    for x in range(experts):
        table[x] = jnp.where(slot[x : x + 1, :] == place, 1.0, 0.0).astype(BF16)
    quarter = part.shape[1]
    first = ((ids[T_ID] // 2) * quarter).astype(F32)
    place = iota((quarter, rows), 0).astype(F32) + first
    for x in range(experts):
        part[x] = jnp.where(slot[x : x + 1, :] == place, 1.0, 0.0).astype(BF16)
    for k in range(experts):
        source = table if blocks[k].shape[0] == cap else part
        blocks[k][...] = dot_nn(source[ids[E_ID] ^ k], cot[...]).astype(BF16)
    router_pad[...] = jnp.zeros_like(router_pad)
    router_pad[:experts, :] = router[...]


def attend_kernel(images, tokens, gain, bias, weight, normed, query, key, value, probs, head_out):
    rows = tokens.shape[0]
    inner = query.shape[1]
    heads = inner // HEAD_DIM
    unit, _ = norm_parts(tokens[...].astype(F32))
    normed[...] = (unit * row_of(gain) + row_of(bias)).astype(BF16)
    query[...] = dot_nt(normed[...], weight[:inner]).astype(BF16)
    key[...] = dot_nt(normed[...], weight[inner : 2 * inner]).astype(BF16)
    value[...] = dot_nt(normed[...], weight[2 * inner :]).astype(BF16)
    same = image_of((rows, 1), 0, images) == image_of((1, rows), 1, images)
    total = jnp.zeros((rows, inner), F32)
    for head in range(heads):
        mask = head_mask(head, inner)
        scores = dot_nt(query[...] * mask, key[...]) * (HEAD_DIM**-0.5)
        scores = jnp.where(same, scores, -1e30)
        top = jnp.max(scores, axis=-1, keepdims=True)
        weights = jnp.exp(scores - top)
        weights = weights * (1.0 / jnp.sum(weights, axis=-1, keepdims=True))
        probs[head] = weights.astype(BF16)
        total = total + dot_nn(probs[head], value[...] * mask)
    head_out[...] = total.astype(BF16)


def middle_kernel(
    n_tensor, experts, ids, tokens, gain, bias, table, *rest
):
    heads = rest[:n_tensor]
    weights = rest[n_tensor : 2 * n_tensor]
    middle = rest[2 * n_tensor]
    blocks = rest[2 * n_tensor + 1 : 2 * n_tensor + 1 + experts]
    held_heads, held_weights, low = rest[2 * n_tensor + 1 + experts :]
    for j in range(n_tensor):
        held_heads[j] = heads[j][...]
        held_weights[j] = weights[j][...]
    total = tokens[...].astype(F32)
    for rank in range(n_tensor):
        place = ids[T_ID] ^ rank
        total = total + dot_nn(held_heads[place], held_weights[place])
    middle[...] = total
    unit, _ = norm_parts(total)
    low[...] = (unit * row_of(gain) + row_of(bias)).astype(BF16)
    for k in range(experts):
        blocks[k][...] = dot_nn(table[ids[E_ID] ^ k], low[...]).astype(BF16)


def expert_kernel(
    experts, places, with_grads, ids, up_a, up_b, down_a, down_b, router, *refs
):
    number = len(places)
    row_blocks, out_blocks = refs[:number], refs[number : 2 * number]
    pair_out = refs[2 * number]
    refs = refs[2 * number + 1 :]
    back_blocks, gated_kept, gated_sent = refs[:number], refs[number], refs[number + 1]
    refs = refs[number + 2 :]
    rows_in, d_result, hidden_a, hidden_b, d_pre_a, d_pre_b, router_part = refs[:7]
    d_out = refs[-1]
    size = row_blocks[0].shape[0]
    count = size * number
    far = ids[T_ID] // 2
    for k in range(number):
        rows_in[k * size : (k + 1) * size, :] = row_blocks[k][...]
        quarter = out_blocks[k].shape[0]
        if quarter == size:
            d_out[k * size : (k + 1) * size, :] = out_blocks[k][...].astype(F32)
        else:
            here = pl.multiple_of(k * size + far * quarter, 8)
            there = pl.multiple_of(k * size + (1 - far) * quarter, 8)
            d_out[pl.ds(here, quarter), :] = out_blocks[k][...].astype(F32)
            d_out[pl.ds(there, quarter), :] = pair_out[places[k] - 2].astype(F32)
    lane = iota((count, LANES), 1)
    logits = dot_nt(rows_in[...], router[...])
    logits = jnp.where(lane < experts, logits, -1e30)
    top = jnp.max(logits, axis=-1, keepdims=True)
    odds = jnp.exp(logits - top)
    odds = odds / jnp.sum(odds, axis=-1, keepdims=True)
    mine = (lane == ids[E_ID]).astype(F32)
    gate = jnp.sum(odds * mine, axis=-1, keepdims=True)
    d_result[...] = (gate * d_out[...]).astype(BF16)
    result = jnp.zeros(d_out.shape, F32)
    back = jnp.zeros(d_out.shape, F32)
    scale = 0.7978845608028654
    for up, down, hidden, d_pre in (
        (up_a, down_a, hidden_a, d_pre_a),
        (up_b, down_b, hidden_b, d_pre_b),
    ):
        act = dot_nn(rows_in[...], up[...])
        square = act * act
        bend = jnp.tanh(scale * act * (1.0 + 0.044715 * square))
        half = 0.5 * (1.0 + bend)
        hidden[...] = (act * half).astype(BF16)
        slope = half + 0.5 * act * (1.0 - bend * bend) * (
            scale * (1.0 + 3 * 0.044715 * square)
        )
        result = result + dot_nn(hidden[...], down[...])
        d_pre[...] = (dot_nt(d_result[...], down[...]) * slope).astype(BF16)
        back = back + dot_nt(d_pre[...], up[...])
    d_gate = jnp.sum(d_out[...] * result, axis=-1, keepdims=True)
    d_logits = (d_gate * gate * (mine - odds)).astype(BF16)
    back = (back + dot_nn(d_logits, router[...])).astype(BF16)
    for k in range(number):
        back_blocks[k][...] = back[k * size : (k + 1) * size, :]
    d_out[...] = gate * result
    quarter = gated_kept.shape[1]
    for k in range(number):
        if quarter == size:
            gated_kept[k] = d_out[k * size : (k + 1) * size, :].astype(BF16)
        else:
            here = pl.multiple_of(k * size + far * quarter, 8)
            there = pl.multiple_of(k * size + (1 - far) * quarter, 8)
            gated_kept[k] = d_out[pl.ds(here, quarter), :].astype(BF16)
            gated_sent[k] = d_out[pl.ds(there, quarter), :].astype(BF16)
    if quarter == size:
        gated_sent[...] = jnp.zeros_like(gated_sent)
    router_part[...] = dot_tn(d_logits, rows_in[...])[: router_part.shape[0]]
    if with_grads:
        own, pair = refs[7:9]
        weight_grads(rows_in, d_pre_a, d_pre_b, hidden_a, hidden_b, d_result, None, None, own, pair)


def weight_grads(
    rows, d_pre_a, d_pre_b, hidden_a, hidden_b, d_result, own_before, pair_before, own, pair
):
    width = own.shape[0] // 2
    for out, before, at, left, right in (
        (pair, pair_before, 0, rows, d_pre_b),
        (pair, pair_before, width, hidden_b, d_result),
        (own, own_before, 0, rows, d_pre_a),
        (own, own_before, width, hidden_a, d_result),
    ):
        total = dot_tn(left[...], right[...])
        if before is not None:
            total = total + before[at : at + width, :].astype(F32)
        out[at : at + width, :] = total.astype(BF16)


def gated_sum_kernel(kept, came, *blocks):
    for k, out in enumerate(blocks):
        out[...] = (kept[k].astype(F32) + came[k].astype(F32)).astype(BF16)


def weight_grad_kernel(*refs):
    rows, d_pre_a, d_pre_b, hidden_a, hidden_b, d_result = refs[:6]
    own_before, pair_before = refs[6:8] if len(refs) == 10 else (None, None)
    weight_grads(
        rows, d_pre_a, d_pre_b, hidden_a, hidden_b, d_result, own_before, pair_before, *refs[-2:]
    )


def split_grad_kernel(ids, own, came, kept, sent_first, sent_rest, total, sent):
    total[...] = own[...].astype(F32) + came[...].astype(F32)
    width = own.shape[1]
    half = width // 2
    mine, other = ids[D_ID], 1 - ids[D_ID]
    kept[:half, :] = total[pl.ds(pl.multiple_of(mine * half, 16), half), :]
    sent[:half, :] = total[pl.ds(pl.multiple_of(other * half, 16), half), :].astype(BF16)
    column = pl.ds(pl.multiple_of(mine * half, LANES), half)
    kept[half:, :half] = total[width : width + half, column]
    kept[half:, half:] = total[width + half :, column]
    column = pl.ds(pl.multiple_of(other * half, LANES), half)
    sent[half:, :half] = total[width : width + half, column].astype(BF16)
    sent[half:, half:] = total[width + half :, column].astype(BF16)
    first = sent_first.shape[0]
    sent_first[...] = sent[:first, :]
    sent_rest[...] = sent[first:, :]


def join_grad_kernel(kept, came_first, came_rest, grad_up, grad_down, came):
    first = came_first.shape[0]
    came[:first, :] = came_first[...]
    came[first:, :] = came_rest[...]
    half = kept.shape[1] // 2
    grad_up[...] = kept[:half, :] + came[:half, :].astype(F32)
    grad_down[:half, :] = kept[half:, :half] + came[half:, :half].astype(F32)
    grad_down[half:, :] = kept[half:, half:] + came[half:, half:].astype(F32)


def combine_kernel(order, parts, base, ids, table, part, *refs):
    experts = len(order)
    blocks = refs[:experts]
    routers = refs[experts : experts + parts]
    kept, sent, total = refs[experts + parts :]
    value = dot_tn(table[ids[E_ID]], blocks[0][...])
    for block, k in zip(blocks[1:], order[1:]):
        spots = table if block.shape[0] == table.shape[1] else part
        value = value + dot_tn(spots[ids[E_ID] ^ k], block[...])
    total[...] = jnp.zeros_like(total)
    total[: value.shape[0], :] = value
    if parts:
        added = routers[0][...]
        for k in range(1, parts):
            added = added + routers[k][...]
        total[base : base + added.shape[0], :] = added
    half = kept.shape[1]
    kept[...] = total[:, pl.ds(pl.multiple_of(ids[C_ID] * half, LANES), half)].astype(BF16)
    sent[...] = total[:, pl.ds(pl.multiple_of((1 - ids[C_ID]) * half, LANES), half)].astype(BF16)


def joined(ids, own, other, whole):
    half = own.shape[1]
    whole[:, pl.ds(pl.multiple_of(ids[C_ID] * half, LANES), half)] = own[...].astype(F32)
    whole[:, pl.ds(pl.multiple_of((1 - ids[C_ID]) * half, LANES), half)] = other[...].astype(F32)


def back_kernel(
    blocks_n, ids, own, other, middle, cot, gain, w_out, head_out, normed, query, key, value,
    probs, weight, *rest
):
    d_middle, kept, sent, small = rest[:4]
    blocks = rest[4 : 4 + blocks_n]
    whole, grads = rest[4 + blocks_n :]
    rows, inner = query.shape
    heads = inner // HEAD_DIM
    joined(ids, own, other, whole)
    d_normed = whole[:rows, :]
    unit, scale = norm_parts(middle[...])
    small[...] = jnp.zeros_like(small)
    base = -(-rows // 16) * 16
    small[8:, :] = whole[base : base + small.shape[0] - 8, :]
    small[2:3, :] = jnp.sum(d_normed * unit, axis=0, keepdims=True)
    small[3:4, :] = jnp.sum(d_normed, axis=0, keepdims=True)
    live = iota((rows, 1), 0) < ids[L_ID]
    d_out = jnp.where(live, cot[...].astype(F32), 0.0)
    d_mid = d_out + norm_back(unit, scale, d_normed * row_of(gain))
    d_middle[...] = d_mid
    d_branch = d_mid.astype(BF16)
    d_head = dot_nt(d_branch, w_out[...]).astype(BF16)
    grads[3 * inner :, :] = dot_tn(head_out[...], d_branch).astype(BF16)
    d_query = jnp.zeros((rows, inner), F32)
    d_key = jnp.zeros((rows, inner), F32)
    d_value = jnp.zeros((rows, inner), F32)
    for head in range(heads):
        mask = head_mask(head, inner)
        chance = probs[head].astype(F32)
        d_probs = dot_nt(d_head, value[...] * mask)
        delta = jnp.sum(d_probs * chance, axis=-1, keepdims=True)
        d_scores = (chance * (d_probs - delta)).astype(BF16)
        d_value = d_value + dot_tn(probs[head], d_head * mask)
        d_query = d_query + dot_nn(d_scores, key[...] * mask)
        d_key = d_key + dot_tn(d_scores, query[...] * mask)
    d_query = (d_query * (HEAD_DIM**-0.5)).astype(BF16)
    d_key = (d_key * (HEAD_DIM**-0.5)).astype(BF16)
    d_value = d_value.astype(BF16)
    grads[:inner, :] = dot_tn(d_query, normed[...]).astype(BF16)
    grads[inner : 2 * inner, :] = dot_tn(d_key, normed[...]).astype(BF16)
    grads[2 * inner : 3 * inner, :] = dot_tn(d_value, normed[...]).astype(BF16)
    if blocks_n == 1:
        blocks[0][...] = grads[...]
    else:
        size = blocks[0].shape[0]
        for m in range(blocks_n):
            at = pl.multiple_of((ids[Q_ID] ^ m) * size, 16)
            blocks[m][...] = grads[pl.ds(at, size), :]
    d_in = dot_nn(d_query, weight[:inner])
    d_in = d_in + dot_nn(d_key, weight[inner : 2 * inner])
    whole[:rows, :] = d_in + dot_nn(d_value, weight[2 * inner :])
    half = kept.shape[1]
    kept[...] = whole[:rows, pl.ds(pl.multiple_of(ids[C_ID] * half, LANES), half)].astype(BF16)
    sent[...] = whole[:rows, pl.ds(pl.multiple_of((1 - ids[C_ID]) * half, LANES), half)].astype(BF16)


def last_norm_kernel(ids, own, other, tokens, d_middle, gain, small2, grad_tokens, small, whole):
    joined(ids, own, other, whole)
    d_normed = whole[...]
    unit, scale = norm_parts(tokens[...].astype(F32))
    small[...] = small2[...]
    small[0:1, :] = jnp.sum(d_normed * unit, axis=0, keepdims=True)
    small[1:2, :] = jnp.sum(d_normed, axis=0, keepdims=True)
    grad_tokens[...] = (
        d_middle[...] + norm_back(unit, scale, d_normed * row_of(gain))
    ).astype(BF16)


def sum_kernel(count, *refs):
    total = refs[0][...].astype(F32)
    for m in range(1, count):
        total = total + refs[m][...].astype(F32)
    refs[count][...] = total.astype(BF16)


def pair_kernel(own, came, small, small_came, out):
    size = own.shape[0]
    out[:size, :] = (own[...].astype(F32) + came[...].astype(F32)).astype(BF16)
    out[size:, :] = (small[...] + small_came[...]).astype(BF16)


def spread_kernel(masks, ids, *refs):
    count = len(masks)
    parts = refs[:count]
    grad_qkv, grad_out, gain1, bias1, gain2, bias2, router, grads, held = refs[count:]
    size = grads.shape[0] // count
    for mask, block in zip(masks, parts):
        quarter = ids[Q_ID] ^ mask
        grads[pl.ds(pl.multiple_of(quarter * size, 16), size), :] = block[:size, :].astype(F32)
        held[quarter] = block[size:, :].astype(F32)
    total = held[0]
    for quarter in range(1, count):
        total = total + held[quarter]
    for row, out in enumerate((gain1, bias1, gain2, bias2)):
        out[...] = total[row : row + 1, :].reshape(out.shape)
    router[...] = total[8 : 8 + router.shape[0], :]
    inner = grad_qkv.shape[0]
    grad_qkv[...] = grads[:inner, :]
    grad_out[...] = grads[inner:, :]


def after(value, *others):
    return lax.optimization_barrier((value,) + others)[0]


def run(kernel, outs, args, scratch=(), micros=1.0, limit=16):
    smem = pl.BlockSpec(memory_space=pltpu.SMEM)
    vmem = pl.BlockSpec(memory_space=pltpu.VMEM)
    return pl.pallas_call(
        kernel,
        out_shape=[jax.ShapeDtypeStruct(shape, kind) for shape, kind in outs],
        in_specs=[smem if arg.dtype == jnp.int32 and arg.ndim == 1 else vmem for arg in args],
        out_specs=[vmem] * len(outs),
        scratch_shapes=[pltpu.VMEM(shape, kind) for shape, kind in scratch],
        compiler_params=pltpu.CompilerParams(vmem_limit_bytes=limit * 1024 * 1024),
        cost_estimate=pl.CostEstimate(
            flops=int(micros * 1.15e9), bytes_accessed=1024, transcendentals=0
        ),
    )(*args)


def make_body(n_tensor, n_expert, n_dp):
    small_slice = n_expert == 4 and n_dp == 2

    def tensor_swap(value, mask):
        return lax.ppermute(value, "tensor", [(i, i ^ mask) for i in range(n_tensor)])

    def expert_swap(value, mask):
        return lax.ppermute(value, "expert", [(i, i ^ mask) for i in range(n_expert)])

    def dp_swap(value):
        return lax.ppermute(value, "dp", [(i, i ^ 1) for i in range(n_dp)])

    def quarter_swap(value, mask):
        pairs = [(i, i ^ mask) for i in range(n_expert * n_dp)]
        return lax.ppermute(value, ("expert", "dp"), pairs)

    def exchange(blocks):
        if small_slice:
            came = {k: expert_swap(blocks[k], k) for k in (3, 2, 1)}
            return [blocks[0]] + [came[k] for k in range(1, n_expert)]
        order = jnp.arange(n_expert) ^ lax.axis_index("expert")
        stacked = lax.all_to_all(
            jnp.stack(blocks)[order], "expert", split_axis=0, concat_axis=0, tiled=True
        )[order]
        return [stacked[k] for k in range(n_expert)]

    def body(
        tokens,
        routes,
        images_live,
        ln1_gain,
        ln1_bias,
        w_qkv,
        w_out,
        ln2_gain,
        ln2_bias,
        w_router,
        w_up,
        w_down,
        cotangent,
    ):
        rows, width = tokens.shape
        inner = w_qkv.shape[2]
        heads = inner // HEAD_DIM
        experts = w_router.shape[1]
        capacity = max(2, 3 * rows // experts // 8 * 8)
        cap = capacity // 2
        images = rows // SEQ
        half = width // 2
        hidden_width = w_up.shape[2]
        rank = lax.axis_index("tensor")
        owner = lax.axis_index("expert")
        copy = lax.axis_index("dp")
        ids = jnp.stack(
            [
                rank,
                rank % 2,
                owner,
                copy,
                (owner % 2) * 2 + copy,
                jnp.minimum(images_live[0] * SEQ, rows),
                rank,
                rank,
            ]
        ).astype(jnp.int32)
        weight = w_qkv.transpose(1, 2, 0).reshape(3 * inner, width)
        up_a, down_a = w_up[0], w_down[0]
        part_rows = max(8, -(-experts // 8) * 8)
        small_rows = 8 + part_rows
        base = -(-rows // 16) * 16
        tall = base + -(-part_rows // 16) * 16

        out_x, out_c = tensor_swap(w_out, 2), tensor_swap(w_out, 1)
        up_b, down_b = tensor_swap(up_a, 1), tensor_swap(down_a, 1)
        normed, query, key, value, probs, head_out = run(
            functools.partial(attend_kernel, images),
            [((rows, width), BF16)]
            + [((rows, inner), BF16)] * 3
            + [((heads, rows, rows), BF16), ((rows, inner), BF16)],
            [tokens, ln1_gain, ln1_bias, weight],
            micros=4,
        )
        head_out, out_x, out_c, up_b, down_b = lax.optimization_barrier(
            (head_out, out_x, out_c, up_b, down_b)
        )
        head_x, head_c = tensor_swap(head_out, 2), tensor_swap(head_out, 1)
        quarter = cap // 2
        cot_shapes = [(quarter if small_slice and k > 1 else cap, width) for k in range(experts)]
        table, part, router, *cot_blocks = run(
            functools.partial(plan_kernel, experts),
            [((experts, cap, rows), BF16), ((experts, quarter, rows), BF16)]
            + [((LANES, width), BF16)]
            + [(shape, BF16) for shape in cot_shapes],
            [ids, after(routes.T, head_out), cotangent, w_router.T],
            micros=2,
        )
        head_x = after(head_x, table)
        if small_slice:
            d_rows_in = cot_blocks[:2] + [expert_swap(cot_blocks[k], k) for k in (2, 3)]
        else:
            d_rows_in = exchange(cot_blocks)
        out_all = [w_out, out_c, out_x, tensor_swap(out_x, 1)]
        heads_all = [head_out, head_c, head_x, tensor_swap(head_x, 1)]
        middle, *row_blocks = run(
            functools.partial(middle_kernel, n_tensor, experts),
            [((rows, width), F32)] + [((cap, width), BF16)] * experts,
            [ids, tokens, ln2_gain, ln2_bias, table] + heads_all + out_all,
            scratch=[
                ((n_tensor, rows, inner), BF16),
                ((n_tensor, inner, width), BF16),
                ((rows, width), BF16),
            ],
            micros=3,
        )
        if small_slice:
            *row_blocks, far_2, far_3 = lax.optimization_barrier((*row_blocks, *d_rows_in[2:]))
            d_rows_in[2:] = [far_2, far_3]
            d_rows_in[1], middle = lax.optimization_barrier((d_rows_in[1], middle))
            d_rows_in[1] = expert_swap(d_rows_in[1], 1)
            pair_out = tensor_swap(jnp.stack([far_2, far_3]), 2)
        else:
            pair_out = router
        rows_in = exchange(list(row_blocks))

        calls = [(0, 1), (2, 3)] if small_slice else [tuple(range(experts))]
        worked = []
        d_back, gated = [], []
        for number, call in enumerate(calls):
            if number == 1:
                router, d_back[1] = lax.optimization_barrier((router, d_back[1]))
            count = cap * len(call)
            last = number == len(calls) - 1
            grads = [] if last else [((2 * width, hidden_width), BF16)] * 2
            results = run(
                functools.partial(expert_kernel, experts, call, not last),
                [((cap, width), BF16)] * len(call)
                + [((len(call), quarter if worked else cap, width), BF16)] * 2
                + [((count, width), BF16)] * 2
                + [((count, hidden_width), BF16)] * 4
                + [((part_rows, width), F32)]
                + grads,
                [ids, up_a, up_b, down_a, down_b]
                + [router]
                + [rows_in[k] for k in call]
                + [d_rows_in[k] for k in call]
                + [pair_out if worked or not small_slice else router],
                scratch=[((count, width), F32)],
                micros=0.05,
                limit=24,
            )
            d_back += results[: len(call)]
            gated.append(results[len(call) : len(call) + 2])
            worked.append(results[len(call) + 2 :])

        order = [0] + list(range(experts - 1, 0, -1))

        def combine(blocks, routers):
            blocks = [blocks[k] for k in order]
            return run(
                functools.partial(combine_kernel, order, len(routers), base),
                [((tall if routers else base, half), BF16)] * 2,
                [ids, table, part] + blocks + routers,
                scratch=[((tall if routers else base, width), F32)],
                micros=2,
            )

        if small_slice:
            d_back[1], d_back[2] = lax.optimization_barrier((d_back[1], d_back[2]))
        d_home = exchange(d_back)

        grad_own, grad_pair = run(
            weight_grad_kernel,
            [((2 * width, hidden_width), BF16)] * 2,
            [worked[-1][at] for at in (0, 4, 5, 2, 3, 1)] + list(worked[0][7:]),
            micros=4,
            limit=24,
        )
        third = width // 96 * 16
        grad_kept, sent_first, sent_rest = run(
            split_grad_kernel,
            [((width, width), F32), ((third, width), BF16), ((width - third, width), BF16)],
            [ids, grad_own, tensor_swap(grad_pair, 1)],
            scratch=[((2 * width, width), F32), ((width, width), BF16)],
            micros=2,
            limit=24,
        )

        if small_slice:
            far_blocks = run(
                gated_sum_kernel,
                [((quarter, width), BF16)] * 2,
                [gated[1][0], tensor_swap(gated[1][1], 2)],
            )
            gated_blocks = [gated[0][0][0], gated[0][0][1], *far_blocks]
        else:
            gated_blocks = [gated[0][0][k] for k in range(experts)]

        came_first = dp_swap(sent_first)
        *gated_blocks, came_first = lax.optimization_barrier(
            (*d_home[::-1], *gated_blocks, came_first)
        )
        d_home, gated_blocks = gated_blocks[:experts][::-1], gated_blocks[experts:]
        kept, sent = combine(list(d_home), [one[6] for one in worked])
        chip = (kept.astype(F32) + tensor_swap(sent, 1).astype(F32)).astype(BF16)
        own = (chip.astype(F32) + tensor_swap(chip, 2).astype(F32)).astype(BF16)
        if small_slice:
            home = {k: expert_swap(gated_blocks[k], k) for k in (2, 3, 1)}
            gated_home = [gated_blocks[0], home[1], home[2], home[3]]
        else:
            gated_home = exchange(list(gated_blocks))
        own, *gated_home = lax.optimization_barrier((own, *gated_home))
        other = tensor_swap(own, 1)

        parts = 4 if small_slice else 1
        d_middle, kept1, sent1, small2, *grad_blocks = run(
            functools.partial(back_kernel, parts),
            [((rows, width), F32)]
            + [((rows, half), BF16)] * 2
            + [((small_rows, width), F32)]
            + [((4 * inner // parts, width), BF16)] * parts,
            [
                ids, own, other, middle, cotangent, ln2_gain, w_out, head_out, normed, query,
                key, value, probs, weight,
            ],
            scratch=[((tall, width), F32), ((4 * inner, width), BF16)],
            micros=6,
        )

        *gated_home, _ = lax.optimization_barrier((*gated_home, d_middle))
        kept_y, sent_y = combine(list(gated_home), [])

        chip1 = (kept1.astype(F32) + tensor_swap(sent1, 1).astype(F32)).astype(BF16)
        own1 = (chip1.astype(F32) + tensor_swap(chip1, 2).astype(F32)).astype(BF16)
        if small_slice:
            arrived = [grad_blocks[0]] + [quarter_swap(grad_blocks[m], m) for m in (3, 1, 2)]
            arrived[0], kept_y, sent_y = lax.optimization_barrier((arrived[0], kept_y, sent_y))
            size = grad_blocks[0].shape[0]
            (summed,) = run(
                functools.partial(sum_kernel, 4), [((size, width), BF16)], arrived, micros=0.5
            )
            sent_rest, own1 = lax.optimization_barrier((sent_rest, own1, summed))[:2]
        other1 = tensor_swap(own1, 1)
        grad_tokens, small = run(
            last_norm_kernel,
            [((rows, width), BF16), ((small_rows, width), F32)],
            [ids, own1, other1, tokens, d_middle, ln1_gain, small2],
            scratch=[((rows, width), F32)],
            micros=0.01,
        )
        chip_y = (kept_y.astype(F32) + tensor_swap(sent_y, 1).astype(F32)).astype(BF16)
        own_y = (chip_y.astype(F32) + tensor_swap(chip_y, 2).astype(F32)).astype(BF16)
        grad_up, grad_down = run(
            join_grad_kernel,
            [((half, hidden_width), F32), ((hidden_width, half), F32)],
            [grad_kept, came_first, dp_swap(sent_rest)],
            scratch=[((width, width), BF16)],
            micros=2,
        )
        if small_slice:
            (ready,) = run(
                pair_kernel,
                [((size + small_rows, width), BF16)],
                [summed, expert_swap(summed, 2), small, expert_swap(small, 2)],
                micros=1,
            )
            own_y, ready = lax.optimization_barrier((own_y, ready))
            everything = [quarter_swap(ready, m) for m in (3, 1, 2)]
            ready, grad_up, grad_down = lax.optimization_barrier((ready, grad_up, grad_down))
            everything = [ready] + everything
            grad_qkv, grad_out, *sums, grad_router = run(
                functools.partial(spread_kernel, (0, 3, 1, 2)),
                [((3 * inner, width), F32), ((inner, width), F32)]
                + [((width,), F32)] * 4
                + [((experts, width), F32)],
                [ids] + everything,
                scratch=[((4 * inner, width), F32), ((4, small_rows, width), F32)],
                micros=3,
            )
        else:
            grads = lax.psum(grad_blocks[0], ("expert", "dp")).astype(F32)
            grad_qkv, grad_out = grads[: 3 * inner], grads[3 * inner :]
            small_sum = lax.psum(small, ("expert", "dp"))
            sums, grad_router = list(small_sum[:4]), small_sum[8 : 8 + experts]

        mix_own, mix_other = own_y, tensor_swap(own_y, 1)
        mixture = jnp.where(
            rank % 2 == 0,
            jnp.concatenate([mix_own, mix_other], axis=1),
            jnp.concatenate([mix_other, mix_own], axis=1),
        )[:rows].astype(F32)
        alive = (jnp.arange(rows, dtype=jnp.int32) < images_live[0] * SEQ)[:, None]
        out = jnp.where(alive, middle + mixture, 0.0).astype(BF16)
        return (
            out,
            grad_tokens,
            sums[0],
            sums[1],
            grad_qkv.reshape(3, inner, width).transpose(2, 0, 1),
            grad_out,
            sums[2],
            sums[3],
            grad_router.T,
            grad_up[None],
            grad_down[None],
        )

    return body


def solution(mesh):
    in_specs = (
        P(("expert", "dp"), None),
        P(("expert", "dp"), None),
        P(("expert", "dp")),
        P(),
        P(),
        P(None, None, "tensor"),
        P("tensor", None),
        P(),
        P(),
        P(),
        P("expert", None, "tensor"),
        P("expert", "tensor", None),
        P(("expert", "dp"), None),
    )
    out_specs = (
        P(("expert", "dp"), None),
        P(("expert", "dp"), None),
        P(),
        P(),
        P(None, None, "tensor"),
        P("tensor", None),
        P(),
        P(),
        P(),
        P("expert", "dp", "tensor"),
        P("expert", "tensor", "dp"),
    )
    body = make_body(mesh.shape["tensor"], mesh.shape["expert"], mesh.shape["dp"])
    return jax.shard_map(body, mesh=mesh, in_specs=in_specs, out_specs=out_specs, check_vma=False)
```

```python
import functools

import jax
import jax.numpy as jnp
from jax import lax
from jax.experimental import pallas as pl
from jax.experimental.pallas import tpu as pltpu
from jax.sharding import PartitionSpec as P

HEAD_DIM = 64
SEQ = 197
EPSILON = 1e-06
F32 = jnp.float32
BF16 = jnp.bfloat16
LANES = 128
SMALL = 16


def dot_nn(left, right):
    return lax.dot_general(left, right, (((1,), (0,)), ((), ())), preferred_element_type=F32)


def dot_tn(left, right):
    return lax.dot_general(left, right, (((0,), (0,)), ((), ())), preferred_element_type=F32)


def dot_nt(left, right):
    return lax.dot_general(left, right, (((1,), (1,)), ((), ())), preferred_element_type=F32)


def norm_parts(values_in):
    row_mean = jnp.mean(values_in, axis=-1, keepdims=True)
    centred = values_in - row_mean
    variance = jnp.mean(centred * centred, axis=-1, keepdims=True)
    scale = lax.rsqrt(variance + EPSILON)
    return centred * scale, scale


def norm_back(normed, scale, u):
    return scale * (
        u
        - jnp.mean(u, axis=-1, keepdims=True)
        - normed * jnp.mean(u * normed, axis=-1, keepdims=True)
    )


def iota(shape, dim):
    return lax.broadcasted_iota(jnp.int32, shape, dim)


def row_of(vector):
    return vector[...].reshape(1, vector.shape[0])


def head_mask(head, width):
    lane = iota((1, width), 1)
    return ((lane >= head * HEAD_DIM) & (lane < (head + 1) * HEAD_DIM)).astype(BF16)


def image_of(shape, dim, images):
    at = iota(shape, dim)
    image = jnp.zeros(shape, jnp.int32)
    for number in range(1, images):
        image = image + (at >= number * SEQ).astype(jnp.int32)
    return image


T_ID, C_ID, E_ID, D_ID, Q_ID, L_ID = range(6)


def plan_kernel(experts, ids, routes, cot, router, table, part, router_pad, *blocks):
    rows = cot.shape[0]
    cap = table.shape[1]
    tall = max(16, -(-experts // 16) * 16)
    picks = routes[...]
    expert = iota((tall, rows), 0)
    named = picks[0:1, :] == expert
    for k in range(1, picks.shape[0]):
        named = named | (picks[k : k + 1, :] == expert)
    named = named & (iota((tall, rows), 1) < ids[L_ID])
    marks = jnp.where(named, 1.0, 0.0).astype(BF16)
    earlier = jnp.where(iota((rows, rows), 0) < iota((rows, rows), 1), 1.0, 0.0).astype(BF16)
    slot = dot_nn(marks, earlier)
    first = (ids[C_ID] * cap).astype(F32)
    slot = jnp.where(named, slot - first, -1.0)
    place = iota((cap, rows), 0).astype(F32)
    for x in range(experts):
        table[x] = jnp.where(slot[x : x + 1, :] == place, 1.0, 0.0).astype(BF16)
    quarter = part.shape[1]
    first = ((ids[T_ID] // 2) * quarter).astype(F32)
    place = iota((quarter, rows), 0).astype(F32) + first
    for x in range(experts):
        part[x] = jnp.where(slot[x : x + 1, :] == place, 1.0, 0.0).astype(BF16)
    for k in range(experts):
        source = table if blocks[k].shape[0] == cap else part
        blocks[k][...] = dot_nn(source[ids[E_ID] ^ k], cot[...]).astype(BF16)
    router_pad[...] = jnp.zeros_like(router_pad)
    router_pad[:experts, :] = router[...]


def attend_kernel(images, tokens, gain, bias, weight, normed, query, key, value, probs, head_out):
    rows = tokens.shape[0]
    inner = query.shape[1]
    heads = inner // HEAD_DIM
    unit, _ = norm_parts(tokens[...].astype(F32))
    normed[...] = (unit * row_of(gain) + row_of(bias)).astype(BF16)
    query[...] = dot_nt(normed[...], weight[:inner]).astype(BF16)
    key[...] = dot_nt(normed[...], weight[inner : 2 * inner]).astype(BF16)
    value[...] = dot_nt(normed[...], weight[2 * inner :]).astype(BF16)
    same = image_of((rows, 1), 0, images) == image_of((1, rows), 1, images)
    total = jnp.zeros((rows, inner), F32)
    for head in range(heads):
        mask = head_mask(head, inner)
        scores = dot_nt(query[...] * mask, key[...]) * (HEAD_DIM**-0.5)
        scores = jnp.where(same, scores, -1e30)
        top = jnp.max(scores, axis=-1, keepdims=True)
        weights = jnp.exp(scores - top)
        weights = weights * (1.0 / jnp.sum(weights, axis=-1, keepdims=True))
        probs[head] = weights.astype(BF16)
        total = total + dot_nn(probs[head], value[...] * mask)
    head_out[...] = total.astype(BF16)


def middle_kernel(
    n_tensor, experts, ids, tokens, gain, bias, table, *rest
):
    heads = rest[:n_tensor]
    weights = rest[n_tensor : 2 * n_tensor]
    middle = rest[2 * n_tensor]
    blocks = rest[2 * n_tensor + 1 : 2 * n_tensor + 1 + experts]
    held_heads, held_weights, low = rest[2 * n_tensor + 1 + experts :]
    for j in range(n_tensor):
        held_heads[j] = heads[j][...]
        held_weights[j] = weights[j][...]
    total = tokens[...].astype(F32)
    for rank in range(n_tensor):
        place = ids[T_ID] ^ rank
        total = total + dot_nn(held_heads[place], held_weights[place])
    middle[...] = total
    unit, _ = norm_parts(total)
    low[...] = (unit * row_of(gain) + row_of(bias)).astype(BF16)
    for k in range(experts):
        blocks[k][...] = dot_nn(table[ids[E_ID] ^ k], low[...]).astype(BF16)


def expert_kernel(
    experts, places, with_grads, ids, up_a, up_b, down_a, down_b, router, *refs
):
    number = len(places)
    row_blocks, out_blocks = refs[:number], refs[number : 2 * number]
    pair_out = refs[2 * number]
    refs = refs[2 * number + 1 :]
    back_blocks, gated_kept, gated_sent = refs[:number], refs[number], refs[number + 1]
    refs = refs[number + 2 :]
    rows_in, d_result, hidden_a, hidden_b, d_pre_a, d_pre_b, router_part = refs[:7]
    d_out = refs[-1]
    size = row_blocks[0].shape[0]
    count = size * number
    far = ids[T_ID] // 2
    for k in range(number):
        rows_in[k * size : (k + 1) * size, :] = row_blocks[k][...]
        quarter = out_blocks[k].shape[0]
        if quarter == size:
            d_out[k * size : (k + 1) * size, :] = out_blocks[k][...].astype(F32)
        else:
            here = pl.multiple_of(k * size + far * quarter, 8)
            there = pl.multiple_of(k * size + (1 - far) * quarter, 8)
            d_out[pl.ds(here, quarter), :] = out_blocks[k][...].astype(F32)
            d_out[pl.ds(there, quarter), :] = pair_out[places[k] - 2].astype(F32)
    lane = iota((count, LANES), 1)
    logits = dot_nt(rows_in[...], router[...])
    logits = jnp.where(lane < experts, logits, -1e30)
    top = jnp.max(logits, axis=-1, keepdims=True)
    odds = jnp.exp(logits - top)
    odds = odds / jnp.sum(odds, axis=-1, keepdims=True)
    mine = (lane == ids[E_ID]).astype(F32)
    gate = jnp.sum(odds * mine, axis=-1, keepdims=True)
    d_result[...] = (gate * d_out[...]).astype(BF16)
    result = jnp.zeros(d_out.shape, F32)
    back = jnp.zeros(d_out.shape, F32)
    scale = 0.7978845608028654
    for up, down, hidden, d_pre in (
        (up_a, down_a, hidden_a, d_pre_a),
        (up_b, down_b, hidden_b, d_pre_b),
    ):
        act = dot_nn(rows_in[...], up[...])
        square = act * act
        bend = jnp.tanh(scale * act * (1.0 + 0.044715 * square))
        half = 0.5 * (1.0 + bend)
        hidden[...] = (act * half).astype(BF16)
        slope = half + 0.5 * act * (1.0 - bend * bend) * (
            scale * (1.0 + 3 * 0.044715 * square)
        )
        result = result + dot_nn(hidden[...], down[...])
        d_pre[...] = (dot_nt(d_result[...], down[...]) * slope).astype(BF16)
        back = back + dot_nt(d_pre[...], up[...])
    d_gate = jnp.sum(d_out[...] * result, axis=-1, keepdims=True)
    d_logits = (d_gate * gate * (mine - odds)).astype(BF16)
    back = (back + dot_nn(d_logits, router[...])).astype(BF16)
    for k in range(number):
        back_blocks[k][...] = back[k * size : (k + 1) * size, :]
    d_out[...] = gate * result
    quarter = gated_kept.shape[1]
    for k in range(number):
        if quarter == size:
            gated_kept[k] = d_out[k * size : (k + 1) * size, :].astype(BF16)
        else:
            here = pl.multiple_of(k * size + far * quarter, 8)
            there = pl.multiple_of(k * size + (1 - far) * quarter, 8)
            gated_kept[k] = d_out[pl.ds(here, quarter), :].astype(BF16)
            gated_sent[k] = d_out[pl.ds(there, quarter), :].astype(BF16)
    if quarter == size:
        gated_sent[...] = jnp.zeros_like(gated_sent)
    router_part[...] = dot_tn(d_logits, rows_in[...])[: router_part.shape[0]]
    if with_grads:
        own, pair = refs[7:9]
        weight_grads(rows_in, d_pre_a, d_pre_b, hidden_a, hidden_b, d_result, None, None, own, pair)


def weight_grads(
    rows, d_pre_a, d_pre_b, hidden_a, hidden_b, d_result, own_before, pair_before, own, pair
):
    width = own.shape[0] // 2
    for out, before, at, left, right in (
        (pair, pair_before, 0, rows, d_pre_b),
        (pair, pair_before, width, hidden_b, d_result),
        (own, own_before, 0, rows, d_pre_a),
        (own, own_before, width, hidden_a, d_result),
    ):
        total = dot_tn(left[...], right[...])
        if before is not None:
            total = total + before[at : at + width, :].astype(F32)
        out[at : at + width, :] = total.astype(BF16)


def gated_sum_kernel(kept, came, *blocks):
    for k, out in enumerate(blocks):
        out[...] = (kept[k].astype(F32) + came[k].astype(F32)).astype(BF16)


def weight_grad_kernel(*refs):
    rows, d_pre_a, d_pre_b, hidden_a, hidden_b, d_result = refs[:6]
    own_before, pair_before = refs[6:8] if len(refs) == 10 else (None, None)
    weight_grads(
        rows, d_pre_a, d_pre_b, hidden_a, hidden_b, d_result, own_before, pair_before, *refs[-2:]
    )


def split_grad_kernel(ids, own, came, kept, sent_first, sent_next, sent_rest, total, sent):
    total[...] = own[...].astype(F32) + came[...].astype(F32)
    width = own.shape[1]
    half = width // 2
    mine, other = ids[D_ID], 1 - ids[D_ID]
    kept[:half, :] = total[pl.ds(pl.multiple_of(mine * half, 16), half), :]
    sent[:half, :] = total[pl.ds(pl.multiple_of(other * half, 16), half), :].astype(BF16)
    column = pl.ds(pl.multiple_of(mine * half, LANES), half)
    kept[half:, :half] = total[width : width + half, column]
    kept[half:, half:] = total[width + half :, column]
    column = pl.ds(pl.multiple_of(other * half, LANES), half)
    sent[half:, :half] = total[width : width + half, column].astype(BF16)
    sent[half:, half:] = total[width + half :, column].astype(BF16)
    first = sent_first.shape[0]
    sent_first[...] = sent[:first, :]
    sent_next[...] = sent[first : 2 * first, :]
    sent_rest[...] = sent[2 * first :, :]


def join_grad_kernel(kept, came_first, came_next, came_rest, grad_up, grad_down, came):
    first = came_first.shape[0]
    came[:first, :] = came_first[...]
    came[first : 2 * first, :] = came_next[...]
    came[2 * first :, :] = came_rest[...]
    half = kept.shape[1] // 2
    grad_up[...] = kept[:half, :] + came[:half, :].astype(F32)
    grad_down[:half, :] = kept[half:, :half] + came[half:, :half].astype(F32)
    grad_down[half:, :] = kept[half:, half:] + came[half:, half:].astype(F32)


def combine_kernel(order, parts, base, ids, table, part, *refs):
    experts = len(order)
    blocks = refs[:experts]
    routers = refs[experts : experts + parts]
    kept, sent, total = refs[experts + parts :]
    value = dot_tn(table[ids[E_ID]], blocks[0][...])
    for block, k in zip(blocks[1:], order[1:]):
        spots = table if block.shape[0] == table.shape[1] else part
        value = value + dot_tn(spots[ids[E_ID] ^ k], block[...])
    total[...] = jnp.zeros_like(total)
    total[: value.shape[0], :] = value
    if parts:
        added = routers[0][...]
        for k in range(1, parts):
            added = added + routers[k][...]
        total[base : base + added.shape[0], :] = added
    half = kept.shape[1]
    kept[...] = total[:, pl.ds(pl.multiple_of(ids[C_ID] * half, LANES), half)].astype(BF16)
    sent[...] = total[:, pl.ds(pl.multiple_of((1 - ids[C_ID]) * half, LANES), half)].astype(BF16)


def joined(ids, own, other, whole):
    half = own.shape[1]
    whole[:, pl.ds(pl.multiple_of(ids[C_ID] * half, LANES), half)] = own[...].astype(F32)
    whole[:, pl.ds(pl.multiple_of((1 - ids[C_ID]) * half, LANES), half)] = other[...].astype(F32)


def back_kernel(
    blocks_n, ids, own, other, middle, cot, gain, w_out, head_out, normed, query, key, value,
    probs, weight, *rest
):
    d_middle, kept, sent, small = rest[:4]
    blocks = rest[4 : 4 + blocks_n]
    whole, grads = rest[4 + blocks_n :]
    rows, inner = query.shape
    heads = inner // HEAD_DIM
    joined(ids, own, other, whole)
    d_normed = whole[:rows, :]
    unit, scale = norm_parts(middle[...])
    small[...] = jnp.zeros_like(small)
    base = -(-rows // 16) * 16
    small[8:, :] = whole[base : base + small.shape[0] - 8, :]
    small[2:3, :] = jnp.sum(d_normed * unit, axis=0, keepdims=True)
    small[3:4, :] = jnp.sum(d_normed, axis=0, keepdims=True)
    live = iota((rows, 1), 0) < ids[L_ID]
    d_out = jnp.where(live, cot[...].astype(F32), 0.0)
    d_mid = d_out + norm_back(unit, scale, d_normed * row_of(gain))
    d_middle[...] = d_mid
    d_branch = d_mid.astype(BF16)
    d_head = dot_nt(d_branch, w_out[...]).astype(BF16)
    grads[3 * inner :, :] = dot_tn(head_out[...], d_branch).astype(BF16)
    d_query = jnp.zeros((rows, inner), F32)
    d_key = jnp.zeros((rows, inner), F32)
    d_value = jnp.zeros((rows, inner), F32)
    for head in range(heads):
        mask = head_mask(head, inner)
        chance = probs[head].astype(F32)
        d_probs = dot_nt(d_head, value[...] * mask)
        delta = jnp.sum(d_probs * chance, axis=-1, keepdims=True)
        d_scores = (chance * (d_probs - delta)).astype(BF16)
        d_value = d_value + dot_tn(probs[head], d_head * mask)
        d_query = d_query + dot_nn(d_scores, key[...] * mask)
        d_key = d_key + dot_tn(d_scores, query[...] * mask)
    d_query = (d_query * (HEAD_DIM**-0.5)).astype(BF16)
    d_key = (d_key * (HEAD_DIM**-0.5)).astype(BF16)
    d_value = d_value.astype(BF16)
    grads[:inner, :] = dot_tn(d_query, normed[...]).astype(BF16)
    grads[inner : 2 * inner, :] = dot_tn(d_key, normed[...]).astype(BF16)
    grads[2 * inner : 3 * inner, :] = dot_tn(d_value, normed[...]).astype(BF16)
    if blocks_n == 1:
        blocks[0][...] = grads[...]
    else:
        size = blocks[0].shape[0]
        for m in range(blocks_n):
            at = pl.multiple_of((ids[Q_ID] ^ m) * size, 16)
            blocks[m][...] = grads[pl.ds(at, size), :]
    d_in = dot_nn(d_query, weight[:inner])
    d_in = d_in + dot_nn(d_key, weight[inner : 2 * inner])
    whole[:rows, :] = d_in + dot_nn(d_value, weight[2 * inner :])
    half = kept.shape[1]
    kept[...] = whole[:rows, pl.ds(pl.multiple_of(ids[C_ID] * half, LANES), half)].astype(BF16)
    sent[...] = whole[:rows, pl.ds(pl.multiple_of((1 - ids[C_ID]) * half, LANES), half)].astype(BF16)


def last_norm_kernel(ids, own, other, tokens, d_middle, gain, small2, grad_tokens, small, whole):
    joined(ids, own, other, whole)
    d_normed = whole[...]
    unit, scale = norm_parts(tokens[...].astype(F32))
    small[...] = small2[...]
    small[0:1, :] = jnp.sum(d_normed * unit, axis=0, keepdims=True)
    small[1:2, :] = jnp.sum(d_normed, axis=0, keepdims=True)
    grad_tokens[...] = (
        d_middle[...] + norm_back(unit, scale, d_normed * row_of(gain))
    ).astype(BF16)


def sum_kernel(count, *refs):
    total = refs[0][...].astype(F32)
    for m in range(1, count):
        total = total + refs[m][...].astype(F32)
    refs[count][...] = total.astype(BF16)


def pair_kernel(own, came, small, small_came, out):
    size = own.shape[0]
    out[:size, :] = (own[...].astype(F32) + came[...].astype(F32)).astype(BF16)
    out[size:, :] = (small[...] + small_came[...]).astype(BF16)


def spread_kernel(masks, ids, *refs):
    count = len(masks)
    parts = refs[:count]
    grad_qkv, grad_out, gain1, bias1, gain2, bias2, router, grads, held = refs[count:]
    size = grads.shape[0] // count
    for mask, block in zip(masks, parts):
        quarter = ids[Q_ID] ^ mask
        grads[pl.ds(pl.multiple_of(quarter * size, 16), size), :] = block[:size, :].astype(F32)
        held[quarter] = block[size:, :].astype(F32)
    total = held[0]
    for quarter in range(1, count):
        total = total + held[quarter]
    for row, out in enumerate((gain1, bias1, gain2, bias2)):
        out[...] = total[row : row + 1, :].reshape(out.shape)
    router[...] = total[8 : 8 + router.shape[0], :]
    inner = grad_qkv.shape[0]
    grad_qkv[...] = grads[:inner, :]
    grad_out[...] = grads[inner:, :]


def after(value, *others):
    return lax.optimization_barrier((value,) + others)[0]


def run(kernel, outs, args, scratch=(), micros=1.0, limit=16):
    smem = pl.BlockSpec(memory_space=pltpu.SMEM)
    vmem = pl.BlockSpec(memory_space=pltpu.VMEM)
    return pl.pallas_call(
        kernel,
        out_shape=[jax.ShapeDtypeStruct(shape, kind) for shape, kind in outs],
        in_specs=[smem if arg.dtype == jnp.int32 and arg.ndim == 1 else vmem for arg in args],
        out_specs=[vmem] * len(outs),
        scratch_shapes=[pltpu.VMEM(shape, kind) for shape, kind in scratch],
        compiler_params=pltpu.CompilerParams(vmem_limit_bytes=limit * 1024 * 1024),
        cost_estimate=pl.CostEstimate(
            flops=int(micros * 1.15e9), bytes_accessed=1024, transcendentals=0
        ),
    )(*args)


def make_body(n_tensor, n_expert, n_dp):
    small_slice = n_expert == 4 and n_dp == 2

    def tensor_swap(value, mask):
        return lax.ppermute(value, "tensor", [(i, i ^ mask) for i in range(n_tensor)])

    def expert_swap(value, mask):
        return lax.ppermute(value, "expert", [(i, i ^ mask) for i in range(n_expert)])

    def dp_swap(value):
        return lax.ppermute(value, "dp", [(i, i ^ 1) for i in range(n_dp)])

    def quarter_swap(value, mask):
        pairs = [(i, i ^ mask) for i in range(n_expert * n_dp)]
        return lax.ppermute(value, ("expert", "dp"), pairs)

    def exchange(blocks):
        if small_slice:
            came = {k: expert_swap(blocks[k], k) for k in (3, 2, 1)}
            return [blocks[0]] + [came[k] for k in range(1, n_expert)]
        order = jnp.arange(n_expert) ^ lax.axis_index("expert")
        stacked = lax.all_to_all(
            jnp.stack(blocks)[order], "expert", split_axis=0, concat_axis=0, tiled=True
        )[order]
        return [stacked[k] for k in range(n_expert)]

    def body(
        tokens,
        routes,
        images_live,
        ln1_gain,
        ln1_bias,
        w_qkv,
        w_out,
        ln2_gain,
        ln2_bias,
        w_router,
        w_up,
        w_down,
        cotangent,
    ):
        rows, width = tokens.shape
        inner = w_qkv.shape[2]
        heads = inner // HEAD_DIM
        experts = w_router.shape[1]
        capacity = max(2, 3 * rows // experts // 8 * 8)
        cap = capacity // 2
        images = rows // SEQ
        half = width // 2
        hidden_width = w_up.shape[2]
        rank = lax.axis_index("tensor")
        owner = lax.axis_index("expert")
        copy = lax.axis_index("dp")
        ids = jnp.stack(
            [
                rank,
                rank % 2,
                owner,
                copy,
                (owner % 2) * 2 + copy,
                jnp.minimum(images_live[0] * SEQ, rows),
                rank,
                rank,
            ]
        ).astype(jnp.int32)
        weight = w_qkv.transpose(1, 2, 0).reshape(3 * inner, width)
        up_a, down_a = w_up[0], w_down[0]
        part_rows = max(8, -(-experts // 8) * 8)
        small_rows = 8 + part_rows
        base = -(-rows // 16) * 16
        tall = base + -(-part_rows // 16) * 16

        out_x, out_c = tensor_swap(w_out, 2), tensor_swap(w_out, 1)
        up_b, down_b = tensor_swap(up_a, 1), tensor_swap(down_a, 1)
        normed, query, key, value, probs, head_out = run(
            functools.partial(attend_kernel, images),
            [((rows, width), BF16)]
            + [((rows, inner), BF16)] * 3
            + [((heads, rows, rows), BF16), ((rows, inner), BF16)],
            [tokens, ln1_gain, ln1_bias, weight],
            micros=4,
        )
        head_out, out_x, out_c, up_b, down_b = lax.optimization_barrier(
            (head_out, out_x, out_c, up_b, down_b)
        )
        head_x, head_c = tensor_swap(head_out, 2), tensor_swap(head_out, 1)
        quarter = cap // 2
        cot_shapes = [(quarter if small_slice and k > 1 else cap, width) for k in range(experts)]
        table, part, router, *cot_blocks = run(
            functools.partial(plan_kernel, experts),
            [((experts, cap, rows), BF16), ((experts, quarter, rows), BF16)]
            + [((LANES, width), BF16)]
            + [(shape, BF16) for shape in cot_shapes],
            [ids, after(routes.T, head_out), cotangent, w_router.T],
            micros=2,
        )
        head_x = after(head_x, table)
        if small_slice:
            d_rows_in = cot_blocks[:2] + [expert_swap(cot_blocks[k], k) for k in (2, 3)]
        else:
            d_rows_in = exchange(cot_blocks)
        out_all = [w_out, out_c, out_x, tensor_swap(out_x, 1)]
        heads_all = [head_out, head_c, head_x, tensor_swap(head_x, 1)]
        middle, *row_blocks = run(
            functools.partial(middle_kernel, n_tensor, experts),
            [((rows, width), F32)] + [((cap, width), BF16)] * experts,
            [ids, tokens, ln2_gain, ln2_bias, table] + heads_all + out_all,
            scratch=[
                ((n_tensor, rows, inner), BF16),
                ((n_tensor, inner, width), BF16),
                ((rows, width), BF16),
            ],
            micros=3,
        )
        if small_slice:
            *row_blocks, far_2, far_3 = lax.optimization_barrier((*row_blocks, *d_rows_in[2:]))
            d_rows_in[2:] = [far_2, far_3]
            d_rows_in[1], middle = lax.optimization_barrier((d_rows_in[1], middle))
            d_rows_in[1] = expert_swap(d_rows_in[1], 1)
            pair_out = tensor_swap(jnp.stack([far_2, far_3]), 2)
        else:
            pair_out = router
        rows_in = exchange(list(row_blocks))

        calls = [(0, 1), (2, 3)] if small_slice else [tuple(range(experts))]
        worked = []
        d_back, gated = [], []
        for number, call in enumerate(calls):
            if number == 1:
                router, d_back[1] = lax.optimization_barrier((router, d_back[1]))
            count = cap * len(call)
            last = number == len(calls) - 1
            grads = [] if last else [((2 * width, hidden_width), BF16)] * 2
            results = run(
                functools.partial(expert_kernel, experts, call, not last),
                [((cap, width), BF16)] * len(call)
                + [((len(call), quarter if worked else cap, width), BF16)] * 2
                + [((count, width), BF16)] * 2
                + [((count, hidden_width), BF16)] * 4
                + [((part_rows, width), F32)]
                + grads,
                [ids, up_a, up_b, down_a, down_b]
                + [router]
                + [rows_in[k] for k in call]
                + [d_rows_in[k] for k in call]
                + [pair_out if worked or not small_slice else router],
                scratch=[((count, width), F32)],
                micros=0.05,
                limit=24,
            )
            d_back += results[: len(call)]
            gated.append(results[len(call) : len(call) + 2])
            worked.append(results[len(call) + 2 :])

        order = [0] + list(range(experts - 1, 0, -1))

        def combine(blocks, routers):
            blocks = [blocks[k] for k in order]
            return run(
                functools.partial(combine_kernel, order, len(routers), base),
                [((tall if routers else base, half), BF16)] * 2,
                [ids, table, part] + blocks + routers,
                scratch=[((tall if routers else base, width), F32)],
                micros=2,
            )

        if small_slice:
            d_back[1], d_back[2] = lax.optimization_barrier((d_back[1], d_back[2]))
        d_home = exchange(d_back)

        grad_own, grad_pair = run(
            weight_grad_kernel,
            [((2 * width, hidden_width), BF16)] * 2,
            [worked[-1][at] for at in (0, 4, 5, 2, 3, 1)] + list(worked[0][7:]),
            micros=4,
            limit=24,
        )
        sixth = width // 96 * 16
        grad_kept, sent_first, sent_next, sent_rest = run(
            split_grad_kernel,
            [((width, width), F32)]
            + [((sixth, width), BF16)] * 2
            + [((width - 2 * sixth, width), BF16)],
            [ids, grad_own, tensor_swap(grad_pair, 1)],
            scratch=[((2 * width, width), F32), ((width, width), BF16)],
            micros=2,
            limit=24,
        )

        if small_slice:
            far_blocks = run(
                gated_sum_kernel,
                [((quarter, width), BF16)] * 2,
                [gated[1][0], tensor_swap(gated[1][1], 2)],
            )
            gated_blocks = [gated[0][0][0], gated[0][0][1], *far_blocks]
        else:
            gated_blocks = [gated[0][0][k] for k in range(experts)]

        came_first, came_next = dp_swap(sent_first), dp_swap(sent_next)
        *gated_blocks, came_first, came_next = lax.optimization_barrier(
            (*d_home[::-1], *gated_blocks, came_first, came_next)
        )
        d_home, gated_blocks = gated_blocks[:experts][::-1], gated_blocks[experts:]
        kept, sent = combine(list(d_home), [one[6] for one in worked])
        chip = (kept.astype(F32) + tensor_swap(sent, 1).astype(F32)).astype(BF16)
        own = (chip.astype(F32) + tensor_swap(chip, 2).astype(F32)).astype(BF16)
        if small_slice:
            home = {k: expert_swap(gated_blocks[k], k) for k in (2, 3, 1)}
            gated_home = [gated_blocks[0], home[1], home[2], home[3]]
        else:
            gated_home = exchange(list(gated_blocks))
        own, *gated_home = lax.optimization_barrier((own, *gated_home))
        other = tensor_swap(own, 1)

        parts = 4 if small_slice else 1
        d_middle, kept1, sent1, small2, *grad_blocks = run(
            functools.partial(back_kernel, parts),
            [((rows, width), F32)]
            + [((rows, half), BF16)] * 2
            + [((small_rows, width), F32)]
            + [((4 * inner // parts, width), BF16)] * parts,
            [
                ids, own, other, middle, cotangent, ln2_gain, w_out, head_out, normed, query,
                key, value, probs, weight,
            ],
            scratch=[((tall, width), F32), ((4 * inner, width), BF16)],
            micros=6,
        )

        *gated_home, _ = lax.optimization_barrier((*gated_home, d_middle))
        kept_y, sent_y = combine(list(gated_home), [])

        chip1 = (kept1.astype(F32) + tensor_swap(sent1, 1).astype(F32)).astype(BF16)
        own1 = (chip1.astype(F32) + tensor_swap(chip1, 2).astype(F32)).astype(BF16)
        if small_slice:
            arrived = [grad_blocks[0]] + [quarter_swap(grad_blocks[m], m) for m in (3, 1, 2)]
            arrived[0], kept_y, sent_y = lax.optimization_barrier((arrived[0], kept_y, sent_y))
            size = grad_blocks[0].shape[0]
            (summed,) = run(
                functools.partial(sum_kernel, 4), [((size, width), BF16)], arrived, micros=0.5
            )
            sent_rest, own1 = lax.optimization_barrier((sent_rest, own1, summed))[:2]
        other1 = tensor_swap(own1, 1)
        grad_tokens, small = run(
            last_norm_kernel,
            [((rows, width), BF16), ((small_rows, width), F32)],
            [ids, own1, other1, tokens, d_middle, ln1_gain, small2],
            scratch=[((rows, width), F32)],
            micros=0.01,
        )
        chip_y = (kept_y.astype(F32) + tensor_swap(sent_y, 1).astype(F32)).astype(BF16)
        own_y = (chip_y.astype(F32) + tensor_swap(chip_y, 2).astype(F32)).astype(BF16)
        grad_up, grad_down = run(
            join_grad_kernel,
            [((half, hidden_width), F32), ((hidden_width, half), F32)],
            [grad_kept, came_first, came_next, dp_swap(sent_rest)],
            scratch=[((width, width), BF16)],
            micros=2,
        )
        if small_slice:
            (ready,) = run(
                pair_kernel,
                [((size + small_rows, width), BF16)],
                [summed, expert_swap(summed, 2), small, expert_swap(small, 2)],
                micros=1,
            )
            own_y, ready = lax.optimization_barrier((own_y, ready))
            everything = [quarter_swap(ready, m) for m in (3, 1, 2)]
            ready, grad_up, grad_down = lax.optimization_barrier((ready, grad_up, grad_down))
            everything = [ready] + everything
            grad_qkv, grad_out, *sums, grad_router = run(
                functools.partial(spread_kernel, (0, 3, 1, 2)),
                [((3 * inner, width), F32), ((inner, width), F32)]
                + [((width,), F32)] * 4
                + [((experts, width), F32)],
                [ids] + everything,
                scratch=[((4 * inner, width), F32), ((4, small_rows, width), F32)],
                micros=3,
            )
        else:
            grads = lax.psum(grad_blocks[0], ("expert", "dp")).astype(F32)
            grad_qkv, grad_out = grads[: 3 * inner], grads[3 * inner :]
            small_sum = lax.psum(small, ("expert", "dp"))
            sums, grad_router = list(small_sum[:4]), small_sum[8 : 8 + experts]

        mix_own, mix_other = own_y, tensor_swap(own_y, 1)
        mixture = jnp.where(
            rank % 2 == 0,
            jnp.concatenate([mix_own, mix_other], axis=1),
            jnp.concatenate([mix_other, mix_own], axis=1),
        )[:rows].astype(F32)
        alive = (jnp.arange(rows, dtype=jnp.int32) < images_live[0] * SEQ)[:, None]
        out = jnp.where(alive, middle + mixture, 0.0).astype(BF16)
        return (
            out,
            grad_tokens,
            sums[0],
            sums[1],
            grad_qkv.reshape(3, inner, width).transpose(2, 0, 1),
            grad_out,
            sums[2],
            sums[3],
            grad_router.T,
            grad_up[None],
            grad_down[None],
        )

    return body


def solution(mesh):
    in_specs = (
        P(("expert", "dp"), None),
        P(("expert", "dp"), None),
        P(("expert", "dp")),
        P(),
        P(),
        P(None, None, "tensor"),
        P("tensor", None),
        P(),
        P(),
        P(),
        P("expert", None, "tensor"),
        P("expert", "tensor", None),
        P(("expert", "dp"), None),
    )
    out_specs = (
        P(("expert", "dp"), None),
        P(("expert", "dp"), None),
        P(),
        P(),
        P(None, None, "tensor"),
        P("tensor", None),
        P(),
        P(),
        P(),
        P("expert", "dp", "tensor"),
        P("expert", "tensor", "dp"),
    )
    body = make_body(mesh.shape["tensor"], mesh.shape["expert"], mesh.shape["dp"])
    return jax.shard_map(body, mesh=mesh, in_specs=in_specs, out_specs=out_specs, check_vma=False)
```

```python
import functools

import jax
import jax.numpy as jnp
from jax import lax
from jax.experimental import pallas as pl
from jax.experimental.pallas import tpu as pltpu
from jax.sharding import PartitionSpec as P

HEAD_DIM = 64
SEQ = 197
EPSILON = 1e-06
F32 = jnp.float32
BF16 = jnp.bfloat16
LANES = 128
SMALL = 16


def dot_nn(left, right):
    return lax.dot_general(left, right, (((1,), (0,)), ((), ())), preferred_element_type=F32)


def dot_tn(left, right):
    return lax.dot_general(left, right, (((0,), (0,)), ((), ())), preferred_element_type=F32)


def dot_nt(left, right):
    return lax.dot_general(left, right, (((1,), (1,)), ((), ())), preferred_element_type=F32)


def norm_parts(values_in):
    row_mean = jnp.mean(values_in, axis=-1, keepdims=True)
    centred = values_in - row_mean
    variance = jnp.mean(centred * centred, axis=-1, keepdims=True)
    scale = lax.rsqrt(variance + EPSILON)
    return centred * scale, scale


def norm_back(normed, scale, u):
    return scale * (
        u
        - jnp.mean(u, axis=-1, keepdims=True)
        - normed * jnp.mean(u * normed, axis=-1, keepdims=True)
    )


def iota(shape, dim):
    return lax.broadcasted_iota(jnp.int32, shape, dim)


def row_of(vector):
    return vector[...].reshape(1, vector.shape[0])


def head_mask(head, width):
    lane = iota((1, width), 1)
    return ((lane >= head * HEAD_DIM) & (lane < (head + 1) * HEAD_DIM)).astype(BF16)


def image_of(shape, dim, images):
    at = iota(shape, dim)
    image = jnp.zeros(shape, jnp.int32)
    for number in range(1, images):
        image = image + (at >= number * SEQ).astype(jnp.int32)
    return image


T_ID, C_ID, E_ID, D_ID, Q_ID, L_ID = range(6)


def plan_kernel(experts, ids, routes, cot, router, table, part, router_pad, *blocks):
    rows = cot.shape[0]
    cap = table.shape[1]
    tall = max(16, -(-experts // 16) * 16)
    picks = routes[...]
    expert = iota((tall, rows), 0)
    named = picks[0:1, :] == expert
    for k in range(1, picks.shape[0]):
        named = named | (picks[k : k + 1, :] == expert)
    named = named & (iota((tall, rows), 1) < ids[L_ID])
    marks = jnp.where(named, 1.0, 0.0).astype(BF16)
    earlier = jnp.where(iota((rows, rows), 0) < iota((rows, rows), 1), 1.0, 0.0).astype(BF16)
    slot = dot_nn(marks, earlier)
    first = (ids[C_ID] * cap).astype(F32)
    slot = jnp.where(named, slot - first, -1.0)
    place = iota((cap, rows), 0).astype(F32)
    for x in range(experts):
        table[x] = jnp.where(slot[x : x + 1, :] == place, 1.0, 0.0).astype(BF16)
    quarter = part.shape[1]
    first = ((ids[T_ID] // 2) * quarter).astype(F32)
    place = iota((quarter, rows), 0).astype(F32) + first
    for x in range(experts):
        part[x] = jnp.where(slot[x : x + 1, :] == place, 1.0, 0.0).astype(BF16)
    for k in range(experts):
        source = table if blocks[k].shape[0] == cap else part
        blocks[k][...] = dot_nn(source[ids[E_ID] ^ k], cot[...]).astype(BF16)
    router_pad[...] = jnp.zeros_like(router_pad)
    router_pad[:experts, :] = router[...]


def attend_kernel(images, tokens, gain, bias, weight, normed, query, key, value, probs, head_out):
    rows = tokens.shape[0]
    inner = query.shape[1]
    heads = inner // HEAD_DIM
    unit, _ = norm_parts(tokens[...].astype(F32))
    normed[...] = (unit * row_of(gain) + row_of(bias)).astype(BF16)
    query[...] = dot_nt(normed[...], weight[:inner]).astype(BF16)
    key[...] = dot_nt(normed[...], weight[inner : 2 * inner]).astype(BF16)
    value[...] = dot_nt(normed[...], weight[2 * inner :]).astype(BF16)
    same = image_of((rows, 1), 0, images) == image_of((1, rows), 1, images)
    total = jnp.zeros((rows, inner), F32)
    for head in range(heads):
        mask = head_mask(head, inner)
        scores = dot_nt(query[...] * mask, key[...]) * (HEAD_DIM**-0.5)
        scores = jnp.where(same, scores, -1e30)
        top = jnp.max(scores, axis=-1, keepdims=True)
        weights = jnp.exp(scores - top)
        weights = weights * (1.0 / jnp.sum(weights, axis=-1, keepdims=True))
        probs[head] = weights.astype(BF16)
        total = total + dot_nn(probs[head], value[...] * mask)
    head_out[...] = total.astype(BF16)


def middle_kernel(
    n_tensor, experts, ids, tokens, gain, bias, table, *rest
):
    heads = rest[:n_tensor]
    weights = rest[n_tensor : 2 * n_tensor]
    middle = rest[2 * n_tensor]
    blocks = rest[2 * n_tensor + 1 : 2 * n_tensor + 1 + experts]
    held_heads, held_weights, low = rest[2 * n_tensor + 1 + experts :]
    for j in range(n_tensor):
        held_heads[j] = heads[j][...]
        held_weights[j] = weights[j][...]
    total = tokens[...].astype(F32)
    for rank in range(n_tensor):
        place = ids[T_ID] ^ rank
        total = total + dot_nn(held_heads[place], held_weights[place])
    middle[...] = total
    unit, _ = norm_parts(total)
    low[...] = (unit * row_of(gain) + row_of(bias)).astype(BF16)
    for k in range(experts):
        blocks[k][...] = dot_nn(table[ids[E_ID] ^ k], low[...]).astype(BF16)


def expert_kernel(
    experts, places, with_grads, ids, up_a, up_b, down_a, down_b, router, *refs
):
    number = len(places)
    row_blocks, out_blocks = refs[:number], refs[number : 2 * number]
    pair_out = refs[2 * number]
    refs = refs[2 * number + 1 :]
    back_blocks, gated_kept, gated_sent = refs[:number], refs[number], refs[number + 1]
    refs = refs[number + 2 :]
    rows_in, d_result, hidden_a, hidden_b, d_pre_a, d_pre_b, router_part = refs[:7]
    d_out = refs[-1]
    size = row_blocks[0].shape[0]
    count = size * number
    far = ids[T_ID] // 2
    for k in range(number):
        rows_in[k * size : (k + 1) * size, :] = row_blocks[k][...]
        quarter = out_blocks[k].shape[0]
        if quarter == size:
            d_out[k * size : (k + 1) * size, :] = out_blocks[k][...].astype(F32)
        else:
            here = pl.multiple_of(k * size + far * quarter, 8)
            there = pl.multiple_of(k * size + (1 - far) * quarter, 8)
            d_out[pl.ds(here, quarter), :] = out_blocks[k][...].astype(F32)
            d_out[pl.ds(there, quarter), :] = pair_out[places[k] - 2].astype(F32)
    lane = iota((count, LANES), 1)
    logits = dot_nt(rows_in[...], router[...])
    logits = jnp.where(lane < experts, logits, -1e30)
    top = jnp.max(logits, axis=-1, keepdims=True)
    odds = jnp.exp(logits - top)
    odds = odds / jnp.sum(odds, axis=-1, keepdims=True)
    mine = (lane == ids[E_ID]).astype(F32)
    gate = jnp.sum(odds * mine, axis=-1, keepdims=True)
    d_result[...] = (gate * d_out[...]).astype(BF16)
    result = jnp.zeros(d_out.shape, F32)
    back = jnp.zeros(d_out.shape, F32)
    scale = 0.7978845608028654
    for up, down, hidden, d_pre in (
        (up_a, down_a, hidden_a, d_pre_a),
        (up_b, down_b, hidden_b, d_pre_b),
    ):
        act = dot_nn(rows_in[...], up[...])
        square = act * act
        bend = jnp.tanh(scale * act * (1.0 + 0.044715 * square))
        half = 0.5 * (1.0 + bend)
        hidden[...] = (act * half).astype(BF16)
        slope = half + 0.5 * act * (1.0 - bend * bend) * (
            scale * (1.0 + 3 * 0.044715 * square)
        )
        result = result + dot_nn(hidden[...], down[...])
        d_pre[...] = (dot_nt(d_result[...], down[...]) * slope).astype(BF16)
        back = back + dot_nt(d_pre[...], up[...])
    d_gate = jnp.sum(d_out[...] * result, axis=-1, keepdims=True)
    d_logits = (d_gate * gate * (mine - odds)).astype(BF16)
    back = (back + dot_nn(d_logits, router[...])).astype(BF16)
    for k in range(number):
        back_blocks[k][...] = back[k * size : (k + 1) * size, :]
    d_out[...] = gate * result
    quarter = gated_kept.shape[1]
    for k in range(number):
        if quarter == size:
            gated_kept[k] = d_out[k * size : (k + 1) * size, :].astype(BF16)
        else:
            here = pl.multiple_of(k * size + far * quarter, 8)
            there = pl.multiple_of(k * size + (1 - far) * quarter, 8)
            gated_kept[k] = d_out[pl.ds(here, quarter), :].astype(BF16)
            gated_sent[k] = d_out[pl.ds(there, quarter), :].astype(BF16)
    if quarter == size:
        gated_sent[...] = jnp.zeros_like(gated_sent)
    router_part[...] = dot_tn(d_logits, rows_in[...])[: router_part.shape[0]]
    if with_grads:
        own, pair = refs[7:9]
        weight_grads(rows_in, d_pre_a, d_pre_b, hidden_a, hidden_b, d_result, None, None, own, pair)


def weight_grads(
    rows, d_pre_a, d_pre_b, hidden_a, hidden_b, d_result, own_before, pair_before, own, pair
):
    width = own.shape[0] // 2
    for out, before, at, left, right in (
        (pair, pair_before, 0, rows, d_pre_b),
        (pair, pair_before, width, hidden_b, d_result),
        (own, own_before, 0, rows, d_pre_a),
        (own, own_before, width, hidden_a, d_result),
    ):
        total = dot_tn(left[...], right[...])
        if before is not None:
            total = total + before[at : at + width, :].astype(F32)
        out[at : at + width, :] = total.astype(BF16)


def gated_sum_kernel(kept, came, *blocks):
    for k, out in enumerate(blocks):
        out[...] = (kept[k].astype(F32) + came[k].astype(F32)).astype(BF16)


def weight_grad_kernel(*refs):
    rows, d_pre_a, d_pre_b, hidden_a, hidden_b, d_result = refs[:6]
    own_before, pair_before = refs[6:8] if len(refs) == 10 else (None, None)
    weight_grads(
        rows, d_pre_a, d_pre_b, hidden_a, hidden_b, d_result, own_before, pair_before, *refs[-2:]
    )


def split_grad_kernel(ids, own, came, kept, sent_first, sent_next, sent_rest, total, sent):
    total[...] = own[...].astype(F32) + came[...].astype(F32)
    width = own.shape[1]
    half = width // 2
    mine, other = ids[D_ID], 1 - ids[D_ID]
    kept[:half, :] = total[pl.ds(pl.multiple_of(mine * half, 16), half), :]
    sent[:half, :] = total[pl.ds(pl.multiple_of(other * half, 16), half), :].astype(BF16)
    column = pl.ds(pl.multiple_of(mine * half, LANES), half)
    kept[half:, :half] = total[width : width + half, column]
    kept[half:, half:] = total[width + half :, column]
    column = pl.ds(pl.multiple_of(other * half, LANES), half)
    sent[half:, :half] = total[width : width + half, column].astype(BF16)
    sent[half:, half:] = total[width + half :, column].astype(BF16)
    first = sent_first.shape[0]
    sent_first[...] = sent[:first, :]
    sent_next[...] = sent[first : 2 * first, :]
    sent_rest[...] = sent[2 * first :, :]


def join_grad_kernel(kept, came_first, came_next, came_rest, grad_up, grad_down, came):
    first = came_first.shape[0]
    came[:first, :] = came_first[...]
    came[first : 2 * first, :] = came_next[...]
    came[2 * first :, :] = came_rest[...]
    half = kept.shape[1] // 2
    grad_up[...] = kept[:half, :] + came[:half, :].astype(F32)
    grad_down[:half, :] = kept[half:, :half] + came[half:, :half].astype(F32)
    grad_down[half:, :] = kept[half:, half:] + came[half:, half:].astype(F32)


def combine_kernel(order, parts, base, ids, table, part, *refs):
    experts = len(order)
    blocks = refs[:experts]
    routers = refs[experts : experts + parts]
    kept, sent, total = refs[experts + parts :]
    value = dot_tn(table[ids[E_ID]], blocks[0][...])
    for block, k in zip(blocks[1:], order[1:]):
        spots = table if block.shape[0] == table.shape[1] else part
        value = value + dot_tn(spots[ids[E_ID] ^ k], block[...])
    total[...] = jnp.zeros_like(total)
    total[: value.shape[0], :] = value
    if parts:
        added = routers[0][...]
        for k in range(1, parts):
            added = added + routers[k][...]
        total[base : base + added.shape[0], :] = added
    half = kept.shape[1]
    kept[...] = total[:, pl.ds(pl.multiple_of(ids[C_ID] * half, LANES), half)].astype(BF16)
    sent[...] = total[:, pl.ds(pl.multiple_of((1 - ids[C_ID]) * half, LANES), half)].astype(BF16)


def joined(ids, own, other, whole):
    half = own.shape[1]
    whole[:, pl.ds(pl.multiple_of(ids[C_ID] * half, LANES), half)] = own[...].astype(F32)
    whole[:, pl.ds(pl.multiple_of((1 - ids[C_ID]) * half, LANES), half)] = other[...].astype(F32)


def back_kernel(
    blocks_n, ids, own, other, middle, cot, gain, w_out, head_out, normed, query, key, value,
    probs, weight, *rest
):
    d_middle, kept, sent, small = rest[:4]
    blocks = rest[4 : 4 + blocks_n]
    whole, grads = rest[4 + blocks_n :]
    rows, inner = query.shape
    heads = inner // HEAD_DIM
    joined(ids, own, other, whole)
    d_normed = whole[:rows, :]
    unit, scale = norm_parts(middle[...])
    small[...] = jnp.zeros_like(small)
    base = -(-rows // 16) * 16
    small[8:, :] = whole[base : base + small.shape[0] - 8, :]
    small[2:3, :] = jnp.sum(d_normed * unit, axis=0, keepdims=True)
    small[3:4, :] = jnp.sum(d_normed, axis=0, keepdims=True)
    live = iota((rows, 1), 0) < ids[L_ID]
    d_out = jnp.where(live, cot[...].astype(F32), 0.0)
    d_mid = d_out + norm_back(unit, scale, d_normed * row_of(gain))
    d_middle[...] = d_mid
    d_branch = d_mid.astype(BF16)
    d_head = dot_nt(d_branch, w_out[...]).astype(BF16)
    grads[3 * inner :, :] = dot_tn(head_out[...], d_branch).astype(BF16)
    d_query = jnp.zeros((rows, inner), F32)
    d_key = jnp.zeros((rows, inner), F32)
    d_value = jnp.zeros((rows, inner), F32)
    for head in range(heads):
        mask = head_mask(head, inner)
        chance = probs[head].astype(F32)
        d_probs = dot_nt(d_head, value[...] * mask)
        delta = jnp.sum(d_probs * chance, axis=-1, keepdims=True)
        d_scores = (chance * (d_probs - delta)).astype(BF16)
        d_value = d_value + dot_tn(probs[head], d_head * mask)
        d_query = d_query + dot_nn(d_scores, key[...] * mask)
        d_key = d_key + dot_tn(d_scores, query[...] * mask)
    d_query = (d_query * (HEAD_DIM**-0.5)).astype(BF16)
    d_key = (d_key * (HEAD_DIM**-0.5)).astype(BF16)
    d_value = d_value.astype(BF16)
    grads[:inner, :] = dot_tn(d_query, normed[...]).astype(BF16)
    grads[inner : 2 * inner, :] = dot_tn(d_key, normed[...]).astype(BF16)
    grads[2 * inner : 3 * inner, :] = dot_tn(d_value, normed[...]).astype(BF16)
    if blocks_n == 1:
        blocks[0][...] = grads[...]
    else:
        size = blocks[0].shape[0]
        for m in range(blocks_n):
            at = pl.multiple_of((ids[Q_ID] ^ m) * size, 16)
            blocks[m][...] = grads[pl.ds(at, size), :]
    d_in = dot_nn(d_query, weight[:inner])
    d_in = d_in + dot_nn(d_key, weight[inner : 2 * inner])
    whole[:rows, :] = d_in + dot_nn(d_value, weight[2 * inner :])
    half = kept.shape[1]
    kept[...] = whole[:rows, pl.ds(pl.multiple_of(ids[C_ID] * half, LANES), half)].astype(BF16)
    sent[...] = whole[:rows, pl.ds(pl.multiple_of((1 - ids[C_ID]) * half, LANES), half)].astype(BF16)


def last_norm_kernel(ids, own, other, tokens, d_middle, gain, small2, grad_tokens, small, whole):
    joined(ids, own, other, whole)
    d_normed = whole[...]
    unit, scale = norm_parts(tokens[...].astype(F32))
    small[...] = small2[...]
    small[0:1, :] = jnp.sum(d_normed * unit, axis=0, keepdims=True)
    small[1:2, :] = jnp.sum(d_normed, axis=0, keepdims=True)
    grad_tokens[...] = (
        d_middle[...] + norm_back(unit, scale, d_normed * row_of(gain))
    ).astype(BF16)


def sum_kernel(count, *refs):
    total = refs[0][...].astype(F32)
    for m in range(1, count):
        total = total + refs[m][...].astype(F32)
    refs[count][...] = total.astype(BF16)


def pair_kernel(own, came, small, small_came, out):
    size = own.shape[0]
    out[:size, :] = (own[...].astype(F32) + came[...].astype(F32)).astype(BF16)
    out[size:, :] = (small[...] + small_came[...]).astype(BF16)


def spread_kernel(masks, ids, *refs):
    count = len(masks)
    parts = refs[:count]
    grad_qkv, grad_out, gain1, bias1, gain2, bias2, router, grads, held = refs[count:]
    size = grads.shape[0] // count
    for mask, block in zip(masks, parts):
        quarter = ids[Q_ID] ^ mask
        grads[pl.ds(pl.multiple_of(quarter * size, 16), size), :] = block[:size, :].astype(F32)
        held[quarter] = block[size:, :].astype(F32)
    total = held[0]
    for quarter in range(1, count):
        total = total + held[quarter]
    for row, out in enumerate((gain1, bias1, gain2, bias2)):
        out[...] = total[row : row + 1, :].reshape(out.shape)
    router[...] = total[8 : 8 + router.shape[0], :]
    inner = grad_qkv.shape[0]
    grad_qkv[...] = grads[:inner, :]
    grad_out[...] = grads[inner:, :]


def after(value, *others):
    return lax.optimization_barrier((value,) + others)[0]


def run(kernel, outs, args, scratch=(), micros=1.0, limit=16):
    smem = pl.BlockSpec(memory_space=pltpu.SMEM)
    vmem = pl.BlockSpec(memory_space=pltpu.VMEM)
    return pl.pallas_call(
        kernel,
        out_shape=[jax.ShapeDtypeStruct(shape, kind) for shape, kind in outs],
        in_specs=[smem if arg.dtype == jnp.int32 and arg.ndim == 1 else vmem for arg in args],
        out_specs=[vmem] * len(outs),
        scratch_shapes=[pltpu.VMEM(shape, kind) for shape, kind in scratch],
        compiler_params=pltpu.CompilerParams(vmem_limit_bytes=limit * 1024 * 1024),
        cost_estimate=pl.CostEstimate(
            flops=int(micros * 1.15e9), bytes_accessed=1024, transcendentals=0
        ),
    )(*args)


def make_body(n_tensor, n_expert, n_dp):
    small_slice = n_expert == 4 and n_dp == 2

    def tensor_swap(value, mask):
        return lax.ppermute(value, "tensor", [(i, i ^ mask) for i in range(n_tensor)])

    def expert_swap(value, mask):
        return lax.ppermute(value, "expert", [(i, i ^ mask) for i in range(n_expert)])

    def dp_swap(value):
        return lax.ppermute(value, "dp", [(i, i ^ 1) for i in range(n_dp)])

    def quarter_swap(value, mask):
        pairs = [(i, i ^ mask) for i in range(n_expert * n_dp)]
        return lax.ppermute(value, ("expert", "dp"), pairs)

    def exchange(blocks):
        if small_slice:
            came = {k: expert_swap(blocks[k], k) for k in (3, 2, 1)}
            return [blocks[0]] + [came[k] for k in range(1, n_expert)]
        order = jnp.arange(n_expert) ^ lax.axis_index("expert")
        stacked = lax.all_to_all(
            jnp.stack(blocks)[order], "expert", split_axis=0, concat_axis=0, tiled=True
        )[order]
        return [stacked[k] for k in range(n_expert)]

    def body(
        tokens,
        routes,
        images_live,
        ln1_gain,
        ln1_bias,
        w_qkv,
        w_out,
        ln2_gain,
        ln2_bias,
        w_router,
        w_up,
        w_down,
        cotangent,
    ):
        rows, width = tokens.shape
        inner = w_qkv.shape[2]
        heads = inner // HEAD_DIM
        experts = w_router.shape[1]
        capacity = max(2, 3 * rows // experts // 8 * 8)
        cap = capacity // 2
        images = rows // SEQ
        half = width // 2
        hidden_width = w_up.shape[2]
        rank = lax.axis_index("tensor")
        owner = lax.axis_index("expert")
        copy = lax.axis_index("dp")
        ids = jnp.stack(
            [
                rank,
                rank % 2,
                owner,
                copy,
                (owner % 2) * 2 + copy,
                jnp.minimum(images_live[0] * SEQ, rows),
                rank,
                rank,
            ]
        ).astype(jnp.int32)
        weight = w_qkv.transpose(1, 2, 0).reshape(3 * inner, width)
        up_a, down_a = w_up[0], w_down[0]
        part_rows = max(8, -(-experts // 8) * 8)
        small_rows = 8 + part_rows
        base = -(-rows // 16) * 16
        tall = base + -(-part_rows // 16) * 16

        out_x, out_c = tensor_swap(w_out, 2), tensor_swap(w_out, 1)
        up_b, down_b = tensor_swap(up_a, 1), tensor_swap(down_a, 1)
        normed, query, key, value, probs, head_out = run(
            functools.partial(attend_kernel, images),
            [((rows, width), BF16)]
            + [((rows, inner), BF16)] * 3
            + [((heads, rows, rows), BF16), ((rows, inner), BF16)],
            [tokens, ln1_gain, ln1_bias, weight],
            micros=4,
        )
        head_out, out_x, out_c, up_b, down_b = lax.optimization_barrier(
            (head_out, out_x, out_c, up_b, down_b)
        )
        head_x, head_c = tensor_swap(head_out, 2), tensor_swap(head_out, 1)
        quarter = cap // 2
        cot_shapes = [(quarter if small_slice and k > 1 else cap, width) for k in range(experts)]
        table, part, router, *cot_blocks = run(
            functools.partial(plan_kernel, experts),
            [((experts, cap, rows), BF16), ((experts, quarter, rows), BF16)]
            + [((LANES, width), BF16)]
            + [(shape, BF16) for shape in cot_shapes],
            [ids, after(routes.T, head_out), cotangent, w_router.T],
            micros=2,
        )
        head_x = after(head_x, table)
        if small_slice:
            d_rows_in = cot_blocks[:2] + [expert_swap(cot_blocks[k], k) for k in (2, 3)]
        else:
            d_rows_in = exchange(cot_blocks)
        out_all = [w_out, out_c, out_x, tensor_swap(out_x, 1)]
        heads_all = [head_out, head_c, head_x, tensor_swap(head_x, 1)]
        middle, *row_blocks = run(
            functools.partial(middle_kernel, n_tensor, experts),
            [((rows, width), F32)] + [((cap, width), BF16)] * experts,
            [ids, tokens, ln2_gain, ln2_bias, table] + heads_all + out_all,
            scratch=[
                ((n_tensor, rows, inner), BF16),
                ((n_tensor, inner, width), BF16),
                ((rows, width), BF16),
            ],
            micros=3,
        )
        if small_slice:
            *row_blocks, far_2, far_3 = lax.optimization_barrier((*row_blocks, *d_rows_in[2:]))
            d_rows_in[2:] = [far_2, far_3]
            d_rows_in[1], middle = lax.optimization_barrier((d_rows_in[1], middle))
            d_rows_in[1] = expert_swap(d_rows_in[1], 1)
            pair_out = tensor_swap(jnp.stack([far_2, far_3]), 2)
        else:
            pair_out = router
        rows_in = exchange(list(row_blocks))

        calls = [(0, 1), (2, 3)] if small_slice else [tuple(range(experts))]
        worked = []
        d_back, gated = [], []
        for number, call in enumerate(calls):
            if number == 1:
                router, d_back[1] = lax.optimization_barrier((router, d_back[1]))
            count = cap * len(call)
            last = number == len(calls) - 1
            grads = [] if last else [((2 * width, hidden_width), BF16)] * 2
            results = run(
                functools.partial(expert_kernel, experts, call, not last),
                [((cap, width), BF16)] * len(call)
                + [((len(call), quarter if worked else cap, width), BF16)] * 2
                + [((count, width), BF16)] * 2
                + [((count, hidden_width), BF16)] * 4
                + [((part_rows, width), F32)]
                + grads,
                [ids, up_a, up_b, down_a, down_b]
                + [router]
                + [rows_in[k] for k in call]
                + [d_rows_in[k] for k in call]
                + [pair_out if worked or not small_slice else router],
                scratch=[((count, width), F32)],
                micros=0.05,
                limit=24,
            )
            d_back += results[: len(call)]
            gated.append(results[len(call) : len(call) + 2])
            worked.append(results[len(call) + 2 :])

        order = [0] + list(range(experts - 1, 0, -1))

        def combine(blocks, routers):
            blocks = [blocks[k] for k in order]
            return run(
                functools.partial(combine_kernel, order, len(routers), base),
                [((tall if routers else base, half), BF16)] * 2,
                [ids, table, part] + blocks + routers,
                scratch=[((tall if routers else base, width), F32)],
                micros=2,
            )

        if small_slice:
            d_back[1], d_back[2] = lax.optimization_barrier((d_back[1], d_back[2]))
        d_home = exchange(d_back)

        grad_own, grad_pair = run(
            weight_grad_kernel,
            [((2 * width, hidden_width), BF16)] * 2,
            [worked[-1][at] for at in (0, 4, 5, 2, 3, 1)] + list(worked[0][7:]),
            micros=4,
            limit=24,
        )
        sixth = width // 96 * 16
        grad_kept, sent_first, sent_next, sent_rest = run(
            split_grad_kernel,
            [((width, width), F32)]
            + [((sixth, width), BF16)] * 2
            + [((width - 2 * sixth, width), BF16)],
            [ids, grad_own, tensor_swap(grad_pair, 1)],
            scratch=[((2 * width, width), F32), ((width, width), BF16)],
            micros=2,
            limit=24,
        )

        if small_slice:
            far_blocks = run(
                gated_sum_kernel,
                [((quarter, width), BF16)] * 2,
                [gated[1][0], tensor_swap(gated[1][1], 2)],
            )
            gated_blocks = [gated[0][0][0], gated[0][0][1], *far_blocks]
        else:
            gated_blocks = [gated[0][0][k] for k in range(experts)]

        came_first, came_next = dp_swap(sent_first), dp_swap(sent_next)
        *gated_blocks, came_first, came_next = lax.optimization_barrier(
            (*d_home[::-1], *gated_blocks, came_first, came_next)
        )
        d_home, gated_blocks = gated_blocks[:experts][::-1], gated_blocks[experts:]
        kept, sent = combine(list(d_home), [one[6] for one in worked])
        chip = (kept.astype(F32) + tensor_swap(sent, 1).astype(F32)).astype(BF16)
        own = (chip.astype(F32) + tensor_swap(chip, 2).astype(F32)).astype(BF16)
        if small_slice:
            home = {k: expert_swap(gated_blocks[k], k) for k in (2, 3, 1)}
            gated_home = [gated_blocks[0], home[1], home[2], home[3]]
        else:
            gated_home = exchange(list(gated_blocks))
        own, *gated_home = lax.optimization_barrier((own, *gated_home))
        other = tensor_swap(own, 1)

        parts = 4 if small_slice else 1
        d_middle, kept1, sent1, small2, *grad_blocks = run(
            functools.partial(back_kernel, parts),
            [((rows, width), F32)]
            + [((rows, half), BF16)] * 2
            + [((small_rows, width), F32)]
            + [((4 * inner // parts, width), BF16)] * parts,
            [
                ids, own, other, middle, cotangent, ln2_gain, w_out, head_out, normed, query,
                key, value, probs, weight,
            ],
            scratch=[((tall, width), F32), ((4 * inner, width), BF16)],
            micros=6,
        )

        *gated_home, _ = lax.optimization_barrier((*gated_home, d_middle))
        kept_y, sent_y = combine(list(gated_home), [])

        chip1 = (kept1.astype(F32) + tensor_swap(sent1, 1).astype(F32)).astype(BF16)
        own1 = (chip1.astype(F32) + tensor_swap(chip1, 2).astype(F32)).astype(BF16)
        if small_slice:
            arrived = [grad_blocks[0]] + [quarter_swap(grad_blocks[m], m) for m in (3, 1, 2)]
            arrived[0], kept_y, sent_y = lax.optimization_barrier((arrived[0], kept_y, sent_y))
            size = grad_blocks[0].shape[0]
            (summed,) = run(
                functools.partial(sum_kernel, 4), [((size, width), BF16)], arrived, micros=0.5
            )
            sent_rest, own1 = lax.optimization_barrier((sent_rest, own1, summed))[:2]
        other1 = tensor_swap(own1, 1)
        grad_tokens, small = run(
            last_norm_kernel,
            [((rows, width), BF16), ((small_rows, width), F32)],
            [ids, own1, other1, tokens, d_middle, ln1_gain, small2],
            scratch=[((rows, width), F32)],
            micros=0.01,
        )
        chip_y = (kept_y.astype(F32) + tensor_swap(sent_y, 1).astype(F32)).astype(BF16)
        own_y = (chip_y.astype(F32) + tensor_swap(chip_y, 2).astype(F32)).astype(BF16)
        grad_up, grad_down = run(
            join_grad_kernel,
            [((half, hidden_width), F32), ((hidden_width, half), F32)],
            [grad_kept, came_first, came_next, dp_swap(sent_rest)],
            scratch=[((width, width), BF16)],
            micros=2,
        )
        if small_slice:
            (ready,) = run(
                pair_kernel,
                [((size + small_rows, width), BF16)],
                [summed, expert_swap(summed, 2), small, expert_swap(small, 2)],
                micros=1,
            )
            everything = [quarter_swap(ready, m) for m in (3, 1, 2)]
            ready, grad_up, grad_down = lax.optimization_barrier((ready, grad_up, grad_down))
            everything = [ready] + everything
            grad_qkv, grad_out, *sums, grad_router = run(
                functools.partial(spread_kernel, (0, 3, 1, 2)),
                [((3 * inner, width), F32), ((inner, width), F32)]
                + [((width,), F32)] * 4
                + [((experts, width), F32)],
                [ids] + everything,
                scratch=[((4 * inner, width), F32), ((4, small_rows, width), F32)],
                micros=3,
            )
        else:
            grads = lax.psum(grad_blocks[0], ("expert", "dp")).astype(F32)
            grad_qkv, grad_out = grads[: 3 * inner], grads[3 * inner :]
            small_sum = lax.psum(small, ("expert", "dp"))
            sums, grad_router = list(small_sum[:4]), small_sum[8 : 8 + experts]

        mix_own, mix_other = own_y, tensor_swap(own_y, 1)
        mixture = jnp.where(
            rank % 2 == 0,
            jnp.concatenate([mix_own, mix_other], axis=1),
            jnp.concatenate([mix_other, mix_own], axis=1),
        )[:rows].astype(F32)
        alive = (jnp.arange(rows, dtype=jnp.int32) < images_live[0] * SEQ)[:, None]
        out = jnp.where(alive, middle + mixture, 0.0).astype(BF16)
        return (
            out,
            grad_tokens,
            sums[0],
            sums[1],
            grad_qkv.reshape(3, inner, width).transpose(2, 0, 1),
            grad_out,
            sums[2],
            sums[3],
            grad_router.T,
            grad_up[None],
            grad_down[None],
        )

    return body


def solution(mesh):
    in_specs = (
        P(("expert", "dp"), None),
        P(("expert", "dp"), None),
        P(("expert", "dp")),
        P(),
        P(),
        P(None, None, "tensor"),
        P("tensor", None),
        P(),
        P(),
        P(),
        P("expert", None, "tensor"),
        P("expert", "tensor", None),
        P(("expert", "dp"), None),
    )
    out_specs = (
        P(("expert", "dp"), None),
        P(("expert", "dp"), None),
        P(),
        P(),
        P(None, None, "tensor"),
        P("tensor", None),
        P(),
        P(),
        P(),
        P("expert", "dp", "tensor"),
        P("expert", "tensor", "dp"),
    )
    body = make_body(mesh.shape["tensor"], mesh.shape["expert"], mesh.shape["dp"])
    return jax.shard_map(body, mesh=mesh, in_specs=in_specs, out_specs=out_specs, check_vma=False)
```
